32 devices in a mesh: dp: 4 (over y, core), seq: 8 (over z, x).
Axes of the slice: x: 2, y: 2, z: 4, core: 2. Of those that a mesh axis runs over, the one named last changes fastest.
Arguments:
- latents: bfloat16 [2, 4, 2048, 16], P(None, 'dp', 'seq'), may hold values from -6 to 6
- noise: bfloat16 [2, 4, 2048, 16], P(None, 'dp', 'seq'), may hold values from -6 to 6
- captions: bfloat16 [2, 4, 960, 4096], P(None, 'dp', 'seq'), may hold values from -6 to 6
- image_sizes: int32 [2, 4, 8], replicated, may hold values from 0 to 1024, as said below
- caption_lengths: int32 [2, 4, 8], replicated, may hold values from 1 to 120
- timesteps: int32 [2, 4, 8], replicated, may hold values from 0 to 999
- weights: float32 [32000, 1152], P(('dp', 'seq'))
- vectors: float32 [78, 1152], replicated
- weights_m: float32 [32000, 1152], P(('dp', 'seq')), may hold values from -2.0861626e-07 to 2.0861626e-07
- weights_v: float32 [32000, 1152], P(('dp', 'seq')), may hold values from 1.082431e-16 to 4.329724e-16
- vectors_m: float32 [78, 1152], replicated, may hold values from -8.34465e-07 to 8.34465e-07
- vectors_v: float32 [78, 1152], replicated, may hold values from 1.7318896e-15 to 6.9275585e-15
Outputs:
- new_weights: float32 [32000, 1152], P(('dp', 'seq'))
- new_weights_m: float32 [32000, 1152], P(('dp', 'seq'))
- new_weights_v: float32 [32000, 1152], P(('dp', 'seq'))
- new_vectors: float32 [78, 1152], replicated
- new_vectors_m: float32 [78, 1152], replicated
- new_vectors_v: float32 [78, 1152], replicated
- loss_sum: float32 [], replicated
- image_count: float32 [], replicated
- grad_norm: float32 [], replicated
- down_bias_grad: float32 [1152], replicated
The draws below stay inside these ranges and needn't reach their ends.
Inputs may be any that keep to these rules, and one draw needn't show every extreme that they name: `image_sizes`: in each row the first slots hold 256 or 1024, the rest 0; each row sums to 2048; every draw has an image of 1024 patches.
All inputs are finite; a program needn't handle non-finite values.
Results may differ from the reference program's by a relative error of at most 0.0062.
The reference program's roundings to bfloat16 on the way count: a program that leaves them out, or rounds other values in their place, can miss the bound.
Values may be sent and summed in bfloat16 or wider, within the bound.
A program may use at most 512 MiB of HBM per device.

```python
import math
import jax
import jax.numpy as jnp
from jax import lax

EMBED_DIMENSION = 1152
HEADS = 16
FF = 4608
TEXT_W = 4096
FREQ = 256
CAP = 120
SIDE = 16
PATCH = 16
MICRO = 2
STEP = 10
HEAD_DIM = 72
SMALL_IMG = 256
IMG = 8
ROWSET = 2048
ROWSETS = 4
ROWS_W = 32000
VROWS = 78
NPARAM = 36953856


def draw_weights(key, part):
    key = jax.random.fold_in(key, 11)
    segments = ((FREQ, FREQ ** (-0.5)), (EMBED_DIMENSION, EMBED_DIMENSION ** (-0.5)), (6 * EMBED_DIMENSION, EMBED_DIMENSION ** (-0.5)), (TEXT_W, TEXT_W ** (-0.5)), (EMBED_DIMENSION, EMBED_DIMENSION ** (-0.5)), (3 * EMBED_DIMENSION, EMBED_DIMENSION ** (-0.5)), (EMBED_DIMENSION, 8.0 * EMBED_DIMENSION ** (-0.5)), (EMBED_DIMENSION, EMBED_DIMENSION ** (-0.5)), (2 * EMBED_DIMENSION, EMBED_DIMENSION ** (-0.5)), (EMBED_DIMENSION, 4.0 * EMBED_DIMENSION ** (-0.5)), (FF, EMBED_DIMENSION ** (-0.5)), (FF, FF ** (-0.5)))
    scales = jnp.concatenate([jnp.full((number,), value, jnp.float32) for number, value in segments])
    return jax.random.normal(key, (ROWS_W, EMBED_DIMENSION), jnp.float32) * scales[:, None]


def draw_vectors(key, part):
    key = jax.random.fold_in(key, 12)
    rest = VROWS - 8 - 3 * PATCH
    scales = jnp.concatenate([jnp.full((8,), 0.3, jnp.float32), jnp.full((PATCH,), PATCH ** (-0.5), jnp.float32), jnp.full((2 * PATCH,), EMBED_DIMENSION ** (-0.5), jnp.float32), jnp.full((rest,), 0.1, jnp.float32)])
    offsets = jnp.zeros((VROWS,), jnp.float32).at[2].set(1.0).at[5].set(1.0)
    return jax.random.normal(key, (VROWS, EMBED_DIMENSION), jnp.float32) * scales[:, None] + offsets[:, None]


def draw_image_sizes(key, part):
    key = jax.random.fold_in(key, 13)
    first_key, second_key = jax.random.split(key)
    most_large = IMG // 4
    rowsets = jnp.arange(ROWSETS, dtype=jnp.int32)
    base = most_large * (ROWSETS - 1 - rowsets) // max(ROWSETS - 1, 1)
    jitter = jax.random.randint(first_key, (MICRO, ROWSETS), -1, 2)
    large = jnp.clip(base[None, :] + jitter, 0, most_large).astype(jnp.int32)
    large = large.at[:, 0].set(jnp.maximum(large[:, 0], 1))
    filled = IMG - 3 * large
    slots = jnp.arange(IMG, dtype=jnp.int32)
    scores = jax.random.randint(second_key, (MICRO, ROWSETS, IMG), 0, 1 << 20) * IMG + slots
    inside = slots[None, None, :] < filled[:, :, None]
    lower = (scores[..., None, :] < scores[..., :, None]) & inside[..., None, :]
    rank = jnp.sum(lower.astype(jnp.int32), axis=-1)
    is_large = inside & (rank < large[:, :, None])
    units = jnp.where(inside, jnp.where(is_large, 4, 1), 0)
    return (units * SMALL_IMG).astype(jnp.int32)


def draw_caption_lengths(key, part):
    key = jax.random.fold_in(key, 14)
    first_key, second_key = jax.random.split(key)
    lengths = jax.random.randint(first_key, (MICRO, ROWSETS, IMG), 1, CAP + 1)
    chosen = jax.random.randint(second_key, (MICRO, ROWSETS, 1), 0, IMG)
    slots = jnp.arange(IMG, dtype=jnp.int32)[None, None, :]
    return jnp.where(slots == chosen, CAP, lengths).astype(jnp.int32)


def touch_ends(array, key, low, high):
    longest = array.shape.index(max(array.shape))
    spots = []
    for shift in (0, 1):
        where = [jax.random.randint(jax.random.fold_in(key, axis), (), 0, length) for axis, length in enumerate(array.shape)]
        where[longest] = (where[longest] + shift) % array.shape[longest]
        spots.append(tuple(where))
    return array.at[spots[0]].set(low).at[spots[1]].set(high)


def shard_levels(rng, extent, shards, smallest, largest):
    def one(dim, parts):
        steps = jax.random.uniform(jax.random.fold_in(jax.random.fold_in(rng, 6), dim), (parts,), jnp.float32, smallest / len(shards), largest / len(shards))
        return jnp.repeat(jnp.exp(steps), extent[dim] // parts).reshape((-1,) + (1,) * (len(extent) - dim - 1))

    level = one(*shards[0])
    for cut in shards[1:]:
        level = level * one(*cut)
    return level


def centred(stream_key, extent, deviation, reach, cuts=(), kind=jnp.bfloat16):
    factor_of = shard_levels(stream_key, extent, cuts, -0.22, 0.18) if cuts else 1.0
    drawn = jax.random.normal(stream_key, extent, jnp.float32) * deviation * factor_of
    return jnp.minimum(jnp.maximum(drawn, -reach), reach).astype(kind)


def setup_inputs(seed: int = 0) -> dict:
    key_of = jax.random.split(jax.random.key(seed), 13)
    return {
        "latents": centred(key_of[0], (MICRO, ROWSETS, ROWSET, PATCH), 1.0, 6.0, ((1, 4), (2, 8))),
        "noise": centred(key_of[1], (MICRO, ROWSETS, ROWSET, PATCH), 1.0, 6.0, ((1, 4), (2, 8))),
        "captions": centred(key_of[2], (MICRO, ROWSETS, IMG * CAP, TEXT_W), 1.0, 6.0, ((1, 4), (2, 8))),
        "image_sizes": draw_image_sizes(jax.random.fold_in(key_of[12], 71), 0),
        "caption_lengths": draw_caption_lengths(jax.random.fold_in(key_of[12], 71), 0),
        "timesteps": touch_ends(jax.random.randint(key_of[5], (MICRO, ROWSETS, IMG), 0, 1000), jax.random.fold_in(key_of[5], 1), 0, 999).astype(jnp.int32),
        "weights": draw_weights(jax.random.fold_in(key_of[12], 71), 0),
        "vectors": draw_vectors(jax.random.fold_in(key_of[12], 71), 0),
        "weights_m": centred(key_of[8], (ROWS_W, EMBED_DIMENSION), (0.000222 * NPARAM ** -0.5), 2.086162567138672e-07, ((0, 32),), jnp.float32),
        "weights_v": jnp.clip(jnp.exp(math.log(4.3297240534316236e-16) - 1.3862944 * jax.random.uniform(key_of[9], (ROWS_W, EMBED_DIMENSION), jnp.float32) ** shard_levels(key_of[9], (ROWS_W, EMBED_DIMENSION), ((0, 32),), -0.2, 0.2)), 1.0824310133579059e-16, 4.3297240534316236e-16),
        "vectors_m": centred(key_of[10], (VROWS, EMBED_DIMENSION), (0.00089 * NPARAM ** -0.5), 8.344650268554688e-07, (), jnp.float32),
        "vectors_v": jnp.clip(jnp.exp(jax.random.uniform(key_of[11], (VROWS, EMBED_DIMENSION), jnp.float32, math.log(1.7318896213726494e-15), math.log(6.927558485490598e-15))), 1.7318896213726494e-15, 6.927558485490598e-15),
    }


exact_arithmetic_mode = lax.Precision.HIGHEST
clip_norm = 0.002
contrastive_sharpness_divisor = 0.1
beta_one = 0.9
beta_two = 0.999
adam_eps = 1e-08
weight_decay = 0.01
rate_matrix = 0.05
rate_vector = 0.3
norm_eps = 1e-06
neg_large = -1e+30

@jax.custom_vjp
def low(v):
    return lax.optimization_barrier(v.astype(jnp.bfloat16)).astype(jnp.float32)

@jax.custom_vjp
def low_back(v):
    return v

def low_keep(v):
    return (low(v), None)

def low_pass(kept, grad):
    return (grad,)

def back_keep(v):
    return (v, None)

def back_low(kept, grad):
    return (low(grad),)
low.defvjp(low_keep, low_pass)
low_back.defvjp(back_keep, back_low)

def matrix_layout(width):
    return (('time_one', FREQ), ('time_two', width), ('time_block', 6 * width), ('text_one', TEXT_W), ('text_two', width), ('joint_qkv', 3 * width), ('self_out', width), ('cross_query', width), ('cross_kv', 2 * width), ('cross_out', width), ('mlp_up', FF), ('mlp_down', FF))

def vector_layout(width):
    return (('table', 6), ('final_table', 2), ('patch_in', PATCH), ('patch_out', 2 * PATCH), ('bias_patch', 1), ('bias_time_one', 1), ('bias_time_two', 1), ('bias_block', 6), ('bias_text_one', 1), ('bias_text_two', 1), ('bias_query', 1), ('bias_value', 1), ('bias_self_out', 1), ('bias_cross_query', 1), ('bias_cross_value', 1), ('bias_cross_out', 1), ('bias_up', FF // width), ('bias_down', 1))

def split_rows(whole, layout):
    pieces = {}
    offset = 0
    for label, number in layout:
        pieces[label] = whole[offset:offset + number]
        offset = offset + number
    return pieces

def modulate(hidden, shift, scale):
    centre = hidden - lax.optimization_barrier(jnp.mean(hidden, axis=-1, keepdims=True))
    normed = centre * lax.rsqrt(lax.optimization_barrier(jnp.mean(centre * centre, axis=-1, keepdims=True)) + norm_eps)
    return normed * (1.0 + scale) + shift

def gelu_tanh(values):
    return jax.nn.gelu(values, approximate=True)

def position_table(along_rows, along_cols, width):
    quarter = width // 4
    omega = 1.0 / 10000.0 ** (jnp.arange(quarter, dtype=jnp.float32) / quarter)
    first = along_rows.astype(jnp.float32)[:, None] * omega[None, :]
    second = along_cols.astype(jnp.float32)[:, None] * omega[None, :]
    return jnp.concatenate([jnp.sin(first), jnp.cos(first), jnp.sin(second), jnp.cos(second)], axis=1)

def time_features(steps_now):
    half_size = FREQ // 2
    frequency = jnp.exp(-math.log(10000.0) * jnp.arange(half_size, dtype=jnp.float32) / half_size)
    angles = steps_now.astype(jnp.float32)[:, None] * frequency[None, :]
    return jnp.concatenate([jnp.cos(angles), jnp.sin(angles)], axis=1)

def noise_level(steps_now):
    phase = (steps_now.astype(jnp.float32) / 1000.0 + 0.008) / 1.008 * (math.pi / 2.0)
    return jnp.cos(phase) ** 2

def variance_logs(level, level_prev):
    beta_now = jnp.minimum(1.0 - level / level_prev, 0.999)
    tilde_log = jnp.log(beta_now * (1.0 - level_prev) / (1.0 - level))
    return (jnp.log(beta_now), tilde_log)

def variance_term(raw, beta_log, tilde_log):
    frac = (raw + 1.0) * 0.5
    model_log = frac * beta_log[:, None] + (1.0 - frac) * tilde_log[:, None]
    return 0.5 * (model_log - tilde_log[:, None] - 1.0 + jnp.exp(tilde_log[:, None] - model_log)) / math.log(2.0)

def lin(inputs, matrix, rows_out):
    product = jnp.dot(low(inputs), matrix.T if rows_out else matrix, precision=exact_arithmetic_mode)
    return low_back(product)

def head_attention(queries, keys, values, allowed):
    scale = HEAD_DIM ** (-0.5)

    def split_heads(tensor):
        return tensor.reshape(tensor.shape[0], HEADS, HEAD_DIM).transpose(1, 0, 2)

    def one_head(triple):
        query_head, key_head, value_head = triple
        scores = low_back(jnp.dot(query_head, key_head.T, precision=exact_arithmetic_mode)) * scale
        probs = jax.nn.softmax(jnp.where(allowed, scores, neg_large), axis=-1)
        return low_back(jnp.dot(low(probs), value_head, precision=exact_arithmetic_mode))
    mixed = lax.map(jax.checkpoint(one_head), (split_heads(queries), split_heads(keys), split_heads(values)))
    return mixed.transpose(1, 0, 2).reshape(queries.shape[0], EMBED_DIMENSION)

def rowset_forward(mats, vecs, clean, target, caption_rows, sizes, lengths, steps_now):
    ends = jnp.cumsum(sizes).astype(jnp.int32)
    starts = (ends - sizes).astype(jnp.int32)
    place = jnp.arange(ROWSET, dtype=jnp.int32)
    segment = lax.optimization_barrier(jnp.sum((ends[None, :] <= place[:, None]).astype(jnp.int32), axis=1)).astype(jnp.int32)
    patch_size = jnp.take(sizes, segment)
    within = place - jnp.take(starts, segment)
    side = jnp.where(patch_size == 4 * SMALL_IMG, 2 * SIDE, SIDE).astype(jnp.int32)
    position = position_table(within // side, within % side, EMBED_DIMENSION)
    level = jnp.take(noise_level(steps_now), segment)
    level_prev = jnp.take(noise_level(steps_now - 1), segment)
    beta_log, tilde_log = variance_logs(level, level_prev)
    noisy = jnp.sqrt(level)[:, None] * clean + jnp.sqrt(1.0 - level)[:, None] * target
    time_first = lin(time_features(steps_now), mats['time_one'], False) + vecs['bias_time_one'][0]
    time_embed = lin(jax.nn.silu(time_first), mats['time_two'], False) + vecs['bias_time_two'][0]
    block_mod = lin(jax.nn.silu(time_embed), mats['time_block'], True) + vecs['bias_block'].reshape(-1)
    patch_mod = jnp.take(vecs['table'].reshape(-1)[None, :] + block_mod, segment, axis=0)
    shift_one, scale_one, gate_one, shift_two, scale_two, gate_two = jnp.split(patch_mod, 6, axis=1)
    final_mod = jnp.take((vecs['final_table'][None, :, :] + time_embed[:, None, :]).reshape(IMG, 2 * EMBED_DIMENSION), segment, axis=0)
    shift_final, scale_final = jnp.split(final_mod, 2, axis=1)
    hidden_zero = jnp.dot(noisy, vecs['patch_in'], precision=exact_arithmetic_mode) + vecs['bias_patch'][0] + position
    joint = lin(modulate(hidden_zero, shift_one, scale_one), mats['joint_qkv'], True)
    queries = low(joint[:, :EMBED_DIMENSION] + vecs['bias_query'][0])
    keys = low(joint[:, EMBED_DIMENSION:2 * EMBED_DIMENSION])
    values = low(joint[:, 2 * EMBED_DIMENSION:] + vecs['bias_value'][0])
    same = segment[:, None] == segment[None, :]
    attended = lin(head_attention(queries, keys, values, same), mats['self_out'], False) + vecs['bias_self_out'][0]
    hidden_one = hidden_zero + gate_one * attended
    text = lin(gelu_tanh(lin(caption_rows, mats['text_one'], False) + vecs['bias_text_one'][0]), mats['text_two'], False) + vecs['bias_text_two'][0]
    text_kv = lin(text, mats['cross_kv'], True)
    key_text = low(text_kv[:, :EMBED_DIMENSION])
    value_text = low(text_kv[:, EMBED_DIMENSION:] + vecs['bias_cross_value'][0])
    cross_q = low(lin(hidden_one, mats['cross_query'], False) + vecs['bias_cross_query'][0])
    key_image = jnp.arange(IMG * CAP, dtype=jnp.int32) // CAP
    key_place = jnp.arange(IMG * CAP, dtype=jnp.int32) % CAP
    allowed = (segment[:, None] == key_image[None, :]) & (key_place < jnp.take(lengths, key_image))[None, :]
    crossed = lin(head_attention(cross_q, key_text, value_text, allowed), mats['cross_out'], False) + vecs['bias_cross_out'][0]
    hidden_two = hidden_one + crossed
    upward = lin(modulate(hidden_two, shift_two, scale_two), mats['mlp_up'], True) + vecs['bias_up'].reshape(-1)
    feed = lin(gelu_tanh(upward), mats['mlp_down'], False) + vecs['bias_down'][0]
    hidden_three = hidden_two + gate_two * feed
    final_normed = modulate(hidden_three, shift_final, scale_final)
    predicted = jnp.dot(final_normed, vecs['patch_out'].T, precision=exact_arithmetic_mode)
    error = predicted[:, :PATCH] - target
    spread = variance_term(predicted[:, PATCH:], beta_log, tilde_log)
    error_weight = 1.0 / (float(PATCH) * patch_size.astype(jnp.float32))
    squared = jnp.sum((error * error + spread) * error_weight[:, None])
    onehot = (segment[:, None] == jnp.arange(IMG, dtype=jnp.int32)[None, :]).astype(jnp.float32)
    image_pool = jnp.dot(onehot.T, final_normed, precision=exact_arithmetic_mode) / jnp.maximum(sizes.astype(jnp.float32), 1.0)[:, None]
    token_live = (jnp.arange(CAP, dtype=jnp.int32)[None, :] < lengths[:, None]).astype(jnp.float32)
    caption_pool = lax.optimization_barrier(jnp.sum(text.reshape(IMG, CAP, EMBED_DIMENSION) * token_live[:, :, None], axis=1)) / lengths.astype(jnp.float32)[:, None]
    return (squared, image_pool, caption_pool)

def unit_length_vectors(tensor):
    return tensor * lax.rsqrt(lax.optimization_barrier(jnp.sum(tensor * tensor, axis=-1, keepdims=True)) + norm_eps)

def contrast_loss(averaged_picture_features, averaged_description_features, sizes):
    valid = sizes.reshape(-1) > 0
    pairwise_cosine_scores = jnp.dot(unit_length_vectors(averaged_picture_features.reshape(-1, EMBED_DIMENSION)), unit_length_vectors(averaged_description_features.reshape(-1, EMBED_DIMENSION)).T, precision=exact_arithmetic_mode) / contrastive_sharpness_divisor
    pairwise_cosine_scores = jnp.where(valid[None, :], pairwise_cosine_scores, neg_large)
    logsum = jax.nn.logsumexp(pairwise_cosine_scores, axis=-1)
    return jnp.sum(jnp.where(valid, logsum - jnp.diagonal(pairwise_cosine_scores), 0.0))

def adamw(param, grad, first, second, rate, decay):
    first_new = beta_one * first + (1.0 - beta_one) * grad
    second_new = beta_two * second + (1.0 - beta_two) * grad * grad
    step_dir = first_new / (1.0 - beta_one ** STEP) / (jnp.sqrt(second_new / (1.0 - beta_two ** STEP)) + adam_eps)
    return (param - rate * (step_dir + decay * param), first_new, second_new)

def reference(latents, noise, captions, image_sizes, caption_lengths, timesteps, weights, vectors, weights_m, weights_v, vectors_m, vectors_v):

    def total_loss(matrix_all, vector_all):
        mats = split_rows(low(matrix_all), matrix_layout(EMBED_DIMENSION))
        vecs = split_rows(low(vector_all), vector_layout(EMBED_DIMENSION))
        total = jnp.zeros((), jnp.float32)

        def one_rowset(inputs):
            clean, target, caption_rows, sizes, lengths, steps_now = inputs
            return rowset_forward(mats, vecs, clean, target, caption_rows, sizes, lengths, steps_now)
        for micro in range(MICRO):
            errors, averaged_picture_features, averaged_description_features = lax.map(jax.checkpoint(one_rowset), (latents[micro].astype(jnp.float32), noise[micro].astype(jnp.float32), captions[micro].astype(jnp.float32), image_sizes[micro], caption_lengths[micro], timesteps[micro]))
            total = total + jnp.sum(errors) + contrast_loss(averaged_picture_features, averaged_description_features, image_sizes[micro])
        return total
    loss_sum, pullback = jax.vjp(total_loss, weights, vectors)
    image_count = jnp.sum((image_sizes > 0).astype(jnp.float32))
    grad_w, grad_v = pullback(1.0 / image_count)
    down_bias_grad = grad_v[VROWS - 1]
    grad_norm = jnp.sqrt(jnp.sum(grad_w * grad_w) + jnp.sum(grad_v * grad_v))
    factor = jnp.minimum(1.0, clip_norm / (grad_norm + 1e-06))
    new_w, first_w, second_w = adamw(weights, grad_w * factor, weights_m, weights_v, rate_matrix, weight_decay)
    new_v, first_v, second_v = adamw(vectors, grad_v * factor, vectors_m, vectors_v, rate_vector, 0.0)
    return (new_w, first_w, second_w, new_v, first_v, second_v, loss_sum, image_count, grad_norm, down_bias_grad)
```

```python
import functools
import math

import jax
import jax.numpy as jnp
from jax import lax
from jax.experimental import pallas as pl
from jax.experimental.pallas import tpu as pltpu
from jax.sharding import PartitionSpec as P

HEADS = 16
FF = 4608
TEXT_W = 4096
FREQ = 256
CAP = 120
CAP_PAD = 128
SIDE = 16
PATCH = 16
MICRO = 2
STEP = 10
BLOCK = 256
LARGE = 1024
VMEM_BYTES = 56 * 1024 * 1024

exact = lax.Precision.HIGHEST
clip_norm = 0.002
contrastive_sharpness_divisor = 0.1
beta_one = 0.9
beta_two = 0.999
adam_eps = 1e-08
weight_decay = 0.01
rate_matrix = 0.05
rate_vector = 0.3
norm_eps = 1e-06
neg_large = -1e30
log_two = math.log(2.0)
both_axes = ("dp", "seq")


def matrix_rows(width):
    return (FREQ, width, 6 * width, TEXT_W, width, 3 * width, width, width, 2 * width, width, FF, FF)


def vector_rows(width):
    return (6, 2, PATCH, 2 * PATCH, 1, 1, 1, 6, 1, 1, 1, 1, 1, 1, 1, 1, FF // width, 1)


def split_rows(whole, rows):
    pieces = []
    offset = 0
    for number in rows:
        pieces.append(whole[offset : offset + number])
        offset = offset + number
    return pieces


def device_index():
    return lax.axis_index("dp") * lax.axis_size("seq") + lax.axis_index("seq")


def modulate(hidden, shift, scale):
    centre = hidden - jnp.mean(hidden, axis=-1, keepdims=True)
    normed = centre * lax.rsqrt(jnp.mean(centre * centre, axis=-1, keepdims=True) + norm_eps)
    return normed * (1.0 + scale) + shift


def gelu_tanh(values):
    return jax.nn.gelu(values, approximate=True)


def time_features(steps_now):
    half_size = FREQ // 2
    frequency = jnp.exp(-math.log(10000.0) * jnp.arange(half_size, dtype=jnp.float32) / half_size)
    angles = steps_now.astype(jnp.float32)[:, None] * frequency[None, :]
    return jnp.concatenate([jnp.cos(angles), jnp.sin(angles)], axis=1)


def noise_level(steps_now):
    phase = (steps_now.astype(jnp.float32) / 1000.0 + 0.008) / 1.008 * (math.pi / 2.0)
    return jnp.cos(phase) ** 2


def variance_logs(level, level_prev):
    beta_now = jnp.minimum(1.0 - level / level_prev, 0.999)
    tilde_log = jnp.log(beta_now * (1.0 - level_prev) / (1.0 - level))
    return (jnp.log(beta_now), tilde_log)


def dot_nn(left, right):
    return lax.dot_general(left, right, (((1,), (0,)), ((), ())), preferred_element_type=jnp.float32)


def dot_nt(left, right):
    return lax.dot_general(left, right, (((1,), (1,)), ((), ())), preferred_element_type=jnp.float32)


def dot_tn(left, right):
    return lax.dot_general(left, right, (((0,), (0,)), ((), ())), preferred_element_type=jnp.float32)


def low(values):
    return values.astype(jnp.bfloat16)


def self_forward_kernel(heads, dim, start_ref, big_ref, qkv_ref, out_ref, key_s, value_s):
    micro = pl.program_id(0)
    blocks = qkv_ref.shape[0]
    scale = dim ** (-0.5)
    for b in range(blocks):
        for h in range(heads):
            rows = pl.ds(b * BLOCK, BLOCK)
            key_s[h, rows, :] = qkv_ref[b, 0, :, (heads + h) * dim : (heads + h + 1) * dim]
            value_s[h, rows, :] = qkv_ref[b, 0, :, (2 * heads + h) * dim : (2 * heads + h + 1) * dim]

    def one_block(b, carry):
        start = pl.multiple_of(start_ref[micro, b] * BLOCK, BLOCK)
        queries = qkv_ref[b, 0]

        def go(span):
            outs = []
            for h in range(heads):
                key = key_s[h, pl.ds(start, span), :]
                value = value_s[h, pl.ds(start, span), :]
                scores = dot_nt(queries[:, h * dim : (h + 1) * dim], key) * scale
                top = jnp.max(scores, axis=-1, keepdims=True)
                weight = jnp.exp(scores - top)
                total = jnp.sum(weight, axis=-1, keepdims=True)
                probs = low(weight * (1.0 / total))
                outs.append(low(dot_nn(probs, value)))
            out_ref[b, 0] = jnp.concatenate(outs, axis=-1)

        big = big_ref[micro, b]

        @pl.when(big == 1)
        def _():
            go(LARGE)

        @pl.when(big == 0)
        def _():
            go(BLOCK)

        return carry

    lax.fori_loop(0, blocks, one_block, 0)


def self_forward(start, big, qkv, heads, dim):
    blocks, micros = qkv.shape[0], qkv.shape[1]
    span = blocks * BLOCK
    return pl.pallas_call(
        functools.partial(self_forward_kernel, heads, dim),
        out_shape=jax.ShapeDtypeStruct((blocks, micros, BLOCK, heads * dim), jnp.bfloat16),
        grid_spec=pltpu.PrefetchScalarGridSpec(
            num_scalar_prefetch=2,
            grid=(micros,),
            in_specs=[pl.BlockSpec((blocks, 1, BLOCK, 3 * heads * dim), lambda m, s, g: (0, m, 0, 0))],
            out_specs=pl.BlockSpec((blocks, 1, BLOCK, heads * dim), lambda m, s, g: (0, m, 0, 0)),
            scratch_shapes=[
                pltpu.VMEM((heads, span, dim), jnp.bfloat16),
                pltpu.VMEM((heads, span, dim), jnp.bfloat16),
            ],
        ),
        compiler_params=pltpu.CompilerParams(vmem_limit_bytes=VMEM_BYTES),
    )(start, big, qkv)


def self_backward_kernel(
    heads, dim, start_ref, big_ref, qkv_ref, grad_ref, out_ref, sum_ref, key_s, value_s, dq_s, dk_s, dv_s
):
    micro = pl.program_id(0)
    blocks = qkv_ref.shape[0]
    scale = dim ** (-0.5)
    for b in range(blocks):
        for h in range(heads):
            rows = pl.ds(b * BLOCK, BLOCK)
            key_s[h, rows, :] = qkv_ref[b, 0, :, (heads + h) * dim : (heads + h + 1) * dim]
            value_s[h, rows, :] = qkv_ref[b, 0, :, (2 * heads + h) * dim : (2 * heads + h + 1) * dim]
    dk_s[...] = jnp.zeros_like(dk_s)
    dv_s[...] = jnp.zeros_like(dv_s)

    def one_block(b, carry):
        start = pl.multiple_of(start_ref[micro, b] * BLOCK, BLOCK)
        place = pl.multiple_of(b * BLOCK, BLOCK)
        queries = qkv_ref[b, 0]
        grads = grad_ref[b, 0]

        def go(span):
            keep = pl.ds(start, span)
            for h in range(heads):
                query = queries[:, h * dim : (h + 1) * dim]
                grad = grads[:, h * dim : (h + 1) * dim]
                key = key_s[h, keep, :]
                value = value_s[h, keep, :]
                scores = dot_nt(key, query) * scale
                top = jnp.max(scores, axis=0, keepdims=True)
                weight = jnp.exp(scores - top)
                probs = weight * (1.0 / jnp.sum(weight, axis=0, keepdims=True))
                dv_s[h, keep, :] += dot_nn(low(probs), grad)
                grad_probs = dot_nt(value, grad)
                inner = jnp.sum(probs * grad_probs, axis=0, keepdims=True)
                grad_scores = low(probs * (grad_probs - inner) * scale)
                dk_s[h, keep, :] += dot_nn(grad_scores, query)
                dq_s[h, pl.ds(place, BLOCK), :] = dot_tn(grad_scores, key)

        big = big_ref[micro, b]

        @pl.when(big == 1)
        def _():
            go(LARGE)

        @pl.when(big == 0)
        def _():
            go(BLOCK)

        return carry

    lax.fori_loop(0, blocks, one_block, 0)
    for b in range(blocks):
        rows = pl.ds(b * BLOCK, BLOCK)
        out_ref[b, 0] = jnp.concatenate(
            [low(part[h, rows, :]) for part in (dq_s, dk_s, dv_s) for h in range(heads)], axis=-1
        )
    sum_ref[0] = jnp.concatenate(
        [jnp.sum(part[h], axis=0, keepdims=True) for part in (dq_s, dv_s) for h in range(heads)], axis=-1
    )


def self_backward(start, big, qkv, grad, heads, dim):
    blocks, micros = qkv.shape[0], qkv.shape[1]
    span = blocks * BLOCK
    wide = pltpu.VMEM((heads, span, dim), jnp.float32)
    narrow = pltpu.VMEM((heads, span, dim), jnp.bfloat16)
    return pl.pallas_call(
        functools.partial(self_backward_kernel, heads, dim),
        out_shape=(
            jax.ShapeDtypeStruct((blocks, micros, BLOCK, 3 * heads * dim), jnp.bfloat16),
            jax.ShapeDtypeStruct((micros, 1, 2 * heads * dim), jnp.float32),
        ),
        grid_spec=pltpu.PrefetchScalarGridSpec(
            num_scalar_prefetch=2,
            grid=(micros,),
            in_specs=[
                pl.BlockSpec((blocks, 1, BLOCK, 3 * heads * dim), lambda m, s, g: (0, m, 0, 0)),
                pl.BlockSpec((blocks, 1, BLOCK, heads * dim), lambda m, s, g: (0, m, 0, 0)),
            ],
            out_specs=(
                pl.BlockSpec((blocks, 1, BLOCK, 3 * heads * dim), lambda m, s, g: (0, m, 0, 0)),
                pl.BlockSpec((1, 1, 2 * heads * dim), lambda m, s, g: (m, 0, 0)),
            ),
            scratch_shapes=[narrow, narrow, wide, wide, wide],
        ),
        compiler_params=pltpu.CompilerParams(vmem_limit_bytes=VMEM_BYTES),
    )(start, big, qkv, grad)


def cross_forward_kernel(dim, length_ref, query_ref, key_ref, value_ref, out_ref):
    length = length_ref[pl.program_id(0)]
    scale = dim ** (-0.5)
    live = lax.broadcasted_iota(jnp.int32, (BLOCK, CAP_PAD), 1) < length
    outs = []
    for h in range(HEADS):
        part = slice(h * dim, (h + 1) * dim)
        scores = jnp.where(live, dot_nt(query_ref[0, :, part], key_ref[0, :, part]) * scale, neg_large)
        weight = jnp.exp(scores - jnp.max(scores, axis=-1, keepdims=True))
        probs = low(weight * (1.0 / jnp.sum(weight, axis=-1, keepdims=True)))
        outs.append(low(dot_nn(probs, value_ref[0, :, part])))
    out_ref[0] = jnp.concatenate(outs, axis=-1)


def cross_backward_kernel(
    dim, length_ref, query_ref, key_ref, value_ref, grad_ref, dq_ref, dk_ref, dv_ref
):
    length = length_ref[pl.program_id(0)]
    scale = dim ** (-0.5)
    live = lax.broadcasted_iota(jnp.int32, (CAP_PAD, BLOCK), 0) < length
    dq, dk, dv = [], [], []
    for h in range(HEADS):
        part = slice(h * dim, (h + 1) * dim)
        query, key, value, grad = (
            query_ref[0, :, part],
            key_ref[0, :, part],
            value_ref[0, :, part],
            grad_ref[0, :, part],
        )
        scores = jnp.where(live, dot_nt(key, query) * scale, neg_large)
        weight = jnp.exp(scores - jnp.max(scores, axis=0, keepdims=True))
        probs = weight * (1.0 / jnp.sum(weight, axis=0, keepdims=True))
        dv.append(dot_nn(low(probs), grad))
        grad_probs = dot_nt(value, grad)
        inner = jnp.sum(probs * grad_probs, axis=0, keepdims=True)
        grad_scores = low(probs * (grad_probs - inner) * scale)
        dk.append(dot_nn(grad_scores, query))
        dq.append(dot_tn(grad_scores, key))
    dq_ref[0] = jnp.concatenate(dq, axis=-1)
    dk_ref[0] = jnp.concatenate(dk, axis=-1)
    dv_ref[0] = jnp.concatenate(dv, axis=-1)


def cross_call(kernel, length, arrays, outs):
    def spec(array):
        return pl.BlockSpec((1,) + array.shape[1:], lambda m, s: (m, 0, 0))

    return pl.pallas_call(
        kernel,
        out_shape=outs,
        grid_spec=pltpu.PrefetchScalarGridSpec(
            num_scalar_prefetch=1,
            grid=(MICRO,),
            in_specs=[spec(array) for array in arrays],
            out_specs=jax.tree.map(spec, outs),
        ),
        compiler_params=pltpu.CompilerParams(vmem_limit_bytes=VMEM_BYTES),
    )(length, *arrays)


UNIT = 8
SPLIT = 640
PIECE = 3
TILE = 96
TILE_START = 1024
LAG = 2
RING = LAG + 1
MESH = pl.DeviceIdType.MESH


def my_place():
    row, seq = lax.axis_index("dp"), lax.axis_index("seq")
    return lax.div(row, 2), lax.rem(row, 2), lax.div(seq, 2), lax.rem(seq, 2)


def peer(y, core, z, x):
    return (y * 2 + core, z * 2 + x)


def greet_all(devices, seq_count):
    me = lax.axis_index("dp") * seq_count + lax.axis_index("seq")
    barrier = pltpu.get_barrier_semaphore()

    def one(step, carry):
        other = lax.rem(me + step, devices)
        pl.semaphore_signal(
            barrier,
            inc=1,
            device_id=(lax.div(other, seq_count), lax.rem(other, seq_count)),
            device_id_type=MESH,
        )
        return carry

    lax.fori_loop(1, devices, one, 0)
    pl.semaphore_wait(barrier, devices - 1)


def global_tile(ranges, index):
    tile = index + ranges[0][0]
    at = ranges[0][1] - ranges[0][0]
    for start, stop in ranges[1:]:
        tile = jnp.where(index >= at, index - at + start, tile)
        at += stop - start
    return tile


def reduce_kernel(
    ranges,
    shard_units,
    devices,
    sources,
    receivers,
    *refs,
):
    rows_refs, refs = refs[: len(sources)], list(refs[len(sources) :])
    if receivers:
        block_ref, all_ref = refs.pop(0), refs.pop(1)
        refs, push_sems = refs[:-3], refs[-3:]
    (
    out_ref,
    own_s,
    core_s,
    first_s,
    second_s,
    first_y_s,
    second_x_s,
    first_two_s,
    second_two_s,
    first_x_s,
    second_y_s,
    third_s,
    along_s,
    leaf_s,
    load_sem,
    core_send,
    core_recv,
    one_send,
    one_recv,
    two_send,
    two_recv,
    z_send,
    z_recv,
    leaf_send,
    leaf_recv,
    ) = refs
    tiles = core_s.shape[0]
    seq_count = devices // 4
    y, core, z, x = my_place()
    me = (y * 2 + core) * seq_count + z * 2 + x
    place = ((core * 2 + y) * 2 + x) * 4 + z
    half, quarter, eighth = TILE // 2, TILE // 4, TILE // 8
    across_core = peer(y, 1 - core, z, x)
    across_y = peer(1 - y, core, z, x)
    across_x = peer(y, core, z, 1 - x)

    def remote(source, target, send, recv, device):
        return pltpu.make_async_remote_copy(
            src_ref=source,
            dst_ref=target,
            send_sem=send,
            recv_sem=recv,
            device_id=device,
            device_id_type=MESH,
        )

    def core_copy(t, rows_ref=None, start=0):
        source = own_s.at[0] if rows_ref is None else rows_ref.at[pl.ds(start, half)]
        return remote(source, core_s.at[t], core_send.at[t], core_recv.at[t], across_core)

    def load(t, rows_ref=None, start=0):
        slot = lax.rem(t, 2)
        source = rows_refs[-1] if rows_ref is None else rows_ref
        return pltpu.make_async_copy(
            source.at[pl.ds(start, half)], own_s.at[slot], load_sem.at[slot]
        )

    def start_from(copy, t, side):
        index = t * 2 + side
        at = 0
        for rows_ref, (start, count) in zip(rows_refs, sources):

            @pl.when((index >= at) & (index < at + count))
            def _(rows_ref=rows_ref, start=start, at=at):
                copy(t, rows_ref, start + (index - at) * half).start()

            at += count

    def first_one(t):
        return remote(
            first_s.at[lax.rem(t, RING), pl.ds((1 - y) * quarter, quarter)],
            first_y_s.at[t],
            one_send.at[lax.rem(t, RING), 0],
            one_recv.at[t, 0],
            across_y,
        )

    def second_one(t, side):
        return remote(
            second_s.at[lax.rem(t, RING), pl.ds(side * quarter + (1 - x) * eighth, eighth)],
            second_x_s.at[t, pl.ds(side * eighth, eighth)],
            one_send.at[lax.rem(t, RING), 1 + side],
            one_recv.at[t, 1 + side],
            across_x,
        )

    def first_two(t):
        return remote(
            first_two_s.at[lax.rem(t, RING), pl.ds((1 - x) * eighth, eighth)],
            first_x_s.at[t],
            two_send.at[lax.rem(t, RING), 0],
            two_recv.at[t, 0],
            across_x,
        )

    def second_two(t):
        return remote(
            second_two_s.at[lax.rem(t, RING), pl.ds((1 - y) * eighth, eighth)],
            second_y_s.at[t],
            two_send.at[lax.rem(t, RING), 1],
            two_recv.at[t, 1],
            across_y,
        )

    def z_copy(t, distance):
        other = z ^ distance
        return remote(
            third_s.at[lax.rem(t, RING), pl.ds(other * PIECE, PIECE)],
            along_s.at[t, distance - 1],
            z_send.at[lax.rem(t, RING), distance - 1],
            z_recv.at[t, distance - 1],
            peer(y, core, other, x),
        )

    def add(count, step, target, *sources):
        def one(index, carry):
            at = index * step
            total = sources[0](at, step).astype(jnp.float32)
            for source in sources[1:]:
                total = total + source(at, step).astype(jnp.float32)
            target(at, step, total.astype(jnp.bfloat16))
            return carry

        lax.fori_loop(0, count // step, one, 0)

    def leaf_send_all(t, stage):
        unit = TILE_START + global_tile(ranges, t) * TILE + place * PIECE
        owner = lax.div(unit, shard_units)
        at = unit - owner * shard_units

        def go(part, count, slot, holder):
            source = leaf_s.at[t, pl.ds(part, count)]
            target = out_ref.at[pl.ds(slot, count)]
            sending = remote(
                source,
                target,
                leaf_send.at[t, part],
                leaf_recv.at[slot],
                (lax.div(holder, seq_count), lax.rem(holder, seq_count)),
            )

            @pl.when(holder != me)
            def _():
                if stage == 0:
                    sending.start()
                else:
                    sending.wait_send()

            if stage == 0:

                @pl.when(holder == me)
                def _():
                    pltpu.make_async_copy(source, target, leaf_recv.at[slot]).start()

        together = at + PIECE <= shard_units

        @pl.when(together)
        def _():
            go(0, PIECE, at, owner)

        @pl.when(jnp.logical_not(together))
        def _():
            for part in range(PIECE):
                over = at + part >= shard_units
                go(
                    part,
                    1,
                    jnp.where(over, at + part - shard_units, at + part),
                    jnp.where(over, owner + 1, owner),
                )

    for t in range(min(2, tiles)):
        start_from(load, t, core)
    greet_all(devices, seq_count)

    def start_core(t, carry):
        start_from(core_copy, t, 1 - core)
        return carry

    lax.fori_loop(0, tiles, start_core, 0)
    if receivers:
        start_push(block_ref, all_ref, devices, receivers, me, *push_sems)

    def one_step(step, carry):
        @pl.when(step < tiles)
        def _():
            t = step
            slot = lax.rem(t, RING)
            load(t).wait()
            core_copy(t).wait_recv()

            def one(index, inner):
                at = pl.ds(index * 4, 4)
                total = own_s[lax.rem(t, 2), at].astype(jnp.float32) + core_s[t, at].astype(jnp.float32)
                total = total.astype(jnp.bfloat16)
                first_s[slot, at] = total[:, :, :SPLIT]
                second_s[slot, at] = total[:, :, SPLIT:]
                return inner

            lax.fori_loop(0, half // 4, one, 0)
            first_one(t).start()
            second_one(t, 0).start()
            second_one(t, 1).start()

            @pl.when(t + 2 < tiles)
            def _():
                start_from(load, t + 2, core)

        @pl.when((step >= LAG) & (step < tiles + LAG))
        def _():
            t = step - LAG
            slot = lax.rem(t, RING)
            first_one(t).wait()

            def one(index, inner):
                at = pl.ds(index * 4, 4)
                mine = first_s[slot, pl.ds(y * quarter + index * 4, 4)].astype(jnp.float32)
                total = mine + first_y_s[t, at].astype(jnp.float32)
                first_two_s[slot, at] = total.astype(jnp.bfloat16)
                return inner

            lax.fori_loop(0, quarter // 4, one, 0)
            first_two(t).start()
            for side in range(2):
                second_one(t, side).wait()

                def two(index, inner):
                    mine = second_s[slot, pl.ds(side * quarter + x * eighth + index * 4, 4)]
                    at = pl.ds(side * eighth + index * 4, 4)
                    total = mine.astype(jnp.float32) + second_x_s[t, at].astype(jnp.float32)
                    second_two_s[slot, at] = total.astype(jnp.bfloat16)
                    return inner

                lax.fori_loop(0, eighth // 4, two, 0)
            second_two(t).start()

        @pl.when((step >= 2 * LAG) & (step < tiles + 2 * LAG))
        def _():
            t = step - 2 * LAG
            slot = lax.rem(t, RING)
            first_two(t).wait()
            second_two(t).wait()

            def one(index, inner):
                at = pl.ds(index * 4, 4)
                mine = first_two_s[slot, pl.ds(x * eighth + index * 4, 4)].astype(jnp.float32)
                total = mine + first_x_s[t, at].astype(jnp.float32)
                third_s[slot, at, :, :SPLIT] = total.astype(jnp.bfloat16)
                mine = second_two_s[slot, pl.ds(y * eighth + index * 4, 4)].astype(jnp.float32)
                total = mine + second_y_s[t, at].astype(jnp.float32)
                third_s[slot, at, :, SPLIT:] = total.astype(jnp.bfloat16)
                return inner

            lax.fori_loop(0, eighth // 4, one, 0)
            for distance in (1, 2, 3):
                z_copy(t, distance).start()

        @pl.when(step >= 3 * LAG)
        def _():
            t = step - 3 * LAG
            slot = lax.rem(t, RING)
            for distance in (1, 2, 3):
                z_copy(t, distance).wait()
            total = third_s[slot, pl.ds(z * PIECE, PIECE)].astype(jnp.float32)
            for distance in (1, 2, 3):
                total = total + along_s[t, distance - 1].astype(jnp.float32)
            leaf_s[t] = total.astype(jnp.bfloat16)
            leaf_send_all(t, 0)

        return carry

    lax.fori_loop(0, tiles + 3 * LAG, one_step, 0)

    def finish(t, carry):
        core_copy(t).wait_send()
        leaf_send_all(t, 1)
        return carry

    lax.fori_loop(0, tiles, finish, 0)
    if receivers:
        finish_push(block_ref, all_ref, devices, receivers, me, *push_sems)
    far = TILE_START - TILE * (TILE_START // TILE)
    begin = me * shard_units
    first_at = lax.rem(PIECE - lax.rem(begin + PIECE - far % PIECE, PIECE), PIECE)

    def arrive(index, count):
        unit = begin + index
        inside = False
        for start, stop in ranges:
            low_end, high_end = TILE_START + start * TILE, TILE_START + stop * TILE
            inside = inside | ((unit >= low_end) & (unit < high_end))

        @pl.when(inside)
        def _():
            part = out_ref.at[pl.ds(index, count)]
            pltpu.make_async_copy(part, part, leaf_recv.at[index]).wait()

    def arrive_three(step, carry):
        index = first_at + step * PIECE

        @pl.when(index + PIECE <= shard_units)
        def _():
            arrive(index, PIECE)

        return carry

    steps = shard_units // PIECE
    lax.fori_loop(0, steps, arrive_three, 0)
    covered = first_at + lax.div(shard_units - first_at, PIECE) * PIECE
    for step in range(PIECE - 1):

        @pl.when(step < first_at)
        def _():
            arrive(step, 1)

        @pl.when(covered + step < shard_units)
        def _():
            arrive(covered + step, 1)


def push_copy(block_ref, all_ref, devices, me, step, send_sem, recv_sem):
    seq_count = devices // 4
    other = lax.rem(me + step, devices)
    return other, pltpu.make_async_remote_copy(
        src_ref=block_ref,
        dst_ref=all_ref.at[me],
        send_sem=send_sem.at[step],
        recv_sem=recv_sem.at[me],
        device_id=(lax.div(other, seq_count), lax.rem(other, seq_count)),
        device_id_type=MESH,
    )


def start_push(block_ref, all_ref, devices, receivers, me, send_sem, recv_sem, keep_sem):
    @pl.when(me < receivers)
    def _():
        pltpu.make_async_copy(block_ref, all_ref.at[me], keep_sem).start()

    def send(step, carry):
        other, sending = push_copy(block_ref, all_ref, devices, me, step, send_sem, recv_sem)

        @pl.when(other < receivers)
        def _():
            sending.start()

        return carry

    lax.fori_loop(1, devices, send, 0)


def finish_push(block_ref, all_ref, devices, receivers, me, send_sem, recv_sem, keep_sem):
    @pl.when(me < receivers)
    def _():
        pltpu.make_async_copy(block_ref, all_ref.at[me], keep_sem).wait()

    def finish(step, carry):
        other, sending = push_copy(block_ref, all_ref, devices, me, step, send_sem, recv_sem)

        @pl.when(other < receivers)
        def _():
            sending.wait_send()

        source = lax.rem(me + devices - step, devices)

        @pl.when(me < receivers)
        def _():
            pltpu.make_async_copy(block_ref, all_ref.at[source], recv_sem.at[source]).wait()

        return carry

    lax.fori_loop(1, devices, finish, 0)


def push_sems(devices):
    dma = pltpu.SemaphoreType.DMA
    return [dma((devices,)), dma((devices,)), dma]


def reduce_rows(ranges, shard_units, devices, collective_id, pieces, block=None, receivers=0):
    tiles = sum(stop - start for start, stop in ranges)
    width = pieces[0][0].shape[1]
    sources = tuple(piece[1:] for piece in pieces)
    assert sum(count for _, count in sources) == 2 * tiles
    half, quarter, eighth = TILE // 2, TILE // 4, TILE // 8
    rest = width - SPLIT

    def vmem(*shape):
        return pltpu.VMEM(shape, jnp.bfloat16)

    dma = pltpu.SemaphoreType.DMA
    blocks = [] if block is None else [block]
    outs = [jax.ShapeDtypeStruct((shard_units, UNIT, width), jnp.bfloat16)]
    outs += [jax.ShapeDtypeStruct((devices,) + one.shape, one.dtype) for one in blocks]
    out = pl.pallas_call(
        functools.partial(reduce_kernel, ranges, shard_units, devices, sources, receivers),
        out_shape=outs,
        in_specs=[pl.BlockSpec(memory_space=pl.ANY)] * (len(pieces) + len(blocks)),
        out_specs=[pl.BlockSpec(memory_space=pl.ANY)] * len(outs),
        scratch_shapes=[
            vmem(2, half, UNIT, width),
            vmem(tiles, half, UNIT, width),
            vmem(RING, half, UNIT, SPLIT),
            vmem(RING, half, UNIT, rest),
            vmem(tiles, quarter, UNIT, SPLIT),
            vmem(tiles, quarter, UNIT, rest),
            vmem(RING, quarter, UNIT, SPLIT),
            vmem(RING, quarter, UNIT, rest),
            vmem(tiles, eighth, UNIT, SPLIT),
            vmem(tiles, eighth, UNIT, rest),
            vmem(RING, eighth, UNIT, width),
            vmem(tiles, 3, PIECE, UNIT, width),
            vmem(tiles, PIECE, UNIT, width),
            dma((2,)),
            dma((tiles,)),
            dma((tiles,)),
            dma((RING, 3)),
            dma((tiles, 3)),
            dma((RING, 2)),
            dma((tiles, 2)),
            dma((RING, 3)),
            dma((tiles, 3)),
            dma((tiles, PIECE)),
            dma((shard_units,)),
        ]
        + (push_sems(devices) if blocks else []),
        compiler_params=pltpu.CompilerParams(
            collective_id=collective_id, has_side_effects=True, vmem_limit_bytes=VMEM_BYTES
        ),
    )(*[piece[0].reshape(-1, UNIT, width) for piece in pieces], *blocks)
    return out if blocks else out[0]


STRIDE = 3
Z_LAG = 2
Z_RING = 3 * Z_LAG + 1


def gather_kernel(
    openings,
    ahead,
    devices,
    shard_ref,
    out_ref,
    later_ref,
    deal_send,
    deal_recv,
    z_send,
    z_recv,
    one_send,
    one_recv,
    two_send,
    two_recv,
    core_send,
    core_recv,
):
    shard_units = shard_ref.shape[0]
    seq_count = devices // 4
    width = shard_ref.shape[2]
    tiles = out_ref.shape[0] // TILE
    later_tiles = later_ref.shape[0] // TILE
    streams = ((openings[0], tiles, out_ref, 0), (openings[1], later_tiles, later_ref, tiles))
    y, core, z, x = my_place()
    me = (y * 2 + core) * seq_count + z * 2 + x
    half, quarter, eighth = TILE // 2, TILE // 4, TILE // 8
    leaves = TILE // PIECE
    upward = peer(y, core, jnp.minimum(z + 1, 3), x)
    downward = peer(y, core, jnp.maximum(z - 1, 0), x)

    def bounds(stream):
        begin = me * shard_units - stream[0]
        finish = begin + shard_units
        return begin, finish, lax.div(begin + PIECE - 1, PIECE), lax.div(finish, PIECE)

    def deal_some(stream, stage, three, part, count):
        begin = bounds(stream)[0]
        ref = stream[2]
        tile = lax.div(three, leaves)
        leaf = three - tile * leaves
        eight = lax.div(leaf, 4)
        slot = leaf - eight * 4 if count == PIECE else 4 + part
        holder_core = lax.div(eight, 4)
        holder_y = lax.rem(lax.div(eight, 2), 2)
        holder_x = lax.rem(eight, 2)
        holder = (holder_y * 2 + holder_core) * seq_count + z * 2 + holder_x
        index = three * PIECE + part - begin
        source = shard_ref.at[pl.ds(index, count)]
        target = ref.at[pl.ds(three * PIECE + part, count)]
        recv = deal_recv.at[stream[3] + tile, slot]
        sending = pltpu.make_async_remote_copy(
            src_ref=source,
            dst_ref=target,
            send_sem=deal_send.at[0 if stream[3] == 0 else 1, index],
            recv_sem=recv,
            device_id=peer(holder_y, holder_core, z, holder_x),
            device_id_type=MESH,
        )

        @pl.when(holder != me)
        def _():
            if stage == 0:
                sending.start()
            else:
                sending.wait_send()

        if stage == 0:

            @pl.when(holder == me)
            def _():
                pltpu.make_async_copy(source, target, recv).start()

    def deal_between(stream, stage, low_three, count, base):
        begin, finish, first_three, last_three = bounds(stream)
        base = first_three if base is None else base

        @pl.when((low_three <= last_three) & (low_three + count >= first_three))
        def _():
            def one(step, carry):
                three = base + step

                @pl.when(
                    (three >= first_three)
                    & (three < last_three)
                    & (three >= low_three)
                    & (three < low_three + count)
                )
                def _():
                    deal_some(stream, stage, three, 0, PIECE)

                return carry

            lax.fori_loop(0, min(count, shard_units // PIECE + 1), one, 0)
            for step in range(PIECE - 1):
                three = first_three - 1
                here = (three >= low_three) & (three < low_three + count)

                @pl.when(here & (begin + step < first_three * PIECE))
                def _(three=three):
                    deal_some(stream, stage, three, begin + step - three * PIECE, 1)

                three = last_three
                here = (three >= low_three) & (three < low_three + count)

                @pl.when(here & (three * PIECE + step < finish))
                def _(three=three):
                    deal_some(stream, stage, three, step, 1)

    def deal_tile(stream, step):
        low_three = tile_at(step, stream[1]) * leaves
        deal_between(stream, 0, low_three, leaves, low_three)

    def each_three(stream, t, visit):
        def one(index, carry):
            row = t * TILE + ((core * 2 + y) * 2 + x) * eighth + index * PIECE
            unit = stream[0] + row
            owner = lax.div(unit, shard_units)
            at = unit - owner * shard_units

            @pl.when(at + PIECE <= shard_units)
            def _():
                visit(row, index, PIECE, lax.rem(lax.div(owner, 2), 4))

            @pl.when(at + PIECE > shard_units)
            def _():
                for part in range(PIECE):
                    holder = jnp.where(at + part >= shard_units, owner + 1, owner)
                    visit(row + part, 4 + part, 1, lax.rem(lax.div(holder, 2), 4))

            return carry

        lax.fori_loop(0, eighth // PIECE, one, 0)

    def wait_units(ref, count, sem):
        part = ref.at[pl.ds(0, count)]
        pltpu.make_async_copy(part, part, sem).wait()

    def z_copy(stream, step, row, slot, count, way):
        part = stream[2].at[pl.ds(row, count)]
        which = 0 if stream[3] == 0 else 1
        return pltpu.make_async_remote_copy(
            src_ref=part,
            dst_ref=part,
            send_sem=z_send.at[which, lax.rem(step, Z_RING), slot, way],
            recv_sem=z_recv.at[stream[3] + tile_at(step, stream[1]), slot],
            device_id=(upward, downward)[way],
            device_id_type=MESH,
        )

    def along_z(stream, step, distance):
        t = tile_at(step, stream[1])

        def visit(row, slot, count, owner_z):
            @pl.when(jnp.abs(owner_z - z) == distance)
            def _():
                sem = deal_recv if distance == 0 else z_recv
                wait_units(out_ref, count, sem.at[stream[3] + t, slot])

                @pl.when((owner_z <= z) & (z < 3))
                def _():
                    z_copy(stream, step, row, slot, count, 0).start()

                @pl.when((owner_z >= z) & (z > 0))
                def _():
                    z_copy(stream, step, row, slot, count, 1).start()

        each_three(stream, t, visit)

    def along_z_done(stream, step):
        t = tile_at(step, stream[1])

        def visit(row, slot, count, owner_z):
            @pl.when((owner_z <= z) & (z < 3))
            def _():
                z_copy(stream, step, row, slot, count, 0).wait_send()

            @pl.when((owner_z >= z) & (z > 0))
            def _():
                z_copy(stream, step, row, slot, count, 1).wait_send()

        each_three(stream, t, visit)

    def z_stage(stream, step):
        for distance in range(4):
            old = step - distance * Z_LAG

            @pl.when((old >= 0) & (old < stream[1]))
            def _(old=old, distance=distance):
                along_z(stream, old, distance)
                if distance == 3:
                    along_z_done(stream, old)

    spreading = spread_steps(
        out_ref, one_send, one_recv, two_send, two_recv, core_send, core_recv
    )
    main, late = streams
    greet_all(devices, seq_count)
    for step in range(min(ahead, tiles)):
        deal_tile(main, step)
    for step in range(min(ahead, later_tiles)):
        deal_tile(late, step)

    def one_step(step, carry):
        @pl.when(step + ahead < tiles)
        def _():
            deal_tile(main, step + ahead)

        @pl.when(step + ahead < later_tiles)
        def _():
            deal_tile(late, step + ahead)

        z_stage(main, step)
        spreading(step - 3 * Z_LAG)
        z_stage(late, step)
        return carry

    lax.fori_loop(0, tiles + 3 * LAG + 3 * Z_LAG, one_step, 0)
    for stream in streams:
        deal_between(stream, 1, 0, stream[1] * leaves, None)


def tile_at(step, tiles):
    return lax.rem(step * STRIDE, tiles)


def spread_steps(out_ref, one_send, one_recv, two_send, two_recv, core_send, core_recv):
    tiles = out_ref.shape[0] // TILE
    width = out_ref.shape[2]
    y, core, z, x = my_place()
    half, quarter, eighth = TILE // 2, TILE // 4, TILE // 8
    left, right = pl.ds(0, SPLIT), pl.ds(SPLIT, width - SPLIT)
    whole = pl.ds(0, width)
    across_core = peer(y, 1 - core, z, x)
    across_y = peer(1 - y, core, z, x)
    across_x = peer(y, core, z, 1 - x)

    def remote(start, count, columns, send, recv, device):
        part = out_ref.at[pl.ds(start, count), :, columns]
        return pltpu.make_async_remote_copy(
            src_ref=part,
            dst_ref=part,
            send_sem=send,
            recv_sem=recv,
            device_id=device,
            device_id_type=MESH,
        )

    def block(t, y_at, x_at):
        return t * TILE + ((core * 2 + y_at) * 2 + x_at) * eighth

    def one_first(step):
        t = tile_at(step, tiles)
        sems = (one_send.at[lax.rem(step, RING), 0], one_recv.at[t, 0])
        return remote(block(t, y, x), eighth, left, *sems, across_x)

    def one_second(step):
        t = tile_at(step, tiles)
        sems = (one_send.at[lax.rem(step, RING), 1], one_recv.at[t, 1])
        return remote(block(t, y, x), eighth, right, *sems, across_y)

    def two_first(step):
        t = tile_at(step, tiles)
        sems = (two_send.at[lax.rem(step, RING), 0], two_recv.at[t, 0])
        return remote(block(t, y, 0), quarter, left, *sems, across_y)

    def two_second(step, side):
        t = tile_at(step, tiles)
        sems = (two_send.at[lax.rem(step, RING), 1 + side], two_recv.at[t, 1 + side])
        return remote(block(t, side, x), eighth, right, *sems, across_x)

    def core_copy(step):
        t = tile_at(step, tiles)
        sems = (core_send.at[lax.rem(step, RING)], core_recv.at[t])
        return remote(t * TILE + core * half, half, whole, *sems, across_core)

    def go(step):
        @pl.when((step >= 0) & (step < tiles))
        def _():
            one_first(step).start()
            one_second(step).start()

        @pl.when((step >= LAG) & (step < tiles + LAG))
        def _():
            old = step - LAG
            one_first(old).wait()
            two_first(old).start()
            one_second(old).wait()
            for side in range(2):
                two_second(old, side).start()

        @pl.when((step >= 2 * LAG) & (step < tiles + 2 * LAG))
        def _():
            old = step - 2 * LAG
            two_first(old).wait()
            for side in range(2):
                two_second(old, side).wait()
            core_copy(old).start()

        @pl.when(step >= 3 * LAG)
        def _():
            core_copy(step - 3 * LAG).wait()

    return go


def spread_sems(tiles):
    dma = pltpu.SemaphoreType.DMA
    return [
        dma((RING, 2)),
        dma((tiles, 2)),
        dma((RING, 3)),
        dma((tiles, 3)),
        dma((RING,)),
        dma((tiles,)),
    ]


def spread_kernel(devices, rows_ref, block_ref, out_ref, all_ref, *sems):
    seq_count = devices // 4
    me = lax.axis_index("dp") * seq_count + lax.axis_index("seq")
    sems, push = sems[:-3], sems[-3:]
    greet_all(devices, seq_count)
    start_push(block_ref, all_ref, devices, devices, me, *push)
    spreading = spread_steps(out_ref, *sems)

    def one_step(step, carry):
        spreading(step)
        return carry

    lax.fori_loop(0, out_ref.shape[0] // TILE + 3 * LAG, one_step, 0)
    finish_push(block_ref, all_ref, devices, devices, me, *push)


def spread_rows(rows, block, devices, collective_id):
    return pl.pallas_call(
        functools.partial(spread_kernel, devices),
        out_shape=(
            jax.ShapeDtypeStruct(rows.shape, rows.dtype),
            jax.ShapeDtypeStruct((devices,) + block.shape, block.dtype),
        ),
        in_specs=[pl.BlockSpec(memory_space=pl.ANY)] * 2,
        out_specs=(pl.BlockSpec(memory_space=pl.ANY), pl.BlockSpec(memory_space=pl.ANY)),
        scratch_shapes=spread_sems(rows.shape[0] // TILE) + push_sems(devices),
        input_output_aliases={0: 0},
        compiler_params=pltpu.CompilerParams(
            collective_id=collective_id, has_side_effects=True, vmem_limit_bytes=VMEM_BYTES
        ),
    )(rows, block)


def gather_rows(openings, counts, ahead, devices, collective_id, shard):
    units, _, width = shard.shape
    assert all(count % STRIDE for count in counts) and counts[1] <= counts[0]
    dma = pltpu.SemaphoreType.DMA
    anywhere = pl.BlockSpec(memory_space=pl.ANY)
    return pl.pallas_call(
        functools.partial(gather_kernel, openings, ahead, devices),
        out_shape=[
            jax.ShapeDtypeStruct((count * TILE, UNIT, width), jnp.bfloat16) for count in counts
        ],
        in_specs=[anywhere],
        out_specs=[anywhere, anywhere],
        scratch_shapes=[
            dma((2, units)),
            dma((sum(counts), 7)),
            dma((2, Z_RING, 7, 2)),
            dma((sum(counts), 7)),
        ]
        + spread_sems(counts[0]),
        compiler_params=pltpu.CompilerParams(
            collective_id=collective_id, has_side_effects=True, vmem_limit_bytes=VMEM_BYTES
        ),
    )(shard)


def share_kernel(devices, block_ref, out_ref, *sems):
    seq_count = devices // 4
    me = lax.axis_index("dp") * seq_count + lax.axis_index("seq")
    greet_all(devices, seq_count)
    start_push(block_ref, out_ref, devices, devices, me, *sems)
    finish_push(block_ref, out_ref, devices, devices, me, *sems)


def share(block, devices, collective_id):
    return pl.pallas_call(
        functools.partial(share_kernel, devices),
        out_shape=jax.ShapeDtypeStruct((devices,) + block.shape, block.dtype),
        in_specs=[pl.BlockSpec(memory_space=pltpu.VMEM)],
        out_specs=pl.BlockSpec(memory_space=pltpu.VMEM),
        scratch_shapes=push_sems(devices),
        compiler_params=pltpu.CompilerParams(
            collective_id=collective_id, has_side_effects=True, vmem_limit_bytes=16 * 1024 * 1024
        ),
    )(block)


def sum_kernel(devices, parts_ref, out_ref, extra_ref, got_s, part_s, send_sem, recv_sem, keep_sem, *sems):
    seq_count = devices // 4
    me = lax.axis_index("dp") * seq_count + lax.axis_index("seq")
    keep = pltpu.make_async_copy(parts_ref.at[me], got_s.at[me], keep_sem)
    keep.start()
    greet_all(devices, seq_count)

    def scatter(step):
        other = lax.rem(me + step, devices)
        return pltpu.make_async_remote_copy(
            src_ref=parts_ref.at[other],
            dst_ref=got_s.at[me],
            send_sem=send_sem.at[step],
            recv_sem=recv_sem.at[me],
            device_id=(lax.div(other, seq_count), lax.rem(other, seq_count)),
            device_id_type=MESH,
        )

    def start(step, carry):
        scatter(step).start()
        return carry

    def finish(step, carry):
        scatter(step).wait_send()
        source = lax.rem(me + devices - step, devices)
        pltpu.make_async_copy(parts_ref.at[0], got_s.at[source], recv_sem.at[source]).wait()
        return carry

    lax.fori_loop(1, devices, start, 0)
    keep.wait()
    lax.fori_loop(1, devices, finish, 0)
    total = jnp.sum(got_s[...], axis=0)
    part_s[...] = total[:-1]
    extra_ref[...] = total[-1]
    start_push(part_s, out_ref, devices, devices, me, *sems)
    finish_push(part_s, out_ref, devices, devices, me, *sems)


def sum_all(array, extra, devices, collective_id):
    tile = 8 * 128
    count = -(-array.size // (tile * devices))
    flat = jnp.pad(array.reshape(-1), (0, count * tile * devices - array.size))
    parts = flat.reshape(devices, count, 8, 128)
    parts = jnp.concatenate([parts, jnp.full((devices, 1, 8, 128), extra)], axis=1)
    vmem = pl.BlockSpec(memory_space=pltpu.VMEM)
    out, total = pl.pallas_call(
        functools.partial(sum_kernel, devices),
        out_shape=(
            jax.ShapeDtypeStruct((devices, count, 8, 128), jnp.float32),
            jax.ShapeDtypeStruct((8, 128), jnp.float32),
        ),
        in_specs=[vmem],
        out_specs=(vmem, vmem),
        scratch_shapes=[
            pltpu.VMEM((devices, count + 1, 8, 128), jnp.float32),
            pltpu.VMEM((count, 8, 128), jnp.float32),
        ]
        + push_sems(devices)
        + push_sems(devices),
        compiler_params=pltpu.CompilerParams(
            collective_id=collective_id, has_side_effects=True, vmem_limit_bytes=16 * 1024 * 1024
        ),
    )(parts)
    return out.reshape(-1)[: array.size].reshape(array.shape), total[0, 0]


def contrast_kernel(pooled_ref, pick_ref, row_ref, col_ref, scale_ref, pool_ref, text_ref, loss_ref):
    count = pick_ref.shape[1]
    scale = scale_ref[0, 0] / contrastive_sharpness_divisor
    diagonal = lax.broadcasted_iota(jnp.int32, (count, count), 0) == lax.broadcasted_iota(
        jnp.int32, (count, count), 1
    )
    loss = jnp.zeros((1, 1), jnp.float32)
    for m in range(MICRO):
        row = row_ref[m]
        col = col_ref[m] > 0.0
        image = jnp.dot(
            pick_ref[m], pooled_ref[m], precision=exact, preferred_element_type=jnp.float32
        )
        words = pooled_ref[MICRO + m]
        image_norm = lax.rsqrt(jnp.sum(image * image, axis=-1, keepdims=True) + norm_eps)
        words_norm = lax.rsqrt(jnp.sum(words * words, axis=-1, keepdims=True) + norm_eps)
        image = image * image_norm
        words = words * words_norm
        cosines = lax.dot_general(
            image,
            words,
            (((1,), (1,)), ((), ())),
            precision=exact,
            preferred_element_type=jnp.float32,
        )
        cosines = jnp.where(col, cosines / contrastive_sharpness_divisor, neg_large)
        top = jnp.max(cosines, axis=-1, keepdims=True)
        weight = jnp.exp(cosines - top)
        total = jnp.sum(weight, axis=-1, keepdims=True)
        matched = jnp.sum(jnp.where(diagonal, cosines, 0.0), axis=-1, keepdims=True)
        lost = jnp.where(row > 0.0, top + jnp.log(total) - matched, 0.0)
        loss = loss + jnp.sum(lost, axis=0, keepdims=True)
        grad = weight / total - jnp.where(diagonal, 1.0, 0.0)
        grad = jnp.where((row > 0.0) & col, grad * scale, 0.0)
        grad_image = jnp.dot(grad, words, precision=exact, preferred_element_type=jnp.float32)
        grad_words = lax.dot_general(
            grad,
            image,
            (((0,), (0,)), ((), ())),
            precision=exact,
            preferred_element_type=jnp.float32,
        )
        inner = jnp.sum(image * grad_image, axis=-1, keepdims=True)
        pool_ref[m] = image_norm * (grad_image - image * inner)
        inner = jnp.sum(words * grad_words, axis=-1, keepdims=True)
        text_ref[m] = words_norm * (grad_words - words * inner)
    loss_ref[...] = jnp.broadcast_to(loss, loss_ref.shape)


def contrast(pooled, pick, valid, scale):
    count, width = pooled.shape[1], pooled.shape[2]
    grads = jax.ShapeDtypeStruct((MICRO, count, width), jnp.float32)
    return pl.pallas_call(
        contrast_kernel,
        out_shape=(grads, grads, jax.ShapeDtypeStruct((1, 128), jnp.float32)),
        compiler_params=pltpu.CompilerParams(vmem_limit_bytes=VMEM_BYTES),
    )(pooled, pick, valid[:, :, None], valid[:, None, :], scale.reshape(1, 1))


def joint_forward_kernel(rows_ref, matrix_ref, bias_ref, out_ref):
    part, width = matrix_ref.shape[2], matrix_ref.shape[3]
    matrix = matrix_ref[...].reshape(3 * part, width)
    out_ref[0] = low(dot_nt(rows_ref[...], matrix) + bias_ref[0])


def joint_forward(rows, matrix, bias):
    count, width = rows.shape
    groups, _, columns = bias.shape
    return pl.pallas_call(
        joint_forward_kernel,
        out_shape=jax.ShapeDtypeStruct((groups, count, columns), jnp.bfloat16),
        grid=(groups,),
        in_specs=[
            pl.BlockSpec((count, width), lambda j: (0, 0)),
            pl.BlockSpec((3, 1, columns // 3, width), lambda j: (0, j, 0, 0)),
            pl.BlockSpec((1, 1, columns), lambda j: (j, 0, 0)),
        ],
        out_specs=pl.BlockSpec((1, count, columns), lambda j: (j, 0, 0)),
        compiler_params=pltpu.CompilerParams(vmem_limit_bytes=VMEM_BYTES),
    )(rows, matrix.reshape(3, groups, columns // 3, width), bias)


def joint_backward_kernel(grad_ref, matrix_ref, rows_ref, out_ref, weight_ref):
    part, width = matrix_ref.shape[2], matrix_ref.shape[3]
    grad = grad_ref[0]
    term = dot_nn(grad, matrix_ref[...].reshape(3 * part, width))
    weight_ref[...] = low(dot_tn(grad, rows_ref[...])).reshape(3, 1, part, width)

    @pl.when(pl.program_id(0) == 0)
    def _():
        out_ref[...] = term

    @pl.when(pl.program_id(0) > 0)
    def _():
        out_ref[...] += term


def joint_backward(grad, matrix, rows):
    groups, count, columns = grad.shape
    width = rows.shape[1]
    part = columns // 3
    out, weight = pl.pallas_call(
        joint_backward_kernel,
        out_shape=(
            jax.ShapeDtypeStruct((count, width), jnp.float32),
            jax.ShapeDtypeStruct((3, groups, part, width), jnp.bfloat16),
        ),
        grid=(groups,),
        in_specs=[
            pl.BlockSpec((1, count, columns), lambda j: (j, 0, 0)),
            pl.BlockSpec((3, 1, part, width), lambda j: (0, j, 0, 0)),
            pl.BlockSpec((count, width), lambda j: (0, 0)),
        ],
        out_specs=(
            pl.BlockSpec((count, width), lambda j: (0, 0)),
            pl.BlockSpec((3, 1, part, width), lambda j: (0, j, 0, 0)),
        ),
        compiler_params=pltpu.CompilerParams(vmem_limit_bytes=VMEM_BYTES),
    )(grad, matrix.reshape(3, groups, part, width), rows)
    return out, weight.reshape(3 * groups * part, width)


def adamw(param, grad, first, second, rate, decay):
    first_new = beta_one * first + (1.0 - beta_one) * grad
    second_new = beta_two * second + (1.0 - beta_two) * grad * grad
    step_dir = (
        first_new
        / (1.0 - beta_one**STEP)
        / (jnp.sqrt(second_new / (1.0 - beta_two**STEP)) + adam_eps)
    )
    return (param - rate * (step_dir + decay * param), first_new, second_new)


def per_device(
    latents,
    noise,
    captions,
    image_sizes,
    caption_lengths,
    timesteps,
    weights,
    vectors,
    weights_m,
    weights_v,
    vectors_m,
    vectors_v,
):
    width = weights.shape[1]
    seq_count = lax.axis_size("seq")
    dp_count = lax.axis_size("dp")
    seq_index = lax.axis_index("seq")
    row_index = lax.axis_index("dp")
    devices = dp_count * seq_count
    layout = matrix_rows(width)
    shard_rows = weights.shape[0]
    paired = dp_count == 4 and seq_count == 8
    weights_low = weights.astype(jnp.bfloat16)
    if paired:
        shard = weights_low.reshape(shard_rows // UNIT, UNIT, width)
        rows_all, rows_late = gather_rows((0, 2176), (23, 19), 8, devices, 7, shard)
        flat = (-1, width)
        self_head = 384
        (
            time_one,
            time_two,
            time_block,
            text_one,
            text_two,
            joint_qkv,
            self_out_head,
        ) = split_rows(rows_all.reshape(flat), layout[:6] + (self_head,))
    else:
        gathered = lax.all_gather(weights_low, both_axes, axis=0, tiled=True)
        (
            time_one,
            time_two,
            time_block,
            text_one,
            text_two,
            joint_qkv,
            self_out,
            cross_query,
            cross_kv,
            cross_out,
            mlp_up,
            mlp_down,
        ) = split_rows(gathered, layout)
    (
        table,
        final_table,
        patch_in,
        patch_out,
        b_patch,
        b_time_one,
        b_time_two,
        b_block,
        b_text_one,
        b_text_two,
        b_query,
        b_value,
        b_self_out,
        b_cross_query,
        b_cross_value,
        b_cross_out,
        b_up,
        b_down,
    ) = split_rows(vectors.astype(jnp.bfloat16).astype(jnp.float32), vector_rows(width))
    head_dim = width // HEADS
    heads = HEADS // seq_count
    part = heads * head_dim
    images = image_sizes.shape[2]
    slots = latents.shape[2]
    assert slots == BLOCK and images == seq_count
    rows = MICRO * slots
    wide = (MICRO, slots, width)
    image_count = jnp.sum((image_sizes > 0).astype(jnp.float32))
    loss_scale = 1.0 / image_count

    ends_all = jnp.cumsum(image_sizes, axis=2)
    firsts = jnp.arange(seq_count, dtype=jnp.int32) * BLOCK
    segment_all = jnp.sum(
        (ends_all[:, :, None, :] <= firsts[None, None, :, None]).astype(jnp.int32), axis=3
    )
    onehot_all = (
        segment_all[:, :, :, None] == jnp.arange(images, dtype=jnp.int32)[None, None, None, :]
    )
    size_all = jnp.sum(jnp.where(onehot_all, image_sizes[:, :, None, :], 0), axis=3)
    start_all = jnp.sum(jnp.where(onehot_all, (ends_all - image_sizes)[:, :, None, :], 0), axis=3)
    step_all = jnp.sum(jnp.where(onehot_all, timesteps[:, :, None, :], 0), axis=3)
    length_all = jnp.sum(jnp.where(onehot_all, caption_lengths[:, :, None, :], 0), axis=3)
    row_start = start_all[:, row_index]
    row_size = size_all[:, row_index]
    kv_start = row_start // BLOCK
    kv_big = (row_size == LARGE).astype(jnp.int32)
    own_segment = segment_all[:, row_index, seq_index]
    own_size = row_size[:, seq_index]
    own_start = row_start[:, seq_index]
    own_step = step_all[:, row_index, seq_index]
    own_length = length_all[:, row_index, seq_index]

    quarter = width // 4
    omega = 1.0 / 10000.0 ** (jnp.arange(quarter, dtype=jnp.float32) / quarter)
    angle = jnp.arange(2 * SIDE, dtype=jnp.float32)[:, None] * omega[None, :]
    angle_table = jnp.concatenate([jnp.sin(angle), jnp.cos(angle)], axis=1)
    within = (
        seq_index * BLOCK - own_start[:, None] + jnp.arange(slots, dtype=jnp.int32)[None, :]
    ).reshape(rows)
    side = jnp.where(own_size == LARGE, 2 * SIDE, SIDE).astype(jnp.int32)
    side = jnp.broadcast_to(side[:, None], (MICRO, slots)).reshape(rows)
    places = jnp.arange(2 * SIDE, dtype=jnp.int32)[None, :]
    pick_row = ((within // side)[:, None] == places).astype(jnp.float32)
    pick_col = ((within % side)[:, None] == places).astype(jnp.float32)
    position = jnp.concatenate(
        [
            jnp.dot(pick_row, angle_table, precision=exact),
            jnp.dot(pick_col, angle_table, precision=exact),
        ],
        axis=1,
    )

    level = noise_level(own_step)[:, None, None]
    level_prev = noise_level(own_step - 1)[:, None, None]
    beta_log, tilde_log = variance_logs(level, level_prev)
    target = noise[:, 0].astype(jnp.float32)
    noisy = jnp.sqrt(level) * latents[:, 0].astype(jnp.float32) + jnp.sqrt(1.0 - level) * target
    noisy = noisy.reshape(rows, PATCH)

    time_low = low(time_features(own_step))
    time_first = dot_nn(time_low, time_one) + b_time_one
    time_act, time_act_back = jax.vjp(jax.nn.silu, time_first)
    time_act_low = low(time_act)
    time_embed = dot_nn(time_act_low, time_two) + b_time_two
    embed_act, embed_act_back = jax.vjp(jax.nn.silu, time_embed)
    embed_low = low(embed_act)
    block_mod = dot_nt(embed_low, time_block) + b_block.reshape(1, -1) + table.reshape(1, -1)
    shift_one, scale_one, gate_one, shift_two, scale_two, gate_two = [
        piece[:, None, :] for piece in jnp.split(block_mod, 6, axis=1)
    ]
    shift_final = (final_table[0][None, :] + time_embed)[:, None, :]
    scale_final = (final_table[1][None, :] + time_embed)[:, None, :]

    hidden_zero = (jnp.dot(noisy, patch_in, precision=exact) + b_patch + position).reshape(wide)
    normed_one, mod_one_back = jax.vjp(modulate, hidden_zero, shift_one, scale_one)
    normed_one_low = low(normed_one).reshape(rows, width)
    joint_bias = jnp.concatenate([b_query, jnp.zeros_like(b_query), b_value], axis=0)
    joint_bias = jnp.transpose(joint_bias.reshape(3, seq_count, part), (1, 0, 2))
    qkv = joint_forward(normed_one_low, joint_qkv, joint_bias.reshape(seq_count, 1, 3 * part))
    caption_low = captions[:, 0].reshape(MICRO * CAP, TEXT_W)
    caption_first = dot_nn(caption_low, text_one) + b_text_one
    caption_act, caption_act_back = jax.vjp(gelu_tanh, caption_first)
    caption_act_low = low(caption_act)
    text = dot_nn(caption_act_low, text_two) + b_text_two
    lengths_slot = lax.dynamic_slice_in_dim(caption_lengths[:, row_index], seq_index, 1, 1)
    token_live = (jnp.arange(CAP, dtype=jnp.int32)[None, :] < lengths_slot).astype(jnp.float32)
    lengths_slot_float = lengths_slot.astype(jnp.float32)
    caption_pool = (
        jnp.sum(text.reshape(MICRO, CAP, width) * token_live[:, :, None], axis=1) / lengths_slot_float
    )
    text_own = low(text)
    if paired:
        qkv, text_own, rows_late = lax.optimization_barrier((qkv, text_own, rows_late))
    qkv = lax.all_to_all(qkv, "seq", split_axis=0, concat_axis=0, tiled=True)
    text_all = lax.all_gather(text_own.reshape(MICRO, CAP, width), "seq", axis=0)
    if paired:
        rows_late, words_all = spread_rows(rows_late, caption_pool.reshape(-1, 128), devices, 8)
        qkv, rows_late = lax.optimization_barrier((qkv, rows_late))
        self_out_tail, cross_query, cross_kv, cross_out, mlp_up, mlp_down = split_rows(
            rows_late.reshape(flat), (layout[6] - self_head,) + layout[7:]
        )
        self_out = jnp.concatenate([self_out_head, self_out_tail], axis=0)
    qkv = qkv.reshape(seq_count, MICRO, slots, 3 * part)
    mixed = self_forward(kv_start, kv_big, qkv, heads, head_dim)
    mixed = lax.all_to_all(
        mixed.reshape(seq_count, rows, part), "seq", split_axis=0, concat_axis=0, tiled=True
    )
    mixed_low = jnp.transpose(mixed, (1, 0, 2)).reshape(rows, width)
    attended = (dot_nn(mixed_low, self_out) + b_self_out).reshape(wide)
    hidden_one = hidden_zero + gate_one * attended

    text_low = jnp.concatenate(
        [
            lax.dynamic_slice(text_all, (own_segment[m], m, 0, 0), (1, 1, CAP, width))[0, 0]
            for m in range(MICRO)
        ],
        axis=0,
    )
    text_kv = dot_nt(text_low, cross_kv)
    pad_rows = ((0, 0), (0, CAP_PAD - CAP), (0, 0))
    key_text = jnp.pad(low(text_kv[:, :width]).reshape(MICRO, CAP, width), pad_rows)
    value_text = jnp.pad(
        low(text_kv[:, width:] + b_cross_value).reshape(MICRO, CAP, width), pad_rows
    )
    hidden_one_low = low(hidden_one).reshape(rows, width)
    query_cross = low(dot_nn(hidden_one_low, cross_query) + b_cross_query).reshape(wide)
    cross_low = cross_call(
        functools.partial(cross_forward_kernel, head_dim),
        own_length,
        (query_cross, key_text, value_text),
        jax.ShapeDtypeStruct(wide, jnp.bfloat16),
    ).reshape(rows, width)
    hidden_two = hidden_one + (dot_nn(cross_low, cross_out) + b_cross_out).reshape(wide)
    normed_two, mod_two_back = jax.vjp(modulate, hidden_two, shift_two, scale_two)
    normed_two_low = low(normed_two).reshape(rows, width)
    upward = dot_nt(normed_two_low, mlp_up) + b_up.reshape(1, -1)
    upward_act, upward_back = jax.vjp(gelu_tanh, upward)
    upward_low = low(upward_act)
    feed = (dot_nn(upward_low, mlp_down) + b_down).reshape(wide)
    hidden_three = hidden_two + gate_two * feed
    final_normed, final_back = jax.vjp(modulate, hidden_three, shift_final, scale_final)
    final_flat = final_normed.reshape(rows, width)
    predicted = jnp.dot(final_flat, patch_out.T, precision=exact).reshape(MICRO, slots, 2 * PATCH)
    error = predicted[:, :, :PATCH] - target
    frac = (predicted[:, :, PATCH:] + 1.0) * 0.5
    model_log = frac * beta_log + (1.0 - frac) * tilde_log
    ratio = jnp.exp(tilde_log - model_log)
    spread = 0.5 * (model_log - tilde_log - 1.0 + ratio) / log_two
    error_weight = (1.0 / (float(PATCH) * own_size.astype(jnp.float32)))[:, None, None]
    squared_loss = jnp.sum((error * error + spread) * error_weight)

    pooled = jnp.sum(final_normed, axis=1)
    if paired:
        pooled_all = share(pooled.reshape(-1, 128), devices, 1)
    else:
        pooled_all = lax.all_gather(pooled, both_axes, axis=0)
        words_all = lax.all_gather(caption_pool, both_axes, axis=0)
    each = (devices, MICRO, width)
    pooled_all = jnp.concatenate([pooled_all.reshape(each), words_all.reshape(each)], axis=1)
    pooled_all = jnp.transpose(pooled_all, (1, 0, 2))
    size_float = jnp.maximum(image_sizes.astype(jnp.float32), 1.0)
    pick = onehot_all.astype(jnp.float32) / size_float[:, :, None, :]
    same_row = jnp.eye(dp_count, dtype=jnp.float32)
    pick = jnp.einsum("mrsi,rq->mriqs", pick, same_row, precision=exact).reshape(
        MICRO, dp_count * images, devices
    )
    valid = (image_sizes > 0).astype(jnp.float32).reshape(MICRO, dp_count * images)
    grad_pool, grad_caption, contrast_value = contrast(pooled_all, pick, valid, loss_scale)
    contrast_value = contrast_value[0, 0]
    own_pool = row_index * images + own_segment
    grad_pool_own = jnp.concatenate(
        [lax.dynamic_slice(grad_pool, (m, own_pool[m], 0), (1, 1, width))[0] for m in range(MICRO)]
    ) / own_size.astype(jnp.float32)[:, None]
    grad_caption = lax.dynamic_slice_in_dim(
        grad_caption, row_index * images + seq_index, 1, 1
    )[:, 0]

    grad_spread = 0.5 * (1.0 - ratio) / log_two * 0.5 * (beta_log - tilde_log)
    grad_predicted = (
        loss_scale * error_weight * jnp.concatenate([2.0 * error, grad_spread], axis=2)
    ).reshape(rows, 2 * PATCH)
    grad_final = grad_pool_own[:, None, :] + jnp.dot(
        grad_predicted, patch_out, precision=exact
    ).reshape(wide)
    grad_patch_out = lax.dot_general(
        grad_predicted, final_flat, (((0,), (0,)), ((), ())), precision=exact
    )
    grad_three, grad_shift_final, grad_scale_final = final_back(grad_final)
    grad_shift_final = grad_shift_final[:, 0]
    grad_scale_final = grad_scale_final[:, 0]
    grad_final_table = jnp.stack([grad_shift_final.sum(axis=0), grad_scale_final.sum(axis=0)])
    grad_embed = grad_shift_final + grad_scale_final

    grad_feed = (grad_three * gate_two).reshape(rows, width)
    grad_feed_low = low(grad_feed)
    grad_upward = upward_back(dot_nt(grad_feed_low, mlp_down))[0]
    grad_upward_low = low(grad_upward)
    weight_down = dot_tn(upward_low, grad_feed_low)
    weight_up = dot_tn(grad_upward_low, normed_two_low)
    grad_two_mod, grad_shift_two, grad_scale_two = mod_two_back(
        dot_nn(grad_upward_low, mlp_up).reshape(wide)
    )
    grad_gate_two = jnp.sum(grad_three * feed, axis=1, keepdims=True)
    grad_two = grad_three + grad_two_mod
    grad_two_flat = grad_two.reshape(rows, width)
    grad_two_low = low(grad_two_flat)
    weight_cross_out = dot_tn(cross_low, grad_two_low)
    grad_cross_low = low(dot_nt(grad_two_low, cross_out)).reshape(wide)
    padded = jax.ShapeDtypeStruct((MICRO, CAP_PAD, width), jnp.float32)
    grad_query_cross, grad_key_text, grad_value_text = cross_call(
        functools.partial(cross_backward_kernel, head_dim),
        own_length,
        (query_cross, key_text, value_text, grad_cross_low),
        (jax.ShapeDtypeStruct(wide, jnp.float32), padded, padded),
    )
    grad_query_cross = grad_query_cross.reshape(rows, width)
    grad_query_low = low(grad_query_cross)
    weight_cross_query = dot_tn(hidden_one_low, grad_query_low)
    grad_one = grad_two + dot_nt(grad_query_low, cross_query).reshape(wide)

    grad_kv = jnp.concatenate([grad_key_text[:, :CAP], grad_value_text[:, :CAP]], axis=2).reshape(
        MICRO * CAP, 2 * width
    )
    grad_kv_low = low(grad_kv)
    weight_cross_kv = dot_tn(grad_kv_low, text_low)
    grad_text_part = low(dot_nn(grad_kv_low, cross_kv)).reshape(MICRO, CAP, width)
    grad_text_all = lax.all_gather(grad_text_part, "seq", axis=0).astype(jnp.float32)
    mine = (segment_all[:, row_index] == seq_index).astype(jnp.float32)
    grad_text = jnp.sum(grad_text_all * jnp.transpose(mine)[:, :, None, None], axis=0) + (
        (grad_caption / lengths_slot_float)[:, None, :] * token_live[:, :, None]
    )
    grad_text = grad_text.reshape(MICRO * CAP, width)
    grad_text_low = low(grad_text)
    weight_text_two = dot_tn(caption_act_low, grad_text_low)
    grad_caption_first = caption_act_back(dot_nt(grad_text_low, text_two))[0]
    grad_caption_low = low(grad_caption_first)
    head_rows = TILE_START * UNIT - sum(layout[:3]) + TILE * UNIT // 2 if paired else 0
    weight_text_one = dot_tn(caption_low[:, head_rows:], grad_caption_low)

    grad_attended = (grad_one * gate_one).reshape(rows, width)
    grad_gate_one = jnp.sum(grad_one * attended, axis=1, keepdims=True)
    grad_attended_low = low(grad_attended)
    weight_self_out = dot_tn(mixed_low, grad_attended_low)
    grad_mixed = low(dot_nt(grad_attended_low, self_out)).reshape(rows, seq_count, part)
    grad_mixed = jnp.transpose(grad_mixed, (1, 0, 2))
    if paired:
        weight_up, weight_down, grad_mixed = lax.optimization_barrier(
            (low(weight_up), low(weight_down), grad_mixed)
        )
    grad_mixed = lax.all_to_all(grad_mixed, "seq", split_axis=0, concat_axis=0, tiled=True)
    if paired:
        summed_feed = reduce_rows(
            ((19, 31),), shard_rows // UNIT, devices, 2, ((weight_up, 0, 12), (weight_down, 0, 12))
        )
        grad_mixed, summed_feed = lax.optimization_barrier((grad_mixed, summed_feed))
    grad_mixed = grad_mixed.reshape(seq_count, MICRO, slots, part)
    grad_qkv, head_sums = self_backward(kv_start, kv_big, qkv, grad_mixed, heads, head_dim)
    head_sums = jnp.sum(head_sums[:, 0], axis=0)
    column = seq_index * part
    grad_bias_query = lax.dynamic_update_slice(
        jnp.zeros((width,), jnp.float32), head_sums[:part], (column,)
    )
    grad_bias_value = lax.dynamic_update_slice(
        jnp.zeros((width,), jnp.float32), head_sums[part:], (column,)
    )
    grad_qkv = grad_qkv.reshape(seq_count, rows, 3 * part)
    if paired:
        time_rows = layout[0] + layout[1]
        block_rows = layout[2]
        weight_self_out = low(weight_self_out)
        first_half = low(dot_tn(caption_low[:, :head_rows], grad_caption_low))
        first_half = jnp.pad(first_half, ((TILE * UNIT // 2 - head_rows, 0), (0, 0)))
        (
            first_half,
            weight_text_one,
            weight_text_two,
            weight_self_out,
            weight_cross_query,
            weight_cross_kv,
            weight_cross_out,
            grad_qkv,
        ) = lax.optimization_barrier(
            (
                first_half,
                low(weight_text_one),
                low(weight_text_two),
                weight_self_out,
                low(weight_cross_query),
                low(weight_cross_kv),
                low(weight_cross_out),
                grad_qkv,
            )
        )
    grad_qkv = lax.all_to_all(
        grad_qkv, "seq", split_axis=0, concat_axis=0, tiled=True
    )
    if paired:
        summed_middle = reduce_rows(
            ((0, 7), (12, 19)),
            shard_rows // UNIT,
            devices,
            3,
            (
                (first_half, 0, 1),
                (weight_text_one, 0, 10),
                (weight_text_two, 0, 3),
                (weight_self_out, TILE // 2, 2),
                (weight_cross_query, 0, 3),
                (weight_cross_kv, 0, 6),
                (weight_cross_out, 0, 3),
            ),
        )
        grad_qkv, summed_middle = lax.optimization_barrier((grad_qkv, summed_middle))
    grad_normed_one, weight_joint = joint_backward(grad_qkv, joint_qkv, normed_one_low)
    grad_zero_mod, grad_shift_one, grad_scale_one = mod_one_back(grad_normed_one.reshape(wide))
    grad_zero = (grad_one + grad_zero_mod).reshape(rows, width)
    grad_patch_in = lax.dot_general(noisy, grad_zero, (((0,), (0,)), ((), ())), precision=exact)

    grad_mod = jnp.concatenate(
        [grad_shift_one, grad_scale_one, grad_gate_one, grad_shift_two, grad_scale_two, grad_gate_two],
        axis=1,
    )
    grad_table = jnp.sum(grad_mod, axis=0)
    grad_mod_low = low(grad_mod.reshape(MICRO, 6 * width))
    weight_block = dot_tn(grad_mod_low, embed_low)
    grad_embed = grad_embed + embed_act_back(dot_nn(grad_mod_low, time_block))[0]
    grad_embed_low = low(grad_embed)
    weight_time_two = dot_tn(time_act_low, grad_embed_low)
    grad_time_first = time_act_back(dot_nt(grad_embed_low, time_two))[0]
    weight_time_one = dot_tn(time_low, low(grad_time_first))

    if paired:
        holders = -(-(time_rows + block_rows) // shard_rows)
        own_grads = jnp.concatenate(
            [grad_mod_low, grad_embed_low, low(grad_time_first), embed_low, time_act_low, time_low],
            axis=1,
        )
        summed_joint, grads_all = reduce_rows(
            ((7, 12),),
            shard_rows // UNIT,
            devices,
            4,
            ((low(weight_joint), 0, 9), (weight_self_out, 0, 1)),
            own_grads.reshape(-1, 128),
            holders,
        )
        grads_all = jnp.where(device_index() < holders, grads_all, 0)
        grads_all = grads_all.reshape(devices * MICRO, -1)
        ends = [6 * width, 7 * width, 8 * width, 9 * width, 10 * width]
        grad_block_all, grad_two_all, grad_one_all, embed_all, act_all, features_all = jnp.split(
            grads_all, ends, axis=1
        )
        first_row = device_index() * shard_rows

        def own_columns(array, start):
            stop = start + array.shape[1]
            spread = jnp.pad(array, ((0, 0), (start, shard_rows + (-stop) % shard_rows)))
            place = jnp.minimum(first_row, spread.shape[1] - shard_rows)
            return lax.dynamic_slice(spread, (0, place), (array.shape[0], shard_rows))

        summed_time = (
            dot_tn(own_columns(features_all, 0), grad_one_all)
            + dot_tn(own_columns(act_all, layout[0]), grad_two_all)
            + dot_tn(own_columns(grad_block_all, time_rows), embed_all)
        )
        row = first_row + jnp.arange(shard_rows, dtype=jnp.int32)
        tile = ((row - TILE_START * UNIT) // (TILE * UNIT))[:, None]
        flat = (shard_rows, width)
        reduced = jnp.where(
            tile >= 19,
            summed_feed.reshape(flat),
            jnp.where(
                (tile >= 7) & (tile < 12), summed_joint.reshape(flat), summed_middle.reshape(flat)
            ),
        ).astype(jnp.float32)
        summed = jnp.where(row[:, None] < time_rows + block_rows, summed_time, reduced)
    else:
        grad_weights = jnp.concatenate(
            [
                low(piece)
                for piece in (
                    weight_time_one,
                    weight_time_two,
                    weight_block,
                    weight_text_one,
                    weight_text_two,
                    weight_joint,
                    weight_self_out,
                    weight_cross_query,
                    weight_cross_kv,
                    weight_cross_out,
                    weight_up,
                    weight_down,
                )
            ],
            axis=0,
        )
        summed = lax.psum_scatter(
            grad_weights, both_axes, scatter_dimension=0, tiled=True
        ).astype(jnp.float32)
    grad_vector = jnp.concatenate(
        [
            grad_table,
            grad_final_table,
            grad_patch_in,
            grad_patch_out,
            jnp.sum(grad_zero, axis=0)[None, :],
            jnp.sum(grad_time_first, axis=0)[None, :],
            jnp.sum(grad_embed, axis=0)[None, :],
            grad_table,
            jnp.sum(grad_caption_first, axis=0)[None, :],
            jnp.sum(grad_text, axis=0)[None, :],
            grad_bias_query[None, :],
            grad_bias_value[None, :],
            jnp.sum(grad_attended, axis=0)[None, :],
            jnp.sum(grad_query_cross, axis=0)[None, :],
            jnp.sum(grad_kv[:, width:], axis=0)[None, :],
            jnp.sum(grad_two_flat, axis=0)[None, :],
            jnp.sum(grad_upward, axis=0).reshape(-1, width),
            jnp.sum(grad_feed, axis=0)[None, :],
            jnp.full((2, width), squared_loss),
        ],
        axis=0,
    )
    squares = jnp.sum(summed * summed)
    if paired:
        grad_vectors, squares_all = sum_all(grad_vector, squares, devices, 6)
    else:
        grad_vectors, squares_all = lax.psum((grad_vector, squares), both_axes)
    loss_sum = grad_vectors[vectors.shape[0], 0] + contrast_value
    grad_vectors = grad_vectors[: vectors.shape[0]]
    down_bias_grad = grad_vectors[grad_vectors.shape[0] - 1]
    grad_norm = jnp.sqrt(squares_all + jnp.sum(grad_vectors * grad_vectors))
    factor = jnp.minimum(1.0, clip_norm / (grad_norm + 1e-06))
    new_w, first_w, second_w = adamw(
        weights, summed * factor, weights_m, weights_v, rate_matrix, weight_decay
    )
    new_v, first_v, second_v = adamw(
        vectors, grad_vectors * factor, vectors_m, vectors_v, rate_vector, 0.0
    )
    return (
        new_w,
        first_w,
        second_w,
        new_v,
        first_v,
        second_v,
        loss_sum,
        image_count,
        grad_norm,
        down_bias_grad,
    )


def solution(mesh):
    shard = P(both_axes, None)
    data = P(None, "dp", "seq", None)
    return jax.shard_map(
        per_device,
        mesh=mesh,
        in_specs=(data, data, data, P(), P(), P(), shard, P(), shard, shard, P(), P()),
        out_specs=(shard, shard, shard, P(), P(), P(), P(), P(), P(), P()),
        check_vma=False,
    )
```

```python
import functools
import math

import jax
import jax.numpy as jnp
from jax import lax
from jax.experimental import pallas as pl
from jax.experimental.pallas import tpu as pltpu
from jax.sharding import PartitionSpec as P

HEADS = 16
FF = 4608
TEXT_W = 4096
FREQ = 256
CAP = 120
CAP_PAD = 128
SIDE = 16
PATCH = 16
MICRO = 2
STEP = 10
BLOCK = 256
LARGE = 1024
VMEM_BYTES = 56 * 1024 * 1024

exact = lax.Precision.HIGHEST
clip_norm = 0.002
contrastive_sharpness_divisor = 0.1
beta_one = 0.9
beta_two = 0.999
adam_eps = 1e-08
weight_decay = 0.01
rate_matrix = 0.05
rate_vector = 0.3
norm_eps = 1e-06
neg_large = -1e30
log_two = math.log(2.0)
both_axes = ("dp", "seq")


def matrix_rows(width):
    return (FREQ, width, 6 * width, TEXT_W, width, 3 * width, width, width, 2 * width, width, FF, FF)


def vector_rows(width):
    return (6, 2, PATCH, 2 * PATCH, 1, 1, 1, 6, 1, 1, 1, 1, 1, 1, 1, 1, FF // width, 1)


def split_rows(whole, rows):
    pieces = []
    offset = 0
    for number in rows:
        pieces.append(whole[offset : offset + number])
        offset = offset + number
    return pieces


def device_index():
    return lax.axis_index("dp") * lax.axis_size("seq") + lax.axis_index("seq")


def modulate(hidden, shift, scale):
    centre = hidden - jnp.mean(hidden, axis=-1, keepdims=True)
    normed = centre * lax.rsqrt(jnp.mean(centre * centre, axis=-1, keepdims=True) + norm_eps)
    return normed * (1.0 + scale) + shift


def gelu_tanh(values):
    return jax.nn.gelu(values, approximate=True)


def time_features(steps_now):
    half_size = FREQ // 2
    frequency = jnp.exp(-math.log(10000.0) * jnp.arange(half_size, dtype=jnp.float32) / half_size)
    angles = steps_now.astype(jnp.float32)[:, None] * frequency[None, :]
    return jnp.concatenate([jnp.cos(angles), jnp.sin(angles)], axis=1)


def noise_level(steps_now):
    phase = (steps_now.astype(jnp.float32) / 1000.0 + 0.008) / 1.008 * (math.pi / 2.0)
    return jnp.cos(phase) ** 2


def variance_logs(level, level_prev):
    beta_now = jnp.minimum(1.0 - level / level_prev, 0.999)
    tilde_log = jnp.log(beta_now * (1.0 - level_prev) / (1.0 - level))
    return (jnp.log(beta_now), tilde_log)


def dot_nn(left, right):
    return lax.dot_general(left, right, (((1,), (0,)), ((), ())), preferred_element_type=jnp.float32)


def dot_nt(left, right):
    return lax.dot_general(left, right, (((1,), (1,)), ((), ())), preferred_element_type=jnp.float32)


def dot_tn(left, right):
    return lax.dot_general(left, right, (((0,), (0,)), ((), ())), preferred_element_type=jnp.float32)


def low(values):
    return values.astype(jnp.bfloat16)


def self_forward_kernel(heads, dim, start_ref, big_ref, qkv_ref, out_ref, key_s, value_s):
    micro = pl.program_id(0)
    blocks = qkv_ref.shape[0]
    scale = dim ** (-0.5)
    for b in range(blocks):
        for h in range(heads):
            rows = pl.ds(b * BLOCK, BLOCK)
            key_s[h, rows, :] = qkv_ref[b, 0, :, (heads + h) * dim : (heads + h + 1) * dim]
            value_s[h, rows, :] = qkv_ref[b, 0, :, (2 * heads + h) * dim : (2 * heads + h + 1) * dim]

    def one_block(b, carry):
        start = pl.multiple_of(start_ref[micro, b] * BLOCK, BLOCK)
        queries = qkv_ref[b, 0]

        def go(span):
            outs = []
            for h in range(heads):
                key = key_s[h, pl.ds(start, span), :]
                value = value_s[h, pl.ds(start, span), :]
                scores = dot_nt(queries[:, h * dim : (h + 1) * dim], key) * scale
                top = jnp.max(scores, axis=-1, keepdims=True)
                weight = jnp.exp(scores - top)
                total = jnp.sum(weight, axis=-1, keepdims=True)
                probs = low(weight * (1.0 / total))
                outs.append(low(dot_nn(probs, value)))
            out_ref[b, 0] = jnp.concatenate(outs, axis=-1)

        big = big_ref[micro, b]

        @pl.when(big == 1)
        def _():
            go(LARGE)

        @pl.when(big == 0)
        def _():
            go(BLOCK)

        return carry

    lax.fori_loop(0, blocks, one_block, 0)


def self_forward(start, big, qkv, heads, dim):
    blocks, micros = qkv.shape[0], qkv.shape[1]
    span = blocks * BLOCK
    return pl.pallas_call(
        functools.partial(self_forward_kernel, heads, dim),
        out_shape=jax.ShapeDtypeStruct((blocks, micros, BLOCK, heads * dim), jnp.bfloat16),
        grid_spec=pltpu.PrefetchScalarGridSpec(
            num_scalar_prefetch=2,
            grid=(micros,),
            in_specs=[pl.BlockSpec((blocks, 1, BLOCK, 3 * heads * dim), lambda m, s, g: (0, m, 0, 0))],
            out_specs=pl.BlockSpec((blocks, 1, BLOCK, heads * dim), lambda m, s, g: (0, m, 0, 0)),
            scratch_shapes=[
                pltpu.VMEM((heads, span, dim), jnp.bfloat16),
                pltpu.VMEM((heads, span, dim), jnp.bfloat16),
            ],
        ),
        compiler_params=pltpu.CompilerParams(vmem_limit_bytes=VMEM_BYTES),
    )(start, big, qkv)


def self_backward_kernel(
    heads, dim, start_ref, big_ref, qkv_ref, grad_ref, out_ref, sum_ref, key_s, value_s, dq_s, dk_s, dv_s
):
    micro = pl.program_id(0)
    blocks = qkv_ref.shape[0]
    scale = dim ** (-0.5)
    for b in range(blocks):
        for h in range(heads):
            rows = pl.ds(b * BLOCK, BLOCK)
            key_s[h, rows, :] = qkv_ref[b, 0, :, (heads + h) * dim : (heads + h + 1) * dim]
            value_s[h, rows, :] = qkv_ref[b, 0, :, (2 * heads + h) * dim : (2 * heads + h + 1) * dim]
    dk_s[...] = jnp.zeros_like(dk_s)
    dv_s[...] = jnp.zeros_like(dv_s)

    def one_block(b, carry):
        start = pl.multiple_of(start_ref[micro, b] * BLOCK, BLOCK)
        place = pl.multiple_of(b * BLOCK, BLOCK)
        queries = qkv_ref[b, 0]
        grads = grad_ref[b, 0]

        def go(span):
            keep = pl.ds(start, span)
            for h in range(heads):
                query = queries[:, h * dim : (h + 1) * dim]
                grad = grads[:, h * dim : (h + 1) * dim]
                key = key_s[h, keep, :]
                value = value_s[h, keep, :]
                scores = dot_nt(key, query) * scale
                top = jnp.max(scores, axis=0, keepdims=True)
                weight = jnp.exp(scores - top)
                probs = weight * (1.0 / jnp.sum(weight, axis=0, keepdims=True))
                dv_s[h, keep, :] += dot_nn(low(probs), grad)
                grad_probs = dot_nt(value, grad)
                inner = jnp.sum(probs * grad_probs, axis=0, keepdims=True)
                grad_scores = low(probs * (grad_probs - inner) * scale)
                dk_s[h, keep, :] += dot_nn(grad_scores, query)
                dq_s[h, pl.ds(place, BLOCK), :] = dot_tn(grad_scores, key)

        big = big_ref[micro, b]

        @pl.when(big == 1)
        def _():
            go(LARGE)

        @pl.when(big == 0)
        def _():
            go(BLOCK)

        return carry

    lax.fori_loop(0, blocks, one_block, 0)
    for b in range(blocks):
        rows = pl.ds(b * BLOCK, BLOCK)
        out_ref[b, 0] = jnp.concatenate(
            [low(part[h, rows, :]) for part in (dq_s, dk_s, dv_s) for h in range(heads)], axis=-1
        )
    sum_ref[0] = jnp.concatenate(
        [jnp.sum(part[h], axis=0, keepdims=True) for part in (dq_s, dv_s) for h in range(heads)], axis=-1
    )


def self_backward(start, big, qkv, grad, heads, dim):
    blocks, micros = qkv.shape[0], qkv.shape[1]
    span = blocks * BLOCK
    wide = pltpu.VMEM((heads, span, dim), jnp.float32)
    narrow = pltpu.VMEM((heads, span, dim), jnp.bfloat16)
    return pl.pallas_call(
        functools.partial(self_backward_kernel, heads, dim),
        out_shape=(
            jax.ShapeDtypeStruct((blocks, micros, BLOCK, 3 * heads * dim), jnp.bfloat16),
            jax.ShapeDtypeStruct((micros, 1, 2 * heads * dim), jnp.float32),
        ),
        grid_spec=pltpu.PrefetchScalarGridSpec(
            num_scalar_prefetch=2,
            grid=(micros,),
            in_specs=[
                pl.BlockSpec((blocks, 1, BLOCK, 3 * heads * dim), lambda m, s, g: (0, m, 0, 0)),
                pl.BlockSpec((blocks, 1, BLOCK, heads * dim), lambda m, s, g: (0, m, 0, 0)),
            ],
            out_specs=(
                pl.BlockSpec((blocks, 1, BLOCK, 3 * heads * dim), lambda m, s, g: (0, m, 0, 0)),
                pl.BlockSpec((1, 1, 2 * heads * dim), lambda m, s, g: (m, 0, 0)),
            ),
            scratch_shapes=[narrow, narrow, wide, wide, wide],
        ),
        compiler_params=pltpu.CompilerParams(vmem_limit_bytes=VMEM_BYTES),
    )(start, big, qkv, grad)


def cross_forward_kernel(dim, length_ref, query_ref, key_ref, value_ref, out_ref):
    length = length_ref[pl.program_id(0)]
    scale = dim ** (-0.5)
    live = lax.broadcasted_iota(jnp.int32, (BLOCK, CAP_PAD), 1) < length
    outs = []
    for h in range(HEADS):
        part = slice(h * dim, (h + 1) * dim)
        scores = jnp.where(live, dot_nt(query_ref[0, :, part], key_ref[0, :, part]) * scale, neg_large)
        weight = jnp.exp(scores - jnp.max(scores, axis=-1, keepdims=True))
        probs = low(weight * (1.0 / jnp.sum(weight, axis=-1, keepdims=True)))
        outs.append(low(dot_nn(probs, value_ref[0, :, part])))
    out_ref[0] = jnp.concatenate(outs, axis=-1)


def cross_backward_kernel(
    dim, length_ref, query_ref, key_ref, value_ref, grad_ref, dq_ref, dk_ref, dv_ref
):
    length = length_ref[pl.program_id(0)]
    scale = dim ** (-0.5)
    live = lax.broadcasted_iota(jnp.int32, (CAP_PAD, BLOCK), 0) < length
    dq, dk, dv = [], [], []
    for h in range(HEADS):
        part = slice(h * dim, (h + 1) * dim)
        query, key, value, grad = (
            query_ref[0, :, part],
            key_ref[0, :, part],
            value_ref[0, :, part],
            grad_ref[0, :, part],
        )
        scores = jnp.where(live, dot_nt(key, query) * scale, neg_large)
        weight = jnp.exp(scores - jnp.max(scores, axis=0, keepdims=True))
        probs = weight * (1.0 / jnp.sum(weight, axis=0, keepdims=True))
        dv.append(dot_nn(low(probs), grad))
        grad_probs = dot_nt(value, grad)
        inner = jnp.sum(probs * grad_probs, axis=0, keepdims=True)
        grad_scores = low(probs * (grad_probs - inner) * scale)
        dk.append(dot_nn(grad_scores, query))
        dq.append(dot_tn(grad_scores, key))
    dq_ref[0] = jnp.concatenate(dq, axis=-1)
    dk_ref[0] = jnp.concatenate(dk, axis=-1)
    dv_ref[0] = jnp.concatenate(dv, axis=-1)


def cross_call(kernel, length, arrays, outs):
    def spec(array):
        return pl.BlockSpec((1,) + array.shape[1:], lambda m, s: (m, 0, 0))

    return pl.pallas_call(
        kernel,
        out_shape=outs,
        grid_spec=pltpu.PrefetchScalarGridSpec(
            num_scalar_prefetch=1,
            grid=(MICRO,),
            in_specs=[spec(array) for array in arrays],
            out_specs=jax.tree.map(spec, outs),
        ),
        compiler_params=pltpu.CompilerParams(vmem_limit_bytes=VMEM_BYTES),
    )(length, *arrays)


UNIT = 8
SPLIT = 640
PIECE = 3
TILE = 96
TILE_START = 1024
LAG = 2
RING = LAG + 1
MESH = pl.DeviceIdType.MESH


def my_place():
    row, seq = lax.axis_index("dp"), lax.axis_index("seq")
    return lax.div(row, 2), lax.rem(row, 2), lax.div(seq, 2), lax.rem(seq, 2)


def peer(y, core, z, x):
    return (y * 2 + core, z * 2 + x)


def greet_all(devices, seq_count):
    me = lax.axis_index("dp") * seq_count + lax.axis_index("seq")
    barrier = pltpu.get_barrier_semaphore()

    def one(step, carry):
        other = lax.rem(me + step, devices)
        pl.semaphore_signal(
            barrier,
            inc=1,
            device_id=(lax.div(other, seq_count), lax.rem(other, seq_count)),
            device_id_type=MESH,
        )
        return carry

    lax.fori_loop(1, devices, one, 0)
    pl.semaphore_wait(barrier, devices - 1)


def global_tile(ranges, index):
    tile = index + ranges[0][0]
    at = ranges[0][1] - ranges[0][0]
    for start, stop in ranges[1:]:
        tile = jnp.where(index >= at, index - at + start, tile)
        at += stop - start
    return tile


def reduce_kernel(
    ranges,
    shard_units,
    devices,
    sources,
    receivers,
    *refs,
):
    rows_refs, refs = refs[: len(sources)], list(refs[len(sources) :])
    if receivers:
        block_ref, all_ref = refs.pop(0), refs.pop(1)
        refs, push_sems = refs[:-3], refs[-3:]
    (
    out_ref,
    own_s,
    core_s,
    first_s,
    second_s,
    first_y_s,
    second_x_s,
    first_two_s,
    second_two_s,
    first_x_s,
    second_y_s,
    third_s,
    along_s,
    leaf_s,
    load_sem,
    core_send,
    core_recv,
    one_send,
    one_recv,
    two_send,
    two_recv,
    z_send,
    z_recv,
    leaf_send,
    leaf_recv,
    ) = refs
    tiles = core_s.shape[0]
    seq_count = devices // 4
    y, core, z, x = my_place()
    me = (y * 2 + core) * seq_count + z * 2 + x
    place = ((core * 2 + y) * 2 + x) * 4 + z
    half, quarter, eighth = TILE // 2, TILE // 4, TILE // 8
    across_core = peer(y, 1 - core, z, x)
    across_y = peer(1 - y, core, z, x)
    across_x = peer(y, core, z, 1 - x)

    def remote(source, target, send, recv, device):
        return pltpu.make_async_remote_copy(
            src_ref=source,
            dst_ref=target,
            send_sem=send,
            recv_sem=recv,
            device_id=device,
            device_id_type=MESH,
        )

    def core_copy(t, rows_ref=None, start=0):
        source = own_s.at[0] if rows_ref is None else rows_ref.at[pl.ds(start, half)]
        return remote(source, core_s.at[t], core_send.at[t], core_recv.at[t], across_core)

    def load(t, rows_ref=None, start=0):
        slot = lax.rem(t, 2)
        source = rows_refs[-1] if rows_ref is None else rows_ref
        return pltpu.make_async_copy(
            source.at[pl.ds(start, half)], own_s.at[slot], load_sem.at[slot]
        )

    def start_from(copy, t, side):
        index = t * 2 + side
        at = 0
        for rows_ref, (start, count) in zip(rows_refs, sources):

            @pl.when((index >= at) & (index < at + count))
            def _(rows_ref=rows_ref, start=start, at=at):
                copy(t, rows_ref, start + (index - at) * half).start()

            at += count

    def first_one(t):
        return remote(
            first_s.at[lax.rem(t, RING), pl.ds((1 - y) * quarter, quarter)],
            first_y_s.at[t],
            one_send.at[lax.rem(t, RING), 0],
            one_recv.at[t, 0],
            across_y,
        )

    def second_one(t, side):
        return remote(
            second_s.at[lax.rem(t, RING), pl.ds(side * quarter + (1 - x) * eighth, eighth)],
            second_x_s.at[t, pl.ds(side * eighth, eighth)],
            one_send.at[lax.rem(t, RING), 1 + side],
            one_recv.at[t, 1 + side],
            across_x,
        )

    def first_two(t):
        return remote(
            first_two_s.at[lax.rem(t, RING), pl.ds((1 - x) * eighth, eighth)],
            first_x_s.at[t],
            two_send.at[lax.rem(t, RING), 0],
            two_recv.at[t, 0],
            across_x,
        )

    def second_two(t):
        return remote(
            second_two_s.at[lax.rem(t, RING), pl.ds((1 - y) * eighth, eighth)],
            second_y_s.at[t],
            two_send.at[lax.rem(t, RING), 1],
            two_recv.at[t, 1],
            across_y,
        )

    def z_copy(t, distance):
        other = z ^ distance
        return remote(
            third_s.at[lax.rem(t, RING), pl.ds(other * PIECE, PIECE)],
            along_s.at[t, distance - 1],
            z_send.at[lax.rem(t, RING), distance - 1],
            z_recv.at[t, distance - 1],
            peer(y, core, other, x),
        )

    def add(count, step, target, *sources):
        def one(index, carry):
            at = index * step
            total = sources[0](at, step).astype(jnp.float32)
            for source in sources[1:]:
                total = total + source(at, step).astype(jnp.float32)
            target(at, step, total.astype(jnp.bfloat16))
            return carry

        lax.fori_loop(0, count // step, one, 0)

    def leaf_send_all(t, stage):
        unit = TILE_START + global_tile(ranges, t) * TILE + place * PIECE
        owner = lax.div(unit, shard_units)
        at = unit - owner * shard_units

        def go(part, count, slot, holder):
            source = leaf_s.at[t, pl.ds(part, count)]
            target = out_ref.at[pl.ds(slot, count)]
            sending = remote(
                source,
                target,
                leaf_send.at[t, part],
                leaf_recv.at[slot],
                (lax.div(holder, seq_count), lax.rem(holder, seq_count)),
            )

            @pl.when(holder != me)
            def _():
                if stage == 0:
                    sending.start()
                else:
                    sending.wait_send()

            if stage == 0:

                @pl.when(holder == me)
                def _():
                    pltpu.make_async_copy(source, target, leaf_recv.at[slot]).start()

        together = at + PIECE <= shard_units

        @pl.when(together)
        def _():
            go(0, PIECE, at, owner)

        @pl.when(jnp.logical_not(together))
        def _():
            for part in range(PIECE):
                over = at + part >= shard_units
                go(
                    part,
                    1,
                    jnp.where(over, at + part - shard_units, at + part),
                    jnp.where(over, owner + 1, owner),
                )

    for t in range(min(2, tiles)):
        start_from(load, t, core)
    greet_all(devices, seq_count)

    def start_core(t, carry):
        start_from(core_copy, t, 1 - core)
        return carry

    lax.fori_loop(0, tiles, start_core, 0)
    if receivers:
        start_push(block_ref, all_ref, devices, receivers, me, *push_sems)

    def one_step(step, carry):
        @pl.when(step < tiles)
        def _():
            t = step
            slot = lax.rem(t, RING)
            load(t).wait()
            core_copy(t).wait_recv()

            def one(index, inner):
                at = pl.ds(index * 4, 4)
                total = own_s[lax.rem(t, 2), at].astype(jnp.float32) + core_s[t, at].astype(jnp.float32)
                total = total.astype(jnp.bfloat16)
                first_s[slot, at] = total[:, :, :SPLIT]
                second_s[slot, at] = total[:, :, SPLIT:]
                return inner

            lax.fori_loop(0, half // 4, one, 0)
            first_one(t).start()
            second_one(t, 0).start()
            second_one(t, 1).start()

            @pl.when(t + 2 < tiles)
            def _():
                start_from(load, t + 2, core)

        @pl.when((step >= LAG) & (step < tiles + LAG))
        def _():
            t = step - LAG
            slot = lax.rem(t, RING)
            first_one(t).wait()

            def one(index, inner):
                at = pl.ds(index * 4, 4)
                mine = first_s[slot, pl.ds(y * quarter + index * 4, 4)].astype(jnp.float32)
                total = mine + first_y_s[t, at].astype(jnp.float32)
                first_two_s[slot, at] = total.astype(jnp.bfloat16)
                return inner

            lax.fori_loop(0, quarter // 4, one, 0)
            first_two(t).start()
            for side in range(2):
                second_one(t, side).wait()

                def two(index, inner):
                    mine = second_s[slot, pl.ds(side * quarter + x * eighth + index * 4, 4)]
                    at = pl.ds(side * eighth + index * 4, 4)
                    total = mine.astype(jnp.float32) + second_x_s[t, at].astype(jnp.float32)
                    second_two_s[slot, at] = total.astype(jnp.bfloat16)
                    return inner

                lax.fori_loop(0, eighth // 4, two, 0)
            second_two(t).start()

        @pl.when((step >= 2 * LAG) & (step < tiles + 2 * LAG))
        def _():
            t = step - 2 * LAG
            slot = lax.rem(t, RING)
            first_two(t).wait()
            second_two(t).wait()

            def one(index, inner):
                at = pl.ds(index * 4, 4)
                mine = first_two_s[slot, pl.ds(x * eighth + index * 4, 4)].astype(jnp.float32)
                total = mine + first_x_s[t, at].astype(jnp.float32)
                third_s[slot, at, :, :SPLIT] = total.astype(jnp.bfloat16)
                mine = second_two_s[slot, pl.ds(y * eighth + index * 4, 4)].astype(jnp.float32)
                total = mine + second_y_s[t, at].astype(jnp.float32)
                third_s[slot, at, :, SPLIT:] = total.astype(jnp.bfloat16)
                return inner

            lax.fori_loop(0, eighth // 4, one, 0)
            for distance in (1, 2, 3):
                z_copy(t, distance).start()

        @pl.when(step >= 3 * LAG)
        def _():
            t = step - 3 * LAG
            slot = lax.rem(t, RING)
            for distance in (1, 2, 3):
                z_copy(t, distance).wait()
            total = third_s[slot, pl.ds(z * PIECE, PIECE)].astype(jnp.float32)
            for distance in (1, 2, 3):
                total = total + along_s[t, distance - 1].astype(jnp.float32)
            leaf_s[t] = total.astype(jnp.bfloat16)
            leaf_send_all(t, 0)

        return carry

    lax.fori_loop(0, tiles + 3 * LAG, one_step, 0)

    def finish(t, carry):
        core_copy(t).wait_send()
        leaf_send_all(t, 1)
        return carry

    lax.fori_loop(0, tiles, finish, 0)
    if receivers:
        finish_push(block_ref, all_ref, devices, receivers, me, *push_sems)
    far = TILE_START - TILE * (TILE_START // TILE)
    begin = me * shard_units
    first_at = lax.rem(PIECE - lax.rem(begin + PIECE - far % PIECE, PIECE), PIECE)

    def arrive(index, count):
        unit = begin + index
        inside = False
        for start, stop in ranges:
            low_end, high_end = TILE_START + start * TILE, TILE_START + stop * TILE
            inside = inside | ((unit >= low_end) & (unit < high_end))

        @pl.when(inside)
        def _():
            part = out_ref.at[pl.ds(index, count)]
            pltpu.make_async_copy(part, part, leaf_recv.at[index]).wait()

    def arrive_three(step, carry):
        index = first_at + step * PIECE

        @pl.when(index + PIECE <= shard_units)
        def _():
            arrive(index, PIECE)

        return carry

    steps = shard_units // PIECE
    lax.fori_loop(0, steps, arrive_three, 0)
    covered = first_at + lax.div(shard_units - first_at, PIECE) * PIECE
    for step in range(PIECE - 1):

        @pl.when(step < first_at)
        def _():
            arrive(step, 1)

        @pl.when(covered + step < shard_units)
        def _():
            arrive(covered + step, 1)


def push_copy(block_ref, all_ref, devices, me, step, send_sem, recv_sem):
    seq_count = devices // 4
    other = lax.rem(me + step, devices)
    return other, pltpu.make_async_remote_copy(
        src_ref=block_ref,
        dst_ref=all_ref.at[me],
        send_sem=send_sem.at[step],
        recv_sem=recv_sem.at[me],
        device_id=(lax.div(other, seq_count), lax.rem(other, seq_count)),
        device_id_type=MESH,
    )


def start_push(block_ref, all_ref, devices, receivers, me, send_sem, recv_sem, keep_sem):
    @pl.when(me < receivers)
    def _():
        pltpu.make_async_copy(block_ref, all_ref.at[me], keep_sem).start()

    def send(step, carry):
        other, sending = push_copy(block_ref, all_ref, devices, me, step, send_sem, recv_sem)

        @pl.when(other < receivers)
        def _():
            sending.start()

        return carry

    lax.fori_loop(1, devices, send, 0)


def finish_push(block_ref, all_ref, devices, receivers, me, send_sem, recv_sem, keep_sem):
    @pl.when(me < receivers)
    def _():
        pltpu.make_async_copy(block_ref, all_ref.at[me], keep_sem).wait()

    def finish(step, carry):
        other, sending = push_copy(block_ref, all_ref, devices, me, step, send_sem, recv_sem)

        @pl.when(other < receivers)
        def _():
            sending.wait_send()

        source = lax.rem(me + devices - step, devices)

        @pl.when(me < receivers)
        def _():
            pltpu.make_async_copy(block_ref, all_ref.at[source], recv_sem.at[source]).wait()

        return carry

    lax.fori_loop(1, devices, finish, 0)


def push_sems(devices):
    dma = pltpu.SemaphoreType.DMA
    return [dma((devices,)), dma((devices,)), dma]


def reduce_rows(ranges, shard_units, devices, collective_id, pieces, block=None, receivers=0):
    tiles = sum(stop - start for start, stop in ranges)
    width = pieces[0][0].shape[1]
    sources = tuple(piece[1:] for piece in pieces)
    assert sum(count for _, count in sources) == 2 * tiles
    half, quarter, eighth = TILE // 2, TILE // 4, TILE // 8
    rest = width - SPLIT

    def vmem(*shape):
        return pltpu.VMEM(shape, jnp.bfloat16)

    dma = pltpu.SemaphoreType.DMA
    blocks = [] if block is None else [block]
    outs = [jax.ShapeDtypeStruct((shard_units, UNIT, width), jnp.bfloat16)]
    outs += [jax.ShapeDtypeStruct((devices,) + one.shape, one.dtype) for one in blocks]
    out = pl.pallas_call(
        functools.partial(reduce_kernel, ranges, shard_units, devices, sources, receivers),
        out_shape=outs,
        in_specs=[pl.BlockSpec(memory_space=pl.ANY)] * (len(pieces) + len(blocks)),
        out_specs=[pl.BlockSpec(memory_space=pl.ANY)] * len(outs),
        scratch_shapes=[
            vmem(2, half, UNIT, width),
            vmem(tiles, half, UNIT, width),
            vmem(RING, half, UNIT, SPLIT),
            vmem(RING, half, UNIT, rest),
            vmem(tiles, quarter, UNIT, SPLIT),
            vmem(tiles, quarter, UNIT, rest),
            vmem(RING, quarter, UNIT, SPLIT),
            vmem(RING, quarter, UNIT, rest),
            vmem(tiles, eighth, UNIT, SPLIT),
            vmem(tiles, eighth, UNIT, rest),
            vmem(RING, eighth, UNIT, width),
            vmem(tiles, 3, PIECE, UNIT, width),
            vmem(tiles, PIECE, UNIT, width),
            dma((2,)),
            dma((tiles,)),
            dma((tiles,)),
            dma((RING, 3)),
            dma((tiles, 3)),
            dma((RING, 2)),
            dma((tiles, 2)),
            dma((RING, 3)),
            dma((tiles, 3)),
            dma((tiles, PIECE)),
            dma((shard_units,)),
        ]
        + (push_sems(devices) if blocks else []),
        compiler_params=pltpu.CompilerParams(
            collective_id=collective_id, has_side_effects=True, vmem_limit_bytes=VMEM_BYTES
        ),
    )(*[piece[0].reshape(-1, UNIT, width) for piece in pieces], *blocks)
    return out if blocks else out[0]


STRIDE = 3
Z_LAG = 2
Z_RING = 3 * Z_LAG + 1


def gather_kernel(
    openings,
    ahead,
    devices,
    shard_ref,
    out_ref,
    later_ref,
    deal_send,
    deal_recv,
    z_send,
    z_recv,
    one_send,
    one_recv,
    two_send,
    two_recv,
    core_send,
    core_recv,
):
    shard_units = shard_ref.shape[0]
    seq_count = devices // 4
    width = shard_ref.shape[2]
    tiles = out_ref.shape[0] // TILE
    later_tiles = later_ref.shape[0] // TILE
    streams = ((openings[0], tiles, out_ref, 0), (openings[1], later_tiles, later_ref, tiles))
    y, core, z, x = my_place()
    me = (y * 2 + core) * seq_count + z * 2 + x
    half, quarter, eighth = TILE // 2, TILE // 4, TILE // 8
    leaves = TILE // PIECE
    upward = peer(y, core, jnp.minimum(z + 1, 3), x)
    downward = peer(y, core, jnp.maximum(z - 1, 0), x)

    def bounds(stream):
        begin = me * shard_units - stream[0]
        finish = begin + shard_units
        return begin, finish, lax.div(begin + PIECE - 1, PIECE), lax.div(finish, PIECE)

    def deal_some(stream, stage, three, part, count):
        begin = bounds(stream)[0]
        ref = stream[2]
        tile = lax.div(three, leaves)
        leaf = three - tile * leaves
        eight = lax.div(leaf, 4)
        slot = leaf - eight * 4 if count == PIECE else 4 + part
        holder_core = lax.div(eight, 4)
        holder_y = lax.rem(lax.div(eight, 2), 2)
        holder_x = lax.rem(eight, 2)
        holder = (holder_y * 2 + holder_core) * seq_count + z * 2 + holder_x
        index = three * PIECE + part - begin
        source = shard_ref.at[pl.ds(index, count)]
        target = ref.at[pl.ds(three * PIECE + part, count)]
        recv = deal_recv.at[stream[3] + tile, slot]
        sending = pltpu.make_async_remote_copy(
            src_ref=source,
            dst_ref=target,
            send_sem=deal_send.at[0 if stream[3] == 0 else 1, index],
            recv_sem=recv,
            device_id=peer(holder_y, holder_core, z, holder_x),
            device_id_type=MESH,
        )

        @pl.when(holder != me)
        def _():
            if stage == 0:
                sending.start()
            else:
                sending.wait_send()

        if stage == 0:

            @pl.when(holder == me)
            def _():
                pltpu.make_async_copy(source, target, recv).start()

    def deal_between(stream, stage, low_three, count, base):
        begin, finish, first_three, last_three = bounds(stream)
        base = first_three if base is None else base

        @pl.when((low_three <= last_three) & (low_three + count >= first_three))
        def _():
            def one(step, carry):
                three = base + step

                @pl.when(
                    (three >= first_three)
                    & (three < last_three)
                    & (three >= low_three)
                    & (three < low_three + count)
                )
                def _():
                    deal_some(stream, stage, three, 0, PIECE)

                return carry

            lax.fori_loop(0, min(count, shard_units // PIECE + 1), one, 0)
            for step in range(PIECE - 1):
                three = first_three - 1
                here = (three >= low_three) & (three < low_three + count)

                @pl.when(here & (begin + step < first_three * PIECE))
                def _(three=three):
                    deal_some(stream, stage, three, begin + step - three * PIECE, 1)

                three = last_three
                here = (three >= low_three) & (three < low_three + count)

                @pl.when(here & (three * PIECE + step < finish))
                def _(three=three):
                    deal_some(stream, stage, three, step, 1)

    def deal_tile(stream, step):
        low_three = tile_at(step, stream[1]) * leaves
        deal_between(stream, 0, low_three, leaves, low_three)

    def each_three(stream, t, visit):
        def one(index, carry):
            row = t * TILE + ((core * 2 + y) * 2 + x) * eighth + index * PIECE
            unit = stream[0] + row
            owner = lax.div(unit, shard_units)
            at = unit - owner * shard_units

            @pl.when(at + PIECE <= shard_units)
            def _():
                visit(row, index, PIECE, lax.rem(lax.div(owner, 2), 4))

            @pl.when(at + PIECE > shard_units)
            def _():
                for part in range(PIECE):
                    holder = jnp.where(at + part >= shard_units, owner + 1, owner)
                    visit(row + part, 4 + part, 1, lax.rem(lax.div(holder, 2), 4))

            return carry

        lax.fori_loop(0, eighth // PIECE, one, 0)

    def wait_units(ref, count, sem):
        part = ref.at[pl.ds(0, count)]
        pltpu.make_async_copy(part, part, sem).wait()

    def z_copy(stream, step, row, slot, count, way):
        part = stream[2].at[pl.ds(row, count)]
        which = 0 if stream[3] == 0 else 1
        return pltpu.make_async_remote_copy(
            src_ref=part,
            dst_ref=part,
            send_sem=z_send.at[which, lax.rem(step, Z_RING), slot, way],
            recv_sem=z_recv.at[stream[3] + tile_at(step, stream[1]), slot],
            device_id=(upward, downward)[way],
            device_id_type=MESH,
        )

    def along_z(stream, step, distance):
        t = tile_at(step, stream[1])

        def visit(row, slot, count, owner_z):
            @pl.when(jnp.abs(owner_z - z) == distance)
            def _():
                sem = deal_recv if distance == 0 else z_recv
                wait_units(out_ref, count, sem.at[stream[3] + t, slot])

                @pl.when((owner_z <= z) & (z < 3))
                def _():
                    z_copy(stream, step, row, slot, count, 0).start()

                @pl.when((owner_z >= z) & (z > 0))
                def _():
                    z_copy(stream, step, row, slot, count, 1).start()

        each_three(stream, t, visit)

    def along_z_done(stream, step):
        t = tile_at(step, stream[1])

        def visit(row, slot, count, owner_z):
            @pl.when((owner_z <= z) & (z < 3))
            def _():
                z_copy(stream, step, row, slot, count, 0).wait_send()

            @pl.when((owner_z >= z) & (z > 0))
            def _():
                z_copy(stream, step, row, slot, count, 1).wait_send()

        each_three(stream, t, visit)

    def z_stage(stream, step):
        for distance in range(4):
            old = step - distance * Z_LAG

            @pl.when((old >= 0) & (old < stream[1]))
            def _(old=old, distance=distance):
                along_z(stream, old, distance)
                if distance == 3:
                    along_z_done(stream, old)

    spreading = spread_steps(
        out_ref, one_send, one_recv, two_send, two_recv, core_send, core_recv
    )
    main, late = streams
    greet_all(devices, seq_count)
    for step in range(min(ahead, tiles)):
        deal_tile(main, step)
    for step in range(min(ahead, later_tiles)):
        deal_tile(late, step)

    def one_step(step, carry):
        @pl.when(step + ahead < tiles)
        def _():
            deal_tile(main, step + ahead)

        @pl.when(step + ahead < later_tiles)
        def _():
            deal_tile(late, step + ahead)

        z_stage(main, step)
        spreading(step - 3 * Z_LAG)
        z_stage(late, step)
        return carry

    lax.fori_loop(0, tiles + 3 * LAG + 3 * Z_LAG, one_step, 0)
    for stream in streams:
        deal_between(stream, 1, 0, stream[1] * leaves, None)


def tile_at(step, tiles):
    return lax.rem(step * STRIDE, tiles)


def spread_steps(out_ref, one_send, one_recv, two_send, two_recv, core_send, core_recv):
    tiles = out_ref.shape[0] // TILE
    width = out_ref.shape[2]
    y, core, z, x = my_place()
    half, quarter, eighth = TILE // 2, TILE // 4, TILE // 8
    left, right = pl.ds(0, SPLIT), pl.ds(SPLIT, width - SPLIT)
    whole = pl.ds(0, width)
    across_core = peer(y, 1 - core, z, x)
    across_y = peer(1 - y, core, z, x)
    across_x = peer(y, core, z, 1 - x)

    def remote(start, count, columns, send, recv, device):
        part = out_ref.at[pl.ds(start, count), :, columns]
        return pltpu.make_async_remote_copy(
            src_ref=part,
            dst_ref=part,
            send_sem=send,
            recv_sem=recv,
            device_id=device,
            device_id_type=MESH,
        )

    def block(t, y_at, x_at):
        return t * TILE + ((core * 2 + y_at) * 2 + x_at) * eighth

    def one_first(step):
        t = tile_at(step, tiles)
        sems = (one_send.at[lax.rem(step, RING), 0], one_recv.at[t, 0])
        return remote(block(t, y, x), eighth, left, *sems, across_x)

    def one_second(step):
        t = tile_at(step, tiles)
        sems = (one_send.at[lax.rem(step, RING), 1], one_recv.at[t, 1])
        return remote(block(t, y, x), eighth, right, *sems, across_y)

    def two_first(step):
        t = tile_at(step, tiles)
        sems = (two_send.at[lax.rem(step, RING), 0], two_recv.at[t, 0])
        return remote(block(t, y, 0), quarter, left, *sems, across_y)

    def two_second(step, side):
        t = tile_at(step, tiles)
        sems = (two_send.at[lax.rem(step, RING), 1 + side], two_recv.at[t, 1 + side])
        return remote(block(t, side, x), eighth, right, *sems, across_x)

    def core_copy(step):
        t = tile_at(step, tiles)
        sems = (core_send.at[lax.rem(step, RING)], core_recv.at[t])
        return remote(t * TILE + core * half, half, whole, *sems, across_core)

    def go(step):
        @pl.when((step >= 0) & (step < tiles))
        def _():
            one_first(step).start()
            one_second(step).start()

        @pl.when((step >= LAG) & (step < tiles + LAG))
        def _():
            old = step - LAG
            one_first(old).wait()
            two_first(old).start()
            one_second(old).wait()
            for side in range(2):
                two_second(old, side).start()

        @pl.when((step >= 2 * LAG) & (step < tiles + 2 * LAG))
        def _():
            old = step - 2 * LAG
            two_first(old).wait()
            for side in range(2):
                two_second(old, side).wait()
            core_copy(old).start()

        @pl.when(step >= 3 * LAG)
        def _():
            core_copy(step - 3 * LAG).wait()

    return go


def spread_sems(tiles):
    dma = pltpu.SemaphoreType.DMA
    return [
        dma((RING, 2)),
        dma((tiles, 2)),
        dma((RING, 3)),
        dma((tiles, 3)),
        dma((RING,)),
        dma((tiles,)),
    ]


def spread_kernel(devices, rows_ref, block_ref, out_ref, all_ref, *sems):
    seq_count = devices // 4
    me = lax.axis_index("dp") * seq_count + lax.axis_index("seq")
    sems, push = sems[:-3], sems[-3:]
    greet_all(devices, seq_count)
    start_push(block_ref, all_ref, devices, devices, me, *push)
    spreading = spread_steps(out_ref, *sems)

    def one_step(step, carry):
        spreading(step)
        return carry

    lax.fori_loop(0, out_ref.shape[0] // TILE + 3 * LAG, one_step, 0)
    finish_push(block_ref, all_ref, devices, devices, me, *push)


def spread_rows(rows, block, devices, collective_id):
    return pl.pallas_call(
        functools.partial(spread_kernel, devices),
        out_shape=(
            jax.ShapeDtypeStruct(rows.shape, rows.dtype),
            jax.ShapeDtypeStruct((devices,) + block.shape, block.dtype),
        ),
        in_specs=[pl.BlockSpec(memory_space=pl.ANY)] * 2,
        out_specs=(pl.BlockSpec(memory_space=pl.ANY), pl.BlockSpec(memory_space=pl.ANY)),
        scratch_shapes=spread_sems(rows.shape[0] // TILE) + push_sems(devices),
        input_output_aliases={0: 0},
        compiler_params=pltpu.CompilerParams(
            collective_id=collective_id, has_side_effects=True, vmem_limit_bytes=VMEM_BYTES
        ),
    )(rows, block)


def gather_rows(openings, counts, ahead, devices, collective_id, shard):
    units, _, width = shard.shape
    assert all(count % STRIDE for count in counts) and counts[1] <= counts[0]
    dma = pltpu.SemaphoreType.DMA
    anywhere = pl.BlockSpec(memory_space=pl.ANY)
    return pl.pallas_call(
        functools.partial(gather_kernel, openings, ahead, devices),
        out_shape=[
            jax.ShapeDtypeStruct((count * TILE, UNIT, width), jnp.bfloat16) for count in counts
        ],
        in_specs=[anywhere],
        out_specs=[anywhere, anywhere],
        scratch_shapes=[
            dma((2, units)),
            dma((sum(counts), 7)),
            dma((2, Z_RING, 7, 2)),
            dma((sum(counts), 7)),
        ]
        + spread_sems(counts[0]),
        compiler_params=pltpu.CompilerParams(
            collective_id=collective_id, has_side_effects=True, vmem_limit_bytes=VMEM_BYTES
        ),
    )(shard)


def share_kernel(devices, block_ref, out_ref, *sems):
    seq_count = devices // 4
    me = lax.axis_index("dp") * seq_count + lax.axis_index("seq")
    greet_all(devices, seq_count)
    start_push(block_ref, out_ref, devices, devices, me, *sems)
    finish_push(block_ref, out_ref, devices, devices, me, *sems)


def share(block, devices, collective_id):
    return pl.pallas_call(
        functools.partial(share_kernel, devices),
        out_shape=jax.ShapeDtypeStruct((devices,) + block.shape, block.dtype),
        in_specs=[pl.BlockSpec(memory_space=pltpu.VMEM)],
        out_specs=pl.BlockSpec(memory_space=pltpu.VMEM),
        scratch_shapes=push_sems(devices),
        compiler_params=pltpu.CompilerParams(
            collective_id=collective_id, has_side_effects=True, vmem_limit_bytes=16 * 1024 * 1024
        ),
    )(block)


def sum_kernel(devices, parts_ref, out_ref, extra_ref, got_s, part_s, send_sem, recv_sem, keep_sem, *sems):
    seq_count = devices // 4
    me = lax.axis_index("dp") * seq_count + lax.axis_index("seq")
    keep = pltpu.make_async_copy(parts_ref.at[me], got_s.at[me], keep_sem)
    keep.start()
    greet_all(devices, seq_count)

    def scatter(step):
        other = lax.rem(me + step, devices)
        return pltpu.make_async_remote_copy(
            src_ref=parts_ref.at[other],
            dst_ref=got_s.at[me],
            send_sem=send_sem.at[step],
            recv_sem=recv_sem.at[me],
            device_id=(lax.div(other, seq_count), lax.rem(other, seq_count)),
            device_id_type=MESH,
        )

    def start(step, carry):
        scatter(step).start()
        return carry

    def finish(step, carry):
        scatter(step).wait_send()
        source = lax.rem(me + devices - step, devices)
        pltpu.make_async_copy(parts_ref.at[0], got_s.at[source], recv_sem.at[source]).wait()
        return carry

    lax.fori_loop(1, devices, start, 0)
    keep.wait()
    lax.fori_loop(1, devices, finish, 0)
    total = jnp.sum(got_s[...], axis=0)
    part_s[...] = total[:-1]
    extra_ref[...] = total[-1]
    start_push(part_s, out_ref, devices, devices, me, *sems)
    finish_push(part_s, out_ref, devices, devices, me, *sems)


def sum_all(array, extra, devices, collective_id):
    tile = 8 * 128
    count = -(-array.size // (tile * devices))
    flat = jnp.pad(array.reshape(-1), (0, count * tile * devices - array.size))
    parts = flat.reshape(devices, count, 8, 128)
    parts = jnp.concatenate([parts, jnp.full((devices, 1, 8, 128), extra)], axis=1)
    vmem = pl.BlockSpec(memory_space=pltpu.VMEM)
    out, total = pl.pallas_call(
        functools.partial(sum_kernel, devices),
        out_shape=(
            jax.ShapeDtypeStruct((devices, count, 8, 128), jnp.float32),
            jax.ShapeDtypeStruct((8, 128), jnp.float32),
        ),
        in_specs=[vmem],
        out_specs=(vmem, vmem),
        scratch_shapes=[
            pltpu.VMEM((devices, count + 1, 8, 128), jnp.float32),
            pltpu.VMEM((count, 8, 128), jnp.float32),
        ]
        + push_sems(devices)
        + push_sems(devices),
        compiler_params=pltpu.CompilerParams(
            collective_id=collective_id, has_side_effects=True, vmem_limit_bytes=16 * 1024 * 1024
        ),
    )(parts)
    return out.reshape(-1)[: array.size].reshape(array.shape), total[0, 0]


def contrast_kernel(pooled_ref, pick_ref, row_ref, col_ref, scale_ref, pool_ref, text_ref, loss_ref):
    count = pick_ref.shape[1]
    scale = scale_ref[0, 0] / contrastive_sharpness_divisor
    diagonal = lax.broadcasted_iota(jnp.int32, (count, count), 0) == lax.broadcasted_iota(
        jnp.int32, (count, count), 1
    )
    loss = jnp.zeros((1, 1), jnp.float32)
    for m in range(MICRO):
        row = row_ref[m]
        col = col_ref[m] > 0.0
        image = jnp.dot(
            pick_ref[m], pooled_ref[m], precision=exact, preferred_element_type=jnp.float32
        )
        words = pooled_ref[MICRO + m]
        image_norm = lax.rsqrt(jnp.sum(image * image, axis=-1, keepdims=True) + norm_eps)
        words_norm = lax.rsqrt(jnp.sum(words * words, axis=-1, keepdims=True) + norm_eps)
        image = image * image_norm
        words = words * words_norm
        cosines = lax.dot_general(
            image,
            words,
            (((1,), (1,)), ((), ())),
            precision=exact,
            preferred_element_type=jnp.float32,
        )
        cosines = jnp.where(col, cosines / contrastive_sharpness_divisor, neg_large)
        top = jnp.max(cosines, axis=-1, keepdims=True)
        weight = jnp.exp(cosines - top)
        total = jnp.sum(weight, axis=-1, keepdims=True)
        matched = jnp.sum(jnp.where(diagonal, cosines, 0.0), axis=-1, keepdims=True)
        lost = jnp.where(row > 0.0, top + jnp.log(total) - matched, 0.0)
        loss = loss + jnp.sum(lost, axis=0, keepdims=True)
        grad = weight / total - jnp.where(diagonal, 1.0, 0.0)
        grad = jnp.where((row > 0.0) & col, grad * scale, 0.0)
        grad_image = jnp.dot(grad, words, precision=exact, preferred_element_type=jnp.float32)
        grad_words = lax.dot_general(
            grad,
            image,
            (((0,), (0,)), ((), ())),
            precision=exact,
            preferred_element_type=jnp.float32,
        )
        inner = jnp.sum(image * grad_image, axis=-1, keepdims=True)
        pool_ref[m] = image_norm * (grad_image - image * inner)
        inner = jnp.sum(words * grad_words, axis=-1, keepdims=True)
        text_ref[m] = words_norm * (grad_words - words * inner)
    loss_ref[...] = jnp.broadcast_to(loss, loss_ref.shape)


def contrast(pooled, pick, valid, scale):
    count, width = pooled.shape[1], pooled.shape[2]
    grads = jax.ShapeDtypeStruct((MICRO, count, width), jnp.float32)
    return pl.pallas_call(
        contrast_kernel,
        out_shape=(grads, grads, jax.ShapeDtypeStruct((1, 128), jnp.float32)),
        compiler_params=pltpu.CompilerParams(vmem_limit_bytes=VMEM_BYTES),
    )(pooled, pick, valid[:, :, None], valid[:, None, :], scale.reshape(1, 1))


def joint_forward_kernel(rows_ref, matrix_ref, bias_ref, out_ref):
    part, width = matrix_ref.shape[2], matrix_ref.shape[3]
    matrix = matrix_ref[...].reshape(3 * part, width)
    out_ref[0] = low(dot_nt(rows_ref[...], matrix) + bias_ref[0])


def joint_forward(rows, matrix, bias):
    count, width = rows.shape
    groups, _, columns = bias.shape
    return pl.pallas_call(
        joint_forward_kernel,
        out_shape=jax.ShapeDtypeStruct((groups, count, columns), jnp.bfloat16),
        grid=(groups,),
        in_specs=[
            pl.BlockSpec((count, width), lambda j: (0, 0)),
            pl.BlockSpec((3, 1, columns // 3, width), lambda j: (0, j, 0, 0)),
            pl.BlockSpec((1, 1, columns), lambda j: (j, 0, 0)),
        ],
        out_specs=pl.BlockSpec((1, count, columns), lambda j: (j, 0, 0)),
        compiler_params=pltpu.CompilerParams(vmem_limit_bytes=VMEM_BYTES),
    )(rows, matrix.reshape(3, groups, columns // 3, width), bias)


def joint_backward_kernel(grad_ref, matrix_ref, rows_ref, out_ref, weight_ref):
    part, width = matrix_ref.shape[2], matrix_ref.shape[3]
    grad = grad_ref[0]
    term = dot_nn(grad, matrix_ref[...].reshape(3 * part, width))
    weight_ref[...] = low(dot_tn(grad, rows_ref[...])).reshape(3, 1, part, width)

    @pl.when(pl.program_id(0) == 0)
    def _():
        out_ref[...] = term

    @pl.when(pl.program_id(0) > 0)
    def _():
        out_ref[...] += term


def joint_backward(grad, matrix, rows):
    groups, count, columns = grad.shape
    width = rows.shape[1]
    part = columns // 3
    out, weight = pl.pallas_call(
        joint_backward_kernel,
        out_shape=(
            jax.ShapeDtypeStruct((count, width), jnp.float32),
            jax.ShapeDtypeStruct((3, groups, part, width), jnp.bfloat16),
        ),
        grid=(groups,),
        in_specs=[
            pl.BlockSpec((1, count, columns), lambda j: (j, 0, 0)),
            pl.BlockSpec((3, 1, part, width), lambda j: (0, j, 0, 0)),
            pl.BlockSpec((count, width), lambda j: (0, 0)),
        ],
        out_specs=(
            pl.BlockSpec((count, width), lambda j: (0, 0)),
            pl.BlockSpec((3, 1, part, width), lambda j: (0, j, 0, 0)),
        ),
        compiler_params=pltpu.CompilerParams(vmem_limit_bytes=VMEM_BYTES),
    )(grad, matrix.reshape(3, groups, part, width), rows)
    return out, weight.reshape(3 * groups * part, width)


FEED_BLOCK = 768


def feed_forward_kernel(rows_ref, up_ref, down_ref, b_up_ref, b_down_ref, before_ref, act_ref, out_ref):
    before = dot_nt(rows_ref[...], up_ref[...]) + b_up_ref[0]
    before_ref[...] = before
    act = low(gelu_tanh(before))
    act_ref[...] = act
    term = dot_nn(act, down_ref[...])

    @pl.when(pl.program_id(0) == 0)
    def _():
        out_ref[...] = term + b_down_ref[...]

    @pl.when(pl.program_id(0) > 0)
    def _():
        out_ref[...] += term


def feed_specs(count, width, up_start, down_start):
    return (
        pl.BlockSpec((count, width), lambda j: (0, 0)),
        pl.BlockSpec((FEED_BLOCK, width), lambda j: (up_start + j, 0)),
        pl.BlockSpec((FEED_BLOCK, width), lambda j: (down_start + j, 0)),
        pl.BlockSpec((1, 1, FEED_BLOCK), lambda j: (j, 0, 0)),
        pl.BlockSpec((count, FEED_BLOCK), lambda j: (0, j)),
    )


def feed_forward(rows, up, up_start, down, down_start, b_up, b_down):
    count, width = rows.shape
    whole, up_spec, down_spec, line, column = feed_specs(count, width, up_start, down_start)
    return pl.pallas_call(
        feed_forward_kernel,
        out_shape=(
            jax.ShapeDtypeStruct((count, FF), jnp.float32),
            jax.ShapeDtypeStruct((count, FF), jnp.bfloat16),
            jax.ShapeDtypeStruct((count, width), jnp.float32),
        ),
        grid=(FF // FEED_BLOCK,),
        in_specs=[whole, up_spec, down_spec, line, pl.BlockSpec((1, width), lambda j: (0, 0))],
        out_specs=(column, column, whole),
        compiler_params=pltpu.CompilerParams(vmem_limit_bytes=VMEM_BYTES),
    )(rows, up, down, b_up.reshape(-1, 1, FEED_BLOCK), b_down)


def feed_backward_kernel(
    grad_ref, up_ref, down_ref, before_ref, act_ref, rows_ref, out_ref, w_up_ref, w_down_ref, sum_ref
):
    grad = grad_ref[...]
    before = before_ref[...]
    factor = math.sqrt(2.0 / math.pi)
    square = before * before
    bend = jnp.tanh(factor * (before + 0.044715 * (square * before)))
    slope = 0.5 * (1.0 + bend) + (0.5 * factor) * before * (1.0 - bend * bend) * (
        1.0 + (3.0 * 0.044715) * square
    )
    grad_up = dot_nt(grad, down_ref[...]) * slope
    sum_ref[0] = jnp.sum(grad_up, axis=0, keepdims=True)
    grad_up = low(grad_up)
    w_up_ref[...] = low(dot_tn(grad_up, rows_ref[...]))
    w_down_ref[...] = low(dot_tn(act_ref[...], grad))
    term = dot_nn(grad_up, up_ref[...])

    @pl.when(pl.program_id(0) == 0)
    def _():
        out_ref[...] = term

    @pl.when(pl.program_id(0) > 0)
    def _():
        out_ref[...] += term


def feed_backward(grad, up, up_start, down, down_start, before, act, rows):
    count, width = rows.shape
    whole, up_spec, down_spec, line, column = feed_specs(count, width, up_start, down_start)
    block = pl.BlockSpec((FEED_BLOCK, width), lambda j: (j, 0))
    return pl.pallas_call(
        feed_backward_kernel,
        out_shape=(
            jax.ShapeDtypeStruct((count, width), jnp.float32),
            jax.ShapeDtypeStruct((FF, width), jnp.bfloat16),
            jax.ShapeDtypeStruct((FF, width), jnp.bfloat16),
            jax.ShapeDtypeStruct((FF // FEED_BLOCK, 1, FEED_BLOCK), jnp.float32),
        ),
        grid=(FF // FEED_BLOCK,),
        in_specs=[whole, up_spec, down_spec, column, column, whole],
        out_specs=(whole, block, block, line),
        compiler_params=pltpu.CompilerParams(vmem_limit_bytes=VMEM_BYTES),
    )(grad, up, down, before, act, rows)


def adamw(param, grad, first, second, rate, decay):
    first_new = beta_one * first + (1.0 - beta_one) * grad
    second_new = beta_two * second + (1.0 - beta_two) * grad * grad
    step_dir = (
        first_new
        / (1.0 - beta_one**STEP)
        / (jnp.sqrt(second_new / (1.0 - beta_two**STEP)) + adam_eps)
    )
    return (param - rate * (step_dir + decay * param), first_new, second_new)


def per_device(
    latents,
    noise,
    captions,
    image_sizes,
    caption_lengths,
    timesteps,
    weights,
    vectors,
    weights_m,
    weights_v,
    vectors_m,
    vectors_v,
):
    width = weights.shape[1]
    seq_count = lax.axis_size("seq")
    dp_count = lax.axis_size("dp")
    seq_index = lax.axis_index("seq")
    row_index = lax.axis_index("dp")
    devices = dp_count * seq_count
    layout = matrix_rows(width)
    shard_rows = weights.shape[0]
    paired = dp_count == 4 and seq_count == 8
    weights_low = weights.astype(jnp.bfloat16)
    if paired:
        shard = weights_low.reshape(shard_rows // UNIT, UNIT, width)
        rows_all, rows_late = gather_rows((0, 2176), (23, 19), 8, devices, 7, shard)
        flat = (-1, width)
        self_head = 384
        (
            time_one,
            time_two,
            time_block,
            text_one,
            text_two,
            joint_qkv,
            self_out_head,
        ) = split_rows(rows_all.reshape(flat), layout[:6] + (self_head,))
    else:
        gathered = lax.all_gather(weights_low, both_axes, axis=0, tiled=True)
        (
            time_one,
            time_two,
            time_block,
            text_one,
            text_two,
            joint_qkv,
            self_out,
            cross_query,
            cross_kv,
            cross_out,
            mlp_up,
            mlp_down,
        ) = split_rows(gathered, layout)
    (
        table,
        final_table,
        patch_in,
        patch_out,
        b_patch,
        b_time_one,
        b_time_two,
        b_block,
        b_text_one,
        b_text_two,
        b_query,
        b_value,
        b_self_out,
        b_cross_query,
        b_cross_value,
        b_cross_out,
        b_up,
        b_down,
    ) = split_rows(vectors.astype(jnp.bfloat16).astype(jnp.float32), vector_rows(width))
    head_dim = width // HEADS
    heads = HEADS // seq_count
    part = heads * head_dim
    images = image_sizes.shape[2]
    slots = latents.shape[2]
    assert slots == BLOCK and images == seq_count
    rows = MICRO * slots
    wide = (MICRO, slots, width)
    image_count = jnp.sum((image_sizes > 0).astype(jnp.float32))
    loss_scale = 1.0 / image_count

    ends_all = jnp.cumsum(image_sizes, axis=2)
    firsts = jnp.arange(seq_count, dtype=jnp.int32) * BLOCK
    segment_all = jnp.sum(
        (ends_all[:, :, None, :] <= firsts[None, None, :, None]).astype(jnp.int32), axis=3
    )
    onehot_all = (
        segment_all[:, :, :, None] == jnp.arange(images, dtype=jnp.int32)[None, None, None, :]
    )
    size_all = jnp.sum(jnp.where(onehot_all, image_sizes[:, :, None, :], 0), axis=3)
    start_all = jnp.sum(jnp.where(onehot_all, (ends_all - image_sizes)[:, :, None, :], 0), axis=3)
    step_all = jnp.sum(jnp.where(onehot_all, timesteps[:, :, None, :], 0), axis=3)
    length_all = jnp.sum(jnp.where(onehot_all, caption_lengths[:, :, None, :], 0), axis=3)
    row_start = start_all[:, row_index]
    row_size = size_all[:, row_index]
    kv_start = row_start // BLOCK
    kv_big = (row_size == LARGE).astype(jnp.int32)
    own_segment = segment_all[:, row_index, seq_index]
    own_size = row_size[:, seq_index]
    own_start = row_start[:, seq_index]
    own_step = step_all[:, row_index, seq_index]
    own_length = length_all[:, row_index, seq_index]

    quarter = width // 4
    omega = 1.0 / 10000.0 ** (jnp.arange(quarter, dtype=jnp.float32) / quarter)
    angle = jnp.arange(2 * SIDE, dtype=jnp.float32)[:, None] * omega[None, :]
    angle_table = jnp.concatenate([jnp.sin(angle), jnp.cos(angle)], axis=1)
    within = (
        seq_index * BLOCK - own_start[:, None] + jnp.arange(slots, dtype=jnp.int32)[None, :]
    ).reshape(rows)
    side = jnp.where(own_size == LARGE, 2 * SIDE, SIDE).astype(jnp.int32)
    side = jnp.broadcast_to(side[:, None], (MICRO, slots)).reshape(rows)
    places = jnp.arange(2 * SIDE, dtype=jnp.int32)[None, :]
    pick_row = ((within // side)[:, None] == places).astype(jnp.float32)
    pick_col = ((within % side)[:, None] == places).astype(jnp.float32)
    position = jnp.concatenate(
        [
            jnp.dot(pick_row, angle_table, precision=exact),
            jnp.dot(pick_col, angle_table, precision=exact),
        ],
        axis=1,
    )

    level = noise_level(own_step)[:, None, None]
    level_prev = noise_level(own_step - 1)[:, None, None]
    beta_log, tilde_log = variance_logs(level, level_prev)
    target = noise[:, 0].astype(jnp.float32)
    noisy = jnp.sqrt(level) * latents[:, 0].astype(jnp.float32) + jnp.sqrt(1.0 - level) * target
    noisy = noisy.reshape(rows, PATCH)

    time_low = low(time_features(own_step))
    time_first = dot_nn(time_low, time_one) + b_time_one
    time_act, time_act_back = jax.vjp(jax.nn.silu, time_first)
    time_act_low = low(time_act)
    time_embed = dot_nn(time_act_low, time_two) + b_time_two
    embed_act, embed_act_back = jax.vjp(jax.nn.silu, time_embed)
    embed_low = low(embed_act)
    block_mod = dot_nt(embed_low, time_block) + b_block.reshape(1, -1) + table.reshape(1, -1)
    shift_one, scale_one, gate_one, shift_two, scale_two, gate_two = [
        piece[:, None, :] for piece in jnp.split(block_mod, 6, axis=1)
    ]
    shift_final = (final_table[0][None, :] + time_embed)[:, None, :]
    scale_final = (final_table[1][None, :] + time_embed)[:, None, :]

    hidden_zero = (jnp.dot(noisy, patch_in, precision=exact) + b_patch + position).reshape(wide)
    normed_one, mod_one_back = jax.vjp(modulate, hidden_zero, shift_one, scale_one)
    normed_one_low = low(normed_one).reshape(rows, width)
    joint_bias = jnp.concatenate([b_query, jnp.zeros_like(b_query), b_value], axis=0)
    joint_bias = jnp.transpose(joint_bias.reshape(3, seq_count, part), (1, 0, 2))
    qkv = joint_forward(normed_one_low, joint_qkv, joint_bias.reshape(seq_count, 1, 3 * part))
    caption_low = captions[:, 0].reshape(MICRO * CAP, TEXT_W)
    caption_first = dot_nn(caption_low, text_one) + b_text_one
    caption_act, caption_act_back = jax.vjp(gelu_tanh, caption_first)
    caption_act_low = low(caption_act)
    text = dot_nn(caption_act_low, text_two) + b_text_two
    lengths_slot = lax.dynamic_slice_in_dim(caption_lengths[:, row_index], seq_index, 1, 1)
    token_live = (jnp.arange(CAP, dtype=jnp.int32)[None, :] < lengths_slot).astype(jnp.float32)
    lengths_slot_float = lengths_slot.astype(jnp.float32)
    caption_pool = (
        jnp.sum(text.reshape(MICRO, CAP, width) * token_live[:, :, None], axis=1) / lengths_slot_float
    )
    text_own = low(text)
    if paired:
        qkv, text_own, rows_late = lax.optimization_barrier((qkv, text_own, rows_late))
    qkv = lax.all_to_all(qkv, "seq", split_axis=0, concat_axis=0, tiled=True)
    text_all = lax.all_gather(text_own.reshape(MICRO, CAP, width), "seq", axis=0)
    if paired:
        rows_late, words_all = spread_rows(rows_late, caption_pool.reshape(-1, 128), devices, 8)
        qkv, rows_late = lax.optimization_barrier((qkv, rows_late))
        rows_late = rows_late.reshape(flat)
        self_out_tail, cross_query, cross_kv, cross_out = split_rows(
            rows_late, (layout[6] - self_head,) + layout[7:10]
        )
        up_start = (layout[6] - self_head + sum(layout[7:10])) // FEED_BLOCK
        feed_weights = (rows_late, up_start, rows_late, up_start + FF // FEED_BLOCK)
    else:
        feed_weights = (mlp_up, 0, mlp_down, 0)
    if paired:
        self_out = jnp.concatenate([self_out_head, self_out_tail], axis=0)
    qkv = qkv.reshape(seq_count, MICRO, slots, 3 * part)
    mixed = self_forward(kv_start, kv_big, qkv, heads, head_dim)
    mixed = lax.all_to_all(
        mixed.reshape(seq_count, rows, part), "seq", split_axis=0, concat_axis=0, tiled=True
    )
    mixed_low = jnp.transpose(mixed, (1, 0, 2)).reshape(rows, width)
    attended = (dot_nn(mixed_low, self_out) + b_self_out).reshape(wide)
    hidden_one = hidden_zero + gate_one * attended

    text_low = jnp.concatenate(
        [
            lax.dynamic_slice(text_all, (own_segment[m], m, 0, 0), (1, 1, CAP, width))[0, 0]
            for m in range(MICRO)
        ],
        axis=0,
    )
    text_kv = dot_nt(text_low, cross_kv)
    pad_rows = ((0, 0), (0, CAP_PAD - CAP), (0, 0))
    key_text = jnp.pad(low(text_kv[:, :width]).reshape(MICRO, CAP, width), pad_rows)
    value_text = jnp.pad(
        low(text_kv[:, width:] + b_cross_value).reshape(MICRO, CAP, width), pad_rows
    )
    hidden_one_low = low(hidden_one).reshape(rows, width)
    query_cross = low(dot_nn(hidden_one_low, cross_query) + b_cross_query).reshape(wide)
    cross_low = cross_call(
        functools.partial(cross_forward_kernel, head_dim),
        own_length,
        (query_cross, key_text, value_text),
        jax.ShapeDtypeStruct(wide, jnp.bfloat16),
    ).reshape(rows, width)
    hidden_two = hidden_one + (dot_nn(cross_low, cross_out) + b_cross_out).reshape(wide)
    normed_two, mod_two_back = jax.vjp(modulate, hidden_two, shift_two, scale_two)
    normed_two_low = low(normed_two).reshape(rows, width)
    upward, upward_low, feed = feed_forward(normed_two_low, *feed_weights, b_up, b_down)
    feed = feed.reshape(wide)
    hidden_three = hidden_two + gate_two * feed
    final_normed, final_back = jax.vjp(modulate, hidden_three, shift_final, scale_final)
    final_flat = final_normed.reshape(rows, width)
    predicted = jnp.dot(final_flat, patch_out.T, precision=exact).reshape(MICRO, slots, 2 * PATCH)
    error = predicted[:, :, :PATCH] - target
    frac = (predicted[:, :, PATCH:] + 1.0) * 0.5
    model_log = frac * beta_log + (1.0 - frac) * tilde_log
    ratio = jnp.exp(tilde_log - model_log)
    spread = 0.5 * (model_log - tilde_log - 1.0 + ratio) / log_two
    error_weight = (1.0 / (float(PATCH) * own_size.astype(jnp.float32)))[:, None, None]
    squared_loss = jnp.sum((error * error + spread) * error_weight)

    pooled = jnp.sum(final_normed, axis=1)
    if paired:
        pooled_all = share(pooled.reshape(-1, 128), devices, 1)
    else:
        pooled_all = lax.all_gather(pooled, both_axes, axis=0)
        words_all = lax.all_gather(caption_pool, both_axes, axis=0)
    each = (devices, MICRO, width)
    pooled_all = jnp.concatenate([pooled_all.reshape(each), words_all.reshape(each)], axis=1)
    pooled_all = jnp.transpose(pooled_all, (1, 0, 2))
    size_float = jnp.maximum(image_sizes.astype(jnp.float32), 1.0)
    pick = onehot_all.astype(jnp.float32) / size_float[:, :, None, :]
    same_row = jnp.eye(dp_count, dtype=jnp.float32)
    pick = jnp.einsum("mrsi,rq->mriqs", pick, same_row, precision=exact).reshape(
        MICRO, dp_count * images, devices
    )
    valid = (image_sizes > 0).astype(jnp.float32).reshape(MICRO, dp_count * images)
    grad_pool, grad_caption, contrast_value = contrast(pooled_all, pick, valid, loss_scale)
    contrast_value = contrast_value[0, 0]
    own_pool = row_index * images + own_segment
    grad_pool_own = jnp.concatenate(
        [lax.dynamic_slice(grad_pool, (m, own_pool[m], 0), (1, 1, width))[0] for m in range(MICRO)]
    ) / own_size.astype(jnp.float32)[:, None]
    grad_caption = lax.dynamic_slice_in_dim(
        grad_caption, row_index * images + seq_index, 1, 1
    )[:, 0]

    grad_spread = 0.5 * (1.0 - ratio) / log_two * 0.5 * (beta_log - tilde_log)
    grad_predicted = (
        loss_scale * error_weight * jnp.concatenate([2.0 * error, grad_spread], axis=2)
    ).reshape(rows, 2 * PATCH)
    grad_final = grad_pool_own[:, None, :] + jnp.dot(
        grad_predicted, patch_out, precision=exact
    ).reshape(wide)
    grad_patch_out = lax.dot_general(
        grad_predicted, final_flat, (((0,), (0,)), ((), ())), precision=exact
    )
    grad_three, grad_shift_final, grad_scale_final = final_back(grad_final)
    grad_shift_final = grad_shift_final[:, 0]
    grad_scale_final = grad_scale_final[:, 0]
    grad_final_table = jnp.stack([grad_shift_final.sum(axis=0), grad_scale_final.sum(axis=0)])
    grad_embed = grad_shift_final + grad_scale_final

    grad_feed = (grad_three * gate_two).reshape(rows, width)
    grad_feed_low = low(grad_feed)
    grad_normed_two, weight_up, weight_down, grad_b_up = feed_backward(
        grad_feed_low, *feed_weights, upward, upward_low, normed_two_low
    )
    grad_two_mod, grad_shift_two, grad_scale_two = mod_two_back(grad_normed_two.reshape(wide))
    grad_gate_two = jnp.sum(grad_three * feed, axis=1, keepdims=True)
    grad_two = grad_three + grad_two_mod
    grad_two_flat = grad_two.reshape(rows, width)
    grad_two_low = low(grad_two_flat)
    weight_cross_out = dot_tn(cross_low, grad_two_low)
    grad_cross_low = low(dot_nt(grad_two_low, cross_out)).reshape(wide)
    padded = jax.ShapeDtypeStruct((MICRO, CAP_PAD, width), jnp.float32)
    grad_query_cross, grad_key_text, grad_value_text = cross_call(
        functools.partial(cross_backward_kernel, head_dim),
        own_length,
        (query_cross, key_text, value_text, grad_cross_low),
        (jax.ShapeDtypeStruct(wide, jnp.float32), padded, padded),
    )
    grad_query_cross = grad_query_cross.reshape(rows, width)
    grad_query_low = low(grad_query_cross)
    weight_cross_query = dot_tn(hidden_one_low, grad_query_low)
    grad_one = grad_two + dot_nt(grad_query_low, cross_query).reshape(wide)

    grad_kv = jnp.concatenate([grad_key_text[:, :CAP], grad_value_text[:, :CAP]], axis=2).reshape(
        MICRO * CAP, 2 * width
    )
    grad_kv_low = low(grad_kv)
    weight_cross_kv = dot_tn(grad_kv_low, text_low)
    grad_text_part = low(dot_nn(grad_kv_low, cross_kv)).reshape(MICRO, CAP, width)
    grad_text_all = lax.all_gather(grad_text_part, "seq", axis=0).astype(jnp.float32)
    mine = (segment_all[:, row_index] == seq_index).astype(jnp.float32)
    grad_text = jnp.sum(grad_text_all * jnp.transpose(mine)[:, :, None, None], axis=0) + (
        (grad_caption / lengths_slot_float)[:, None, :] * token_live[:, :, None]
    )
    grad_text = grad_text.reshape(MICRO * CAP, width)
    grad_text_low = low(grad_text)
    weight_text_two = dot_tn(caption_act_low, grad_text_low)
    grad_caption_first = caption_act_back(dot_nt(grad_text_low, text_two))[0]
    grad_caption_low = low(grad_caption_first)
    head_rows = TILE_START * UNIT - sum(layout[:3]) + TILE * UNIT // 2 if paired else 0
    weight_text_one = dot_tn(caption_low[:, head_rows:], grad_caption_low)

    grad_attended = (grad_one * gate_one).reshape(rows, width)
    grad_gate_one = jnp.sum(grad_one * attended, axis=1, keepdims=True)
    grad_attended_low = low(grad_attended)
    weight_self_out = dot_tn(mixed_low, grad_attended_low)
    grad_mixed = low(dot_nt(grad_attended_low, self_out)).reshape(rows, seq_count, part)
    grad_mixed = jnp.transpose(grad_mixed, (1, 0, 2))
    if paired:
        weight_up, weight_down, grad_mixed = lax.optimization_barrier(
            (low(weight_up), low(weight_down), grad_mixed)
        )
    grad_mixed = lax.all_to_all(grad_mixed, "seq", split_axis=0, concat_axis=0, tiled=True)
    if paired:
        summed_feed = reduce_rows(
            ((19, 31),), shard_rows // UNIT, devices, 2, ((weight_up, 0, 12), (weight_down, 0, 12))
        )
        grad_mixed, summed_feed = lax.optimization_barrier((grad_mixed, summed_feed))
    grad_mixed = grad_mixed.reshape(seq_count, MICRO, slots, part)
    grad_qkv, head_sums = self_backward(kv_start, kv_big, qkv, grad_mixed, heads, head_dim)
    head_sums = jnp.sum(head_sums[:, 0], axis=0)
    column = seq_index * part
    grad_bias_query = lax.dynamic_update_slice(
        jnp.zeros((width,), jnp.float32), head_sums[:part], (column,)
    )
    grad_bias_value = lax.dynamic_update_slice(
        jnp.zeros((width,), jnp.float32), head_sums[part:], (column,)
    )
    grad_qkv = grad_qkv.reshape(seq_count, rows, 3 * part)
    if paired:
        time_rows = layout[0] + layout[1]
        block_rows = layout[2]
        weight_self_out = low(weight_self_out)
        first_half = low(dot_tn(caption_low[:, :head_rows], grad_caption_low))
        first_half = jnp.pad(first_half, ((TILE * UNIT // 2 - head_rows, 0), (0, 0)))
        (
            first_half,
            weight_text_one,
            weight_text_two,
            weight_self_out,
            weight_cross_query,
            weight_cross_kv,
            weight_cross_out,
            grad_qkv,
        ) = lax.optimization_barrier(
            (
                first_half,
                low(weight_text_one),
                low(weight_text_two),
                weight_self_out,
                low(weight_cross_query),
                low(weight_cross_kv),
                low(weight_cross_out),
                grad_qkv,
            )
        )
    grad_qkv = lax.all_to_all(
        grad_qkv, "seq", split_axis=0, concat_axis=0, tiled=True
    )
    if paired:
        summed_middle = reduce_rows(
            ((0, 7), (12, 19)),
            shard_rows // UNIT,
            devices,
            3,
            (
                (first_half, 0, 1),
                (weight_text_one, 0, 10),
                (weight_text_two, 0, 3),
                (weight_self_out, TILE // 2, 2),
                (weight_cross_query, 0, 3),
                (weight_cross_kv, 0, 6),
                (weight_cross_out, 0, 3),
            ),
        )
        grad_qkv, summed_middle = lax.optimization_barrier((grad_qkv, summed_middle))
    grad_normed_one, weight_joint = joint_backward(grad_qkv, joint_qkv, normed_one_low)
    grad_zero_mod, grad_shift_one, grad_scale_one = mod_one_back(grad_normed_one.reshape(wide))
    grad_zero = (grad_one + grad_zero_mod).reshape(rows, width)
    grad_patch_in = lax.dot_general(noisy, grad_zero, (((0,), (0,)), ((), ())), precision=exact)

    grad_mod = jnp.concatenate(
        [grad_shift_one, grad_scale_one, grad_gate_one, grad_shift_two, grad_scale_two, grad_gate_two],
        axis=1,
    )
    grad_table = jnp.sum(grad_mod, axis=0)
    grad_mod_low = low(grad_mod.reshape(MICRO, 6 * width))
    weight_block = dot_tn(grad_mod_low, embed_low)
    grad_embed = grad_embed + embed_act_back(dot_nn(grad_mod_low, time_block))[0]
    grad_embed_low = low(grad_embed)
    weight_time_two = dot_tn(time_act_low, grad_embed_low)
    grad_time_first = time_act_back(dot_nt(grad_embed_low, time_two))[0]
    weight_time_one = dot_tn(time_low, low(grad_time_first))

    if paired:
        holders = -(-(time_rows + block_rows) // shard_rows)
        own_grads = jnp.concatenate(
            [grad_mod_low, grad_embed_low, low(grad_time_first), embed_low, time_act_low, time_low],
            axis=1,
        )
        summed_joint, grads_all = reduce_rows(
            ((7, 12),),
            shard_rows // UNIT,
            devices,
            4,
            ((low(weight_joint), 0, 9), (weight_self_out, 0, 1)),
            own_grads.reshape(-1, 128),
            holders,
        )
        grads_all = jnp.where(device_index() < holders, grads_all, 0)
        grads_all = grads_all.reshape(devices * MICRO, -1)
        ends = [6 * width, 7 * width, 8 * width, 9 * width, 10 * width]
        grad_block_all, grad_two_all, grad_one_all, embed_all, act_all, features_all = jnp.split(
            grads_all, ends, axis=1
        )
        first_row = device_index() * shard_rows

        def own_columns(array, start):
            stop = start + array.shape[1]
            spread = jnp.pad(array, ((0, 0), (start, shard_rows + (-stop) % shard_rows)))
            place = jnp.minimum(first_row, spread.shape[1] - shard_rows)
            return lax.dynamic_slice(spread, (0, place), (array.shape[0], shard_rows))

        summed_time = (
            dot_tn(own_columns(features_all, 0), grad_one_all)
            + dot_tn(own_columns(act_all, layout[0]), grad_two_all)
            + dot_tn(own_columns(grad_block_all, time_rows), embed_all)
        )
        row = first_row + jnp.arange(shard_rows, dtype=jnp.int32)
        tile = ((row - TILE_START * UNIT) // (TILE * UNIT))[:, None]
        flat = (shard_rows, width)
        reduced = jnp.where(
            tile >= 19,
            summed_feed.reshape(flat),
            jnp.where(
                (tile >= 7) & (tile < 12), summed_joint.reshape(flat), summed_middle.reshape(flat)
            ),
        ).astype(jnp.float32)
        summed = jnp.where(row[:, None] < time_rows + block_rows, summed_time, reduced)
    else:
        grad_weights = jnp.concatenate(
            [
                low(piece)
                for piece in (
                    weight_time_one,
                    weight_time_two,
                    weight_block,
                    weight_text_one,
                    weight_text_two,
                    weight_joint,
                    weight_self_out,
                    weight_cross_query,
                    weight_cross_kv,
                    weight_cross_out,
                    weight_up,
                    weight_down,
                )
            ],
            axis=0,
        )
        summed = lax.psum_scatter(
            grad_weights, both_axes, scatter_dimension=0, tiled=True
        ).astype(jnp.float32)
    grad_vector = jnp.concatenate(
        [
            grad_table,
            grad_final_table,
            grad_patch_in,
            grad_patch_out,
            jnp.sum(grad_zero, axis=0)[None, :],
            jnp.sum(grad_time_first, axis=0)[None, :],
            jnp.sum(grad_embed, axis=0)[None, :],
            grad_table,
            jnp.sum(grad_caption_first, axis=0)[None, :],
            jnp.sum(grad_text, axis=0)[None, :],
            grad_bias_query[None, :],
            grad_bias_value[None, :],
            jnp.sum(grad_attended, axis=0)[None, :],
            jnp.sum(grad_query_cross, axis=0)[None, :],
            jnp.sum(grad_kv[:, width:], axis=0)[None, :],
            jnp.sum(grad_two_flat, axis=0)[None, :],
            grad_b_up.reshape(-1, width),
            jnp.sum(grad_feed, axis=0)[None, :],
            jnp.full((2, width), squared_loss),
        ],
        axis=0,
    )
    squares = jnp.sum(summed * summed)
    if paired:
        grad_vectors, squares_all = sum_all(grad_vector, squares, devices, 6)
    else:
        grad_vectors, squares_all = lax.psum((grad_vector, squares), both_axes)
    loss_sum = grad_vectors[vectors.shape[0], 0] + contrast_value
    grad_vectors = grad_vectors[: vectors.shape[0]]
    down_bias_grad = grad_vectors[grad_vectors.shape[0] - 1]
    grad_norm = jnp.sqrt(squares_all + jnp.sum(grad_vectors * grad_vectors))
    factor = jnp.minimum(1.0, clip_norm / (grad_norm + 1e-06))
    new_w, first_w, second_w = adamw(
        weights, summed * factor, weights_m, weights_v, rate_matrix, weight_decay
    )
    new_v, first_v, second_v = adamw(
        vectors, grad_vectors * factor, vectors_m, vectors_v, rate_vector, 0.0
    )
    return (
        new_w,
        first_w,
        second_w,
        new_v,
        first_v,
        second_v,
        loss_sum,
        image_count,
        grad_norm,
        down_bias_grad,
    )


def solution(mesh):
    shard = P(both_axes, None)
    data = P(None, "dp", "seq", None)
    return jax.shard_map(
        per_device,
        mesh=mesh,
        in_specs=(data, data, data, P(), P(), P(), shard, P(), shard, shard, P(), P()),
        out_specs=(shard, shard, shard, P(), P(), P(), P(), P(), P(), P()),
        check_vma=False,
    )
```

```python
import functools
import math

import jax
import jax.numpy as jnp
from jax import lax
from jax.experimental import pallas as pl
from jax.experimental.pallas import tpu as pltpu
from jax.sharding import PartitionSpec as P

HEADS = 16
FF = 4608
TEXT_W = 4096
FREQ = 256
CAP = 120
CAP_PAD = 128
SIDE = 16
PATCH = 16
MICRO = 2
STEP = 10
BLOCK = 256
LARGE = 1024
VMEM_BYTES = 56 * 1024 * 1024

exact = lax.Precision.HIGHEST
clip_norm = 0.002
contrastive_sharpness_divisor = 0.1
beta_one = 0.9
beta_two = 0.999
adam_eps = 1e-08
weight_decay = 0.01
rate_matrix = 0.05
rate_vector = 0.3
norm_eps = 1e-06
neg_large = -1e30
log_two = math.log(2.0)
both_axes = ("dp", "seq")


def matrix_rows(width):
    return (FREQ, width, 6 * width, TEXT_W, width, 3 * width, width, width, 2 * width, width, FF, FF)


def vector_rows(width):
    return (6, 2, PATCH, 2 * PATCH, 1, 1, 1, 6, 1, 1, 1, 1, 1, 1, 1, 1, FF // width, 1)


def split_rows(whole, rows):
    pieces = []
    offset = 0
    for number in rows:
        pieces.append(whole[offset : offset + number])
        offset = offset + number
    return pieces


def device_index():
    return lax.axis_index("dp") * lax.axis_size("seq") + lax.axis_index("seq")


def modulate(hidden, shift, scale):
    centre = hidden - jnp.mean(hidden, axis=-1, keepdims=True)
    normed = centre * lax.rsqrt(jnp.mean(centre * centre, axis=-1, keepdims=True) + norm_eps)
    return normed * (1.0 + scale) + shift


def gelu_tanh(values):
    return jax.nn.gelu(values, approximate=True)


def time_features(steps_now):
    half_size = FREQ // 2
    frequency = jnp.exp(-math.log(10000.0) * jnp.arange(half_size, dtype=jnp.float32) / half_size)
    angles = steps_now.astype(jnp.float32)[:, None] * frequency[None, :]
    return jnp.concatenate([jnp.cos(angles), jnp.sin(angles)], axis=1)


def noise_level(steps_now):
    phase = (steps_now.astype(jnp.float32) / 1000.0 + 0.008) / 1.008 * (math.pi / 2.0)
    return jnp.cos(phase) ** 2


def variance_logs(level, level_prev):
    beta_now = jnp.minimum(1.0 - level / level_prev, 0.999)
    tilde_log = jnp.log(beta_now * (1.0 - level_prev) / (1.0 - level))
    return (jnp.log(beta_now), tilde_log)


def dot_nn(left, right):
    return lax.dot_general(left, right, (((1,), (0,)), ((), ())), preferred_element_type=jnp.float32)


def dot_nt(left, right):
    return lax.dot_general(left, right, (((1,), (1,)), ((), ())), preferred_element_type=jnp.float32)


def dot_tn(left, right):
    return lax.dot_general(left, right, (((0,), (0,)), ((), ())), preferred_element_type=jnp.float32)


def low(values):
    return values.astype(jnp.bfloat16)


def self_forward_kernel(heads, dim, start_ref, big_ref, qkv_ref, out_ref, key_s, value_s):
    micro = pl.program_id(0)
    blocks = qkv_ref.shape[0]
    scale = dim ** (-0.5)
    for b in range(blocks):
        for h in range(heads):
            rows = pl.ds(b * BLOCK, BLOCK)
            key_s[h, rows, :] = qkv_ref[b, 0, :, (heads + h) * dim : (heads + h + 1) * dim]
            value_s[h, rows, :] = qkv_ref[b, 0, :, (2 * heads + h) * dim : (2 * heads + h + 1) * dim]

    def one_block(b, carry):
        start = pl.multiple_of(start_ref[micro, b] * BLOCK, BLOCK)
        queries = qkv_ref[b, 0]

        def go(span):
            outs = []
            for h in range(heads):
                key = key_s[h, pl.ds(start, span), :]
                value = value_s[h, pl.ds(start, span), :]
                scores = dot_nt(queries[:, h * dim : (h + 1) * dim], key) * scale
                top = jnp.max(scores, axis=-1, keepdims=True)
                weight = jnp.exp(scores - top)
                total = jnp.sum(weight, axis=-1, keepdims=True)
                probs = low(weight * (1.0 / total))
                outs.append(low(dot_nn(probs, value)))
            out_ref[b, 0] = jnp.concatenate(outs, axis=-1)

        big = big_ref[micro, b]

        @pl.when(big == 1)
        def _():
            go(LARGE)

        @pl.when(big == 0)
        def _():
            go(BLOCK)

        return carry

    lax.fori_loop(0, blocks, one_block, 0)


def self_forward(start, big, qkv, heads, dim):
    blocks, micros = qkv.shape[0], qkv.shape[1]
    span = blocks * BLOCK
    return pl.pallas_call(
        functools.partial(self_forward_kernel, heads, dim),
        out_shape=jax.ShapeDtypeStruct((blocks, micros, BLOCK, heads * dim), jnp.bfloat16),
        grid_spec=pltpu.PrefetchScalarGridSpec(
            num_scalar_prefetch=2,
            grid=(micros,),
            in_specs=[pl.BlockSpec((blocks, 1, BLOCK, 3 * heads * dim), lambda m, s, g: (0, m, 0, 0))],
            out_specs=pl.BlockSpec((blocks, 1, BLOCK, heads * dim), lambda m, s, g: (0, m, 0, 0)),
            scratch_shapes=[
                pltpu.VMEM((heads, span, dim), jnp.bfloat16),
                pltpu.VMEM((heads, span, dim), jnp.bfloat16),
            ],
        ),
        compiler_params=pltpu.CompilerParams(vmem_limit_bytes=VMEM_BYTES),
    )(start, big, qkv)


def self_backward_kernel(
    heads, dim, start_ref, big_ref, qkv_ref, grad_ref, out_ref, sum_ref, key_s, value_s, dq_s, dk_s, dv_s
):
    micro = pl.program_id(0)
    blocks = qkv_ref.shape[0]
    scale = dim ** (-0.5)
    for b in range(blocks):
        for h in range(heads):
            rows = pl.ds(b * BLOCK, BLOCK)
            key_s[h, rows, :] = qkv_ref[b, 0, :, (heads + h) * dim : (heads + h + 1) * dim]
            value_s[h, rows, :] = qkv_ref[b, 0, :, (2 * heads + h) * dim : (2 * heads + h + 1) * dim]
    dk_s[...] = jnp.zeros_like(dk_s)
    dv_s[...] = jnp.zeros_like(dv_s)

    def one_block(b, carry):
        start = pl.multiple_of(start_ref[micro, b] * BLOCK, BLOCK)
        place = pl.multiple_of(b * BLOCK, BLOCK)
        queries = qkv_ref[b, 0]
        grads = grad_ref[b, 0]

        def go(span):
            keep = pl.ds(start, span)
            for h in range(heads):
                query = queries[:, h * dim : (h + 1) * dim]
                grad = grads[:, h * dim : (h + 1) * dim]
                key = key_s[h, keep, :]
                value = value_s[h, keep, :]
                scores = dot_nt(key, query) * scale
                top = jnp.max(scores, axis=0, keepdims=True)
                weight = jnp.exp(scores - top)
                probs = weight * (1.0 / jnp.sum(weight, axis=0, keepdims=True))
                dv_s[h, keep, :] += dot_nn(low(probs), grad)
                grad_probs = dot_nt(value, grad)
                inner = jnp.sum(probs * grad_probs, axis=0, keepdims=True)
                grad_scores = low(probs * (grad_probs - inner) * scale)
                dk_s[h, keep, :] += dot_nn(grad_scores, query)
                dq_s[h, pl.ds(place, BLOCK), :] = dot_tn(grad_scores, key)

        big = big_ref[micro, b]

        @pl.when(big == 1)
        def _():
            go(LARGE)

        @pl.when(big == 0)
        def _():
            go(BLOCK)

        return carry

    lax.fori_loop(0, blocks, one_block, 0)
    for b in range(blocks):
        rows = pl.ds(b * BLOCK, BLOCK)
        out_ref[b, 0] = jnp.concatenate(
            [low(part[h, rows, :]) for part in (dq_s, dk_s, dv_s) for h in range(heads)], axis=-1
        )
    sum_ref[0] = jnp.concatenate(
        [jnp.sum(part[h], axis=0, keepdims=True) for part in (dq_s, dv_s) for h in range(heads)], axis=-1
    )


def self_backward(start, big, qkv, grad, heads, dim):
    blocks, micros = qkv.shape[0], qkv.shape[1]
    span = blocks * BLOCK
    wide = pltpu.VMEM((heads, span, dim), jnp.float32)
    narrow = pltpu.VMEM((heads, span, dim), jnp.bfloat16)
    return pl.pallas_call(
        functools.partial(self_backward_kernel, heads, dim),
        out_shape=(
            jax.ShapeDtypeStruct((blocks, micros, BLOCK, 3 * heads * dim), jnp.bfloat16),
            jax.ShapeDtypeStruct((micros, 1, 2 * heads * dim), jnp.float32),
        ),
        grid_spec=pltpu.PrefetchScalarGridSpec(
            num_scalar_prefetch=2,
            grid=(micros,),
            in_specs=[
                pl.BlockSpec((blocks, 1, BLOCK, 3 * heads * dim), lambda m, s, g: (0, m, 0, 0)),
                pl.BlockSpec((blocks, 1, BLOCK, heads * dim), lambda m, s, g: (0, m, 0, 0)),
            ],
            out_specs=(
                pl.BlockSpec((blocks, 1, BLOCK, 3 * heads * dim), lambda m, s, g: (0, m, 0, 0)),
                pl.BlockSpec((1, 1, 2 * heads * dim), lambda m, s, g: (m, 0, 0)),
            ),
            scratch_shapes=[narrow, narrow, wide, wide, wide],
        ),
        compiler_params=pltpu.CompilerParams(vmem_limit_bytes=VMEM_BYTES),
    )(start, big, qkv, grad)


def cross_forward_kernel(dim, length_ref, query_ref, key_ref, value_ref, out_ref):
    length = length_ref[pl.program_id(0)]
    scale = dim ** (-0.5)
    live = lax.broadcasted_iota(jnp.int32, (BLOCK, CAP_PAD), 1) < length
    outs = []
    for h in range(HEADS):
        part = slice(h * dim, (h + 1) * dim)
        scores = jnp.where(live, dot_nt(query_ref[0, :, part], key_ref[0, :, part]) * scale, neg_large)
        weight = jnp.exp(scores - jnp.max(scores, axis=-1, keepdims=True))
        probs = low(weight * (1.0 / jnp.sum(weight, axis=-1, keepdims=True)))
        outs.append(low(dot_nn(probs, value_ref[0, :, part])))
    out_ref[0] = jnp.concatenate(outs, axis=-1)


def cross_backward_kernel(
    dim, length_ref, query_ref, key_ref, value_ref, grad_ref, dq_ref, dk_ref, dv_ref
):
    length = length_ref[pl.program_id(0)]
    scale = dim ** (-0.5)
    live = lax.broadcasted_iota(jnp.int32, (CAP_PAD, BLOCK), 0) < length
    dq, dk, dv = [], [], []
    for h in range(HEADS):
        part = slice(h * dim, (h + 1) * dim)
        query, key, value, grad = (
            query_ref[0, :, part],
            key_ref[0, :, part],
            value_ref[0, :, part],
            grad_ref[0, :, part],
        )
        scores = jnp.where(live, dot_nt(key, query) * scale, neg_large)
        weight = jnp.exp(scores - jnp.max(scores, axis=0, keepdims=True))
        probs = weight * (1.0 / jnp.sum(weight, axis=0, keepdims=True))
        dv.append(dot_nn(low(probs), grad))
        grad_probs = dot_nt(value, grad)
        inner = jnp.sum(probs * grad_probs, axis=0, keepdims=True)
        grad_scores = low(probs * (grad_probs - inner) * scale)
        dk.append(dot_nn(grad_scores, query))
        dq.append(dot_tn(grad_scores, key))
    dq_ref[0] = jnp.concatenate(dq, axis=-1)
    dk_ref[0] = jnp.concatenate(dk, axis=-1)
    dv_ref[0] = jnp.concatenate(dv, axis=-1)


def cross_call(kernel, length, arrays, outs):
    def spec(array):
        return pl.BlockSpec((1,) + array.shape[1:], lambda m, s: (m, 0, 0))

    return pl.pallas_call(
        kernel,
        out_shape=outs,
        grid_spec=pltpu.PrefetchScalarGridSpec(
            num_scalar_prefetch=1,
            grid=(MICRO,),
            in_specs=[spec(array) for array in arrays],
            out_specs=jax.tree.map(spec, outs),
        ),
        compiler_params=pltpu.CompilerParams(vmem_limit_bytes=VMEM_BYTES),
    )(length, *arrays)


UNIT = 8
SPLIT = 640
PIECE = 3
TILE = 96
TILE_START = 1024
LAG = 2
RING = LAG + 1
MESH = pl.DeviceIdType.MESH


def my_place():
    row, seq = lax.axis_index("dp"), lax.axis_index("seq")
    return lax.div(row, 2), lax.rem(row, 2), lax.div(seq, 2), lax.rem(seq, 2)


def peer(y, core, z, x):
    return (y * 2 + core, z * 2 + x)


def greet_all(devices, seq_count):
    me = lax.axis_index("dp") * seq_count + lax.axis_index("seq")
    barrier = pltpu.get_barrier_semaphore()

    def one(step, carry):
        other = lax.rem(me + step, devices)
        pl.semaphore_signal(
            barrier,
            inc=1,
            device_id=(lax.div(other, seq_count), lax.rem(other, seq_count)),
            device_id_type=MESH,
        )
        return carry

    lax.fori_loop(1, devices, one, 0)
    pl.semaphore_wait(barrier, devices - 1)


def global_tile(ranges, index):
    tile = index + ranges[0][0]
    at = ranges[0][1] - ranges[0][0]
    for start, stop in ranges[1:]:
        tile = jnp.where(index >= at, index - at + start, tile)
        at += stop - start
    return tile


def reduce_kernel(
    ranges,
    shard_units,
    devices,
    sources,
    receivers,
    *refs,
):
    rows_refs, refs = refs[: len(sources)], list(refs[len(sources) :])
    if receivers:
        block_ref, parts_ref = refs.pop(0), refs.pop(0)
        all_ref, got_ref = refs.pop(1), refs.pop(1)
        refs, push, push_parts = refs[:-6], refs[-6:-3], refs[-3:]
    (
    out_ref,
    own_s,
    core_s,
    first_s,
    second_s,
    first_y_s,
    second_x_s,
    first_two_s,
    second_two_s,
    first_x_s,
    second_y_s,
    third_s,
    along_s,
    leaf_s,
    load_sem,
    core_send,
    core_recv,
    one_send,
    one_recv,
    two_send,
    two_recv,
    z_send,
    z_recv,
    leaf_send,
    leaf_recv,
    ) = refs
    tiles = core_s.shape[0]
    seq_count = devices // 4
    y, core, z, x = my_place()
    me = (y * 2 + core) * seq_count + z * 2 + x
    place = ((core * 2 + y) * 2 + x) * 4 + z
    half, quarter, eighth = TILE // 2, TILE // 4, TILE // 8
    across_core = peer(y, 1 - core, z, x)
    across_y = peer(1 - y, core, z, x)
    across_x = peer(y, core, z, 1 - x)

    def remote(source, target, send, recv, device):
        return pltpu.make_async_remote_copy(
            src_ref=source,
            dst_ref=target,
            send_sem=send,
            recv_sem=recv,
            device_id=device,
            device_id_type=MESH,
        )

    def core_copy(t, rows_ref=None, start=0):
        source = own_s.at[0] if rows_ref is None else rows_ref.at[pl.ds(start, half)]
        return remote(source, core_s.at[t], core_send.at[t], core_recv.at[t], across_core)

    def load(t, rows_ref=None, start=0):
        slot = lax.rem(t, 2)
        source = rows_refs[-1] if rows_ref is None else rows_ref
        return pltpu.make_async_copy(
            source.at[pl.ds(start, half)], own_s.at[slot], load_sem.at[slot]
        )

    def start_from(copy, t, side):
        index = t * 2 + side
        at = 0
        for rows_ref, (start, count) in zip(rows_refs, sources):

            @pl.when((index >= at) & (index < at + count))
            def _(rows_ref=rows_ref, start=start, at=at):
                copy(t, rows_ref, start + (index - at) * half).start()

            at += count

    def first_one(t):
        return remote(
            first_s.at[lax.rem(t, RING), pl.ds((1 - y) * quarter, quarter)],
            first_y_s.at[t],
            one_send.at[lax.rem(t, RING), 0],
            one_recv.at[t, 0],
            across_y,
        )

    def second_one(t, side):
        return remote(
            second_s.at[lax.rem(t, RING), pl.ds(side * quarter + (1 - x) * eighth, eighth)],
            second_x_s.at[t, pl.ds(side * eighth, eighth)],
            one_send.at[lax.rem(t, RING), 1 + side],
            one_recv.at[t, 1 + side],
            across_x,
        )

    def first_two(t):
        return remote(
            first_two_s.at[lax.rem(t, RING), pl.ds((1 - x) * eighth, eighth)],
            first_x_s.at[t],
            two_send.at[lax.rem(t, RING), 0],
            two_recv.at[t, 0],
            across_x,
        )

    def second_two(t):
        return remote(
            second_two_s.at[lax.rem(t, RING), pl.ds((1 - y) * eighth, eighth)],
            second_y_s.at[t],
            two_send.at[lax.rem(t, RING), 1],
            two_recv.at[t, 1],
            across_y,
        )

    def z_copy(t, distance):
        other = z ^ distance
        return remote(
            third_s.at[lax.rem(t, RING), pl.ds(other * PIECE, PIECE)],
            along_s.at[t, distance - 1],
            z_send.at[lax.rem(t, RING), distance - 1],
            z_recv.at[t, distance - 1],
            peer(y, core, other, x),
        )

    def add(count, step, target, *sources):
        def one(index, carry):
            at = index * step
            total = sources[0](at, step).astype(jnp.float32)
            for source in sources[1:]:
                total = total + source(at, step).astype(jnp.float32)
            target(at, step, total.astype(jnp.bfloat16))
            return carry

        lax.fori_loop(0, count // step, one, 0)

    def leaf_send_all(t, stage):
        unit = TILE_START + global_tile(ranges, t) * TILE + place * PIECE
        owner = lax.div(unit, shard_units)
        at = unit - owner * shard_units

        def go(part, count, slot, holder):
            source = leaf_s.at[t, pl.ds(part, count)]
            target = out_ref.at[pl.ds(slot, count)]
            sending = remote(
                source,
                target,
                leaf_send.at[t, part],
                leaf_recv.at[slot],
                (lax.div(holder, seq_count), lax.rem(holder, seq_count)),
            )

            @pl.when(holder != me)
            def _():
                if stage == 0:
                    sending.start()
                else:
                    sending.wait_send()

            if stage == 0:

                @pl.when(holder == me)
                def _():
                    pltpu.make_async_copy(source, target, leaf_recv.at[slot]).start()

        together = at + PIECE <= shard_units

        @pl.when(together)
        def _():
            go(0, PIECE, at, owner)

        @pl.when(jnp.logical_not(together))
        def _():
            for part in range(PIECE):
                over = at + part >= shard_units
                go(
                    part,
                    1,
                    jnp.where(over, at + part - shard_units, at + part),
                    jnp.where(over, owner + 1, owner),
                )

    for t in range(min(2, tiles)):
        start_from(load, t, core)
    greet_all(devices, seq_count)

    def start_core(t, carry):
        start_from(core_copy, t, 1 - core)
        return carry

    lax.fori_loop(0, tiles, start_core, 0)
    if receivers:
        start_push(parts_ref, got_ref, devices, devices, me, *push_parts, scatter=True)
        start_push(block_ref, all_ref, devices, receivers, me, *push)

    def one_step(step, carry):
        @pl.when(step < tiles)
        def _():
            t = step
            slot = lax.rem(t, RING)
            load(t).wait()
            core_copy(t).wait_recv()

            def one(index, inner):
                at = pl.ds(index * 4, 4)
                total = own_s[lax.rem(t, 2), at].astype(jnp.float32) + core_s[t, at].astype(jnp.float32)
                total = total.astype(jnp.bfloat16)
                first_s[slot, at] = total[:, :, :SPLIT]
                second_s[slot, at] = total[:, :, SPLIT:]
                return inner

            lax.fori_loop(0, half // 4, one, 0)
            first_one(t).start()
            second_one(t, 0).start()
            second_one(t, 1).start()

            @pl.when(t + 2 < tiles)
            def _():
                start_from(load, t + 2, core)

        @pl.when((step >= LAG) & (step < tiles + LAG))
        def _():
            t = step - LAG
            slot = lax.rem(t, RING)
            first_one(t).wait()

            def one(index, inner):
                at = pl.ds(index * 4, 4)
                mine = first_s[slot, pl.ds(y * quarter + index * 4, 4)].astype(jnp.float32)
                total = mine + first_y_s[t, at].astype(jnp.float32)
                first_two_s[slot, at] = total.astype(jnp.bfloat16)
                return inner

            lax.fori_loop(0, quarter // 4, one, 0)
            first_two(t).start()
            for side in range(2):
                second_one(t, side).wait()

                def two(index, inner):
                    mine = second_s[slot, pl.ds(side * quarter + x * eighth + index * 4, 4)]
                    at = pl.ds(side * eighth + index * 4, 4)
                    total = mine.astype(jnp.float32) + second_x_s[t, at].astype(jnp.float32)
                    second_two_s[slot, at] = total.astype(jnp.bfloat16)
                    return inner

                lax.fori_loop(0, eighth // 4, two, 0)
            second_two(t).start()

        @pl.when((step >= 2 * LAG) & (step < tiles + 2 * LAG))
        def _():
            t = step - 2 * LAG
            slot = lax.rem(t, RING)
            first_two(t).wait()
            second_two(t).wait()

            def one(index, inner):
                at = pl.ds(index * 4, 4)
                mine = first_two_s[slot, pl.ds(x * eighth + index * 4, 4)].astype(jnp.float32)
                total = mine + first_x_s[t, at].astype(jnp.float32)
                third_s[slot, at, :, :SPLIT] = total.astype(jnp.bfloat16)
                mine = second_two_s[slot, pl.ds(y * eighth + index * 4, 4)].astype(jnp.float32)
                total = mine + second_y_s[t, at].astype(jnp.float32)
                third_s[slot, at, :, SPLIT:] = total.astype(jnp.bfloat16)
                return inner

            lax.fori_loop(0, eighth // 4, one, 0)
            for distance in (1, 2, 3):
                z_copy(t, distance).start()

        @pl.when(step >= 3 * LAG)
        def _():
            t = step - 3 * LAG
            slot = lax.rem(t, RING)
            for distance in (1, 2, 3):
                z_copy(t, distance).wait()
            total = third_s[slot, pl.ds(z * PIECE, PIECE)].astype(jnp.float32)
            for distance in (1, 2, 3):
                total = total + along_s[t, distance - 1].astype(jnp.float32)
            leaf_s[t] = total.astype(jnp.bfloat16)
            leaf_send_all(t, 0)

        return carry

    lax.fori_loop(0, tiles + 3 * LAG, one_step, 0)

    def finish(t, carry):
        core_copy(t).wait_send()
        leaf_send_all(t, 1)
        return carry

    lax.fori_loop(0, tiles, finish, 0)
    if receivers:
        finish_push(parts_ref, got_ref, devices, devices, me, *push_parts, scatter=True)
        finish_push(block_ref, all_ref, devices, receivers, me, *push)
    far = TILE_START - TILE * (TILE_START // TILE)
    begin = me * shard_units
    first_at = lax.rem(PIECE - lax.rem(begin + PIECE - far % PIECE, PIECE), PIECE)

    def arrive(index, count):
        unit = begin + index
        inside = False
        for start, stop in ranges:
            low_end, high_end = TILE_START + start * TILE, TILE_START + stop * TILE
            inside = inside | ((unit >= low_end) & (unit < high_end))

        @pl.when(inside)
        def _():
            part = out_ref.at[pl.ds(index, count)]
            pltpu.make_async_copy(part, part, leaf_recv.at[index]).wait()

    def arrive_three(step, carry):
        index = first_at + step * PIECE

        @pl.when(index + PIECE <= shard_units)
        def _():
            arrive(index, PIECE)

        return carry

    steps = shard_units // PIECE
    lax.fori_loop(0, steps, arrive_three, 0)
    covered = first_at + lax.div(shard_units - first_at, PIECE) * PIECE
    for step in range(PIECE - 1):

        @pl.when(step < first_at)
        def _():
            arrive(step, 1)

        @pl.when(covered + step < shard_units)
        def _():
            arrive(covered + step, 1)


def push_copy(block_ref, all_ref, devices, me, step, send_sem, recv_sem, scatter):
    seq_count = devices // 4
    other = lax.rem(me + step, devices)
    return other, pltpu.make_async_remote_copy(
        src_ref=block_ref.at[other] if scatter else block_ref,
        dst_ref=all_ref.at[me],
        send_sem=send_sem.at[step],
        recv_sem=recv_sem.at[me],
        device_id=(lax.div(other, seq_count), lax.rem(other, seq_count)),
        device_id_type=MESH,
    )


def start_push(block_ref, all_ref, devices, receivers, me, send_sem, recv_sem, keep_sem, scatter=False):
    own_ref = block_ref.at[me] if scatter else block_ref

    @pl.when(me < receivers)
    def _():
        pltpu.make_async_copy(own_ref, all_ref.at[me], keep_sem).start()

    def send(step, carry):
        other, sending = push_copy(
            block_ref, all_ref, devices, me, step, send_sem, recv_sem, scatter
        )

        @pl.when(other < receivers)
        def _():
            sending.start()

        return carry

    lax.fori_loop(1, devices, send, 0)


def finish_push(
    block_ref, all_ref, devices, receivers, me, send_sem, recv_sem, keep_sem, scatter=False
):
    own_ref = block_ref.at[me] if scatter else block_ref

    @pl.when(me < receivers)
    def _():
        pltpu.make_async_copy(own_ref, all_ref.at[me], keep_sem).wait()

    def finish(step, carry):
        other, sending = push_copy(
            block_ref, all_ref, devices, me, step, send_sem, recv_sem, scatter
        )

        @pl.when(other < receivers)
        def _():
            sending.wait_send()

        source = lax.rem(me + devices - step, devices)

        @pl.when(me < receivers)
        def _():
            pltpu.make_async_copy(own_ref, all_ref.at[source], recv_sem.at[source]).wait()

        return carry

    lax.fori_loop(1, devices, finish, 0)


def push_sems(devices):
    dma = pltpu.SemaphoreType.DMA
    return [dma((devices,)), dma((devices,)), dma]


def reduce_rows(ranges, shard_units, devices, collective_id, pieces, blocks=(), receivers=0):
    tiles = sum(stop - start for start, stop in ranges)
    width = pieces[0][0].shape[1]
    sources = tuple(piece[1:] for piece in pieces)
    assert sum(count for _, count in sources) == 2 * tiles
    half, quarter, eighth = TILE // 2, TILE // 4, TILE // 8
    rest = width - SPLIT

    def vmem(*shape):
        return pltpu.VMEM(shape, jnp.bfloat16)

    dma = pltpu.SemaphoreType.DMA
    outs = [jax.ShapeDtypeStruct((shard_units, UNIT, width), jnp.bfloat16)]
    if blocks:
        outs.append(jax.ShapeDtypeStruct((devices,) + blocks[0].shape, blocks[0].dtype))
        outs.append(jax.ShapeDtypeStruct(blocks[1].shape, blocks[1].dtype))
    out = pl.pallas_call(
        functools.partial(reduce_kernel, ranges, shard_units, devices, sources, receivers),
        out_shape=outs,
        in_specs=[pl.BlockSpec(memory_space=pl.ANY)] * (len(pieces) + len(blocks)),
        out_specs=[pl.BlockSpec(memory_space=pl.ANY)] * len(outs),
        scratch_shapes=[
            vmem(2, half, UNIT, width),
            vmem(tiles, half, UNIT, width),
            vmem(RING, half, UNIT, SPLIT),
            vmem(RING, half, UNIT, rest),
            vmem(tiles, quarter, UNIT, SPLIT),
            vmem(tiles, quarter, UNIT, rest),
            vmem(RING, quarter, UNIT, SPLIT),
            vmem(RING, quarter, UNIT, rest),
            vmem(tiles, eighth, UNIT, SPLIT),
            vmem(tiles, eighth, UNIT, rest),
            vmem(RING, eighth, UNIT, width),
            vmem(tiles, 3, PIECE, UNIT, width),
            vmem(tiles, PIECE, UNIT, width),
            dma((2,)),
            dma((tiles,)),
            dma((tiles,)),
            dma((RING, 3)),
            dma((tiles, 3)),
            dma((RING, 2)),
            dma((tiles, 2)),
            dma((RING, 3)),
            dma((tiles, 3)),
            dma((tiles, PIECE)),
            dma((shard_units,)),
        ]
        + (push_sems(devices) + push_sems(devices) if blocks else []),
        compiler_params=pltpu.CompilerParams(
            collective_id=collective_id, has_side_effects=True, vmem_limit_bytes=VMEM_BYTES
        ),
    )(*[piece[0].reshape(-1, UNIT, width) for piece in pieces], *blocks)
    return out if blocks else out[0]


STRIDE = 3
Z_LAG = 2
Z_RING = 3 * Z_LAG + 1


def gather_kernel(
    openings,
    ahead,
    devices,
    shard_ref,
    out_ref,
    later_ref,
    deal_send,
    deal_recv,
    z_send,
    z_recv,
    one_send,
    one_recv,
    two_send,
    two_recv,
    core_send,
    core_recv,
):
    shard_units = shard_ref.shape[0]
    seq_count = devices // 4
    width = shard_ref.shape[2]
    tiles = out_ref.shape[0] // TILE
    later_tiles = later_ref.shape[0] // TILE
    streams = ((openings[0], tiles, out_ref, 0), (openings[1], later_tiles, later_ref, tiles))
    y, core, z, x = my_place()
    me = (y * 2 + core) * seq_count + z * 2 + x
    half, quarter, eighth = TILE // 2, TILE // 4, TILE // 8
    leaves = TILE // PIECE
    upward = peer(y, core, jnp.minimum(z + 1, 3), x)
    downward = peer(y, core, jnp.maximum(z - 1, 0), x)

    def bounds(stream):
        begin = me * shard_units - stream[0]
        finish = begin + shard_units
        return begin, finish, lax.div(begin + PIECE - 1, PIECE), lax.div(finish, PIECE)

    def deal_some(stream, stage, three, part, count):
        begin = bounds(stream)[0]
        ref = stream[2]
        tile = lax.div(three, leaves)
        leaf = three - tile * leaves
        eight = lax.div(leaf, 4)
        slot = leaf - eight * 4 if count == PIECE else 4 + part
        holder_core = lax.div(eight, 4)
        holder_y = lax.rem(lax.div(eight, 2), 2)
        holder_x = lax.rem(eight, 2)
        holder = (holder_y * 2 + holder_core) * seq_count + z * 2 + holder_x
        index = three * PIECE + part - begin
        source = shard_ref.at[pl.ds(index, count)]
        target = ref.at[pl.ds(three * PIECE + part, count)]
        recv = deal_recv.at[stream[3] + tile, slot]
        sending = pltpu.make_async_remote_copy(
            src_ref=source,
            dst_ref=target,
            send_sem=deal_send.at[0 if stream[3] == 0 else 1, index],
            recv_sem=recv,
            device_id=peer(holder_y, holder_core, z, holder_x),
            device_id_type=MESH,
        )

        @pl.when(holder != me)
        def _():
            if stage == 0:
                sending.start()
            else:
                sending.wait_send()

        if stage == 0:

            @pl.when(holder == me)
            def _():
                pltpu.make_async_copy(source, target, recv).start()

    def deal_between(stream, stage, low_three, count, base):
        begin, finish, first_three, last_three = bounds(stream)
        base = first_three if base is None else base

        @pl.when((low_three <= last_three) & (low_three + count >= first_three))
        def _():
            def one(step, carry):
                three = base + step

                @pl.when(
                    (three >= first_three)
                    & (three < last_three)
                    & (three >= low_three)
                    & (three < low_three + count)
                )
                def _():
                    deal_some(stream, stage, three, 0, PIECE)

                return carry

            lax.fori_loop(0, min(count, shard_units // PIECE + 1), one, 0)
            for step in range(PIECE - 1):
                three = first_three - 1
                here = (three >= low_three) & (three < low_three + count)

                @pl.when(here & (begin + step < first_three * PIECE))
                def _(three=three):
                    deal_some(stream, stage, three, begin + step - three * PIECE, 1)

                three = last_three
                here = (three >= low_three) & (three < low_three + count)

                @pl.when(here & (three * PIECE + step < finish))
                def _(three=three):
                    deal_some(stream, stage, three, step, 1)

    def deal_tile(stream, step):
        low_three = tile_at(step, stream[1]) * leaves
        deal_between(stream, 0, low_three, leaves, low_three)

    def each_three(stream, t, visit):
        def one(index, carry):
            row = t * TILE + ((core * 2 + y) * 2 + x) * eighth + index * PIECE
            unit = stream[0] + row
            owner = lax.div(unit, shard_units)
            at = unit - owner * shard_units

            @pl.when(at + PIECE <= shard_units)
            def _():
                visit(row, index, PIECE, lax.rem(lax.div(owner, 2), 4))

            @pl.when(at + PIECE > shard_units)
            def _():
                for part in range(PIECE):
                    holder = jnp.where(at + part >= shard_units, owner + 1, owner)
                    visit(row + part, 4 + part, 1, lax.rem(lax.div(holder, 2), 4))

            return carry

        lax.fori_loop(0, eighth // PIECE, one, 0)

    def wait_units(ref, count, sem):
        part = ref.at[pl.ds(0, count)]
        pltpu.make_async_copy(part, part, sem).wait()

    def z_copy(stream, step, row, slot, count, way):
        part = stream[2].at[pl.ds(row, count)]
        which = 0 if stream[3] == 0 else 1
        return pltpu.make_async_remote_copy(
            src_ref=part,
            dst_ref=part,
            send_sem=z_send.at[which, lax.rem(step, Z_RING), slot, way],
            recv_sem=z_recv.at[stream[3] + tile_at(step, stream[1]), slot],
            device_id=(upward, downward)[way],
            device_id_type=MESH,
        )

    def along_z(stream, step, distance):
        t = tile_at(step, stream[1])

        def visit(row, slot, count, owner_z):
            @pl.when(jnp.abs(owner_z - z) == distance)
            def _():
                sem = deal_recv if distance == 0 else z_recv
                wait_units(out_ref, count, sem.at[stream[3] + t, slot])

                @pl.when((owner_z <= z) & (z < 3))
                def _():
                    z_copy(stream, step, row, slot, count, 0).start()

                @pl.when((owner_z >= z) & (z > 0))
                def _():
                    z_copy(stream, step, row, slot, count, 1).start()

        each_three(stream, t, visit)

    def along_z_done(stream, step):
        t = tile_at(step, stream[1])

        def visit(row, slot, count, owner_z):
            @pl.when((owner_z <= z) & (z < 3))
            def _():
                z_copy(stream, step, row, slot, count, 0).wait_send()

            @pl.when((owner_z >= z) & (z > 0))
            def _():
                z_copy(stream, step, row, slot, count, 1).wait_send()

        each_three(stream, t, visit)

    def z_stage(stream, step):
        for distance in range(4):
            old = step - distance * Z_LAG

            @pl.when((old >= 0) & (old < stream[1]))
            def _(old=old, distance=distance):
                along_z(stream, old, distance)
                if distance == 3:
                    along_z_done(stream, old)

    spreading = spread_steps(
        out_ref, one_send, one_recv, two_send, two_recv, core_send, core_recv
    )
    main, late = streams
    greet_all(devices, seq_count)
    for step in range(min(ahead, tiles)):
        deal_tile(main, step)
    for step in range(min(ahead, later_tiles)):
        deal_tile(late, step)

    def one_step(step, carry):
        @pl.when(step + ahead < tiles)
        def _():
            deal_tile(main, step + ahead)

        @pl.when(step + ahead < later_tiles)
        def _():
            deal_tile(late, step + ahead)

        z_stage(main, step)
        spreading(step - 3 * Z_LAG)
        z_stage(late, step)
        return carry

    lax.fori_loop(0, tiles + 3 * LAG + 3 * Z_LAG, one_step, 0)
    for stream in streams:
        deal_between(stream, 1, 0, stream[1] * leaves, None)


def tile_at(step, tiles):
    return lax.rem(step * STRIDE, tiles)


def spread_steps(out_ref, one_send, one_recv, two_send, two_recv, core_send, core_recv):
    tiles = out_ref.shape[0] // TILE
    width = out_ref.shape[2]
    y, core, z, x = my_place()
    half, quarter, eighth = TILE // 2, TILE // 4, TILE // 8
    left, right = pl.ds(0, SPLIT), pl.ds(SPLIT, width - SPLIT)
    whole = pl.ds(0, width)
    across_core = peer(y, 1 - core, z, x)
    across_y = peer(1 - y, core, z, x)
    across_x = peer(y, core, z, 1 - x)

    def remote(start, count, columns, send, recv, device):
        part = out_ref.at[pl.ds(start, count), :, columns]
        return pltpu.make_async_remote_copy(
            src_ref=part,
            dst_ref=part,
            send_sem=send,
            recv_sem=recv,
            device_id=device,
            device_id_type=MESH,
        )

    def block(t, y_at, x_at):
        return t * TILE + ((core * 2 + y_at) * 2 + x_at) * eighth

    def one_first(step):
        t = tile_at(step, tiles)
        sems = (one_send.at[lax.rem(step, RING), 0], one_recv.at[t, 0])
        return remote(block(t, y, x), eighth, left, *sems, across_x)

    def one_second(step):
        t = tile_at(step, tiles)
        sems = (one_send.at[lax.rem(step, RING), 1], one_recv.at[t, 1])
        return remote(block(t, y, x), eighth, right, *sems, across_y)

    def two_first(step):
        t = tile_at(step, tiles)
        sems = (two_send.at[lax.rem(step, RING), 0], two_recv.at[t, 0])
        return remote(block(t, y, 0), quarter, left, *sems, across_y)

    def two_second(step, side):
        t = tile_at(step, tiles)
        sems = (two_send.at[lax.rem(step, RING), 1 + side], two_recv.at[t, 1 + side])
        return remote(block(t, side, x), eighth, right, *sems, across_x)

    def core_copy(step):
        t = tile_at(step, tiles)
        sems = (core_send.at[lax.rem(step, RING)], core_recv.at[t])
        return remote(t * TILE + core * half, half, whole, *sems, across_core)

    def go(step):
        @pl.when((step >= 0) & (step < tiles))
        def _():
            one_first(step).start()
            one_second(step).start()

        @pl.when((step >= LAG) & (step < tiles + LAG))
        def _():
            old = step - LAG
            one_first(old).wait()
            two_first(old).start()
            one_second(old).wait()
            for side in range(2):
                two_second(old, side).start()

        @pl.when((step >= 2 * LAG) & (step < tiles + 2 * LAG))
        def _():
            old = step - 2 * LAG
            two_first(old).wait()
            for side in range(2):
                two_second(old, side).wait()
            core_copy(old).start()

        @pl.when(step >= 3 * LAG)
        def _():
            core_copy(step - 3 * LAG).wait()

    return go


def spread_sems(tiles):
    dma = pltpu.SemaphoreType.DMA
    return [
        dma((RING, 2)),
        dma((tiles, 2)),
        dma((RING, 3)),
        dma((tiles, 3)),
        dma((RING,)),
        dma((tiles,)),
    ]


def spread_kernel(devices, rows_ref, block_ref, out_ref, all_ref, *sems):
    seq_count = devices // 4
    me = lax.axis_index("dp") * seq_count + lax.axis_index("seq")
    sems, push = sems[:-3], sems[-3:]
    greet_all(devices, seq_count)
    start_push(block_ref, all_ref, devices, devices, me, *push)
    spreading = spread_steps(out_ref, *sems)

    def one_step(step, carry):
        spreading(step)
        return carry

    lax.fori_loop(0, out_ref.shape[0] // TILE + 3 * LAG, one_step, 0)
    finish_push(block_ref, all_ref, devices, devices, me, *push)


def spread_rows(rows, block, devices, collective_id):
    return pl.pallas_call(
        functools.partial(spread_kernel, devices),
        out_shape=(
            jax.ShapeDtypeStruct(rows.shape, rows.dtype),
            jax.ShapeDtypeStruct((devices,) + block.shape, block.dtype),
        ),
        in_specs=[pl.BlockSpec(memory_space=pl.ANY)] * 2,
        out_specs=(pl.BlockSpec(memory_space=pl.ANY), pl.BlockSpec(memory_space=pl.ANY)),
        scratch_shapes=spread_sems(rows.shape[0] // TILE) + push_sems(devices),
        input_output_aliases={0: 0},
        compiler_params=pltpu.CompilerParams(
            collective_id=collective_id, has_side_effects=True, vmem_limit_bytes=VMEM_BYTES
        ),
    )(rows, block)


def gather_rows(openings, counts, ahead, devices, collective_id, shard):
    units, _, width = shard.shape
    assert all(count % STRIDE for count in counts) and counts[1] <= counts[0]
    dma = pltpu.SemaphoreType.DMA
    anywhere = pl.BlockSpec(memory_space=pl.ANY)
    return pl.pallas_call(
        functools.partial(gather_kernel, openings, ahead, devices),
        out_shape=[
            jax.ShapeDtypeStruct((count * TILE, UNIT, width), jnp.bfloat16) for count in counts
        ],
        in_specs=[anywhere],
        out_specs=[anywhere, anywhere],
        scratch_shapes=[
            dma((2, units)),
            dma((sum(counts), 7)),
            dma((2, Z_RING, 7, 2)),
            dma((sum(counts), 7)),
        ]
        + spread_sems(counts[0]),
        compiler_params=pltpu.CompilerParams(
            collective_id=collective_id, has_side_effects=True, vmem_limit_bytes=VMEM_BYTES
        ),
    )(shard)


def share_kernel(devices, block_ref, out_ref, *sems):
    seq_count = devices // 4
    me = lax.axis_index("dp") * seq_count + lax.axis_index("seq")
    greet_all(devices, seq_count)
    start_push(block_ref, out_ref, devices, devices, me, *sems)
    finish_push(block_ref, out_ref, devices, devices, me, *sems)


def share(block, devices, collective_id):
    return pl.pallas_call(
        functools.partial(share_kernel, devices),
        out_shape=jax.ShapeDtypeStruct((devices,) + block.shape, block.dtype),
        in_specs=[pl.BlockSpec(memory_space=pltpu.VMEM)],
        out_specs=pl.BlockSpec(memory_space=pltpu.VMEM),
        scratch_shapes=push_sems(devices),
        compiler_params=pltpu.CompilerParams(
            collective_id=collective_id, has_side_effects=True, vmem_limit_bytes=16 * 1024 * 1024
        ),
    )(block)


def contrast_kernel(pooled_ref, pick_ref, row_ref, col_ref, scale_ref, pool_ref, text_ref, loss_ref):
    count = pick_ref.shape[1]
    scale = scale_ref[0, 0] / contrastive_sharpness_divisor
    diagonal = lax.broadcasted_iota(jnp.int32, (count, count), 0) == lax.broadcasted_iota(
        jnp.int32, (count, count), 1
    )
    loss = jnp.zeros((1, 1), jnp.float32)
    for m in range(MICRO):
        row = row_ref[m]
        col = col_ref[m] > 0.0
        image = jnp.dot(
            pick_ref[m], pooled_ref[m], precision=exact, preferred_element_type=jnp.float32
        )
        words = pooled_ref[MICRO + m]
        image_norm = lax.rsqrt(jnp.sum(image * image, axis=-1, keepdims=True) + norm_eps)
        words_norm = lax.rsqrt(jnp.sum(words * words, axis=-1, keepdims=True) + norm_eps)
        image = image * image_norm
        words = words * words_norm
        cosines = lax.dot_general(
            image,
            words,
            (((1,), (1,)), ((), ())),
            precision=exact,
            preferred_element_type=jnp.float32,
        )
        cosines = jnp.where(col, cosines / contrastive_sharpness_divisor, neg_large)
        top = jnp.max(cosines, axis=-1, keepdims=True)
        weight = jnp.exp(cosines - top)
        total = jnp.sum(weight, axis=-1, keepdims=True)
        matched = jnp.sum(jnp.where(diagonal, cosines, 0.0), axis=-1, keepdims=True)
        lost = jnp.where(row > 0.0, top + jnp.log(total) - matched, 0.0)
        loss = loss + jnp.sum(lost, axis=0, keepdims=True)
        grad = weight / total - jnp.where(diagonal, 1.0, 0.0)
        grad = jnp.where((row > 0.0) & col, grad * scale, 0.0)
        grad_image = jnp.dot(grad, words, precision=exact, preferred_element_type=jnp.float32)
        grad_words = lax.dot_general(
            grad,
            image,
            (((0,), (0,)), ((), ())),
            precision=exact,
            preferred_element_type=jnp.float32,
        )
        inner = jnp.sum(image * grad_image, axis=-1, keepdims=True)
        pool_ref[m] = image_norm * (grad_image - image * inner)
        inner = jnp.sum(words * grad_words, axis=-1, keepdims=True)
        text_ref[m] = words_norm * (grad_words - words * inner)
    loss_ref[...] = jnp.broadcast_to(loss, loss_ref.shape)


def contrast(pooled, pick, valid, scale):
    count, width = pooled.shape[1], pooled.shape[2]
    grads = jax.ShapeDtypeStruct((MICRO, count, width), jnp.float32)
    return pl.pallas_call(
        contrast_kernel,
        out_shape=(grads, grads, jax.ShapeDtypeStruct((1, 128), jnp.float32)),
        compiler_params=pltpu.CompilerParams(vmem_limit_bytes=VMEM_BYTES),
    )(pooled, pick, valid[:, :, None], valid[:, None, :], scale.reshape(1, 1))


def joint_forward_kernel(rows_ref, matrix_ref, bias_ref, out_ref):
    part, width = matrix_ref.shape[2], matrix_ref.shape[3]
    matrix = matrix_ref[...].reshape(3 * part, width)
    out_ref[0] = low(dot_nt(rows_ref[...], matrix) + bias_ref[0])


def joint_forward(rows, matrix, bias):
    count, width = rows.shape
    groups, _, columns = bias.shape
    return pl.pallas_call(
        joint_forward_kernel,
        out_shape=jax.ShapeDtypeStruct((groups, count, columns), jnp.bfloat16),
        grid=(groups,),
        in_specs=[
            pl.BlockSpec((count, width), lambda j: (0, 0)),
            pl.BlockSpec((3, 1, columns // 3, width), lambda j: (0, j, 0, 0)),
            pl.BlockSpec((1, 1, columns), lambda j: (j, 0, 0)),
        ],
        out_specs=pl.BlockSpec((1, count, columns), lambda j: (j, 0, 0)),
        compiler_params=pltpu.CompilerParams(vmem_limit_bytes=VMEM_BYTES),
    )(rows, matrix.reshape(3, groups, columns // 3, width), bias)


def joint_backward_kernel(grad_ref, matrix_ref, rows_ref, out_ref, weight_ref):
    part, width = matrix_ref.shape[2], matrix_ref.shape[3]
    grad = grad_ref[0]
    term = dot_nn(grad, matrix_ref[...].reshape(3 * part, width))
    weight_ref[...] = low(dot_tn(grad, rows_ref[...])).reshape(3, 1, part, width)

    @pl.when(pl.program_id(0) == 0)
    def _():
        out_ref[...] = term

    @pl.when(pl.program_id(0) > 0)
    def _():
        out_ref[...] += term


def joint_backward(grad, matrix, rows):
    groups, count, columns = grad.shape
    width = rows.shape[1]
    part = columns // 3
    out, weight = pl.pallas_call(
        joint_backward_kernel,
        out_shape=(
            jax.ShapeDtypeStruct((count, width), jnp.float32),
            jax.ShapeDtypeStruct((3, groups, part, width), jnp.bfloat16),
        ),
        grid=(groups,),
        in_specs=[
            pl.BlockSpec((1, count, columns), lambda j: (j, 0, 0)),
            pl.BlockSpec((3, 1, part, width), lambda j: (0, j, 0, 0)),
            pl.BlockSpec((count, width), lambda j: (0, 0)),
        ],
        out_specs=(
            pl.BlockSpec((count, width), lambda j: (0, 0)),
            pl.BlockSpec((3, 1, part, width), lambda j: (0, j, 0, 0)),
        ),
        compiler_params=pltpu.CompilerParams(vmem_limit_bytes=VMEM_BYTES),
    )(grad, matrix.reshape(3, groups, part, width), rows)
    return out, weight.reshape(3 * groups * part, width)


FEED_BLOCK = 768


def feed_forward_kernel(rows_ref, up_ref, down_ref, b_up_ref, b_down_ref, before_ref, act_ref, out_ref):
    before = dot_nt(rows_ref[...], up_ref[...]) + b_up_ref[0]
    before_ref[...] = before
    act = low(gelu_tanh(before))
    act_ref[...] = act
    term = dot_nn(act, down_ref[...])

    @pl.when(pl.program_id(0) == 0)
    def _():
        out_ref[...] = term + b_down_ref[...]

    @pl.when(pl.program_id(0) > 0)
    def _():
        out_ref[...] += term


def feed_specs(count, width, up_start, down_start):
    return (
        pl.BlockSpec((count, width), lambda j: (0, 0)),
        pl.BlockSpec((FEED_BLOCK, width), lambda j: (up_start + j, 0)),
        pl.BlockSpec((FEED_BLOCK, width), lambda j: (down_start + j, 0)),
        pl.BlockSpec((1, 1, FEED_BLOCK), lambda j: (j, 0, 0)),
        pl.BlockSpec((count, FEED_BLOCK), lambda j: (0, j)),
    )


def feed_forward(rows, up, up_start, down, down_start, b_up, b_down):
    count, width = rows.shape
    whole, up_spec, down_spec, line, column = feed_specs(count, width, up_start, down_start)
    return pl.pallas_call(
        feed_forward_kernel,
        out_shape=(
            jax.ShapeDtypeStruct((count, FF), jnp.float32),
            jax.ShapeDtypeStruct((count, FF), jnp.bfloat16),
            jax.ShapeDtypeStruct((count, width), jnp.float32),
        ),
        grid=(FF // FEED_BLOCK,),
        in_specs=[whole, up_spec, down_spec, line, pl.BlockSpec((1, width), lambda j: (0, 0))],
        out_specs=(column, column, whole),
        compiler_params=pltpu.CompilerParams(vmem_limit_bytes=VMEM_BYTES),
    )(rows, up, down, b_up.reshape(-1, 1, FEED_BLOCK), b_down)


def feed_backward_kernel(
    grad_ref, up_ref, down_ref, before_ref, act_ref, rows_ref, out_ref, w_up_ref, w_down_ref, sum_ref
):
    grad = grad_ref[...]
    before = before_ref[...]
    factor = math.sqrt(2.0 / math.pi)
    square = before * before
    bend = jnp.tanh(factor * (before + 0.044715 * (square * before)))
    slope = 0.5 * (1.0 + bend) + (0.5 * factor) * before * (1.0 - bend * bend) * (
        1.0 + (3.0 * 0.044715) * square
    )
    grad_up = dot_nt(grad, down_ref[...]) * slope
    sum_ref[0] = jnp.sum(grad_up, axis=0, keepdims=True)
    grad_up = low(grad_up)
    w_up_ref[...] = low(dot_tn(grad_up, rows_ref[...]))
    w_down_ref[...] = low(dot_tn(act_ref[...], grad))
    term = dot_nn(grad_up, up_ref[...])

    @pl.when(pl.program_id(0) == 0)
    def _():
        out_ref[...] = term

    @pl.when(pl.program_id(0) > 0)
    def _():
        out_ref[...] += term


def feed_backward(grad, up, up_start, down, down_start, before, act, rows):
    count, width = rows.shape
    whole, up_spec, down_spec, line, column = feed_specs(count, width, up_start, down_start)
    block = pl.BlockSpec((FEED_BLOCK, width), lambda j: (j, 0))
    return pl.pallas_call(
        feed_backward_kernel,
        out_shape=(
            jax.ShapeDtypeStruct((count, width), jnp.float32),
            jax.ShapeDtypeStruct((FF, width), jnp.bfloat16),
            jax.ShapeDtypeStruct((FF, width), jnp.bfloat16),
            jax.ShapeDtypeStruct((FF // FEED_BLOCK, 1, FEED_BLOCK), jnp.float32),
        ),
        grid=(FF // FEED_BLOCK,),
        in_specs=[whole, up_spec, down_spec, column, column, whole],
        out_specs=(whole, block, block, line),
        compiler_params=pltpu.CompilerParams(vmem_limit_bytes=VMEM_BYTES),
    )(grad, up, down, before, act, rows)


def caption_grad_kernel(rows_ref, grad_ref, out_ref):
    out_ref[...] = low(dot_tn(rows_ref[...], grad_ref[...]))


def caption_grad(rows, grad):
    count, depth = rows.shape
    block = 512
    return pl.pallas_call(
        caption_grad_kernel,
        out_shape=jax.ShapeDtypeStruct((depth, grad.shape[1]), jnp.bfloat16),
        grid=(depth // block,),
        in_specs=[
            pl.BlockSpec((count, block), lambda j: (0, j)),
            pl.BlockSpec(grad.shape, lambda j: (0, 0)),
        ],
        out_specs=pl.BlockSpec((block, grad.shape[1]), lambda j: (j, 0)),
        compiler_params=pltpu.CompilerParams(vmem_limit_bytes=VMEM_BYTES),
    )(rows, grad)


def adamw(param, grad, first, second, rate, decay):
    first_new = beta_one * first + (1.0 - beta_one) * grad
    second_new = beta_two * second + (1.0 - beta_two) * grad * grad
    step_dir = (
        first_new
        / (1.0 - beta_one**STEP)
        / (jnp.sqrt(second_new / (1.0 - beta_two**STEP)) + adam_eps)
    )
    return (param - rate * (step_dir + decay * param), first_new, second_new)


def per_device(
    latents,
    noise,
    captions,
    image_sizes,
    caption_lengths,
    timesteps,
    weights,
    vectors,
    weights_m,
    weights_v,
    vectors_m,
    vectors_v,
):
    width = weights.shape[1]
    seq_count = lax.axis_size("seq")
    dp_count = lax.axis_size("dp")
    seq_index = lax.axis_index("seq")
    row_index = lax.axis_index("dp")
    devices = dp_count * seq_count
    layout = matrix_rows(width)
    shard_rows = weights.shape[0]
    paired = dp_count == 4 and seq_count == 8
    weights_low = weights.astype(jnp.bfloat16)
    if paired:
        shard = weights_low.reshape(shard_rows // UNIT, UNIT, width)
        rows_all, rows_late = gather_rows((0, 2176), (23, 19), 8, devices, 7, shard)
        flat = (-1, width)
        self_head = 384
        (
            time_one,
            time_two,
            time_block,
            text_one,
            text_two,
            joint_qkv,
            self_out_head,
        ) = split_rows(rows_all.reshape(flat), layout[:6] + (self_head,))
    else:
        gathered = lax.all_gather(weights_low, both_axes, axis=0, tiled=True)
        (
            time_one,
            time_two,
            time_block,
            text_one,
            text_two,
            joint_qkv,
            self_out,
            cross_query,
            cross_kv,
            cross_out,
            mlp_up,
            mlp_down,
        ) = split_rows(gathered, layout)
    (
        table,
        final_table,
        patch_in,
        patch_out,
        b_patch,
        b_time_one,
        b_time_two,
        b_block,
        b_text_one,
        b_text_two,
        b_query,
        b_value,
        b_self_out,
        b_cross_query,
        b_cross_value,
        b_cross_out,
        b_up,
        b_down,
    ) = split_rows(vectors.astype(jnp.bfloat16).astype(jnp.float32), vector_rows(width))
    head_dim = width // HEADS
    heads = HEADS // seq_count
    part = heads * head_dim
    images = image_sizes.shape[2]
    slots = latents.shape[2]
    assert slots == BLOCK and images == seq_count
    rows = MICRO * slots
    wide = (MICRO, slots, width)
    image_count = jnp.sum((image_sizes > 0).astype(jnp.float32))
    loss_scale = 1.0 / image_count

    ends_all = jnp.cumsum(image_sizes, axis=2)
    firsts = jnp.arange(seq_count, dtype=jnp.int32) * BLOCK
    segment_all = jnp.sum(
        (ends_all[:, :, None, :] <= firsts[None, None, :, None]).astype(jnp.int32), axis=3
    )
    onehot_all = (
        segment_all[:, :, :, None] == jnp.arange(images, dtype=jnp.int32)[None, None, None, :]
    )
    size_all = jnp.sum(jnp.where(onehot_all, image_sizes[:, :, None, :], 0), axis=3)
    start_all = jnp.sum(jnp.where(onehot_all, (ends_all - image_sizes)[:, :, None, :], 0), axis=3)
    step_all = jnp.sum(jnp.where(onehot_all, timesteps[:, :, None, :], 0), axis=3)
    length_all = jnp.sum(jnp.where(onehot_all, caption_lengths[:, :, None, :], 0), axis=3)
    row_start = start_all[:, row_index]
    row_size = size_all[:, row_index]
    kv_start = row_start // BLOCK
    kv_big = (row_size == LARGE).astype(jnp.int32)
    own_segment = segment_all[:, row_index, seq_index]
    own_size = row_size[:, seq_index]
    own_start = row_start[:, seq_index]
    own_step = step_all[:, row_index, seq_index]
    own_length = length_all[:, row_index, seq_index]

    quarter = width // 4
    omega = 1.0 / 10000.0 ** (jnp.arange(quarter, dtype=jnp.float32) / quarter)
    angle = jnp.arange(2 * SIDE, dtype=jnp.float32)[:, None] * omega[None, :]
    angle_table = jnp.concatenate([jnp.sin(angle), jnp.cos(angle)], axis=1)
    within = (
        seq_index * BLOCK - own_start[:, None] + jnp.arange(slots, dtype=jnp.int32)[None, :]
    ).reshape(rows)
    side = jnp.where(own_size == LARGE, 2 * SIDE, SIDE).astype(jnp.int32)
    side = jnp.broadcast_to(side[:, None], (MICRO, slots)).reshape(rows)
    places = jnp.arange(2 * SIDE, dtype=jnp.int32)[None, :]
    pick_row = ((within // side)[:, None] == places).astype(jnp.float32)
    pick_col = ((within % side)[:, None] == places).astype(jnp.float32)
    position = jnp.concatenate(
        [
            jnp.dot(pick_row, angle_table, precision=exact),
            jnp.dot(pick_col, angle_table, precision=exact),
        ],
        axis=1,
    )

    level = noise_level(own_step)[:, None, None]
    level_prev = noise_level(own_step - 1)[:, None, None]
    beta_log, tilde_log = variance_logs(level, level_prev)
    target = noise[:, 0].astype(jnp.float32)
    noisy = jnp.sqrt(level) * latents[:, 0].astype(jnp.float32) + jnp.sqrt(1.0 - level) * target
    noisy = noisy.reshape(rows, PATCH)

    time_low = low(time_features(own_step))
    time_first = dot_nn(time_low, time_one) + b_time_one
    time_act, time_act_back = jax.vjp(jax.nn.silu, time_first)
    time_act_low = low(time_act)
    time_embed = dot_nn(time_act_low, time_two) + b_time_two
    embed_act, embed_act_back = jax.vjp(jax.nn.silu, time_embed)
    embed_low = low(embed_act)
    block_mod = dot_nt(embed_low, time_block) + b_block.reshape(1, -1) + table.reshape(1, -1)
    shift_one, scale_one, gate_one, shift_two, scale_two, gate_two = [
        piece[:, None, :] for piece in jnp.split(block_mod, 6, axis=1)
    ]
    shift_final = (final_table[0][None, :] + time_embed)[:, None, :]
    scale_final = (final_table[1][None, :] + time_embed)[:, None, :]

    hidden_zero = (jnp.dot(noisy, patch_in, precision=exact) + b_patch + position).reshape(wide)
    normed_one, mod_one_back = jax.vjp(modulate, hidden_zero, shift_one, scale_one)
    normed_one_low = low(normed_one).reshape(rows, width)
    joint_bias = jnp.concatenate([b_query, jnp.zeros_like(b_query), b_value], axis=0)
    joint_bias = jnp.transpose(joint_bias.reshape(3, seq_count, part), (1, 0, 2))
    qkv = joint_forward(normed_one_low, joint_qkv, joint_bias.reshape(seq_count, 1, 3 * part))
    caption_low = captions[:, 0].reshape(MICRO * CAP, TEXT_W)
    caption_first = dot_nn(caption_low, text_one) + b_text_one
    caption_act, caption_act_back = jax.vjp(gelu_tanh, caption_first)
    caption_act_low = low(caption_act)
    text = dot_nn(caption_act_low, text_two) + b_text_two
    lengths_slot = lax.dynamic_slice_in_dim(caption_lengths[:, row_index], seq_index, 1, 1)
    token_live = (jnp.arange(CAP, dtype=jnp.int32)[None, :] < lengths_slot).astype(jnp.float32)
    lengths_slot_float = lengths_slot.astype(jnp.float32)
    caption_pool = (
        jnp.sum(text.reshape(MICRO, CAP, width) * token_live[:, :, None], axis=1) / lengths_slot_float
    )
    text_own = low(text)
    if paired:
        qkv, text_own, rows_late = lax.optimization_barrier((qkv, text_own, rows_late))
    qkv = lax.all_to_all(qkv, "seq", split_axis=0, concat_axis=0, tiled=True)
    text_all = lax.all_gather(text_own.reshape(MICRO, CAP, width), "seq", axis=0)
    if paired:
        rows_late, words_all = spread_rows(rows_late, caption_pool.reshape(-1, 128), devices, 8)
        qkv, rows_late = lax.optimization_barrier((qkv, rows_late))
        rows_late = rows_late.reshape(flat)
        self_out_tail, cross_query, cross_kv, cross_out = split_rows(
            rows_late, (layout[6] - self_head,) + layout[7:10]
        )
        up_start = (layout[6] - self_head + sum(layout[7:10])) // FEED_BLOCK
        feed_weights = (rows_late, up_start, rows_late, up_start + FF // FEED_BLOCK)
    else:
        feed_weights = (mlp_up, 0, mlp_down, 0)
    if paired:
        self_out = jnp.concatenate([self_out_head, self_out_tail], axis=0)
    qkv = qkv.reshape(seq_count, MICRO, slots, 3 * part)
    mixed = self_forward(kv_start, kv_big, qkv, heads, head_dim)
    mixed = lax.all_to_all(
        mixed.reshape(seq_count, rows, part), "seq", split_axis=0, concat_axis=0, tiled=True
    )
    mixed_low = jnp.transpose(mixed, (1, 0, 2)).reshape(rows, width)
    attended = (dot_nn(mixed_low, self_out) + b_self_out).reshape(wide)
    hidden_one = hidden_zero + gate_one * attended

    text_low = jnp.concatenate(
        [
            lax.dynamic_slice(text_all, (own_segment[m], m, 0, 0), (1, 1, CAP, width))[0, 0]
            for m in range(MICRO)
        ],
        axis=0,
    )
    text_kv = dot_nt(text_low, cross_kv)
    pad_rows = ((0, 0), (0, CAP_PAD - CAP), (0, 0))
    key_text = jnp.pad(low(text_kv[:, :width]).reshape(MICRO, CAP, width), pad_rows)
    value_text = jnp.pad(
        low(text_kv[:, width:] + b_cross_value).reshape(MICRO, CAP, width), pad_rows
    )
    hidden_one_low = low(hidden_one).reshape(rows, width)
    query_cross = low(dot_nn(hidden_one_low, cross_query) + b_cross_query).reshape(wide)
    cross_low = cross_call(
        functools.partial(cross_forward_kernel, head_dim),
        own_length,
        (query_cross, key_text, value_text),
        jax.ShapeDtypeStruct(wide, jnp.bfloat16),
    ).reshape(rows, width)
    hidden_two = hidden_one + (dot_nn(cross_low, cross_out) + b_cross_out).reshape(wide)
    normed_two, mod_two_back = jax.vjp(modulate, hidden_two, shift_two, scale_two)
    normed_two_low = low(normed_two).reshape(rows, width)
    upward, upward_low, feed = feed_forward(normed_two_low, *feed_weights, b_up, b_down)
    feed = feed.reshape(wide)
    hidden_three = hidden_two + gate_two * feed
    final_normed, final_back = jax.vjp(modulate, hidden_three, shift_final, scale_final)
    final_flat = final_normed.reshape(rows, width)
    predicted = jnp.dot(final_flat, patch_out.T, precision=exact).reshape(MICRO, slots, 2 * PATCH)
    error = predicted[:, :, :PATCH] - target
    frac = (predicted[:, :, PATCH:] + 1.0) * 0.5
    model_log = frac * beta_log + (1.0 - frac) * tilde_log
    ratio = jnp.exp(tilde_log - model_log)
    spread = 0.5 * (model_log - tilde_log - 1.0 + ratio) / log_two
    error_weight = (1.0 / (float(PATCH) * own_size.astype(jnp.float32)))[:, None, None]
    squared_loss = jnp.sum((error * error + spread) * error_weight)

    pooled = jnp.sum(final_normed, axis=1)
    if paired:
        pooled_all = share(pooled.reshape(-1, 128), devices, 1)
    else:
        pooled_all = lax.all_gather(pooled, both_axes, axis=0)
        words_all = lax.all_gather(caption_pool, both_axes, axis=0)
    each = (devices, MICRO, width)
    pooled_all = jnp.concatenate([pooled_all.reshape(each), words_all.reshape(each)], axis=1)
    pooled_all = jnp.transpose(pooled_all, (1, 0, 2))
    size_float = jnp.maximum(image_sizes.astype(jnp.float32), 1.0)
    pick = onehot_all.astype(jnp.float32) / size_float[:, :, None, :]
    same_row = jnp.eye(dp_count, dtype=jnp.float32)
    pick = jnp.einsum("mrsi,rq->mriqs", pick, same_row, precision=exact).reshape(
        MICRO, dp_count * images, devices
    )
    valid = (image_sizes > 0).astype(jnp.float32).reshape(MICRO, dp_count * images)
    grad_pool, grad_caption, contrast_value = contrast(pooled_all, pick, valid, loss_scale)
    contrast_value = contrast_value[0, 0]
    own_pool = row_index * images + own_segment
    grad_pool_own = jnp.concatenate(
        [lax.dynamic_slice(grad_pool, (m, own_pool[m], 0), (1, 1, width))[0] for m in range(MICRO)]
    ) / own_size.astype(jnp.float32)[:, None]
    grad_caption = lax.dynamic_slice_in_dim(
        grad_caption, row_index * images + seq_index, 1, 1
    )[:, 0]

    grad_spread = 0.5 * (1.0 - ratio) / log_two * 0.5 * (beta_log - tilde_log)
    grad_predicted = (
        loss_scale * error_weight * jnp.concatenate([2.0 * error, grad_spread], axis=2)
    ).reshape(rows, 2 * PATCH)
    grad_final = grad_pool_own[:, None, :] + jnp.dot(
        grad_predicted, patch_out, precision=exact
    ).reshape(wide)
    grad_patch_out = lax.dot_general(
        grad_predicted, final_flat, (((0,), (0,)), ((), ())), precision=exact
    )
    grad_three, grad_shift_final, grad_scale_final = final_back(grad_final)
    grad_shift_final = grad_shift_final[:, 0]
    grad_scale_final = grad_scale_final[:, 0]
    grad_final_table = jnp.stack([grad_shift_final.sum(axis=0), grad_scale_final.sum(axis=0)])
    grad_embed = grad_shift_final + grad_scale_final

    grad_feed = (grad_three * gate_two).reshape(rows, width)
    grad_feed_low = low(grad_feed)
    grad_normed_two, weight_up, weight_down, grad_b_up = feed_backward(
        grad_feed_low, *feed_weights, upward, upward_low, normed_two_low
    )
    grad_two_mod, grad_shift_two, grad_scale_two = mod_two_back(grad_normed_two.reshape(wide))
    grad_gate_two = jnp.sum(grad_three * feed, axis=1, keepdims=True)
    grad_two = grad_three + grad_two_mod
    grad_two_flat = grad_two.reshape(rows, width)
    grad_two_low = low(grad_two_flat)
    weight_cross_out = dot_tn(cross_low, grad_two_low)
    grad_cross_low = low(dot_nt(grad_two_low, cross_out)).reshape(wide)
    padded = jax.ShapeDtypeStruct((MICRO, CAP_PAD, width), jnp.float32)
    grad_query_cross, grad_key_text, grad_value_text = cross_call(
        functools.partial(cross_backward_kernel, head_dim),
        own_length,
        (query_cross, key_text, value_text, grad_cross_low),
        (jax.ShapeDtypeStruct(wide, jnp.float32), padded, padded),
    )
    grad_query_cross = grad_query_cross.reshape(rows, width)
    grad_query_low = low(grad_query_cross)
    weight_cross_query = dot_tn(hidden_one_low, grad_query_low)
    grad_one = grad_two + dot_nt(grad_query_low, cross_query).reshape(wide)

    grad_kv = jnp.concatenate([grad_key_text[:, :CAP], grad_value_text[:, :CAP]], axis=2).reshape(
        MICRO * CAP, 2 * width
    )
    grad_kv_low = low(grad_kv)
    weight_cross_kv = dot_tn(grad_kv_low, text_low)
    grad_text_part = low(dot_nn(grad_kv_low, cross_kv)).reshape(MICRO, CAP, width)
    grad_text_all = lax.all_gather(grad_text_part, "seq", axis=0).astype(jnp.float32)
    mine = (segment_all[:, row_index] == seq_index).astype(jnp.float32)
    grad_text = jnp.sum(grad_text_all * jnp.transpose(mine)[:, :, None, None], axis=0) + (
        (grad_caption / lengths_slot_float)[:, None, :] * token_live[:, :, None]
    )
    grad_text = grad_text.reshape(MICRO * CAP, width)
    grad_text_low = low(grad_text)
    weight_text_two = dot_tn(caption_act_low, grad_text_low)
    grad_caption_first = caption_act_back(dot_nt(grad_text_low, text_two))[0]
    grad_caption_low = low(grad_caption_first)
    head_rows = TILE_START * UNIT - sum(layout[:3]) + TILE * UNIT // 2 if paired else 0
    weight_text_one = caption_grad(caption_low, grad_caption_low)

    grad_attended = (grad_one * gate_one).reshape(rows, width)
    grad_gate_one = jnp.sum(grad_one * attended, axis=1, keepdims=True)
    grad_attended_low = low(grad_attended)
    weight_self_out = dot_tn(mixed_low, grad_attended_low)
    grad_mixed = low(dot_nt(grad_attended_low, self_out)).reshape(rows, seq_count, part)
    grad_mixed = jnp.transpose(grad_mixed, (1, 0, 2))
    if paired:
        weight_up, weight_down, grad_mixed = lax.optimization_barrier(
            (low(weight_up), low(weight_down), grad_mixed)
        )
    grad_mixed = lax.all_to_all(grad_mixed, "seq", split_axis=0, concat_axis=0, tiled=True)
    if paired:
        summed_feed = reduce_rows(
            ((19, 31),), shard_rows // UNIT, devices, 2, ((weight_up, 0, 12), (weight_down, 0, 12))
        )
        grad_mixed, summed_feed = lax.optimization_barrier((grad_mixed, summed_feed))
    grad_mixed = grad_mixed.reshape(seq_count, MICRO, slots, part)
    grad_qkv, head_sums = self_backward(kv_start, kv_big, qkv, grad_mixed, heads, head_dim)
    head_sums = jnp.sum(head_sums[:, 0], axis=0)
    column = seq_index * part
    grad_bias_query = lax.dynamic_update_slice(
        jnp.zeros((width,), jnp.float32), head_sums[:part], (column,)
    )
    grad_bias_value = lax.dynamic_update_slice(
        jnp.zeros((width,), jnp.float32), head_sums[part:], (column,)
    )
    grad_qkv = grad_qkv.reshape(seq_count, rows, 3 * part)
    if paired:
        time_rows = layout[0] + layout[1]
        block_rows = layout[2]
        weight_self_out = low(weight_self_out)
        first_half = jnp.pad(weight_text_one[:head_rows], ((TILE * UNIT // 2 - head_rows, 0), (0, 0)))
        (
            first_half,
            weight_text_one,
            weight_text_two,
            weight_self_out,
            weight_cross_query,
            weight_cross_kv,
            weight_cross_out,
            grad_qkv,
        ) = lax.optimization_barrier(
            (
                first_half,
                low(weight_text_one),
                low(weight_text_two),
                weight_self_out,
                low(weight_cross_query),
                low(weight_cross_kv),
                low(weight_cross_out),
                grad_qkv,
            )
        )
    grad_qkv = lax.all_to_all(
        grad_qkv, "seq", split_axis=0, concat_axis=0, tiled=True
    )
    if paired:
        summed_middle = reduce_rows(
            ((0, 7), (12, 19)),
            shard_rows // UNIT,
            devices,
            3,
            (
                (first_half, 0, 1),
                (weight_text_one, head_rows // UNIT, 10),
                (weight_text_two, 0, 3),
                (weight_self_out, TILE // 2, 2),
                (weight_cross_query, 0, 3),
                (weight_cross_kv, 0, 6),
                (weight_cross_out, 0, 3),
            ),
        )
        grad_qkv, summed_middle = lax.optimization_barrier((grad_qkv, summed_middle))
    grad_normed_one, weight_joint = joint_backward(grad_qkv, joint_qkv, normed_one_low)
    grad_zero_mod, grad_shift_one, grad_scale_one = mod_one_back(grad_normed_one.reshape(wide))
    grad_zero = (grad_one + grad_zero_mod).reshape(rows, width)
    grad_patch_in = lax.dot_general(noisy, grad_zero, (((0,), (0,)), ((), ())), precision=exact)

    grad_mod = jnp.concatenate(
        [grad_shift_one, grad_scale_one, grad_gate_one, grad_shift_two, grad_scale_two, grad_gate_two],
        axis=1,
    )
    grad_table = jnp.sum(grad_mod, axis=0)
    grad_mod_low = low(grad_mod.reshape(MICRO, 6 * width))
    weight_block = dot_tn(grad_mod_low, embed_low)
    grad_embed = grad_embed + embed_act_back(dot_nn(grad_mod_low, time_block))[0]
    grad_embed_low = low(grad_embed)
    weight_time_two = dot_tn(time_act_low, grad_embed_low)
    grad_time_first = time_act_back(dot_nt(grad_embed_low, time_two))[0]
    weight_time_one = dot_tn(time_low, low(grad_time_first))

    grad_vector = jnp.concatenate(
        [
            grad_table,
            grad_final_table,
            grad_patch_in,
            grad_patch_out,
            jnp.sum(grad_zero, axis=0)[None, :],
            jnp.sum(grad_time_first, axis=0)[None, :],
            jnp.sum(grad_embed, axis=0)[None, :],
            grad_table,
            jnp.sum(grad_caption_first, axis=0)[None, :],
            jnp.sum(grad_text, axis=0)[None, :],
            grad_bias_query[None, :],
            grad_bias_value[None, :],
            jnp.sum(grad_attended, axis=0)[None, :],
            jnp.sum(grad_query_cross, axis=0)[None, :],
            jnp.sum(grad_kv[:, width:], axis=0)[None, :],
            jnp.sum(grad_two_flat, axis=0)[None, :],
            grad_b_up.reshape(-1, width),
            jnp.sum(grad_feed, axis=0)[None, :],
            jnp.full((2, width), squared_loss),
        ],
        axis=0,
    )
    if paired:
        tile_size = UNIT * 128
        tile_count = -(-grad_vector.size // (tile_size * devices))
        parts = jnp.pad(
            grad_vector.reshape(-1), (0, tile_count * tile_size * devices - grad_vector.size)
        ).reshape(devices, tile_count, UNIT, 128)
        holders = -(-(time_rows + block_rows) // shard_rows)
        own_grads = jnp.concatenate(
            [grad_mod_low, grad_embed_low, low(grad_time_first), embed_low, time_act_low, time_low],
            axis=1,
        )
        summed_joint, grads_all, vector_got = reduce_rows(
            ((7, 12),),
            shard_rows // UNIT,
            devices,
            4,
            ((low(weight_joint), 0, 9), (weight_self_out, 0, 1)),
            (own_grads.reshape(-1, 128), parts),
            holders,
        )
        vector_part = jnp.sum(vector_got, axis=0)
        grads_all = jnp.where(device_index() < holders, grads_all, 0)
        grads_all = grads_all.reshape(devices * MICRO, -1)
        ends = [6 * width, 7 * width, 8 * width, 9 * width, 10 * width]
        grad_block_all, grad_two_all, grad_one_all, embed_all, act_all, features_all = jnp.split(
            grads_all, ends, axis=1
        )
        first_row = device_index() * shard_rows

        def own_columns(array, start):
            stop = start + array.shape[1]
            spread = jnp.pad(array, ((0, 0), (start, shard_rows + (-stop) % shard_rows)))
            place = jnp.minimum(first_row, spread.shape[1] - shard_rows)
            return lax.dynamic_slice(spread, (0, place), (array.shape[0], shard_rows))

        summed_time = (
            dot_tn(own_columns(features_all, 0), grad_one_all)
            + dot_tn(own_columns(act_all, layout[0]), grad_two_all)
            + dot_tn(own_columns(grad_block_all, time_rows), embed_all)
        )
        row = first_row + jnp.arange(shard_rows, dtype=jnp.int32)
        tile = ((row - TILE_START * UNIT) // (TILE * UNIT))[:, None]
        flat = (shard_rows, width)
        reduced = jnp.where(
            tile >= 19,
            summed_feed.reshape(flat),
            jnp.where(
                (tile >= 7) & (tile < 12), summed_joint.reshape(flat), summed_middle.reshape(flat)
            ),
        ).astype(jnp.float32)
        summed = jnp.where(row[:, None] < time_rows + block_rows, summed_time, reduced)
    else:
        grad_weights = jnp.concatenate(
            [
                low(piece)
                for piece in (
                    weight_time_one,
                    weight_time_two,
                    weight_block,
                    weight_text_one,
                    weight_text_two,
                    weight_joint,
                    weight_self_out,
                    weight_cross_query,
                    weight_cross_kv,
                    weight_cross_out,
                    weight_up,
                    weight_down,
                )
            ],
            axis=0,
        )
        summed = lax.psum_scatter(
            grad_weights, both_axes, scatter_dimension=0, tiled=True
        ).astype(jnp.float32)
    squares = jnp.sum(summed * summed)
    if paired:
        last = jnp.concatenate([vector_part, jnp.full((1, UNIT, 128), squares)], axis=0)
        last = share(last, devices, 6)
        squares_all = jnp.sum(last[:, -1, 0, 0])
        grad_vectors = last[:, :-1].reshape(-1)[: grad_vector.size].reshape(grad_vector.shape)
    else:
        grad_vectors, squares_all = lax.psum((grad_vector, squares), both_axes)
    loss_sum = grad_vectors[vectors.shape[0], 0] + contrast_value
    grad_vectors = grad_vectors[: vectors.shape[0]]
    down_bias_grad = grad_vectors[grad_vectors.shape[0] - 1]
    grad_norm = jnp.sqrt(squares_all + jnp.sum(grad_vectors * grad_vectors))
    factor = jnp.minimum(1.0, clip_norm / (grad_norm + 1e-06))
    new_w, first_w, second_w = adamw(
        weights, summed * factor, weights_m, weights_v, rate_matrix, weight_decay
    )
    new_v, first_v, second_v = adamw(
        vectors, grad_vectors * factor, vectors_m, vectors_v, rate_vector, 0.0
    )
    return (
        new_w,
        first_w,
        second_w,
        new_v,
        first_v,
        second_v,
        loss_sum,
        image_count,
        grad_norm,
        down_bias_grad,
    )


def solution(mesh):
    shard = P(both_axes, None)
    data = P(None, "dp", "seq", None)
    return jax.shard_map(
        per_device,
        mesh=mesh,
        in_specs=(data, data, data, P(), P(), P(), shard, P(), shard, shard, P(), P()),
        out_specs=(shard, shard, shard, P(), P(), P(), P(), P(), P(), P()),
        check_vma=False,
    )
```

```python
import functools
import math

import jax
import jax.numpy as jnp
from jax import lax
from jax.experimental import pallas as pl
from jax.experimental.pallas import tpu as pltpu
from jax.sharding import PartitionSpec as P

HEADS = 16
FF = 4608
TEXT_W = 4096
FREQ = 256
CAP = 120
CAP_PAD = 128
SIDE = 16
PATCH = 16
MICRO = 2
STEP = 10
BLOCK = 256
LARGE = 1024
VMEM_BYTES = 56 * 1024 * 1024

exact = lax.Precision.HIGHEST
clip_norm = 0.002
contrastive_sharpness_divisor = 0.1
beta_one = 0.9
beta_two = 0.999
adam_eps = 1e-08
weight_decay = 0.01
rate_matrix = 0.05
rate_vector = 0.3
norm_eps = 1e-06
neg_large = -1e30
log_two = math.log(2.0)
both_axes = ("dp", "seq")


def matrix_rows(width):
    return (FREQ, width, 6 * width, TEXT_W, width, 3 * width, width, width, 2 * width, width, FF, FF)


def vector_rows(width):
    return (6, 2, PATCH, 2 * PATCH, 1, 1, 1, 6, 1, 1, 1, 1, 1, 1, 1, 1, FF // width, 1)


def split_rows(whole, rows):
    pieces = []
    offset = 0
    for number in rows:
        pieces.append(whole[offset : offset + number])
        offset = offset + number
    return pieces


def device_index():
    return lax.axis_index("dp") * lax.axis_size("seq") + lax.axis_index("seq")


def modulate(hidden, shift, scale):
    centre = hidden - jnp.mean(hidden, axis=-1, keepdims=True)
    normed = centre * lax.rsqrt(jnp.mean(centre * centre, axis=-1, keepdims=True) + norm_eps)
    return normed * (1.0 + scale) + shift


def gelu_tanh(values):
    return jax.nn.gelu(values, approximate=True)


def time_features(steps_now):
    half_size = FREQ // 2
    frequency = jnp.exp(-math.log(10000.0) * jnp.arange(half_size, dtype=jnp.float32) / half_size)
    angles = steps_now.astype(jnp.float32)[:, None] * frequency[None, :]
    return jnp.concatenate([jnp.cos(angles), jnp.sin(angles)], axis=1)


def noise_level(steps_now):
    phase = (steps_now.astype(jnp.float32) / 1000.0 + 0.008) / 1.008 * (math.pi / 2.0)
    return jnp.cos(phase) ** 2


def variance_logs(level, level_prev):
    beta_now = jnp.minimum(1.0 - level / level_prev, 0.999)
    tilde_log = jnp.log(beta_now * (1.0 - level_prev) / (1.0 - level))
    return (jnp.log(beta_now), tilde_log)


def dot_nn(left, right):
    return lax.dot_general(left, right, (((1,), (0,)), ((), ())), preferred_element_type=jnp.float32)


def dot_nt(left, right):
    return lax.dot_general(left, right, (((1,), (1,)), ((), ())), preferred_element_type=jnp.float32)


def dot_tn(left, right):
    return lax.dot_general(left, right, (((0,), (0,)), ((), ())), preferred_element_type=jnp.float32)


def low(values):
    return values.astype(jnp.bfloat16)


def self_forward_kernel(heads, dim, start_ref, big_ref, qkv_ref, out_ref, key_s, value_s):
    micro = pl.program_id(0)
    blocks = qkv_ref.shape[0]
    scale = dim ** (-0.5)
    for b in range(blocks):
        for h in range(heads):
            rows = pl.ds(b * BLOCK, BLOCK)
            key_s[h, rows, :] = qkv_ref[b, 0, :, (heads + h) * dim : (heads + h + 1) * dim]
            value_s[h, rows, :] = qkv_ref[b, 0, :, (2 * heads + h) * dim : (2 * heads + h + 1) * dim]

    def one_block(b, carry):
        start = pl.multiple_of(start_ref[micro, b] * BLOCK, BLOCK)
        queries = qkv_ref[b, 0]

        def go(span):
            outs = []
            for h in range(heads):
                key = key_s[h, pl.ds(start, span), :]
                value = value_s[h, pl.ds(start, span), :]
                scores = dot_nt(queries[:, h * dim : (h + 1) * dim], key) * scale
                top = jnp.max(scores, axis=-1, keepdims=True)
                weight = jnp.exp(scores - top)
                total = jnp.sum(weight, axis=-1, keepdims=True)
                probs = low(weight * (1.0 / total))
                outs.append(low(dot_nn(probs, value)))
            out_ref[b, 0] = jnp.concatenate(outs, axis=-1)

        big = big_ref[micro, b]

        @pl.when(big == 1)
        def _():
            go(LARGE)

        @pl.when(big == 0)
        def _():
            go(BLOCK)

        return carry

    lax.fori_loop(0, blocks, one_block, 0)


def self_forward(start, big, qkv, heads, dim):
    blocks, micros = qkv.shape[0], qkv.shape[1]
    span = blocks * BLOCK
    return pl.pallas_call(
        functools.partial(self_forward_kernel, heads, dim),
        out_shape=jax.ShapeDtypeStruct((blocks, micros, BLOCK, heads * dim), jnp.bfloat16),
        grid_spec=pltpu.PrefetchScalarGridSpec(
            num_scalar_prefetch=2,
            grid=(micros,),
            in_specs=[pl.BlockSpec((blocks, 1, BLOCK, 3 * heads * dim), lambda m, s, g: (0, m, 0, 0))],
            out_specs=pl.BlockSpec((blocks, 1, BLOCK, heads * dim), lambda m, s, g: (0, m, 0, 0)),
            scratch_shapes=[
                pltpu.VMEM((heads, span, dim), jnp.bfloat16),
                pltpu.VMEM((heads, span, dim), jnp.bfloat16),
            ],
        ),
        compiler_params=pltpu.CompilerParams(vmem_limit_bytes=VMEM_BYTES),
    )(start, big, qkv)


def self_backward_kernel(
    heads, dim, start_ref, big_ref, qkv_ref, grad_ref, out_ref, sum_ref, key_s, value_s, dq_s, dk_s, dv_s
):
    micro = pl.program_id(0)
    blocks = qkv_ref.shape[0]
    scale = dim ** (-0.5)
    for b in range(blocks):
        for h in range(heads):
            rows = pl.ds(b * BLOCK, BLOCK)
            key_s[h, rows, :] = qkv_ref[b, 0, :, (heads + h) * dim : (heads + h + 1) * dim]
            value_s[h, rows, :] = qkv_ref[b, 0, :, (2 * heads + h) * dim : (2 * heads + h + 1) * dim]
    dk_s[...] = jnp.zeros_like(dk_s)
    dv_s[...] = jnp.zeros_like(dv_s)

    def one_block(b, carry):
        start = pl.multiple_of(start_ref[micro, b] * BLOCK, BLOCK)
        place = pl.multiple_of(b * BLOCK, BLOCK)
        queries = qkv_ref[b, 0]
        grads = grad_ref[b, 0]

        def go(span):
            keep = pl.ds(start, span)
            for h in range(heads):
                query = queries[:, h * dim : (h + 1) * dim]
                grad = grads[:, h * dim : (h + 1) * dim]
                key = key_s[h, keep, :]
                value = value_s[h, keep, :]
                scores = dot_nt(key, query) * scale
                top = jnp.max(scores, axis=0, keepdims=True)
                weight = jnp.exp(scores - top)
                probs = weight * (1.0 / jnp.sum(weight, axis=0, keepdims=True))
                dv_s[h, keep, :] += dot_nn(low(probs), grad)
                grad_probs = dot_nt(value, grad)
                inner = jnp.sum(probs * grad_probs, axis=0, keepdims=True)
                grad_scores = low(probs * (grad_probs - inner) * scale)
                dk_s[h, keep, :] += dot_nn(grad_scores, query)
                dq_s[h, pl.ds(place, BLOCK), :] = dot_tn(grad_scores, key)

        big = big_ref[micro, b]

        @pl.when(big == 1)
        def _():
            go(LARGE)

        @pl.when(big == 0)
        def _():
            go(BLOCK)

        return carry

    lax.fori_loop(0, blocks, one_block, 0)
    for b in range(blocks):
        rows = pl.ds(b * BLOCK, BLOCK)
        out_ref[b, 0] = jnp.concatenate(
            [low(part[h, rows, :]) for part in (dq_s, dk_s, dv_s) for h in range(heads)], axis=-1
        )
    sum_ref[0] = jnp.concatenate(
        [jnp.sum(part[h], axis=0, keepdims=True) for part in (dq_s, dv_s) for h in range(heads)], axis=-1
    )


def self_backward(start, big, qkv, grad, heads, dim):
    blocks, micros = qkv.shape[0], qkv.shape[1]
    span = blocks * BLOCK
    wide = pltpu.VMEM((heads, span, dim), jnp.float32)
    narrow = pltpu.VMEM((heads, span, dim), jnp.bfloat16)
    return pl.pallas_call(
        functools.partial(self_backward_kernel, heads, dim),
        out_shape=(
            jax.ShapeDtypeStruct((blocks, micros, BLOCK, 3 * heads * dim), jnp.bfloat16),
            jax.ShapeDtypeStruct((micros, 1, 2 * heads * dim), jnp.float32),
        ),
        grid_spec=pltpu.PrefetchScalarGridSpec(
            num_scalar_prefetch=2,
            grid=(micros,),
            in_specs=[
                pl.BlockSpec((blocks, 1, BLOCK, 3 * heads * dim), lambda m, s, g: (0, m, 0, 0)),
                pl.BlockSpec((blocks, 1, BLOCK, heads * dim), lambda m, s, g: (0, m, 0, 0)),
            ],
            out_specs=(
                pl.BlockSpec((blocks, 1, BLOCK, 3 * heads * dim), lambda m, s, g: (0, m, 0, 0)),
                pl.BlockSpec((1, 1, 2 * heads * dim), lambda m, s, g: (m, 0, 0)),
            ),
            scratch_shapes=[narrow, narrow, wide, wide, wide],
        ),
        compiler_params=pltpu.CompilerParams(vmem_limit_bytes=VMEM_BYTES),
    )(start, big, qkv, grad)


def cross_forward_kernel(dim, length_ref, query_ref, key_ref, value_ref, out_ref):
    length = length_ref[pl.program_id(0)]
    scale = dim ** (-0.5)
    live = lax.broadcasted_iota(jnp.int32, (BLOCK, CAP_PAD), 1) < length
    outs = []
    for h in range(HEADS):
        part = slice(h * dim, (h + 1) * dim)
        scores = jnp.where(live, dot_nt(query_ref[0, :, part], key_ref[0, :, part]) * scale, neg_large)
        weight = jnp.exp(scores - jnp.max(scores, axis=-1, keepdims=True))
        probs = low(weight * (1.0 / jnp.sum(weight, axis=-1, keepdims=True)))
        outs.append(low(dot_nn(probs, value_ref[0, :, part])))
    out_ref[0] = jnp.concatenate(outs, axis=-1)


def cross_backward_kernel(
    dim, length_ref, query_ref, key_ref, value_ref, grad_ref, dq_ref, dk_ref, dv_ref
):
    length = length_ref[pl.program_id(0)]
    scale = dim ** (-0.5)
    live = lax.broadcasted_iota(jnp.int32, (CAP_PAD, BLOCK), 0) < length
    dq, dk, dv = [], [], []
    for h in range(HEADS):
        part = slice(h * dim, (h + 1) * dim)
        query, key, value, grad = (
            query_ref[0, :, part],
            key_ref[0, :, part],
            value_ref[0, :, part],
            grad_ref[0, :, part],
        )
        scores = jnp.where(live, dot_nt(key, query) * scale, neg_large)
        weight = jnp.exp(scores - jnp.max(scores, axis=0, keepdims=True))
        probs = weight * (1.0 / jnp.sum(weight, axis=0, keepdims=True))
        dv.append(dot_nn(low(probs), grad))
        grad_probs = dot_nt(value, grad)
        inner = jnp.sum(probs * grad_probs, axis=0, keepdims=True)
        grad_scores = low(probs * (grad_probs - inner) * scale)
        dk.append(dot_nn(grad_scores, query))
        dq.append(dot_tn(grad_scores, key))
    dq_ref[0] = jnp.concatenate(dq, axis=-1)
    dk_ref[0] = jnp.concatenate(dk, axis=-1)
    dv_ref[0] = jnp.concatenate(dv, axis=-1)


def cross_call(kernel, length, arrays, outs):
    def spec(array):
        return pl.BlockSpec((1,) + array.shape[1:], lambda m, s: (m, 0, 0))

    return pl.pallas_call(
        kernel,
        out_shape=outs,
        grid_spec=pltpu.PrefetchScalarGridSpec(
            num_scalar_prefetch=1,
            grid=(MICRO,),
            in_specs=[spec(array) for array in arrays],
            out_specs=jax.tree.map(spec, outs),
        ),
        compiler_params=pltpu.CompilerParams(vmem_limit_bytes=VMEM_BYTES),
    )(length, *arrays)


UNIT = 8
SPLIT = 640
PIECE = 3
TILE = 96
TILE_START = 1024
LAG = 2
RING = LAG + 1
HOPS = 4
MESH = pl.DeviceIdType.MESH


def my_place():
    row, seq = lax.axis_index("dp"), lax.axis_index("seq")
    return lax.div(row, 2), lax.rem(row, 2), lax.div(seq, 2), lax.rem(seq, 2)


def peer(y, core, z, x):
    return (y * 2 + core, z * 2 + x)


def greet_all(devices, seq_count):
    me = lax.axis_index("dp") * seq_count + lax.axis_index("seq")
    barrier = pltpu.get_barrier_semaphore()

    def one(step, carry):
        other = lax.rem(me + step, devices)
        pl.semaphore_signal(
            barrier,
            inc=1,
            device_id=(lax.div(other, seq_count), lax.rem(other, seq_count)),
            device_id_type=MESH,
        )
        return carry

    lax.fori_loop(1, devices, one, 0)
    pl.semaphore_wait(barrier, devices - 1)


def global_tile(ranges, index):
    tile = index + ranges[0][0]
    at = ranges[0][1] - ranges[0][0]
    for start, stop in ranges[1:]:
        tile = jnp.where(index >= at, index - at + start, tile)
        at += stop - start
    return tile


def reduce_kernel(
    ranges,
    shard_units,
    devices,
    sources,
    receivers,
    *refs,
):
    rows_refs, refs = refs[: len(sources)], list(refs[len(sources) :])
    if receivers:
        block_ref, parts_ref = refs.pop(0), refs.pop(0)
        all_ref, got_ref = refs.pop(1), refs.pop(1)
        refs, push, push_parts = refs[:-6], refs[-6:-3], refs[-3:]
    (
    out_ref,
    own_s,
    core_s,
    first_s,
    second_s,
    first_y_s,
    second_x_s,
    first_two_s,
    second_two_s,
    first_x_s,
    second_y_s,
    third_s,
    along_s,
    leaf_s,
    load_sem,
    core_send,
    core_recv,
    one_send,
    one_recv,
    two_send,
    two_recv,
    z_send,
    z_recv,
    leaf_send,
    leaf_recv,
    ) = refs
    tiles = core_s.shape[0]
    seq_count = devices // 4
    y, core, z, x = my_place()
    me = (y * 2 + core) * seq_count + z * 2 + x
    stride = 5 if tiles % 5 else 3
    half, quarter, eighth = TILE // 2, TILE // 4, TILE // 8
    across_core = peer(y, 1 - core, z, x)
    across_y = peer(1 - y, core, z, x)
    across_x = peer(y, core, z, 1 - x)

    def remote(source, target, send, recv, device):
        return pltpu.make_async_remote_copy(
            src_ref=source,
            dst_ref=target,
            send_sem=send,
            recv_sem=recv,
            device_id=device,
            device_id_type=MESH,
        )

    def core_copy(t, rows_ref=None, start=0):
        source = own_s.at[0] if rows_ref is None else rows_ref.at[pl.ds(start, half)]
        return remote(source, core_s.at[t], core_send.at[t], core_recv.at[t], across_core)

    def load(t, rows_ref=None, start=0):
        slot = lax.rem(t, 2)
        source = rows_refs[-1] if rows_ref is None else rows_ref
        return pltpu.make_async_copy(
            source.at[pl.ds(start, half)], own_s.at[slot], load_sem.at[slot]
        )

    def start_from(copy, t, side):
        index = lax.rem(t * stride, tiles) * 2 + side
        at = 0
        for rows_ref, (start, count) in zip(rows_refs, sources):

            @pl.when((index >= at) & (index < at + count))
            def _(rows_ref=rows_ref, start=start, at=at):
                copy(t, rows_ref, start + (index - at) * half).start()

            at += count

    def first_one(t):
        return remote(
            first_s.at[lax.rem(t, RING), pl.ds((1 - y) * quarter, quarter)],
            first_y_s.at[t],
            one_send.at[lax.rem(t, RING), 0],
            one_recv.at[t, 0],
            across_y,
        )

    def second_one(t, side):
        return remote(
            second_s.at[lax.rem(t, RING), pl.ds(side * quarter + (1 - x) * eighth, eighth)],
            second_x_s.at[t, pl.ds(side * eighth, eighth)],
            one_send.at[lax.rem(t, RING), 1 + side],
            one_recv.at[t, 1 + side],
            across_x,
        )

    def first_two(t):
        return remote(
            first_two_s.at[lax.rem(t, RING), pl.ds((1 - x) * eighth, eighth)],
            first_x_s.at[t],
            two_send.at[lax.rem(t, RING), 0],
            two_recv.at[t, 0],
            across_x,
        )

    def second_two(t):
        return remote(
            second_two_s.at[lax.rem(t, RING), pl.ds((1 - y) * eighth, eighth)],
            second_y_s.at[t],
            two_send.at[lax.rem(t, RING), 1],
            two_recv.at[t, 1],
            across_y,
        )

    def each_three(t, visit):
        tile = global_tile(ranges, lax.rem(t * stride, tiles))

        def one(index, carry):
            row = index * PIECE
            unit = TILE_START + tile * TILE + ((core * 2 + y) * 2 + x) * eighth + row
            owner = lax.div(unit, shard_units)
            at = unit - owner * shard_units

            @pl.when(at + PIECE <= shard_units)
            def _():
                visit(row, index, PIECE, owner, at)

            @pl.when(at + PIECE > shard_units)
            def _():
                for part in range(PIECE):
                    over = at + part >= shard_units
                    visit(
                        row + part,
                        4 + part,
                        1,
                        jnp.where(over, owner + 1, owner),
                        jnp.where(over, at + part - shard_units, at + part),
                    )

            return carry

        lax.fori_loop(0, eighth // PIECE, one, 0)

    def z_copy(t, row, slot, count, way):
        other = (jnp.maximum(z - 1, 0), jnp.minimum(z + 1, 3))[way]
        return remote(
            third_s.at[lax.rem(t, HOPS), pl.ds(row, count)],
            along_s.at[t, way, pl.ds(row, count)],
            z_send.at[lax.rem(t, HOPS), slot],
            z_recv.at[t, way, slot],
            peer(y, core, other, x),
        )

    def arrived(t, row, slot, count, way):
        part = along_s.at[t, way, pl.ds(row, count)]
        pltpu.make_async_copy(part, part, z_recv.at[t, way, slot]).wait()

    def total_of(t, row, count, *ways):
        total = third_s[lax.rem(t, HOPS), pl.ds(row, count)].astype(jnp.float32)
        for way in ways:
            total = total + along_s[t, way, pl.ds(row, count)].astype(jnp.float32)
        return total.astype(jnp.bfloat16)

    def owner_plane(owner):
        return lax.rem(lax.div(owner, 2), 4)

    def hop(t, number):
        def visit(row, slot, count, owner, at):
            to = owner_plane(owner)
            for way, here, more in (
                (0, (z > to) & (3 - z == number), z < 3),
                (1, (z < to) & (z == number), z > 0),
            ):

                @pl.when(here)
                def _(way=way, more=more):
                    @pl.when(more)
                    def _():
                        arrived(t, row, slot, count, way)
                        total = total_of(t, row, count, way)
                        third_s[lax.rem(t, HOPS), pl.ds(row, count)] = total

                    z_copy(t, row, slot, count, way).start()

        each_three(t, visit)

    def hand_over(t):
        def visit(row, slot, count, owner, at):
            to = owner_plane(owner)

            @pl.when(to == z)
            def _():
                for here, ways in (
                    (z == 0, (0,)),
                    ((z > 0) & (z < 3), (0, 1)),
                    (z == 3, (1,)),
                ):

                    @pl.when(here)
                    def _(ways=ways):
                        for way in ways:
                            arrived(t, row, slot, count, way)
                        leaf_s[t, pl.ds(row, count)] = total_of(t, row, count, *ways)

                leaf_copy(t, row, slot, count, owner, at, 0)

            @pl.when(to != z)
            def _():
                z_copy(t, row, slot, count, 0).wait_send()

        each_three(t, visit)

    def leaf_copy(t, row, slot, count, owner, at, stage):
        source = leaf_s.at[t, pl.ds(row, count)]
        target = out_ref.at[pl.ds(at, count)]
        sending = remote(
            source,
            target,
            leaf_send.at[t, slot],
            leaf_recv.at[at],
            (lax.div(owner, seq_count), lax.rem(owner, seq_count)),
        )

        @pl.when(owner != me)
        def _():
            if stage == 0:
                sending.start()
            else:
                sending.wait_send()

        if stage == 0:

            @pl.when(owner == me)
            def _():
                pltpu.make_async_copy(source, target, leaf_recv.at[at]).start()

    def leaf_done(t):
        def visit(row, slot, count, owner, at):
            @pl.when(owner_plane(owner) == z)
            def _():
                leaf_copy(t, row, slot, count, owner, at, 1)

        each_three(t, visit)

    for t in range(min(2, tiles)):
        start_from(load, t, core)
    greet_all(devices, seq_count)

    def start_core(t, carry):
        start_from(core_copy, t, 1 - core)
        return carry

    lax.fori_loop(0, tiles, start_core, 0)
    if receivers:
        start_push(parts_ref, got_ref, devices, devices, me, *push_parts, scatter=True)
        start_push(block_ref, all_ref, devices, receivers, me, *push)

    def one_step(step, carry):
        @pl.when(step < tiles)
        def _():
            t = step
            slot = lax.rem(t, RING)
            load(t).wait()
            core_copy(t).wait_recv()

            def one(index, inner):
                at = pl.ds(index * 4, 4)
                total = own_s[lax.rem(t, 2), at].astype(jnp.float32) + core_s[t, at].astype(jnp.float32)
                total = total.astype(jnp.bfloat16)
                first_s[slot, at] = total[:, :, :SPLIT]
                second_s[slot, at] = total[:, :, SPLIT:]
                return inner

            lax.fori_loop(0, half // 4, one, 0)
            first_one(t).start()
            second_one(t, 0).start()
            second_one(t, 1).start()

            @pl.when(t + 2 < tiles)
            def _():
                start_from(load, t + 2, core)

        @pl.when((step >= LAG) & (step < tiles + LAG))
        def _():
            t = step - LAG
            slot = lax.rem(t, RING)
            first_one(t).wait()

            def one(index, inner):
                at = pl.ds(index * 4, 4)
                mine = first_s[slot, pl.ds(y * quarter + index * 4, 4)].astype(jnp.float32)
                total = mine + first_y_s[t, at].astype(jnp.float32)
                first_two_s[slot, at] = total.astype(jnp.bfloat16)
                return inner

            lax.fori_loop(0, quarter // 4, one, 0)
            first_two(t).start()
            for side in range(2):
                second_one(t, side).wait()

                def two(index, inner):
                    mine = second_s[slot, pl.ds(side * quarter + x * eighth + index * 4, 4)]
                    at = pl.ds(side * eighth + index * 4, 4)
                    total = mine.astype(jnp.float32) + second_x_s[t, at].astype(jnp.float32)
                    second_two_s[slot, at] = total.astype(jnp.bfloat16)
                    return inner

                lax.fori_loop(0, eighth // 4, two, 0)
            second_two(t).start()

        @pl.when((step >= 2 * LAG) & (step < tiles + 2 * LAG))
        def _():
            t = step - 2 * LAG
            slot = lax.rem(t, RING)
            first_two(t).wait()
            second_two(t).wait()

            def one(index, inner):
                at = pl.ds(index * 4, 4)
                mine = first_two_s[slot, pl.ds(x * eighth + index * 4, 4)].astype(jnp.float32)
                total = mine + first_x_s[t, at].astype(jnp.float32)
                third_s[lax.rem(t, HOPS), at, :, :SPLIT] = total.astype(jnp.bfloat16)
                mine = second_two_s[slot, pl.ds(y * eighth + index * 4, 4)].astype(jnp.float32)
                total = mine + second_y_s[t, at].astype(jnp.float32)
                third_s[lax.rem(t, HOPS), at, :, SPLIT:] = total.astype(jnp.bfloat16)
                return inner

            lax.fori_loop(0, eighth // 4, one, 0)

        for number in range(4):
            old = step - 2 * LAG - number

            @pl.when((old >= 0) & (old < tiles))
            def _(old=old, number=number):
                if number < 3:
                    hop(old, number)
                else:
                    hand_over(old)

        return carry

    lax.fori_loop(0, tiles + 2 * LAG + 3, one_step, 0)

    def finish(t, carry):
        core_copy(t).wait_send()
        leaf_done(t)
        return carry

    lax.fori_loop(0, tiles, finish, 0)
    if receivers:
        finish_push(parts_ref, got_ref, devices, devices, me, *push_parts, scatter=True)
        finish_push(block_ref, all_ref, devices, receivers, me, *push)
    far = TILE_START - TILE * (TILE_START // TILE)
    begin = me * shard_units
    first_at = lax.rem(PIECE - lax.rem(begin + PIECE - far % PIECE, PIECE), PIECE)

    def arrive(index, count):
        unit = begin + index
        inside = False
        for start, stop in ranges:
            low_end, high_end = TILE_START + start * TILE, TILE_START + stop * TILE
            inside = inside | ((unit >= low_end) & (unit < high_end))

        @pl.when(inside)
        def _():
            part = out_ref.at[pl.ds(index, count)]
            pltpu.make_async_copy(part, part, leaf_recv.at[index]).wait()

    def arrive_three(step, carry):
        index = first_at + step * PIECE

        @pl.when(index + PIECE <= shard_units)
        def _():
            arrive(index, PIECE)

        return carry

    steps = shard_units // PIECE
    lax.fori_loop(0, steps, arrive_three, 0)
    covered = first_at + lax.div(shard_units - first_at, PIECE) * PIECE
    for step in range(PIECE - 1):

        @pl.when(step < first_at)
        def _():
            arrive(step, 1)

        @pl.when(covered + step < shard_units)
        def _():
            arrive(covered + step, 1)


def push_copy(block_ref, all_ref, devices, me, step, send_sem, recv_sem, scatter):
    seq_count = devices // 4
    other = lax.rem(me + step, devices)
    return other, pltpu.make_async_remote_copy(
        src_ref=block_ref.at[other] if scatter else block_ref,
        dst_ref=all_ref.at[me],
        send_sem=send_sem.at[step],
        recv_sem=recv_sem.at[me],
        device_id=(lax.div(other, seq_count), lax.rem(other, seq_count)),
        device_id_type=MESH,
    )


def start_push(block_ref, all_ref, devices, receivers, me, send_sem, recv_sem, keep_sem, scatter=False):
    own_ref = block_ref.at[me] if scatter else block_ref

    @pl.when(me < receivers)
    def _():
        pltpu.make_async_copy(own_ref, all_ref.at[me], keep_sem).start()

    def send(step, carry):
        other, sending = push_copy(
            block_ref, all_ref, devices, me, step, send_sem, recv_sem, scatter
        )

        @pl.when(other < receivers)
        def _():
            sending.start()

        return carry

    lax.fori_loop(1, devices, send, 0)


def finish_push(
    block_ref, all_ref, devices, receivers, me, send_sem, recv_sem, keep_sem, scatter=False
):
    own_ref = block_ref.at[me] if scatter else block_ref

    @pl.when(me < receivers)
    def _():
        pltpu.make_async_copy(own_ref, all_ref.at[me], keep_sem).wait()

    def finish(step, carry):
        other, sending = push_copy(
            block_ref, all_ref, devices, me, step, send_sem, recv_sem, scatter
        )

        @pl.when(other < receivers)
        def _():
            sending.wait_send()

        source = lax.rem(me + devices - step, devices)

        @pl.when(me < receivers)
        def _():
            pltpu.make_async_copy(own_ref, all_ref.at[source], recv_sem.at[source]).wait()

        return carry

    lax.fori_loop(1, devices, finish, 0)


def push_sems(devices):
    dma = pltpu.SemaphoreType.DMA
    return [dma((devices,)), dma((devices,)), dma]


def reduce_rows(ranges, shard_units, devices, collective_id, pieces, blocks=(), receivers=0):
    tiles = sum(stop - start for start, stop in ranges)
    width = pieces[0][0].shape[1]
    sources = tuple(piece[1:] for piece in pieces)
    assert sum(count for _, count in sources) == 2 * tiles
    half, quarter, eighth = TILE // 2, TILE // 4, TILE // 8
    rest = width - SPLIT

    def vmem(*shape):
        return pltpu.VMEM(shape, jnp.bfloat16)

    dma = pltpu.SemaphoreType.DMA
    outs = [jax.ShapeDtypeStruct((shard_units, UNIT, width), jnp.bfloat16)]
    if blocks:
        outs.append(jax.ShapeDtypeStruct((devices,) + blocks[0].shape, blocks[0].dtype))
        outs.append(jax.ShapeDtypeStruct(blocks[1].shape, blocks[1].dtype))
    out = pl.pallas_call(
        functools.partial(reduce_kernel, ranges, shard_units, devices, sources, receivers),
        out_shape=outs,
        in_specs=[pl.BlockSpec(memory_space=pl.ANY)] * (len(pieces) + len(blocks)),
        out_specs=[pl.BlockSpec(memory_space=pl.ANY)] * len(outs),
        scratch_shapes=[
            vmem(2, half, UNIT, width),
            vmem(tiles, half, UNIT, width),
            vmem(RING, half, UNIT, SPLIT),
            vmem(RING, half, UNIT, rest),
            vmem(tiles, quarter, UNIT, SPLIT),
            vmem(tiles, quarter, UNIT, rest),
            vmem(RING, quarter, UNIT, SPLIT),
            vmem(RING, quarter, UNIT, rest),
            vmem(tiles, eighth, UNIT, SPLIT),
            vmem(tiles, eighth, UNIT, rest),
            vmem(HOPS, eighth, UNIT, width),
            vmem(tiles, 2, eighth, UNIT, width),
            vmem(tiles, eighth, UNIT, width),
            dma((2,)),
            dma((tiles,)),
            dma((tiles,)),
            dma((RING, 3)),
            dma((tiles, 3)),
            dma((RING, 2)),
            dma((tiles, 2)),
            dma((HOPS, 7)),
            dma((tiles, 2, 7)),
            dma((tiles, 7)),
            dma((shard_units,)),
        ]
        + (push_sems(devices) + push_sems(devices) if blocks else []),
        compiler_params=pltpu.CompilerParams(
            collective_id=collective_id, has_side_effects=True, vmem_limit_bytes=VMEM_BYTES
        ),
    )(*[piece[0].reshape(-1, UNIT, width) for piece in pieces], *blocks)
    return out if blocks else out[0]


STRIDE = 3
Z_LAG = 2
Z_RING = 3 * Z_LAG + 1


def gather_kernel(
    openings,
    ahead,
    devices,
    shard_ref,
    out_ref,
    later_ref,
    deal_send,
    deal_recv,
    z_send,
    z_recv,
    one_send,
    one_recv,
    two_send,
    two_recv,
    core_send,
    core_recv,
):
    shard_units = shard_ref.shape[0]
    seq_count = devices // 4
    width = shard_ref.shape[2]
    tiles = out_ref.shape[0] // TILE
    later_tiles = later_ref.shape[0] // TILE
    streams = ((openings[0], tiles, out_ref, 0), (openings[1], later_tiles, later_ref, tiles))
    y, core, z, x = my_place()
    me = (y * 2 + core) * seq_count + z * 2 + x
    half, quarter, eighth = TILE // 2, TILE // 4, TILE // 8
    leaves = TILE // PIECE
    upward = peer(y, core, jnp.minimum(z + 1, 3), x)
    downward = peer(y, core, jnp.maximum(z - 1, 0), x)

    def bounds(stream):
        begin = me * shard_units - stream[0]
        finish = begin + shard_units
        return begin, finish, lax.div(begin + PIECE - 1, PIECE), lax.div(finish, PIECE)

    def deal_some(stream, stage, three, part, count):
        begin = bounds(stream)[0]
        ref = stream[2]
        tile = lax.div(three, leaves)
        leaf = three - tile * leaves
        eight = lax.div(leaf, 4)
        slot = leaf - eight * 4 if count == PIECE else 4 + part
        holder_core = lax.div(eight, 4)
        holder_y = lax.rem(lax.div(eight, 2), 2)
        holder_x = lax.rem(eight, 2)
        holder = (holder_y * 2 + holder_core) * seq_count + z * 2 + holder_x
        index = three * PIECE + part - begin
        source = shard_ref.at[pl.ds(index, count)]
        target = ref.at[pl.ds(three * PIECE + part, count)]
        recv = deal_recv.at[stream[3] + tile, slot]
        sending = pltpu.make_async_remote_copy(
            src_ref=source,
            dst_ref=target,
            send_sem=deal_send.at[0 if stream[3] == 0 else 1, index],
            recv_sem=recv,
            device_id=peer(holder_y, holder_core, z, holder_x),
            device_id_type=MESH,
        )

        @pl.when(holder != me)
        def _():
            if stage == 0:
                sending.start()
            else:
                sending.wait_send()

        if stage == 0:

            @pl.when(holder == me)
            def _():
                pltpu.make_async_copy(source, target, recv).start()

    def deal_between(stream, stage, low_three, count, base):
        begin, finish, first_three, last_three = bounds(stream)
        base = first_three if base is None else base

        @pl.when((low_three <= last_three) & (low_three + count >= first_three))
        def _():
            def one(step, carry):
                three = base + step

                @pl.when(
                    (three >= first_three)
                    & (three < last_three)
                    & (three >= low_three)
                    & (three < low_three + count)
                )
                def _():
                    deal_some(stream, stage, three, 0, PIECE)

                return carry

            lax.fori_loop(0, min(count, shard_units // PIECE + 1), one, 0)
            for step in range(PIECE - 1):
                three = first_three - 1
                here = (three >= low_three) & (three < low_three + count)

                @pl.when(here & (begin + step < first_three * PIECE))
                def _(three=three):
                    deal_some(stream, stage, three, begin + step - three * PIECE, 1)

                three = last_three
                here = (three >= low_three) & (three < low_three + count)

                @pl.when(here & (three * PIECE + step < finish))
                def _(three=three):
                    deal_some(stream, stage, three, step, 1)

    def deal_tile(stream, step):
        low_three = tile_at(step, stream[1]) * leaves
        deal_between(stream, 0, low_three, leaves, low_three)

    def each_three(stream, t, visit):
        def one(index, carry):
            row = t * TILE + ((core * 2 + y) * 2 + x) * eighth + index * PIECE
            unit = stream[0] + row
            owner = lax.div(unit, shard_units)
            at = unit - owner * shard_units

            @pl.when(at + PIECE <= shard_units)
            def _():
                visit(row, index, PIECE, lax.rem(lax.div(owner, 2), 4))

            @pl.when(at + PIECE > shard_units)
            def _():
                for part in range(PIECE):
                    holder = jnp.where(at + part >= shard_units, owner + 1, owner)
                    visit(row + part, 4 + part, 1, lax.rem(lax.div(holder, 2), 4))

            return carry

        lax.fori_loop(0, eighth // PIECE, one, 0)

    def wait_units(ref, count, sem):
        part = ref.at[pl.ds(0, count)]
        pltpu.make_async_copy(part, part, sem).wait()

    def z_copy(stream, step, row, slot, count, way):
        part = stream[2].at[pl.ds(row, count)]
        which = 0 if stream[3] == 0 else 1
        return pltpu.make_async_remote_copy(
            src_ref=part,
            dst_ref=part,
            send_sem=z_send.at[which, lax.rem(step, Z_RING), slot, way],
            recv_sem=z_recv.at[stream[3] + tile_at(step, stream[1]), slot],
            device_id=(upward, downward)[way],
            device_id_type=MESH,
        )

    def along_z(stream, step, distance):
        t = tile_at(step, stream[1])

        def visit(row, slot, count, owner_z):
            @pl.when(jnp.abs(owner_z - z) == distance)
            def _():
                sem = deal_recv if distance == 0 else z_recv
                wait_units(out_ref, count, sem.at[stream[3] + t, slot])

                @pl.when((owner_z <= z) & (z < 3))
                def _():
                    z_copy(stream, step, row, slot, count, 0).start()

                @pl.when((owner_z >= z) & (z > 0))
                def _():
                    z_copy(stream, step, row, slot, count, 1).start()

        each_three(stream, t, visit)

    def along_z_done(stream, step):
        t = tile_at(step, stream[1])

        def visit(row, slot, count, owner_z):
            @pl.when((owner_z <= z) & (z < 3))
            def _():
                z_copy(stream, step, row, slot, count, 0).wait_send()

            @pl.when((owner_z >= z) & (z > 0))
            def _():
                z_copy(stream, step, row, slot, count, 1).wait_send()

        each_three(stream, t, visit)

    def z_stage(stream, step):
        for distance in range(4):
            old = step - distance * Z_LAG

            @pl.when((old >= 0) & (old < stream[1]))
            def _(old=old, distance=distance):
                along_z(stream, old, distance)
                if distance == 3:
                    along_z_done(stream, old)

    spreading = spread_steps(
        out_ref, one_send, one_recv, two_send, two_recv, core_send, core_recv
    )
    main, late = streams
    greet_all(devices, seq_count)
    for step in range(min(ahead, tiles)):
        deal_tile(main, step)
    for step in range(min(ahead, later_tiles)):
        deal_tile(late, step)

    def one_step(step, carry):
        @pl.when(step + ahead < tiles)
        def _():
            deal_tile(main, step + ahead)

        @pl.when(step + ahead < later_tiles)
        def _():
            deal_tile(late, step + ahead)

        z_stage(main, step)
        spreading(step - 3 * Z_LAG)
        z_stage(late, step)
        return carry

    lax.fori_loop(0, tiles + 3 * LAG + 3 * Z_LAG, one_step, 0)
    for stream in streams:
        deal_between(stream, 1, 0, stream[1] * leaves, None)


def tile_at(step, tiles):
    return lax.rem(step * STRIDE, tiles)


def spread_steps(out_ref, one_send, one_recv, two_send, two_recv, core_send, core_recv):
    tiles = out_ref.shape[0] // TILE
    width = out_ref.shape[2]
    y, core, z, x = my_place()
    half, quarter, eighth = TILE // 2, TILE // 4, TILE // 8
    left, right = pl.ds(0, SPLIT), pl.ds(SPLIT, width - SPLIT)
    whole = pl.ds(0, width)
    across_core = peer(y, 1 - core, z, x)
    across_y = peer(1 - y, core, z, x)
    across_x = peer(y, core, z, 1 - x)

    def remote(start, count, columns, send, recv, device):
        part = out_ref.at[pl.ds(start, count), :, columns]
        return pltpu.make_async_remote_copy(
            src_ref=part,
            dst_ref=part,
            send_sem=send,
            recv_sem=recv,
            device_id=device,
            device_id_type=MESH,
        )

    def block(t, y_at, x_at):
        return t * TILE + ((core * 2 + y_at) * 2 + x_at) * eighth

    def one_first(step):
        t = tile_at(step, tiles)
        sems = (one_send.at[lax.rem(step, RING), 0], one_recv.at[t, 0])
        return remote(block(t, y, x), eighth, left, *sems, across_x)

    def one_second(step):
        t = tile_at(step, tiles)
        sems = (one_send.at[lax.rem(step, RING), 1], one_recv.at[t, 1])
        return remote(block(t, y, x), eighth, right, *sems, across_y)

    def two_first(step):
        t = tile_at(step, tiles)
        sems = (two_send.at[lax.rem(step, RING), 0], two_recv.at[t, 0])
        return remote(block(t, y, 0), quarter, left, *sems, across_y)

    def two_second(step, side):
        t = tile_at(step, tiles)
        sems = (two_send.at[lax.rem(step, RING), 1 + side], two_recv.at[t, 1 + side])
        return remote(block(t, side, x), eighth, right, *sems, across_x)

    def core_copy(step):
        t = tile_at(step, tiles)
        sems = (core_send.at[lax.rem(step, RING)], core_recv.at[t])
        return remote(t * TILE + core * half, half, whole, *sems, across_core)

    def go(step):
        @pl.when((step >= 0) & (step < tiles))
        def _():
            one_first(step).start()
            one_second(step).start()

        @pl.when((step >= LAG) & (step < tiles + LAG))
        def _():
            old = step - LAG
            one_first(old).wait()
            two_first(old).start()
            one_second(old).wait()
            for side in range(2):
                two_second(old, side).start()

        @pl.when((step >= 2 * LAG) & (step < tiles + 2 * LAG))
        def _():
            old = step - 2 * LAG
            two_first(old).wait()
            for side in range(2):
                two_second(old, side).wait()
            core_copy(old).start()

        @pl.when(step >= 3 * LAG)
        def _():
            core_copy(step - 3 * LAG).wait()

    return go


def spread_sems(tiles):
    dma = pltpu.SemaphoreType.DMA
    return [
        dma((RING, 2)),
        dma((tiles, 2)),
        dma((RING, 3)),
        dma((tiles, 3)),
        dma((RING,)),
        dma((tiles,)),
    ]


def spread_kernel(devices, rows_ref, block_ref, out_ref, all_ref, *sems):
    seq_count = devices // 4
    me = lax.axis_index("dp") * seq_count + lax.axis_index("seq")
    sems, push = sems[:-3], sems[-3:]
    greet_all(devices, seq_count)
    start_push(block_ref, all_ref, devices, devices, me, *push)
    spreading = spread_steps(out_ref, *sems)

    def one_step(step, carry):
        spreading(step)
        return carry

    lax.fori_loop(0, out_ref.shape[0] // TILE + 3 * LAG, one_step, 0)
    finish_push(block_ref, all_ref, devices, devices, me, *push)


def spread_rows(rows, block, devices, collective_id):
    return pl.pallas_call(
        functools.partial(spread_kernel, devices),
        out_shape=(
            jax.ShapeDtypeStruct(rows.shape, rows.dtype),
            jax.ShapeDtypeStruct((devices,) + block.shape, block.dtype),
        ),
        in_specs=[pl.BlockSpec(memory_space=pl.ANY)] * 2,
        out_specs=(pl.BlockSpec(memory_space=pl.ANY), pl.BlockSpec(memory_space=pl.ANY)),
        scratch_shapes=spread_sems(rows.shape[0] // TILE) + push_sems(devices),
        input_output_aliases={0: 0},
        compiler_params=pltpu.CompilerParams(
            collective_id=collective_id, has_side_effects=True, vmem_limit_bytes=VMEM_BYTES
        ),
    )(rows, block)


def gather_rows(openings, counts, ahead, devices, collective_id, shard):
    units, _, width = shard.shape
    assert all(count % STRIDE for count in counts) and counts[1] <= counts[0]
    dma = pltpu.SemaphoreType.DMA
    anywhere = pl.BlockSpec(memory_space=pl.ANY)
    return pl.pallas_call(
        functools.partial(gather_kernel, openings, ahead, devices),
        out_shape=[
            jax.ShapeDtypeStruct((count * TILE, UNIT, width), jnp.bfloat16) for count in counts
        ],
        in_specs=[anywhere],
        out_specs=[anywhere, anywhere],
        scratch_shapes=[
            dma((2, units)),
            dma((sum(counts), 7)),
            dma((2, Z_RING, 7, 2)),
            dma((sum(counts), 7)),
        ]
        + spread_sems(counts[0]),
        compiler_params=pltpu.CompilerParams(
            collective_id=collective_id, has_side_effects=True, vmem_limit_bytes=VMEM_BYTES
        ),
    )(shard)


def share_kernel(devices, block_ref, out_ref, *sems):
    seq_count = devices // 4
    me = lax.axis_index("dp") * seq_count + lax.axis_index("seq")
    greet_all(devices, seq_count)
    start_push(block_ref, out_ref, devices, devices, me, *sems)
    finish_push(block_ref, out_ref, devices, devices, me, *sems)


def share(block, devices, collective_id):
    return pl.pallas_call(
        functools.partial(share_kernel, devices),
        out_shape=jax.ShapeDtypeStruct((devices,) + block.shape, block.dtype),
        in_specs=[pl.BlockSpec(memory_space=pltpu.VMEM)],
        out_specs=pl.BlockSpec(memory_space=pltpu.VMEM),
        scratch_shapes=push_sems(devices),
        compiler_params=pltpu.CompilerParams(
            collective_id=collective_id, has_side_effects=True, vmem_limit_bytes=16 * 1024 * 1024
        ),
    )(block)


def contrast_kernel(pooled_ref, pick_ref, row_ref, col_ref, scale_ref, pool_ref, text_ref, loss_ref):
    count = pick_ref.shape[1]
    scale = scale_ref[0, 0] / contrastive_sharpness_divisor
    diagonal = lax.broadcasted_iota(jnp.int32, (count, count), 0) == lax.broadcasted_iota(
        jnp.int32, (count, count), 1
    )
    loss = jnp.zeros((1, 1), jnp.float32)
    for m in range(MICRO):
        row = row_ref[m]
        col = col_ref[m] > 0.0
        image = jnp.dot(
            pick_ref[m], pooled_ref[m], precision=exact, preferred_element_type=jnp.float32
        )
        words = pooled_ref[MICRO + m]
        image_norm = lax.rsqrt(jnp.sum(image * image, axis=-1, keepdims=True) + norm_eps)
        words_norm = lax.rsqrt(jnp.sum(words * words, axis=-1, keepdims=True) + norm_eps)
        image = image * image_norm
        words = words * words_norm
        cosines = lax.dot_general(
            image,
            words,
            (((1,), (1,)), ((), ())),
            precision=exact,
            preferred_element_type=jnp.float32,
        )
        cosines = jnp.where(col, cosines / contrastive_sharpness_divisor, neg_large)
        top = jnp.max(cosines, axis=-1, keepdims=True)
        weight = jnp.exp(cosines - top)
        total = jnp.sum(weight, axis=-1, keepdims=True)
        matched = jnp.sum(jnp.where(diagonal, cosines, 0.0), axis=-1, keepdims=True)
        lost = jnp.where(row > 0.0, top + jnp.log(total) - matched, 0.0)
        loss = loss + jnp.sum(lost, axis=0, keepdims=True)
        grad = weight / total - jnp.where(diagonal, 1.0, 0.0)
        grad = jnp.where((row > 0.0) & col, grad * scale, 0.0)
        grad_image = jnp.dot(grad, words, precision=exact, preferred_element_type=jnp.float32)
        grad_words = lax.dot_general(
            grad,
            image,
            (((0,), (0,)), ((), ())),
            precision=exact,
            preferred_element_type=jnp.float32,
        )
        inner = jnp.sum(image * grad_image, axis=-1, keepdims=True)
        pool_ref[m] = image_norm * (grad_image - image * inner)
        inner = jnp.sum(words * grad_words, axis=-1, keepdims=True)
        text_ref[m] = words_norm * (grad_words - words * inner)
    loss_ref[...] = jnp.broadcast_to(loss, loss_ref.shape)


def contrast(pooled, pick, valid, scale):
    count, width = pooled.shape[1], pooled.shape[2]
    grads = jax.ShapeDtypeStruct((MICRO, count, width), jnp.float32)
    return pl.pallas_call(
        contrast_kernel,
        out_shape=(grads, grads, jax.ShapeDtypeStruct((1, 128), jnp.float32)),
        compiler_params=pltpu.CompilerParams(vmem_limit_bytes=VMEM_BYTES),
    )(pooled, pick, valid[:, :, None], valid[:, None, :], scale.reshape(1, 1))


def joint_forward_kernel(rows_ref, matrix_ref, bias_ref, out_ref):
    part, width = matrix_ref.shape[2], matrix_ref.shape[3]
    matrix = matrix_ref[...].reshape(3 * part, width)
    out_ref[0] = low(dot_nt(rows_ref[...], matrix) + bias_ref[0])


def joint_forward(rows, matrix, bias):
    count, width = rows.shape
    groups, _, columns = bias.shape
    return pl.pallas_call(
        joint_forward_kernel,
        out_shape=jax.ShapeDtypeStruct((groups, count, columns), jnp.bfloat16),
        grid=(groups,),
        in_specs=[
            pl.BlockSpec((count, width), lambda j: (0, 0)),
            pl.BlockSpec((3, 1, columns // 3, width), lambda j: (0, j, 0, 0)),
            pl.BlockSpec((1, 1, columns), lambda j: (j, 0, 0)),
        ],
        out_specs=pl.BlockSpec((1, count, columns), lambda j: (j, 0, 0)),
        compiler_params=pltpu.CompilerParams(vmem_limit_bytes=VMEM_BYTES),
    )(rows, matrix.reshape(3, groups, columns // 3, width), bias)


def joint_backward_kernel(grad_ref, matrix_ref, rows_ref, out_ref, weight_ref):
    part, width = matrix_ref.shape[2], matrix_ref.shape[3]
    grad = grad_ref[0]
    term = dot_nn(grad, matrix_ref[...].reshape(3 * part, width))
    weight_ref[...] = low(dot_tn(grad, rows_ref[...])).reshape(3, 1, part, width)

    @pl.when(pl.program_id(0) == 0)
    def _():
        out_ref[...] = term

    @pl.when(pl.program_id(0) > 0)
    def _():
        out_ref[...] += term


def joint_backward(grad, matrix, rows):
    groups, count, columns = grad.shape
    width = rows.shape[1]
    part = columns // 3
    out, weight = pl.pallas_call(
        joint_backward_kernel,
        out_shape=(
            jax.ShapeDtypeStruct((count, width), jnp.float32),
            jax.ShapeDtypeStruct((3, groups, part, width), jnp.bfloat16),
        ),
        grid=(groups,),
        in_specs=[
            pl.BlockSpec((1, count, columns), lambda j: (j, 0, 0)),
            pl.BlockSpec((3, 1, part, width), lambda j: (0, j, 0, 0)),
            pl.BlockSpec((count, width), lambda j: (0, 0)),
        ],
        out_specs=(
            pl.BlockSpec((count, width), lambda j: (0, 0)),
            pl.BlockSpec((3, 1, part, width), lambda j: (0, j, 0, 0)),
        ),
        compiler_params=pltpu.CompilerParams(vmem_limit_bytes=VMEM_BYTES),
    )(grad, matrix.reshape(3, groups, part, width), rows)
    return out, weight.reshape(3 * groups * part, width)


FEED_BLOCK = 768


def feed_forward_kernel(rows_ref, up_ref, down_ref, b_up_ref, b_down_ref, before_ref, act_ref, out_ref):
    before = dot_nt(rows_ref[...], up_ref[...]) + b_up_ref[0]
    before_ref[...] = before
    act = low(gelu_tanh(before))
    act_ref[...] = act
    term = dot_nn(act, down_ref[...])

    @pl.when(pl.program_id(0) == 0)
    def _():
        out_ref[...] = term + b_down_ref[...]

    @pl.when(pl.program_id(0) > 0)
    def _():
        out_ref[...] += term


def feed_specs(count, width, up_start, down_start):
    return (
        pl.BlockSpec((count, width), lambda j: (0, 0)),
        pl.BlockSpec((FEED_BLOCK, width), lambda j: (up_start + j, 0)),
        pl.BlockSpec((FEED_BLOCK, width), lambda j: (down_start + j, 0)),
        pl.BlockSpec((1, 1, FEED_BLOCK), lambda j: (j, 0, 0)),
        pl.BlockSpec((count, FEED_BLOCK), lambda j: (0, j)),
    )


def feed_forward(rows, up, up_start, down, down_start, b_up, b_down):
    count, width = rows.shape
    whole, up_spec, down_spec, line, column = feed_specs(count, width, up_start, down_start)
    return pl.pallas_call(
        feed_forward_kernel,
        out_shape=(
            jax.ShapeDtypeStruct((count, FF), jnp.float32),
            jax.ShapeDtypeStruct((count, FF), jnp.bfloat16),
            jax.ShapeDtypeStruct((count, width), jnp.float32),
        ),
        grid=(FF // FEED_BLOCK,),
        in_specs=[whole, up_spec, down_spec, line, pl.BlockSpec((1, width), lambda j: (0, 0))],
        out_specs=(column, column, whole),
        compiler_params=pltpu.CompilerParams(vmem_limit_bytes=VMEM_BYTES),
    )(rows, up, down, b_up.reshape(-1, 1, FEED_BLOCK), b_down)


def feed_backward_kernel(
    grad_ref, up_ref, down_ref, before_ref, act_ref, rows_ref, out_ref, w_up_ref, w_down_ref, sum_ref
):
    grad = grad_ref[...]
    before = before_ref[...]
    factor = math.sqrt(2.0 / math.pi)
    square = before * before
    bend = jnp.tanh(factor * (before + 0.044715 * (square * before)))
    slope = 0.5 * (1.0 + bend) + (0.5 * factor) * before * (1.0 - bend * bend) * (
        1.0 + (3.0 * 0.044715) * square
    )
    grad_up = dot_nt(grad, down_ref[...]) * slope
    sum_ref[0] = jnp.sum(grad_up, axis=0, keepdims=True)
    grad_up = low(grad_up)
    w_up_ref[...] = low(dot_tn(grad_up, rows_ref[...]))
    w_down_ref[...] = low(dot_tn(act_ref[...], grad))
    term = dot_nn(grad_up, up_ref[...])

    @pl.when(pl.program_id(0) == 0)
    def _():
        out_ref[...] = term

    @pl.when(pl.program_id(0) > 0)
    def _():
        out_ref[...] += term


def feed_backward(grad, up, up_start, down, down_start, before, act, rows):
    count, width = rows.shape
    whole, up_spec, down_spec, line, column = feed_specs(count, width, up_start, down_start)
    block = pl.BlockSpec((FEED_BLOCK, width), lambda j: (j, 0))
    return pl.pallas_call(
        feed_backward_kernel,
        out_shape=(
            jax.ShapeDtypeStruct((count, width), jnp.float32),
            jax.ShapeDtypeStruct((FF, width), jnp.bfloat16),
            jax.ShapeDtypeStruct((FF, width), jnp.bfloat16),
            jax.ShapeDtypeStruct((FF // FEED_BLOCK, 1, FEED_BLOCK), jnp.float32),
        ),
        grid=(FF // FEED_BLOCK,),
        in_specs=[whole, up_spec, down_spec, column, column, whole],
        out_specs=(whole, block, block, line),
        compiler_params=pltpu.CompilerParams(vmem_limit_bytes=VMEM_BYTES),
    )(grad, up, down, before, act, rows)


def caption_grad_kernel(rows_ref, grad_ref, out_ref):
    out_ref[...] = low(dot_tn(rows_ref[...], grad_ref[...]))


def caption_grad(rows, grad):
    count, depth = rows.shape
    block = 512
    return pl.pallas_call(
        caption_grad_kernel,
        out_shape=jax.ShapeDtypeStruct((depth, grad.shape[1]), jnp.bfloat16),
        grid=(depth // block,),
        in_specs=[
            pl.BlockSpec((count, block), lambda j: (0, j)),
            pl.BlockSpec(grad.shape, lambda j: (0, 0)),
        ],
        out_specs=pl.BlockSpec((block, grad.shape[1]), lambda j: (j, 0)),
        compiler_params=pltpu.CompilerParams(vmem_limit_bytes=VMEM_BYTES),
    )(rows, grad)


def adamw(param, grad, first, second, rate, decay):
    first_new = beta_one * first + (1.0 - beta_one) * grad
    second_new = beta_two * second + (1.0 - beta_two) * grad * grad
    step_dir = (
        first_new
        / (1.0 - beta_one**STEP)
        / (jnp.sqrt(second_new / (1.0 - beta_two**STEP)) + adam_eps)
    )
    return (param - rate * (step_dir + decay * param), first_new, second_new)


def per_device(
    latents,
    noise,
    captions,
    image_sizes,
    caption_lengths,
    timesteps,
    weights,
    vectors,
    weights_m,
    weights_v,
    vectors_m,
    vectors_v,
):
    width = weights.shape[1]
    seq_count = lax.axis_size("seq")
    dp_count = lax.axis_size("dp")
    seq_index = lax.axis_index("seq")
    row_index = lax.axis_index("dp")
    devices = dp_count * seq_count
    layout = matrix_rows(width)
    shard_rows = weights.shape[0]
    paired = dp_count == 4 and seq_count == 8
    weights_low = weights.astype(jnp.bfloat16)
    if paired:
        shard = weights_low.reshape(shard_rows // UNIT, UNIT, width)
        rows_all, rows_late = gather_rows((0, 2176), (23, 19), 8, devices, 7, shard)
        flat = (-1, width)
        self_head = 384
        (
            time_one,
            time_two,
            time_block,
            text_one,
            text_two,
            joint_qkv,
            self_out_head,
        ) = split_rows(rows_all.reshape(flat), layout[:6] + (self_head,))
    else:
        gathered = lax.all_gather(weights_low, both_axes, axis=0, tiled=True)
        (
            time_one,
            time_two,
            time_block,
            text_one,
            text_two,
            joint_qkv,
            self_out,
            cross_query,
            cross_kv,
            cross_out,
            mlp_up,
            mlp_down,
        ) = split_rows(gathered, layout)
    (
        table,
        final_table,
        patch_in,
        patch_out,
        b_patch,
        b_time_one,
        b_time_two,
        b_block,
        b_text_one,
        b_text_two,
        b_query,
        b_value,
        b_self_out,
        b_cross_query,
        b_cross_value,
        b_cross_out,
        b_up,
        b_down,
    ) = split_rows(vectors.astype(jnp.bfloat16).astype(jnp.float32), vector_rows(width))
    head_dim = width // HEADS
    heads = HEADS // seq_count
    part = heads * head_dim
    images = image_sizes.shape[2]
    slots = latents.shape[2]
    assert slots == BLOCK and images == seq_count
    rows = MICRO * slots
    wide = (MICRO, slots, width)
    image_count = jnp.sum((image_sizes > 0).astype(jnp.float32))
    loss_scale = 1.0 / image_count

    ends_all = jnp.cumsum(image_sizes, axis=2)
    firsts = jnp.arange(seq_count, dtype=jnp.int32) * BLOCK
    segment_all = jnp.sum(
        (ends_all[:, :, None, :] <= firsts[None, None, :, None]).astype(jnp.int32), axis=3
    )
    onehot_all = (
        segment_all[:, :, :, None] == jnp.arange(images, dtype=jnp.int32)[None, None, None, :]
    )
    size_all = jnp.sum(jnp.where(onehot_all, image_sizes[:, :, None, :], 0), axis=3)
    start_all = jnp.sum(jnp.where(onehot_all, (ends_all - image_sizes)[:, :, None, :], 0), axis=3)
    step_all = jnp.sum(jnp.where(onehot_all, timesteps[:, :, None, :], 0), axis=3)
    length_all = jnp.sum(jnp.where(onehot_all, caption_lengths[:, :, None, :], 0), axis=3)
    row_start = start_all[:, row_index]
    row_size = size_all[:, row_index]
    kv_start = row_start // BLOCK
    kv_big = (row_size == LARGE).astype(jnp.int32)
    own_segment = segment_all[:, row_index, seq_index]
    own_size = row_size[:, seq_index]
    own_start = row_start[:, seq_index]
    own_step = step_all[:, row_index, seq_index]
    own_length = length_all[:, row_index, seq_index]

    quarter = width // 4
    omega = 1.0 / 10000.0 ** (jnp.arange(quarter, dtype=jnp.float32) / quarter)
    angle = jnp.arange(2 * SIDE, dtype=jnp.float32)[:, None] * omega[None, :]
    angle_table = jnp.concatenate([jnp.sin(angle), jnp.cos(angle)], axis=1)
    within = (
        seq_index * BLOCK - own_start[:, None] + jnp.arange(slots, dtype=jnp.int32)[None, :]
    ).reshape(rows)
    side = jnp.where(own_size == LARGE, 2 * SIDE, SIDE).astype(jnp.int32)
    side = jnp.broadcast_to(side[:, None], (MICRO, slots)).reshape(rows)
    places = jnp.arange(2 * SIDE, dtype=jnp.int32)[None, :]
    pick_row = ((within // side)[:, None] == places).astype(jnp.float32)
    pick_col = ((within % side)[:, None] == places).astype(jnp.float32)
    position = jnp.concatenate(
        [
            jnp.dot(pick_row, angle_table, precision=exact),
            jnp.dot(pick_col, angle_table, precision=exact),
        ],
        axis=1,
    )

    level = noise_level(own_step)[:, None, None]
    level_prev = noise_level(own_step - 1)[:, None, None]
    beta_log, tilde_log = variance_logs(level, level_prev)
    target = noise[:, 0].astype(jnp.float32)
    noisy = jnp.sqrt(level) * latents[:, 0].astype(jnp.float32) + jnp.sqrt(1.0 - level) * target
    noisy = noisy.reshape(rows, PATCH)

    time_low = low(time_features(own_step))
    time_first = dot_nn(time_low, time_one) + b_time_one
    time_act, time_act_back = jax.vjp(jax.nn.silu, time_first)
    time_act_low = low(time_act)
    time_embed = dot_nn(time_act_low, time_two) + b_time_two
    embed_act, embed_act_back = jax.vjp(jax.nn.silu, time_embed)
    embed_low = low(embed_act)
    block_mod = dot_nt(embed_low, time_block) + b_block.reshape(1, -1) + table.reshape(1, -1)
    shift_one, scale_one, gate_one, shift_two, scale_two, gate_two = [
        piece[:, None, :] for piece in jnp.split(block_mod, 6, axis=1)
    ]
    shift_final = (final_table[0][None, :] + time_embed)[:, None, :]
    scale_final = (final_table[1][None, :] + time_embed)[:, None, :]

    hidden_zero = (jnp.dot(noisy, patch_in, precision=exact) + b_patch + position).reshape(wide)
    normed_one, mod_one_back = jax.vjp(modulate, hidden_zero, shift_one, scale_one)
    normed_one_low = low(normed_one).reshape(rows, width)
    joint_bias = jnp.concatenate([b_query, jnp.zeros_like(b_query), b_value], axis=0)
    joint_bias = jnp.transpose(joint_bias.reshape(3, seq_count, part), (1, 0, 2))
    qkv = joint_forward(normed_one_low, joint_qkv, joint_bias.reshape(seq_count, 1, 3 * part))
    caption_low = captions[:, 0].reshape(MICRO * CAP, TEXT_W)
    caption_first = dot_nn(caption_low, text_one) + b_text_one
    caption_act, caption_act_back = jax.vjp(gelu_tanh, caption_first)
    caption_act_low = low(caption_act)
    text = dot_nn(caption_act_low, text_two) + b_text_two
    lengths_slot = lax.dynamic_slice_in_dim(caption_lengths[:, row_index], seq_index, 1, 1)
    token_live = (jnp.arange(CAP, dtype=jnp.int32)[None, :] < lengths_slot).astype(jnp.float32)
    lengths_slot_float = lengths_slot.astype(jnp.float32)
    caption_pool = (
        jnp.sum(text.reshape(MICRO, CAP, width) * token_live[:, :, None], axis=1) / lengths_slot_float
    )
    text_own = low(text)
    if paired:
        qkv, text_own, rows_late = lax.optimization_barrier((qkv, text_own, rows_late))
    qkv = lax.all_to_all(qkv, "seq", split_axis=0, concat_axis=0, tiled=True)
    text_all = lax.all_gather(text_own.reshape(MICRO, CAP, width), "seq", axis=0)
    if paired:
        rows_late, words_all = spread_rows(rows_late, caption_pool.reshape(-1, 128), devices, 8)
        qkv, rows_late = lax.optimization_barrier((qkv, rows_late))
        rows_late = rows_late.reshape(flat)
        self_out_tail, cross_query, cross_kv, cross_out = split_rows(
            rows_late, (layout[6] - self_head,) + layout[7:10]
        )
        up_start = (layout[6] - self_head + sum(layout[7:10])) // FEED_BLOCK
        feed_weights = (rows_late, up_start, rows_late, up_start + FF // FEED_BLOCK)
    else:
        feed_weights = (mlp_up, 0, mlp_down, 0)
    if paired:
        self_out = jnp.concatenate([self_out_head, self_out_tail], axis=0)
    qkv = qkv.reshape(seq_count, MICRO, slots, 3 * part)
    mixed = self_forward(kv_start, kv_big, qkv, heads, head_dim)
    mixed = lax.all_to_all(
        mixed.reshape(seq_count, rows, part), "seq", split_axis=0, concat_axis=0, tiled=True
    )
    mixed_low = jnp.transpose(mixed, (1, 0, 2)).reshape(rows, width)
    attended = (dot_nn(mixed_low, self_out) + b_self_out).reshape(wide)
    hidden_one = hidden_zero + gate_one * attended

    text_low = jnp.concatenate(
        [
            lax.dynamic_slice(text_all, (own_segment[m], m, 0, 0), (1, 1, CAP, width))[0, 0]
            for m in range(MICRO)
        ],
        axis=0,
    )
    text_kv = dot_nt(text_low, cross_kv)
    pad_rows = ((0, 0), (0, CAP_PAD - CAP), (0, 0))
    key_text = jnp.pad(low(text_kv[:, :width]).reshape(MICRO, CAP, width), pad_rows)
    value_text = jnp.pad(
        low(text_kv[:, width:] + b_cross_value).reshape(MICRO, CAP, width), pad_rows
    )
    hidden_one_low = low(hidden_one).reshape(rows, width)
    query_cross = low(dot_nn(hidden_one_low, cross_query) + b_cross_query).reshape(wide)
    cross_low = cross_call(
        functools.partial(cross_forward_kernel, head_dim),
        own_length,
        (query_cross, key_text, value_text),
        jax.ShapeDtypeStruct(wide, jnp.bfloat16),
    ).reshape(rows, width)
    hidden_two = hidden_one + (dot_nn(cross_low, cross_out) + b_cross_out).reshape(wide)
    normed_two, mod_two_back = jax.vjp(modulate, hidden_two, shift_two, scale_two)
    normed_two_low = low(normed_two).reshape(rows, width)
    upward, upward_low, feed = feed_forward(normed_two_low, *feed_weights, b_up, b_down)
    feed = feed.reshape(wide)
    hidden_three = hidden_two + gate_two * feed
    final_normed, final_back = jax.vjp(modulate, hidden_three, shift_final, scale_final)
    final_flat = final_normed.reshape(rows, width)
    predicted = jnp.dot(final_flat, patch_out.T, precision=exact).reshape(MICRO, slots, 2 * PATCH)
    error = predicted[:, :, :PATCH] - target
    frac = (predicted[:, :, PATCH:] + 1.0) * 0.5
    model_log = frac * beta_log + (1.0 - frac) * tilde_log
    ratio = jnp.exp(tilde_log - model_log)
    spread = 0.5 * (model_log - tilde_log - 1.0 + ratio) / log_two
    error_weight = (1.0 / (float(PATCH) * own_size.astype(jnp.float32)))[:, None, None]
    squared_loss = jnp.sum((error * error + spread) * error_weight)

    pooled = jnp.sum(final_normed, axis=1)
    if paired:
        pooled_all = share(pooled.reshape(-1, 128), devices, 1)
    else:
        pooled_all = lax.all_gather(pooled, both_axes, axis=0)
        words_all = lax.all_gather(caption_pool, both_axes, axis=0)
    each = (devices, MICRO, width)
    pooled_all = jnp.concatenate([pooled_all.reshape(each), words_all.reshape(each)], axis=1)
    pooled_all = jnp.transpose(pooled_all, (1, 0, 2))
    size_float = jnp.maximum(image_sizes.astype(jnp.float32), 1.0)
    pick = onehot_all.astype(jnp.float32) / size_float[:, :, None, :]
    same_row = jnp.eye(dp_count, dtype=jnp.float32)
    pick = jnp.einsum("mrsi,rq->mriqs", pick, same_row, precision=exact).reshape(
        MICRO, dp_count * images, devices
    )
    valid = (image_sizes > 0).astype(jnp.float32).reshape(MICRO, dp_count * images)
    grad_pool, grad_caption, contrast_value = contrast(pooled_all, pick, valid, loss_scale)
    contrast_value = contrast_value[0, 0]
    own_pool = row_index * images + own_segment
    grad_pool_own = jnp.concatenate(
        [lax.dynamic_slice(grad_pool, (m, own_pool[m], 0), (1, 1, width))[0] for m in range(MICRO)]
    ) / own_size.astype(jnp.float32)[:, None]
    grad_caption = lax.dynamic_slice_in_dim(
        grad_caption, row_index * images + seq_index, 1, 1
    )[:, 0]

    grad_spread = 0.5 * (1.0 - ratio) / log_two * 0.5 * (beta_log - tilde_log)
    grad_predicted = (
        loss_scale * error_weight * jnp.concatenate([2.0 * error, grad_spread], axis=2)
    ).reshape(rows, 2 * PATCH)
    grad_final = grad_pool_own[:, None, :] + jnp.dot(
        grad_predicted, patch_out, precision=exact
    ).reshape(wide)
    grad_patch_out = lax.dot_general(
        grad_predicted, final_flat, (((0,), (0,)), ((), ())), precision=exact
    )
    grad_three, grad_shift_final, grad_scale_final = final_back(grad_final)
    grad_shift_final = grad_shift_final[:, 0]
    grad_scale_final = grad_scale_final[:, 0]
    grad_final_table = jnp.stack([grad_shift_final.sum(axis=0), grad_scale_final.sum(axis=0)])
    grad_embed = grad_shift_final + grad_scale_final

    grad_feed = (grad_three * gate_two).reshape(rows, width)
    grad_feed_low = low(grad_feed)
    grad_normed_two, weight_up, weight_down, grad_b_up = feed_backward(
        grad_feed_low, *feed_weights, upward, upward_low, normed_two_low
    )
    grad_two_mod, grad_shift_two, grad_scale_two = mod_two_back(grad_normed_two.reshape(wide))
    grad_gate_two = jnp.sum(grad_three * feed, axis=1, keepdims=True)
    grad_two = grad_three + grad_two_mod
    grad_two_flat = grad_two.reshape(rows, width)
    grad_two_low = low(grad_two_flat)
    weight_cross_out = dot_tn(cross_low, grad_two_low)
    grad_cross_low = low(dot_nt(grad_two_low, cross_out)).reshape(wide)
    padded = jax.ShapeDtypeStruct((MICRO, CAP_PAD, width), jnp.float32)
    grad_query_cross, grad_key_text, grad_value_text = cross_call(
        functools.partial(cross_backward_kernel, head_dim),
        own_length,
        (query_cross, key_text, value_text, grad_cross_low),
        (jax.ShapeDtypeStruct(wide, jnp.float32), padded, padded),
    )
    grad_query_cross = grad_query_cross.reshape(rows, width)
    grad_query_low = low(grad_query_cross)
    weight_cross_query = dot_tn(hidden_one_low, grad_query_low)
    grad_one = grad_two + dot_nt(grad_query_low, cross_query).reshape(wide)

    grad_kv = jnp.concatenate([grad_key_text[:, :CAP], grad_value_text[:, :CAP]], axis=2).reshape(
        MICRO * CAP, 2 * width
    )
    grad_kv_low = low(grad_kv)
    weight_cross_kv = dot_tn(grad_kv_low, text_low)
    grad_text_part = low(dot_nn(grad_kv_low, cross_kv)).reshape(MICRO, CAP, width)
    grad_text_all = lax.all_gather(grad_text_part, "seq", axis=0).astype(jnp.float32)
    mine = (segment_all[:, row_index] == seq_index).astype(jnp.float32)
    grad_text = jnp.sum(grad_text_all * jnp.transpose(mine)[:, :, None, None], axis=0) + (
        (grad_caption / lengths_slot_float)[:, None, :] * token_live[:, :, None]
    )
    grad_text = grad_text.reshape(MICRO * CAP, width)
    grad_text_low = low(grad_text)
    weight_text_two = dot_tn(caption_act_low, grad_text_low)
    grad_caption_first = caption_act_back(dot_nt(grad_text_low, text_two))[0]
    grad_caption_low = low(grad_caption_first)
    head_rows = TILE_START * UNIT - sum(layout[:3]) + TILE * UNIT // 2 if paired else 0
    weight_text_one = caption_grad(caption_low, grad_caption_low)

    grad_attended = (grad_one * gate_one).reshape(rows, width)
    grad_gate_one = jnp.sum(grad_one * attended, axis=1, keepdims=True)
    grad_attended_low = low(grad_attended)
    weight_self_out = dot_tn(mixed_low, grad_attended_low)
    grad_mixed = low(dot_nt(grad_attended_low, self_out)).reshape(rows, seq_count, part)
    grad_mixed = jnp.transpose(grad_mixed, (1, 0, 2))
    if paired:
        weight_up, weight_down, grad_mixed = lax.optimization_barrier(
            (low(weight_up), low(weight_down), grad_mixed)
        )
    grad_mixed = lax.all_to_all(grad_mixed, "seq", split_axis=0, concat_axis=0, tiled=True)
    if paired:
        summed_feed = reduce_rows(
            ((19, 31),), shard_rows // UNIT, devices, 2, ((weight_up, 0, 12), (weight_down, 0, 12))
        )
        grad_mixed, summed_feed = lax.optimization_barrier((grad_mixed, summed_feed))
    grad_mixed = grad_mixed.reshape(seq_count, MICRO, slots, part)
    grad_qkv, head_sums = self_backward(kv_start, kv_big, qkv, grad_mixed, heads, head_dim)
    head_sums = jnp.sum(head_sums[:, 0], axis=0)
    column = seq_index * part
    grad_bias_query = lax.dynamic_update_slice(
        jnp.zeros((width,), jnp.float32), head_sums[:part], (column,)
    )
    grad_bias_value = lax.dynamic_update_slice(
        jnp.zeros((width,), jnp.float32), head_sums[part:], (column,)
    )
    grad_qkv = grad_qkv.reshape(seq_count, rows, 3 * part)
    if paired:
        time_rows = layout[0] + layout[1]
        block_rows = layout[2]
        weight_self_out = low(weight_self_out)
        first_half = jnp.pad(weight_text_one[:head_rows], ((TILE * UNIT // 2 - head_rows, 0), (0, 0)))
        (
            first_half,
            weight_text_one,
            weight_text_two,
            weight_self_out,
            weight_cross_query,
            weight_cross_kv,
            weight_cross_out,
            grad_qkv,
        ) = lax.optimization_barrier(
            (
                first_half,
                low(weight_text_one),
                low(weight_text_two),
                weight_self_out,
                low(weight_cross_query),
                low(weight_cross_kv),
                low(weight_cross_out),
                grad_qkv,
            )
        )
    grad_qkv = lax.all_to_all(
        grad_qkv, "seq", split_axis=0, concat_axis=0, tiled=True
    )
    if paired:
        summed_middle = reduce_rows(
            ((0, 7), (12, 19)),
            shard_rows // UNIT,
            devices,
            3,
            (
                (first_half, 0, 1),
                (weight_text_one, head_rows // UNIT, 10),
                (weight_text_two, 0, 3),
                (weight_self_out, TILE // 2, 2),
                (weight_cross_query, 0, 3),
                (weight_cross_kv, 0, 6),
                (weight_cross_out, 0, 3),
            ),
        )
        grad_qkv, summed_middle = lax.optimization_barrier((grad_qkv, summed_middle))
    grad_normed_one, weight_joint = joint_backward(grad_qkv, joint_qkv, normed_one_low)
    grad_zero_mod, grad_shift_one, grad_scale_one = mod_one_back(grad_normed_one.reshape(wide))
    grad_zero = (grad_one + grad_zero_mod).reshape(rows, width)
    grad_patch_in = lax.dot_general(noisy, grad_zero, (((0,), (0,)), ((), ())), precision=exact)

    grad_mod = jnp.concatenate(
        [grad_shift_one, grad_scale_one, grad_gate_one, grad_shift_two, grad_scale_two, grad_gate_two],
        axis=1,
    )
    grad_table = jnp.sum(grad_mod, axis=0)
    grad_mod_low = low(grad_mod.reshape(MICRO, 6 * width))
    weight_block = dot_tn(grad_mod_low, embed_low)
    grad_embed = grad_embed + embed_act_back(dot_nn(grad_mod_low, time_block))[0]
    grad_embed_low = low(grad_embed)
    weight_time_two = dot_tn(time_act_low, grad_embed_low)
    grad_time_first = time_act_back(dot_nt(grad_embed_low, time_two))[0]
    weight_time_one = dot_tn(time_low, low(grad_time_first))

    grad_vector = jnp.concatenate(
        [
            grad_table,
            grad_final_table,
            grad_patch_in,
            grad_patch_out,
            jnp.sum(grad_zero, axis=0)[None, :],
            jnp.sum(grad_time_first, axis=0)[None, :],
            jnp.sum(grad_embed, axis=0)[None, :],
            grad_table,
            jnp.sum(grad_caption_first, axis=0)[None, :],
            jnp.sum(grad_text, axis=0)[None, :],
            grad_bias_query[None, :],
            grad_bias_value[None, :],
            jnp.sum(grad_attended, axis=0)[None, :],
            jnp.sum(grad_query_cross, axis=0)[None, :],
            jnp.sum(grad_kv[:, width:], axis=0)[None, :],
            jnp.sum(grad_two_flat, axis=0)[None, :],
            grad_b_up.reshape(-1, width),
            jnp.sum(grad_feed, axis=0)[None, :],
            jnp.full((2, width), squared_loss),
        ],
        axis=0,
    )
    if paired:
        tile_size = UNIT * 128
        tile_count = -(-grad_vector.size // (tile_size * devices))
        parts = jnp.pad(
            grad_vector.reshape(-1), (0, tile_count * tile_size * devices - grad_vector.size)
        ).reshape(devices, tile_count, UNIT, 128)
        holders = -(-(time_rows + block_rows) // shard_rows)
        own_grads = jnp.concatenate(
            [grad_mod_low, grad_embed_low, low(grad_time_first), embed_low, time_act_low, time_low],
            axis=1,
        )
        summed_joint, grads_all, vector_got = reduce_rows(
            ((7, 12),),
            shard_rows // UNIT,
            devices,
            4,
            ((low(weight_joint), 0, 9), (weight_self_out, 0, 1)),
            (own_grads.reshape(-1, 128), parts),
            holders,
        )
        vector_part = jnp.sum(vector_got, axis=0)
        grads_all = jnp.where(device_index() < holders, grads_all, 0)
        grads_all = grads_all.reshape(devices * MICRO, -1)
        ends = [6 * width, 7 * width, 8 * width, 9 * width, 10 * width]
        grad_block_all, grad_two_all, grad_one_all, embed_all, act_all, features_all = jnp.split(
            grads_all, ends, axis=1
        )
        first_row = device_index() * shard_rows

        def own_columns(array, start):
            stop = start + array.shape[1]
            spread = jnp.pad(array, ((0, 0), (start, shard_rows + (-stop) % shard_rows)))
            place = jnp.minimum(first_row, spread.shape[1] - shard_rows)
            return lax.dynamic_slice(spread, (0, place), (array.shape[0], shard_rows))

        summed_time = (
            dot_tn(own_columns(features_all, 0), grad_one_all)
            + dot_tn(own_columns(act_all, layout[0]), grad_two_all)
            + dot_tn(own_columns(grad_block_all, time_rows), embed_all)
        )
        row = first_row + jnp.arange(shard_rows, dtype=jnp.int32)
        tile = ((row - TILE_START * UNIT) // (TILE * UNIT))[:, None]
        flat = (shard_rows, width)
        reduced = jnp.where(
            tile >= 19,
            summed_feed.reshape(flat),
            jnp.where(
                (tile >= 7) & (tile < 12), summed_joint.reshape(flat), summed_middle.reshape(flat)
            ),
        ).astype(jnp.float32)
        summed = jnp.where(row[:, None] < time_rows + block_rows, summed_time, reduced)
    else:
        grad_weights = jnp.concatenate(
            [
                low(piece)
                for piece in (
                    weight_time_one,
                    weight_time_two,
                    weight_block,
                    weight_text_one,
                    weight_text_two,
                    weight_joint,
                    weight_self_out,
                    weight_cross_query,
                    weight_cross_kv,
                    weight_cross_out,
                    weight_up,
                    weight_down,
                )
            ],
            axis=0,
        )
        summed = lax.psum_scatter(
            grad_weights, both_axes, scatter_dimension=0, tiled=True
        ).astype(jnp.float32)
    squares = jnp.sum(summed * summed)
    if paired:
        last = jnp.concatenate([vector_part, jnp.full((1, UNIT, 128), squares)], axis=0)
        last = share(last, devices, 6)
        squares_all = jnp.sum(last[:, -1, 0, 0])
        grad_vectors = last[:, :-1].reshape(-1)[: grad_vector.size].reshape(grad_vector.shape)
    else:
        grad_vectors, squares_all = lax.psum((grad_vector, squares), both_axes)
    loss_sum = grad_vectors[vectors.shape[0], 0] + contrast_value
    grad_vectors = grad_vectors[: vectors.shape[0]]
    down_bias_grad = grad_vectors[grad_vectors.shape[0] - 1]
    grad_norm = jnp.sqrt(squares_all + jnp.sum(grad_vectors * grad_vectors))
    factor = jnp.minimum(1.0, clip_norm / (grad_norm + 1e-06))
    new_w, first_w, second_w = adamw(
        weights, summed * factor, weights_m, weights_v, rate_matrix, weight_decay
    )
    new_v, first_v, second_v = adamw(
        vectors, grad_vectors * factor, vectors_m, vectors_v, rate_vector, 0.0
    )
    return (
        new_w,
        first_w,
        second_w,
        new_v,
        first_v,
        second_v,
        loss_sum,
        image_count,
        grad_norm,
        down_bias_grad,
    )


def solution(mesh):
    shard = P(both_axes, None)
    data = P(None, "dp", "seq", None)
    return jax.shard_map(
        per_device,
        mesh=mesh,
        in_specs=(data, data, data, P(), P(), P(), shard, P(), shard, shard, P(), P()),
        out_specs=(shard, shard, shard, P(), P(), P(), P(), P(), P(), P()),
        check_vma=False,
    )
```

```python
import functools
import math

import jax
import jax.numpy as jnp
from jax import lax
from jax.experimental import pallas as pl
from jax.experimental.pallas import tpu as pltpu
from jax.sharding import PartitionSpec as P

HEADS = 16
FF = 4608
TEXT_W = 4096
FREQ = 256
CAP = 120
CAP_PAD = 128
SIDE = 16
PATCH = 16
MICRO = 2
STEP = 10
BLOCK = 256
LARGE = 1024
VMEM_BYTES = 56 * 1024 * 1024

exact = lax.Precision.HIGHEST
clip_norm = 0.002
contrastive_sharpness_divisor = 0.1
beta_one = 0.9
beta_two = 0.999
adam_eps = 1e-08
weight_decay = 0.01
rate_matrix = 0.05
rate_vector = 0.3
norm_eps = 1e-06
neg_large = -1e30
log_two = math.log(2.0)
both_axes = ("dp", "seq")


def matrix_rows(width):
    return (FREQ, width, 6 * width, TEXT_W, width, 3 * width, width, width, 2 * width, width, FF, FF)


def vector_rows(width):
    return (6, 2, PATCH, 2 * PATCH, 1, 1, 1, 6, 1, 1, 1, 1, 1, 1, 1, 1, FF // width, 1)


def split_rows(whole, rows):
    pieces = []
    offset = 0
    for number in rows:
        pieces.append(whole[offset : offset + number])
        offset = offset + number
    return pieces


def device_index():
    return lax.axis_index("dp") * lax.axis_size("seq") + lax.axis_index("seq")


def modulate(hidden, shift, scale):
    centre = hidden - jnp.mean(hidden, axis=-1, keepdims=True)
    normed = centre * lax.rsqrt(jnp.mean(centre * centre, axis=-1, keepdims=True) + norm_eps)
    return normed * (1.0 + scale) + shift


def gelu_tanh(values):
    return jax.nn.gelu(values, approximate=True)


def time_features(steps_now):
    half_size = FREQ // 2
    frequency = jnp.exp(-math.log(10000.0) * jnp.arange(half_size, dtype=jnp.float32) / half_size)
    angles = steps_now.astype(jnp.float32)[:, None] * frequency[None, :]
    return jnp.concatenate([jnp.cos(angles), jnp.sin(angles)], axis=1)


def noise_level(steps_now):
    phase = (steps_now.astype(jnp.float32) / 1000.0 + 0.008) / 1.008 * (math.pi / 2.0)
    return jnp.cos(phase) ** 2


def variance_logs(level, level_prev):
    beta_now = jnp.minimum(1.0 - level / level_prev, 0.999)
    tilde_log = jnp.log(beta_now * (1.0 - level_prev) / (1.0 - level))
    return (jnp.log(beta_now), tilde_log)


def dot_nn(left, right):
    return lax.dot_general(left, right, (((1,), (0,)), ((), ())), preferred_element_type=jnp.float32)


def dot_nt(left, right):
    return lax.dot_general(left, right, (((1,), (1,)), ((), ())), preferred_element_type=jnp.float32)


def dot_tn(left, right):
    return lax.dot_general(left, right, (((0,), (0,)), ((), ())), preferred_element_type=jnp.float32)


def low(values):
    return values.astype(jnp.bfloat16)


def self_forward_kernel(heads, dim, start_ref, big_ref, qkv_ref, out_ref, key_s, value_s):
    micro = pl.program_id(0)
    blocks = qkv_ref.shape[0]
    scale = dim ** (-0.5)
    for b in range(blocks):
        for h in range(heads):
            rows = pl.ds(b * BLOCK, BLOCK)
            key_s[h, rows, :] = qkv_ref[b, 0, :, (heads + h) * dim : (heads + h + 1) * dim]
            value_s[h, rows, :] = qkv_ref[b, 0, :, (2 * heads + h) * dim : (2 * heads + h + 1) * dim]

    def one_block(b, carry):
        start = pl.multiple_of(start_ref[micro, b] * BLOCK, BLOCK)
        queries = qkv_ref[b, 0]

        def go(span):
            outs = []
            for h in range(heads):
                key = key_s[h, pl.ds(start, span), :]
                value = value_s[h, pl.ds(start, span), :]
                scores = dot_nt(queries[:, h * dim : (h + 1) * dim], key) * scale
                top = jnp.max(scores, axis=-1, keepdims=True)
                weight = jnp.exp(scores - top)
                total = jnp.sum(weight, axis=-1, keepdims=True)
                probs = low(weight * (1.0 / total))
                outs.append(low(dot_nn(probs, value)))
            out_ref[b, 0] = jnp.concatenate(outs, axis=-1)

        big = big_ref[micro, b]

        @pl.when(big == 1)
        def _():
            go(LARGE)

        @pl.when(big == 0)
        def _():
            go(BLOCK)

        return carry

    lax.fori_loop(0, blocks, one_block, 0)


def self_forward(start, big, qkv, heads, dim):
    blocks, micros = qkv.shape[0], qkv.shape[1]
    span = blocks * BLOCK
    return pl.pallas_call(
        functools.partial(self_forward_kernel, heads, dim),
        out_shape=jax.ShapeDtypeStruct((blocks, micros, BLOCK, heads * dim), jnp.bfloat16),
        grid_spec=pltpu.PrefetchScalarGridSpec(
            num_scalar_prefetch=2,
            grid=(micros,),
            in_specs=[pl.BlockSpec((blocks, 1, BLOCK, 3 * heads * dim), lambda m, s, g: (0, m, 0, 0))],
            out_specs=pl.BlockSpec((blocks, 1, BLOCK, heads * dim), lambda m, s, g: (0, m, 0, 0)),
            scratch_shapes=[
                pltpu.VMEM((heads, span, dim), jnp.bfloat16),
                pltpu.VMEM((heads, span, dim), jnp.bfloat16),
            ],
        ),
        compiler_params=pltpu.CompilerParams(vmem_limit_bytes=VMEM_BYTES),
    )(start, big, qkv)


def self_backward_kernel(
    heads, dim, start_ref, big_ref, qkv_ref, grad_ref, out_ref, sum_ref, key_s, value_s, dq_s, dk_s, dv_s
):
    micro = pl.program_id(0)
    blocks = qkv_ref.shape[0]
    scale = dim ** (-0.5)
    for b in range(blocks):
        for h in range(heads):
            rows = pl.ds(b * BLOCK, BLOCK)
            key_s[h, rows, :] = qkv_ref[b, 0, :, (heads + h) * dim : (heads + h + 1) * dim]
            value_s[h, rows, :] = qkv_ref[b, 0, :, (2 * heads + h) * dim : (2 * heads + h + 1) * dim]
    dk_s[...] = jnp.zeros_like(dk_s)
    dv_s[...] = jnp.zeros_like(dv_s)

    def one_block(b, carry):
        start = pl.multiple_of(start_ref[micro, b] * BLOCK, BLOCK)
        place = pl.multiple_of(b * BLOCK, BLOCK)
        queries = qkv_ref[b, 0]
        grads = grad_ref[b, 0]

        def go(span):
            keep = pl.ds(start, span)
            for h in range(heads):
                query = queries[:, h * dim : (h + 1) * dim]
                grad = grads[:, h * dim : (h + 1) * dim]
                key = key_s[h, keep, :]
                value = value_s[h, keep, :]
                scores = dot_nt(key, query) * scale
                top = jnp.max(scores, axis=0, keepdims=True)
                weight = jnp.exp(scores - top)
                probs = weight * (1.0 / jnp.sum(weight, axis=0, keepdims=True))
                dv_s[h, keep, :] += dot_nn(low(probs), grad)
                grad_probs = dot_nt(value, grad)
                inner = jnp.sum(probs * grad_probs, axis=0, keepdims=True)
                grad_scores = low(probs * (grad_probs - inner) * scale)
                dk_s[h, keep, :] += dot_nn(grad_scores, query)
                dq_s[h, pl.ds(place, BLOCK), :] = dot_tn(grad_scores, key)

        big = big_ref[micro, b]

        @pl.when(big == 1)
        def _():
            go(LARGE)

        @pl.when(big == 0)
        def _():
            go(BLOCK)

        return carry

    lax.fori_loop(0, blocks, one_block, 0)
    for b in range(blocks):
        rows = pl.ds(b * BLOCK, BLOCK)
        out_ref[b, 0] = jnp.concatenate(
            [low(part[h, rows, :]) for part in (dq_s, dk_s, dv_s) for h in range(heads)], axis=-1
        )
    sum_ref[0] = jnp.concatenate(
        [jnp.sum(part[h], axis=0, keepdims=True) for part in (dq_s, dv_s) for h in range(heads)], axis=-1
    )


def self_backward(start, big, qkv, grad, heads, dim):
    blocks, micros = qkv.shape[0], qkv.shape[1]
    span = blocks * BLOCK
    wide = pltpu.VMEM((heads, span, dim), jnp.float32)
    narrow = pltpu.VMEM((heads, span, dim), jnp.bfloat16)
    return pl.pallas_call(
        functools.partial(self_backward_kernel, heads, dim),
        out_shape=(
            jax.ShapeDtypeStruct((blocks, micros, BLOCK, 3 * heads * dim), jnp.bfloat16),
            jax.ShapeDtypeStruct((micros, 1, 2 * heads * dim), jnp.float32),
        ),
        grid_spec=pltpu.PrefetchScalarGridSpec(
            num_scalar_prefetch=2,
            grid=(micros,),
            in_specs=[
                pl.BlockSpec((blocks, 1, BLOCK, 3 * heads * dim), lambda m, s, g: (0, m, 0, 0)),
                pl.BlockSpec((blocks, 1, BLOCK, heads * dim), lambda m, s, g: (0, m, 0, 0)),
            ],
            out_specs=(
                pl.BlockSpec((blocks, 1, BLOCK, 3 * heads * dim), lambda m, s, g: (0, m, 0, 0)),
                pl.BlockSpec((1, 1, 2 * heads * dim), lambda m, s, g: (m, 0, 0)),
            ),
            scratch_shapes=[narrow, narrow, wide, wide, wide],
        ),
        compiler_params=pltpu.CompilerParams(vmem_limit_bytes=VMEM_BYTES),
    )(start, big, qkv, grad)


def cross_forward_kernel(dim, length_ref, query_ref, key_ref, value_ref, out_ref):
    length = length_ref[pl.program_id(0)]
    scale = dim ** (-0.5)
    live = lax.broadcasted_iota(jnp.int32, (BLOCK, CAP_PAD), 1) < length
    outs = []
    for h in range(HEADS):
        part = slice(h * dim, (h + 1) * dim)
        scores = jnp.where(live, dot_nt(query_ref[0, :, part], key_ref[0, :, part]) * scale, neg_large)
        weight = jnp.exp(scores - jnp.max(scores, axis=-1, keepdims=True))
        probs = low(weight * (1.0 / jnp.sum(weight, axis=-1, keepdims=True)))
        outs.append(low(dot_nn(probs, value_ref[0, :, part])))
    out_ref[0] = jnp.concatenate(outs, axis=-1)


def cross_backward_kernel(
    dim, length_ref, query_ref, key_ref, value_ref, grad_ref, dq_ref, dk_ref, dv_ref
):
    length = length_ref[pl.program_id(0)]
    scale = dim ** (-0.5)
    live = lax.broadcasted_iota(jnp.int32, (CAP_PAD, BLOCK), 0) < length
    dq, dk, dv = [], [], []
    for h in range(HEADS):
        part = slice(h * dim, (h + 1) * dim)
        query, key, value, grad = (
            query_ref[0, :, part],
            key_ref[0, :, part],
            value_ref[0, :, part],
            grad_ref[0, :, part],
        )
        scores = jnp.where(live, dot_nt(key, query) * scale, neg_large)
        weight = jnp.exp(scores - jnp.max(scores, axis=0, keepdims=True))
        probs = weight * (1.0 / jnp.sum(weight, axis=0, keepdims=True))
        dv.append(dot_nn(low(probs), grad))
        grad_probs = dot_nt(value, grad)
        inner = jnp.sum(probs * grad_probs, axis=0, keepdims=True)
        grad_scores = low(probs * (grad_probs - inner) * scale)
        dk.append(dot_nn(grad_scores, query))
        dq.append(dot_tn(grad_scores, key))
    dq_ref[0] = jnp.concatenate(dq, axis=-1)
    dk_ref[0] = jnp.concatenate(dk, axis=-1)
    dv_ref[0] = jnp.concatenate(dv, axis=-1)


def cross_call(kernel, length, arrays, outs):
    def spec(array):
        return pl.BlockSpec((1,) + array.shape[1:], lambda m, s: (m, 0, 0))

    return pl.pallas_call(
        kernel,
        out_shape=outs,
        grid_spec=pltpu.PrefetchScalarGridSpec(
            num_scalar_prefetch=1,
            grid=(MICRO,),
            in_specs=[spec(array) for array in arrays],
            out_specs=jax.tree.map(spec, outs),
        ),
        compiler_params=pltpu.CompilerParams(vmem_limit_bytes=VMEM_BYTES),
    )(length, *arrays)


UNIT = 8
SPLIT = 640
PIECE = 3
TILE = 96
TILE_START = 1024
LAG = 2
RING = LAG + 1
HOP_LAG = 2
HOPS = 3 * HOP_LAG + 1
MESH = pl.DeviceIdType.MESH


def my_place():
    row, seq = lax.axis_index("dp"), lax.axis_index("seq")
    return lax.div(row, 2), lax.rem(row, 2), lax.div(seq, 2), lax.rem(seq, 2)


def peer(y, core, z, x):
    return (y * 2 + core, z * 2 + x)


def greet_all(devices, seq_count):
    me = lax.axis_index("dp") * seq_count + lax.axis_index("seq")
    barrier = pltpu.get_barrier_semaphore()

    def one(step, carry):
        other = lax.rem(me + step, devices)
        pl.semaphore_signal(
            barrier,
            inc=1,
            device_id=(lax.div(other, seq_count), lax.rem(other, seq_count)),
            device_id_type=MESH,
        )
        return carry

    lax.fori_loop(1, devices, one, 0)
    pl.semaphore_wait(barrier, devices - 1)


def global_tile(ranges, index):
    tile = index + ranges[0][0]
    at = ranges[0][1] - ranges[0][0]
    for start, stop in ranges[1:]:
        tile = jnp.where(index >= at, index - at + start, tile)
        at += stop - start
    return tile


def reduce_kernel(
    ranges,
    shard_units,
    devices,
    sources,
    receivers,
    *refs,
):
    rows_refs, refs = refs[: len(sources)], list(refs[len(sources) :])
    if receivers:
        block_ref, parts_ref = refs.pop(0), refs.pop(0)
        all_ref, got_ref = refs.pop(1), refs.pop(1)
        refs, push, push_parts = refs[:-6], refs[-6:-3], refs[-3:]
    (
    out_ref,
    own_s,
    core_s,
    first_s,
    second_s,
    first_y_s,
    second_x_s,
    first_two_s,
    second_two_s,
    first_x_s,
    second_y_s,
    third_s,
    along_s,
    leaf_s,
    load_sem,
    core_send,
    core_recv,
    one_send,
    one_recv,
    two_send,
    two_recv,
    z_send,
    z_recv,
    leaf_send,
    leaf_recv,
    ) = refs
    tiles = core_s.shape[0]
    seq_count = devices // 4
    y, core, z, x = my_place()
    me = (y * 2 + core) * seq_count + z * 2 + x
    stride = 5 if tiles % 5 else 3
    half, quarter, eighth = TILE // 2, TILE // 4, TILE // 8
    across_core = peer(y, 1 - core, z, x)
    across_y = peer(1 - y, core, z, x)
    across_x = peer(y, core, z, 1 - x)

    def remote(source, target, send, recv, device):
        return pltpu.make_async_remote_copy(
            src_ref=source,
            dst_ref=target,
            send_sem=send,
            recv_sem=recv,
            device_id=device,
            device_id_type=MESH,
        )

    def core_copy(t, rows_ref=None, start=0):
        source = own_s.at[0] if rows_ref is None else rows_ref.at[pl.ds(start, half)]
        return remote(source, core_s.at[t], core_send.at[t], core_recv.at[t], across_core)

    def load(t, rows_ref=None, start=0):
        slot = lax.rem(t, 2)
        source = rows_refs[-1] if rows_ref is None else rows_ref
        return pltpu.make_async_copy(
            source.at[pl.ds(start, half)], own_s.at[slot], load_sem.at[slot]
        )

    def start_from(copy, t, side):
        index = lax.rem(t * stride, tiles) * 2 + side
        at = 0
        for rows_ref, (start, count) in zip(rows_refs, sources):

            @pl.when((index >= at) & (index < at + count))
            def _(rows_ref=rows_ref, start=start, at=at):
                copy(t, rows_ref, start + (index - at) * half).start()

            at += count

    def first_one(t):
        return remote(
            first_s.at[lax.rem(t, RING), pl.ds((1 - y) * quarter, quarter)],
            first_y_s.at[t],
            one_send.at[lax.rem(t, RING), 0],
            one_recv.at[t, 0],
            across_y,
        )

    def second_one(t, side):
        return remote(
            second_s.at[lax.rem(t, RING), pl.ds(side * quarter + (1 - x) * eighth, eighth)],
            second_x_s.at[t, pl.ds(side * eighth, eighth)],
            one_send.at[lax.rem(t, RING), 1 + side],
            one_recv.at[t, 1 + side],
            across_x,
        )

    def first_two(t):
        return remote(
            first_two_s.at[lax.rem(t, RING), pl.ds((1 - x) * eighth, eighth)],
            first_x_s.at[t],
            two_send.at[lax.rem(t, RING), 0],
            two_recv.at[t, 0],
            across_x,
        )

    def second_two(t):
        return remote(
            second_two_s.at[lax.rem(t, RING), pl.ds((1 - y) * eighth, eighth)],
            second_y_s.at[t],
            two_send.at[lax.rem(t, RING), 1],
            two_recv.at[t, 1],
            across_y,
        )

    def each_three(t, visit):
        tile = global_tile(ranges, lax.rem(t * stride, tiles))

        def one(index, carry):
            row = index * PIECE
            unit = TILE_START + tile * TILE + ((core * 2 + y) * 2 + x) * eighth + row
            owner = lax.div(unit, shard_units)
            at = unit - owner * shard_units

            @pl.when(at + PIECE <= shard_units)
            def _():
                visit(row, index, PIECE, owner, at)

            @pl.when(at + PIECE > shard_units)
            def _():
                for part in range(PIECE):
                    over = at + part >= shard_units
                    visit(
                        row + part,
                        4 + part,
                        1,
                        jnp.where(over, owner + 1, owner),
                        jnp.where(over, at + part - shard_units, at + part),
                    )

            return carry

        lax.fori_loop(0, eighth // PIECE, one, 0)

    def z_copy(t, row, slot, count, way):
        other = (jnp.maximum(z - 1, 0), jnp.minimum(z + 1, 3))[way]
        return remote(
            third_s.at[lax.rem(t, HOPS), pl.ds(row, count)],
            along_s.at[t, way, pl.ds(row, count)],
            z_send.at[lax.rem(t, HOPS), slot],
            z_recv.at[t, way, slot],
            peer(y, core, other, x),
        )

    def arrived(t, row, slot, count, way):
        part = along_s.at[t, way, pl.ds(row, count)]
        pltpu.make_async_copy(part, part, z_recv.at[t, way, slot]).wait()

    def total_of(t, row, count, *ways):
        total = third_s[lax.rem(t, HOPS), pl.ds(row, count)].astype(jnp.float32)
        for way in ways:
            total = total + along_s[t, way, pl.ds(row, count)].astype(jnp.float32)
        return total.astype(jnp.bfloat16)

    def owner_plane(owner):
        return lax.rem(lax.div(owner, 2), 4)

    def hop(t, number):
        def visit(row, slot, count, owner, at):
            to = owner_plane(owner)
            for way, here, more in (
                (0, (z > to) & (3 - z == number), z < 3),
                (1, (z < to) & (z == number), z > 0),
            ):

                @pl.when(here)
                def _(way=way, more=more):
                    @pl.when(more)
                    def _():
                        arrived(t, row, slot, count, way)
                        total = total_of(t, row, count, way)
                        third_s[lax.rem(t, HOPS), pl.ds(row, count)] = total

                    z_copy(t, row, slot, count, way).start()

        each_three(t, visit)

    def hand_over(t):
        def visit(row, slot, count, owner, at):
            to = owner_plane(owner)

            @pl.when(to == z)
            def _():
                for here, ways in (
                    (z == 0, (0,)),
                    ((z > 0) & (z < 3), (0, 1)),
                    (z == 3, (1,)),
                ):

                    @pl.when(here)
                    def _(ways=ways):
                        for way in ways:
                            arrived(t, row, slot, count, way)
                        leaf_s[t, pl.ds(row, count)] = total_of(t, row, count, *ways)

                leaf_copy(t, row, slot, count, owner, at, 0)

            @pl.when(to != z)
            def _():
                z_copy(t, row, slot, count, 0).wait_send()

        each_three(t, visit)

    def leaf_copy(t, row, slot, count, owner, at, stage):
        source = leaf_s.at[t, pl.ds(row, count)]
        target = out_ref.at[pl.ds(at, count)]
        sending = remote(
            source,
            target,
            leaf_send.at[t, slot],
            leaf_recv.at[at],
            (lax.div(owner, seq_count), lax.rem(owner, seq_count)),
        )

        @pl.when(owner != me)
        def _():
            if stage == 0:
                sending.start()
            else:
                sending.wait_send()

        if stage == 0:

            @pl.when(owner == me)
            def _():
                pltpu.make_async_copy(source, target, leaf_recv.at[at]).start()

    def leaf_done(t):
        def visit(row, slot, count, owner, at):
            @pl.when(owner_plane(owner) == z)
            def _():
                leaf_copy(t, row, slot, count, owner, at, 1)

        each_three(t, visit)

    for t in range(min(2, tiles)):
        start_from(load, t, core)
    greet_all(devices, seq_count)

    def start_core(t, carry):
        start_from(core_copy, t, 1 - core)
        return carry

    lax.fori_loop(0, tiles, start_core, 0)
    if receivers:
        start_push(parts_ref, got_ref, devices, devices, me, *push_parts, scatter=True)
        start_push(block_ref, all_ref, devices, receivers, me, *push)

    def one_step(step, carry):
        @pl.when(step < tiles)
        def _():
            t = step
            slot = lax.rem(t, RING)
            load(t).wait()
            core_copy(t).wait_recv()

            def one(index, inner):
                at = pl.ds(index * 4, 4)
                total = own_s[lax.rem(t, 2), at].astype(jnp.float32) + core_s[t, at].astype(jnp.float32)
                total = total.astype(jnp.bfloat16)
                first_s[slot, at] = total[:, :, :SPLIT]
                second_s[slot, at] = total[:, :, SPLIT:]
                return inner

            lax.fori_loop(0, half // 4, one, 0)
            first_one(t).start()
            second_one(t, 0).start()
            second_one(t, 1).start()

            @pl.when(t + 2 < tiles)
            def _():
                start_from(load, t + 2, core)

        @pl.when((step >= LAG) & (step < tiles + LAG))
        def _():
            t = step - LAG
            slot = lax.rem(t, RING)
            first_one(t).wait()

            def one(index, inner):
                at = pl.ds(index * 4, 4)
                mine = first_s[slot, pl.ds(y * quarter + index * 4, 4)].astype(jnp.float32)
                total = mine + first_y_s[t, at].astype(jnp.float32)
                first_two_s[slot, at] = total.astype(jnp.bfloat16)
                return inner

            lax.fori_loop(0, quarter // 4, one, 0)
            first_two(t).start()
            for side in range(2):
                second_one(t, side).wait()

                def two(index, inner):
                    mine = second_s[slot, pl.ds(side * quarter + x * eighth + index * 4, 4)]
                    at = pl.ds(side * eighth + index * 4, 4)
                    total = mine.astype(jnp.float32) + second_x_s[t, at].astype(jnp.float32)
                    second_two_s[slot, at] = total.astype(jnp.bfloat16)
                    return inner

                lax.fori_loop(0, eighth // 4, two, 0)
            second_two(t).start()

        @pl.when((step >= 2 * LAG) & (step < tiles + 2 * LAG))
        def _():
            t = step - 2 * LAG
            slot = lax.rem(t, RING)
            first_two(t).wait()
            second_two(t).wait()

            def one(index, inner):
                at = pl.ds(index * 4, 4)
                mine = first_two_s[slot, pl.ds(x * eighth + index * 4, 4)].astype(jnp.float32)
                total = mine + first_x_s[t, at].astype(jnp.float32)
                third_s[lax.rem(t, HOPS), at, :, :SPLIT] = total.astype(jnp.bfloat16)
                mine = second_two_s[slot, pl.ds(y * eighth + index * 4, 4)].astype(jnp.float32)
                total = mine + second_y_s[t, at].astype(jnp.float32)
                third_s[lax.rem(t, HOPS), at, :, SPLIT:] = total.astype(jnp.bfloat16)
                return inner

            lax.fori_loop(0, eighth // 4, one, 0)

        for number in range(4):
            old = step - 2 * LAG - number * HOP_LAG

            @pl.when((old >= 0) & (old < tiles))
            def _(old=old, number=number):
                if number < 3:
                    hop(old, number)
                else:
                    hand_over(old)

        return carry

    lax.fori_loop(0, tiles + 2 * LAG + 3 * HOP_LAG, one_step, 0)

    def finish(t, carry):
        core_copy(t).wait_send()
        leaf_done(t)
        return carry

    lax.fori_loop(0, tiles, finish, 0)
    if receivers:
        finish_push(parts_ref, got_ref, devices, devices, me, *push_parts, scatter=True)
        finish_push(block_ref, all_ref, devices, receivers, me, *push)
    far = TILE_START - TILE * (TILE_START // TILE)
    begin = me * shard_units
    first_at = lax.rem(PIECE - lax.rem(begin + PIECE - far % PIECE, PIECE), PIECE)

    def arrive(index, count):
        unit = begin + index
        inside = False
        for start, stop in ranges:
            low_end, high_end = TILE_START + start * TILE, TILE_START + stop * TILE
            inside = inside | ((unit >= low_end) & (unit < high_end))

        @pl.when(inside)
        def _():
            part = out_ref.at[pl.ds(index, count)]
            pltpu.make_async_copy(part, part, leaf_recv.at[index]).wait()

    def arrive_three(step, carry):
        index = first_at + step * PIECE

        @pl.when(index + PIECE <= shard_units)
        def _():
            arrive(index, PIECE)

        return carry

    steps = shard_units // PIECE
    lax.fori_loop(0, steps, arrive_three, 0)
    covered = first_at + lax.div(shard_units - first_at, PIECE) * PIECE
    for step in range(PIECE - 1):

        @pl.when(step < first_at)
        def _():
            arrive(step, 1)

        @pl.when(covered + step < shard_units)
        def _():
            arrive(covered + step, 1)


def push_copy(block_ref, all_ref, devices, me, step, send_sem, recv_sem, scatter):
    seq_count = devices // 4
    other = lax.rem(me + step, devices)
    return other, pltpu.make_async_remote_copy(
        src_ref=block_ref.at[other] if scatter else block_ref,
        dst_ref=all_ref.at[me],
        send_sem=send_sem.at[step],
        recv_sem=recv_sem.at[me],
        device_id=(lax.div(other, seq_count), lax.rem(other, seq_count)),
        device_id_type=MESH,
    )


def start_push(block_ref, all_ref, devices, receivers, me, send_sem, recv_sem, keep_sem, scatter=False):
    own_ref = block_ref.at[me] if scatter else block_ref

    @pl.when(me < receivers)
    def _():
        pltpu.make_async_copy(own_ref, all_ref.at[me], keep_sem).start()

    def send(step, carry):
        other, sending = push_copy(
            block_ref, all_ref, devices, me, step, send_sem, recv_sem, scatter
        )

        @pl.when(other < receivers)
        def _():
            sending.start()

        return carry

    lax.fori_loop(1, devices, send, 0)


def finish_push(
    block_ref, all_ref, devices, receivers, me, send_sem, recv_sem, keep_sem, scatter=False
):
    own_ref = block_ref.at[me] if scatter else block_ref

    @pl.when(me < receivers)
    def _():
        pltpu.make_async_copy(own_ref, all_ref.at[me], keep_sem).wait()

    def finish(step, carry):
        other, sending = push_copy(
            block_ref, all_ref, devices, me, step, send_sem, recv_sem, scatter
        )

        @pl.when(other < receivers)
        def _():
            sending.wait_send()

        source = lax.rem(me + devices - step, devices)

        @pl.when(me < receivers)
        def _():
            pltpu.make_async_copy(own_ref, all_ref.at[source], recv_sem.at[source]).wait()

        return carry

    lax.fori_loop(1, devices, finish, 0)


def push_sems(devices):
    dma = pltpu.SemaphoreType.DMA
    return [dma((devices,)), dma((devices,)), dma]


def reduce_rows(ranges, shard_units, devices, collective_id, pieces, blocks=(), receivers=0):
    tiles = sum(stop - start for start, stop in ranges)
    width = pieces[0][0].shape[1]
    sources = tuple(piece[1:] for piece in pieces)
    assert sum(count for _, count in sources) == 2 * tiles
    half, quarter, eighth = TILE // 2, TILE // 4, TILE // 8
    rest = width - SPLIT

    def vmem(*shape):
        return pltpu.VMEM(shape, jnp.bfloat16)

    dma = pltpu.SemaphoreType.DMA
    outs = [jax.ShapeDtypeStruct((shard_units, UNIT, width), jnp.bfloat16)]
    if blocks:
        outs.append(jax.ShapeDtypeStruct((devices,) + blocks[0].shape, blocks[0].dtype))
        outs.append(jax.ShapeDtypeStruct(blocks[1].shape, blocks[1].dtype))
    out = pl.pallas_call(
        functools.partial(reduce_kernel, ranges, shard_units, devices, sources, receivers),
        out_shape=outs,
        in_specs=[pl.BlockSpec(memory_space=pl.ANY)] * (len(pieces) + len(blocks)),
        out_specs=[pl.BlockSpec(memory_space=pl.ANY)] * len(outs),
        scratch_shapes=[
            vmem(2, half, UNIT, width),
            vmem(tiles, half, UNIT, width),
            vmem(RING, half, UNIT, SPLIT),
            vmem(RING, half, UNIT, rest),
            vmem(tiles, quarter, UNIT, SPLIT),
            vmem(tiles, quarter, UNIT, rest),
            vmem(RING, quarter, UNIT, SPLIT),
            vmem(RING, quarter, UNIT, rest),
            vmem(tiles, eighth, UNIT, SPLIT),
            vmem(tiles, eighth, UNIT, rest),
            vmem(HOPS, eighth, UNIT, width),
            vmem(tiles, 2, eighth, UNIT, width),
            vmem(tiles, eighth, UNIT, width),
            dma((2,)),
            dma((tiles,)),
            dma((tiles,)),
            dma((RING, 3)),
            dma((tiles, 3)),
            dma((RING, 2)),
            dma((tiles, 2)),
            dma((HOPS, 7)),
            dma((tiles, 2, 7)),
            dma((tiles, 7)),
            dma((shard_units,)),
        ]
        + (push_sems(devices) + push_sems(devices) if blocks else []),
        compiler_params=pltpu.CompilerParams(
            collective_id=collective_id, has_side_effects=True, vmem_limit_bytes=VMEM_BYTES
        ),
    )(*[piece[0].reshape(-1, UNIT, width) for piece in pieces], *blocks)
    return out if blocks else out[0]


STRIDE = 3
Z_LAG = 2
Z_RING = 3 * Z_LAG + 1


def gather_kernel(
    openings,
    ahead,
    devices,
    shard_ref,
    out_ref,
    later_ref,
    deal_send,
    deal_recv,
    z_send,
    z_recv,
    one_send,
    one_recv,
    two_send,
    two_recv,
    core_send,
    core_recv,
):
    shard_units = shard_ref.shape[0]
    seq_count = devices // 4
    width = shard_ref.shape[2]
    tiles = out_ref.shape[0] // TILE
    later_tiles = later_ref.shape[0] // TILE
    streams = ((openings[0], tiles, out_ref, 0), (openings[1], later_tiles, later_ref, tiles))
    y, core, z, x = my_place()
    me = (y * 2 + core) * seq_count + z * 2 + x
    half, quarter, eighth = TILE // 2, TILE // 4, TILE // 8
    leaves = TILE // PIECE
    upward = peer(y, core, jnp.minimum(z + 1, 3), x)
    downward = peer(y, core, jnp.maximum(z - 1, 0), x)

    def bounds(stream):
        begin = me * shard_units - stream[0]
        finish = begin + shard_units
        return begin, finish, lax.div(begin + PIECE - 1, PIECE), lax.div(finish, PIECE)

    def deal_some(stream, stage, three, part, count):
        begin = bounds(stream)[0]
        ref = stream[2]
        tile = lax.div(three, leaves)
        leaf = three - tile * leaves
        eight = lax.div(leaf, 4)
        slot = leaf - eight * 4 if count == PIECE else 4 + part
        holder_core = lax.div(eight, 4)
        holder_y = lax.rem(lax.div(eight, 2), 2)
        holder_x = lax.rem(eight, 2)
        holder = (holder_y * 2 + holder_core) * seq_count + z * 2 + holder_x
        index = three * PIECE + part - begin
        source = shard_ref.at[pl.ds(index, count)]
        target = ref.at[pl.ds(three * PIECE + part, count)]
        recv = deal_recv.at[stream[3] + tile, slot]
        sending = pltpu.make_async_remote_copy(
            src_ref=source,
            dst_ref=target,
            send_sem=deal_send.at[0 if stream[3] == 0 else 1, index],
            recv_sem=recv,
            device_id=peer(holder_y, holder_core, z, holder_x),
            device_id_type=MESH,
        )

        @pl.when(holder != me)
        def _():
            if stage == 0:
                sending.start()
            else:
                sending.wait_send()

        if stage == 0:

            @pl.when(holder == me)
            def _():
                pltpu.make_async_copy(source, target, recv).start()

    def deal_between(stream, stage, low_three, count, base):
        begin, finish, first_three, last_three = bounds(stream)
        base = first_three if base is None else base

        @pl.when((low_three <= last_three) & (low_three + count >= first_three))
        def _():
            def one(step, carry):
                three = base + step

                @pl.when(
                    (three >= first_three)
                    & (three < last_three)
                    & (three >= low_three)
                    & (three < low_three + count)
                )
                def _():
                    deal_some(stream, stage, three, 0, PIECE)

                return carry

            lax.fori_loop(0, min(count, shard_units // PIECE + 1), one, 0)
            for step in range(PIECE - 1):
                three = first_three - 1
                here = (three >= low_three) & (three < low_three + count)

                @pl.when(here & (begin + step < first_three * PIECE))
                def _(three=three):
                    deal_some(stream, stage, three, begin + step - three * PIECE, 1)

                three = last_three
                here = (three >= low_three) & (three < low_three + count)

                @pl.when(here & (three * PIECE + step < finish))
                def _(three=three):
                    deal_some(stream, stage, three, step, 1)

    def deal_tile(stream, step):
        low_three = tile_at(step, stream[1]) * leaves
        deal_between(stream, 0, low_three, leaves, low_three)

    def each_three(stream, t, visit):
        def one(index, carry):
            row = t * TILE + ((core * 2 + y) * 2 + x) * eighth + index * PIECE
            unit = stream[0] + row
            owner = lax.div(unit, shard_units)
            at = unit - owner * shard_units

            @pl.when(at + PIECE <= shard_units)
            def _():
                visit(row, index, PIECE, lax.rem(lax.div(owner, 2), 4))

            @pl.when(at + PIECE > shard_units)
            def _():
                for part in range(PIECE):
                    holder = jnp.where(at + part >= shard_units, owner + 1, owner)
                    visit(row + part, 4 + part, 1, lax.rem(lax.div(holder, 2), 4))

            return carry

        lax.fori_loop(0, eighth // PIECE, one, 0)

    def wait_units(ref, count, sem):
        part = ref.at[pl.ds(0, count)]
        pltpu.make_async_copy(part, part, sem).wait()

    def z_copy(stream, step, row, slot, count, way):
        part = stream[2].at[pl.ds(row, count)]
        which = 0 if stream[3] == 0 else 1
        return pltpu.make_async_remote_copy(
            src_ref=part,
            dst_ref=part,
            send_sem=z_send.at[which, lax.rem(step, Z_RING), slot, way],
            recv_sem=z_recv.at[stream[3] + tile_at(step, stream[1]), slot],
            device_id=(upward, downward)[way],
            device_id_type=MESH,
        )

    def along_z(stream, step, distance):
        t = tile_at(step, stream[1])

        def visit(row, slot, count, owner_z):
            @pl.when(jnp.abs(owner_z - z) == distance)
            def _():
                sem = deal_recv if distance == 0 else z_recv
                wait_units(out_ref, count, sem.at[stream[3] + t, slot])

                @pl.when((owner_z <= z) & (z < 3))
                def _():
                    z_copy(stream, step, row, slot, count, 0).start()

                @pl.when((owner_z >= z) & (z > 0))
                def _():
                    z_copy(stream, step, row, slot, count, 1).start()

        each_three(stream, t, visit)

    def along_z_done(stream, step):
        t = tile_at(step, stream[1])

        def visit(row, slot, count, owner_z):
            @pl.when((owner_z <= z) & (z < 3))
            def _():
                z_copy(stream, step, row, slot, count, 0).wait_send()

            @pl.when((owner_z >= z) & (z > 0))
            def _():
                z_copy(stream, step, row, slot, count, 1).wait_send()

        each_three(stream, t, visit)

    def z_stage(stream, step):
        for distance in range(4):
            old = step - distance * Z_LAG

            @pl.when((old >= 0) & (old < stream[1]))
            def _(old=old, distance=distance):
                along_z(stream, old, distance)
                if distance == 3:
                    along_z_done(stream, old)

    spreading = spread_steps(
        out_ref, one_send, one_recv, two_send, two_recv, core_send, core_recv
    )
    main, late = streams
    greet_all(devices, seq_count)
    for step in range(min(ahead, tiles)):
        deal_tile(main, step)
    for step in range(min(ahead, later_tiles)):
        deal_tile(late, step)

    def one_step(step, carry):
        @pl.when(step + ahead < tiles)
        def _():
            deal_tile(main, step + ahead)

        @pl.when(step + ahead < later_tiles)
        def _():
            deal_tile(late, step + ahead)

        z_stage(main, step)
        spreading(step - 3 * Z_LAG)
        z_stage(late, step)
        return carry

    lax.fori_loop(0, tiles + 3 * LAG + 3 * Z_LAG, one_step, 0)
    for stream in streams:
        deal_between(stream, 1, 0, stream[1] * leaves, None)


def tile_at(step, tiles):
    return lax.rem(step * STRIDE, tiles)


def spread_steps(out_ref, one_send, one_recv, two_send, two_recv, core_send, core_recv):
    tiles = out_ref.shape[0] // TILE
    width = out_ref.shape[2]
    y, core, z, x = my_place()
    half, quarter, eighth = TILE // 2, TILE // 4, TILE // 8
    left, right = pl.ds(0, SPLIT), pl.ds(SPLIT, width - SPLIT)
    whole = pl.ds(0, width)
    across_core = peer(y, 1 - core, z, x)
    across_y = peer(1 - y, core, z, x)
    across_x = peer(y, core, z, 1 - x)

    def remote(start, count, columns, send, recv, device):
        part = out_ref.at[pl.ds(start, count), :, columns]
        return pltpu.make_async_remote_copy(
            src_ref=part,
            dst_ref=part,
            send_sem=send,
            recv_sem=recv,
            device_id=device,
            device_id_type=MESH,
        )

    def block(t, y_at, x_at):
        return t * TILE + ((core * 2 + y_at) * 2 + x_at) * eighth

    def one_first(step):
        t = tile_at(step, tiles)
        sems = (one_send.at[lax.rem(step, RING), 0], one_recv.at[t, 0])
        return remote(block(t, y, x), eighth, left, *sems, across_x)

    def one_second(step):
        t = tile_at(step, tiles)
        sems = (one_send.at[lax.rem(step, RING), 1], one_recv.at[t, 1])
        return remote(block(t, y, x), eighth, right, *sems, across_y)

    def two_first(step):
        t = tile_at(step, tiles)
        sems = (two_send.at[lax.rem(step, RING), 0], two_recv.at[t, 0])
        return remote(block(t, y, 0), quarter, left, *sems, across_y)

    def two_second(step, side):
        t = tile_at(step, tiles)
        sems = (two_send.at[lax.rem(step, RING), 1 + side], two_recv.at[t, 1 + side])
        return remote(block(t, side, x), eighth, right, *sems, across_x)

    def core_copy(step):
        t = tile_at(step, tiles)
        sems = (core_send.at[lax.rem(step, RING)], core_recv.at[t])
        return remote(t * TILE + core * half, half, whole, *sems, across_core)

    def go(step):
        @pl.when((step >= 0) & (step < tiles))
        def _():
            one_first(step).start()
            one_second(step).start()

        @pl.when((step >= LAG) & (step < tiles + LAG))
        def _():
            old = step - LAG
            one_first(old).wait()
            two_first(old).start()
            one_second(old).wait()
            for side in range(2):
                two_second(old, side).start()

        @pl.when((step >= 2 * LAG) & (step < tiles + 2 * LAG))
        def _():
            old = step - 2 * LAG
            two_first(old).wait()
            for side in range(2):
                two_second(old, side).wait()
            core_copy(old).start()

        @pl.when(step >= 3 * LAG)
        def _():
            core_copy(step - 3 * LAG).wait()

    return go


def spread_sems(tiles):
    dma = pltpu.SemaphoreType.DMA
    return [
        dma((RING, 2)),
        dma((tiles, 2)),
        dma((RING, 3)),
        dma((tiles, 3)),
        dma((RING,)),
        dma((tiles,)),
    ]


def spread_kernel(devices, rows_ref, block_ref, out_ref, all_ref, *sems):
    seq_count = devices // 4
    me = lax.axis_index("dp") * seq_count + lax.axis_index("seq")
    sems, push = sems[:-3], sems[-3:]
    greet_all(devices, seq_count)
    start_push(block_ref, all_ref, devices, devices, me, *push)
    spreading = spread_steps(out_ref, *sems)

    def one_step(step, carry):
        spreading(step)
        return carry

    lax.fori_loop(0, out_ref.shape[0] // TILE + 3 * LAG, one_step, 0)
    finish_push(block_ref, all_ref, devices, devices, me, *push)


def spread_rows(rows, block, devices, collective_id):
    return pl.pallas_call(
        functools.partial(spread_kernel, devices),
        out_shape=(
            jax.ShapeDtypeStruct(rows.shape, rows.dtype),
            jax.ShapeDtypeStruct((devices,) + block.shape, block.dtype),
        ),
        in_specs=[pl.BlockSpec(memory_space=pl.ANY)] * 2,
        out_specs=(pl.BlockSpec(memory_space=pl.ANY), pl.BlockSpec(memory_space=pl.ANY)),
        scratch_shapes=spread_sems(rows.shape[0] // TILE) + push_sems(devices),
        input_output_aliases={0: 0},
        compiler_params=pltpu.CompilerParams(
            collective_id=collective_id, has_side_effects=True, vmem_limit_bytes=VMEM_BYTES
        ),
    )(rows, block)


def gather_rows(openings, counts, ahead, devices, collective_id, shard):
    units, _, width = shard.shape
    assert all(count % STRIDE for count in counts) and counts[1] <= counts[0]
    dma = pltpu.SemaphoreType.DMA
    anywhere = pl.BlockSpec(memory_space=pl.ANY)
    return pl.pallas_call(
        functools.partial(gather_kernel, openings, ahead, devices),
        out_shape=[
            jax.ShapeDtypeStruct((count * TILE, UNIT, width), jnp.bfloat16) for count in counts
        ],
        in_specs=[anywhere],
        out_specs=[anywhere, anywhere],
        scratch_shapes=[
            dma((2, units)),
            dma((sum(counts), 7)),
            dma((2, Z_RING, 7, 2)),
            dma((sum(counts), 7)),
        ]
        + spread_sems(counts[0]),
        compiler_params=pltpu.CompilerParams(
            collective_id=collective_id, has_side_effects=True, vmem_limit_bytes=VMEM_BYTES
        ),
    )(shard)


def share_kernel(devices, block_ref, out_ref, *sems):
    seq_count = devices // 4
    me = lax.axis_index("dp") * seq_count + lax.axis_index("seq")
    greet_all(devices, seq_count)
    start_push(block_ref, out_ref, devices, devices, me, *sems)
    finish_push(block_ref, out_ref, devices, devices, me, *sems)


def share(block, devices, collective_id):
    return pl.pallas_call(
        functools.partial(share_kernel, devices),
        out_shape=jax.ShapeDtypeStruct((devices,) + block.shape, block.dtype),
        in_specs=[pl.BlockSpec(memory_space=pltpu.VMEM)],
        out_specs=pl.BlockSpec(memory_space=pltpu.VMEM),
        scratch_shapes=push_sems(devices),
        compiler_params=pltpu.CompilerParams(
            collective_id=collective_id, has_side_effects=True, vmem_limit_bytes=16 * 1024 * 1024
        ),
    )(block)


def contrast_kernel(pooled_ref, pick_ref, row_ref, col_ref, scale_ref, pool_ref, text_ref, loss_ref):
    count = pick_ref.shape[1]
    scale = scale_ref[0, 0] / contrastive_sharpness_divisor
    diagonal = lax.broadcasted_iota(jnp.int32, (count, count), 0) == lax.broadcasted_iota(
        jnp.int32, (count, count), 1
    )
    loss = jnp.zeros((1, 1), jnp.float32)
    for m in range(MICRO):
        row = row_ref[m]
        col = col_ref[m] > 0.0
        image = jnp.dot(
            pick_ref[m], pooled_ref[m], precision=exact, preferred_element_type=jnp.float32
        )
        words = pooled_ref[MICRO + m]
        image_norm = lax.rsqrt(jnp.sum(image * image, axis=-1, keepdims=True) + norm_eps)
        words_norm = lax.rsqrt(jnp.sum(words * words, axis=-1, keepdims=True) + norm_eps)
        image = image * image_norm
        words = words * words_norm
        cosines = lax.dot_general(
            image,
            words,
            (((1,), (1,)), ((), ())),
            precision=exact,
            preferred_element_type=jnp.float32,
        )
        cosines = jnp.where(col, cosines / contrastive_sharpness_divisor, neg_large)
        top = jnp.max(cosines, axis=-1, keepdims=True)
        weight = jnp.exp(cosines - top)
        total = jnp.sum(weight, axis=-1, keepdims=True)
        matched = jnp.sum(jnp.where(diagonal, cosines, 0.0), axis=-1, keepdims=True)
        lost = jnp.where(row > 0.0, top + jnp.log(total) - matched, 0.0)
        loss = loss + jnp.sum(lost, axis=0, keepdims=True)
        grad = weight / total - jnp.where(diagonal, 1.0, 0.0)
        grad = jnp.where((row > 0.0) & col, grad * scale, 0.0)
        grad_image = jnp.dot(grad, words, precision=exact, preferred_element_type=jnp.float32)
        grad_words = lax.dot_general(
            grad,
            image,
            (((0,), (0,)), ((), ())),
            precision=exact,
            preferred_element_type=jnp.float32,
        )
        inner = jnp.sum(image * grad_image, axis=-1, keepdims=True)
        pool_ref[m] = image_norm * (grad_image - image * inner)
        inner = jnp.sum(words * grad_words, axis=-1, keepdims=True)
        text_ref[m] = words_norm * (grad_words - words * inner)
    loss_ref[...] = jnp.broadcast_to(loss, loss_ref.shape)


def contrast(pooled, pick, valid, scale):
    count, width = pooled.shape[1], pooled.shape[2]
    grads = jax.ShapeDtypeStruct((MICRO, count, width), jnp.float32)
    return pl.pallas_call(
        contrast_kernel,
        out_shape=(grads, grads, jax.ShapeDtypeStruct((1, 128), jnp.float32)),
        compiler_params=pltpu.CompilerParams(vmem_limit_bytes=VMEM_BYTES),
    )(pooled, pick, valid[:, :, None], valid[:, None, :], scale.reshape(1, 1))


def joint_forward_kernel(rows_ref, matrix_ref, bias_ref, out_ref):
    part, width = matrix_ref.shape[2], matrix_ref.shape[3]
    matrix = matrix_ref[...].reshape(3 * part, width)
    out_ref[0] = low(dot_nt(rows_ref[...], matrix) + bias_ref[0])


def joint_forward(rows, matrix, bias):
    count, width = rows.shape
    groups, _, columns = bias.shape
    return pl.pallas_call(
        joint_forward_kernel,
        out_shape=jax.ShapeDtypeStruct((groups, count, columns), jnp.bfloat16),
        grid=(groups,),
        in_specs=[
            pl.BlockSpec((count, width), lambda j: (0, 0)),
            pl.BlockSpec((3, 1, columns // 3, width), lambda j: (0, j, 0, 0)),
            pl.BlockSpec((1, 1, columns), lambda j: (j, 0, 0)),
        ],
        out_specs=pl.BlockSpec((1, count, columns), lambda j: (j, 0, 0)),
        compiler_params=pltpu.CompilerParams(vmem_limit_bytes=VMEM_BYTES),
    )(rows, matrix.reshape(3, groups, columns // 3, width), bias)


def joint_backward_kernel(grad_ref, matrix_ref, rows_ref, out_ref, weight_ref):
    part, width = matrix_ref.shape[2], matrix_ref.shape[3]
    grad = grad_ref[0]
    term = dot_nn(grad, matrix_ref[...].reshape(3 * part, width))
    weight_ref[...] = low(dot_tn(grad, rows_ref[...])).reshape(3, 1, part, width)

    @pl.when(pl.program_id(0) == 0)
    def _():
        out_ref[...] = term

    @pl.when(pl.program_id(0) > 0)
    def _():
        out_ref[...] += term


def joint_backward(grad, matrix, rows):
    groups, count, columns = grad.shape
    width = rows.shape[1]
    part = columns // 3
    out, weight = pl.pallas_call(
        joint_backward_kernel,
        out_shape=(
            jax.ShapeDtypeStruct((count, width), jnp.float32),
            jax.ShapeDtypeStruct((3, groups, part, width), jnp.bfloat16),
        ),
        grid=(groups,),
        in_specs=[
            pl.BlockSpec((1, count, columns), lambda j: (j, 0, 0)),
            pl.BlockSpec((3, 1, part, width), lambda j: (0, j, 0, 0)),
            pl.BlockSpec((count, width), lambda j: (0, 0)),
        ],
        out_specs=(
            pl.BlockSpec((count, width), lambda j: (0, 0)),
            pl.BlockSpec((3, 1, part, width), lambda j: (0, j, 0, 0)),
        ),
        compiler_params=pltpu.CompilerParams(vmem_limit_bytes=VMEM_BYTES),
    )(grad, matrix.reshape(3, groups, part, width), rows)
    return out, weight.reshape(3 * groups * part, width)


FEED_BLOCK = 768


def feed_forward_kernel(rows_ref, up_ref, down_ref, b_up_ref, b_down_ref, before_ref, act_ref, out_ref):
    before = dot_nt(rows_ref[...], up_ref[...]) + b_up_ref[0]
    before_ref[...] = before
    act = low(gelu_tanh(before))
    act_ref[...] = act
    term = dot_nn(act, down_ref[...])

    @pl.when(pl.program_id(0) == 0)
    def _():
        out_ref[...] = term + b_down_ref[...]

    @pl.when(pl.program_id(0) > 0)
    def _():
        out_ref[...] += term


def feed_specs(count, width, up_start, down_start):
    return (
        pl.BlockSpec((count, width), lambda j: (0, 0)),
        pl.BlockSpec((FEED_BLOCK, width), lambda j: (up_start + j, 0)),
        pl.BlockSpec((FEED_BLOCK, width), lambda j: (down_start + j, 0)),
        pl.BlockSpec((1, 1, FEED_BLOCK), lambda j: (j, 0, 0)),
        pl.BlockSpec((count, FEED_BLOCK), lambda j: (0, j)),
    )


def feed_forward(rows, up, up_start, down, down_start, b_up, b_down):
    count, width = rows.shape
    whole, up_spec, down_spec, line, column = feed_specs(count, width, up_start, down_start)
    return pl.pallas_call(
        feed_forward_kernel,
        out_shape=(
            jax.ShapeDtypeStruct((count, FF), jnp.float32),
            jax.ShapeDtypeStruct((count, FF), jnp.bfloat16),
            jax.ShapeDtypeStruct((count, width), jnp.float32),
        ),
        grid=(FF // FEED_BLOCK,),
        in_specs=[whole, up_spec, down_spec, line, pl.BlockSpec((1, width), lambda j: (0, 0))],
        out_specs=(column, column, whole),
        compiler_params=pltpu.CompilerParams(vmem_limit_bytes=VMEM_BYTES),
    )(rows, up, down, b_up.reshape(-1, 1, FEED_BLOCK), b_down)


def feed_backward_kernel(
    grad_ref, up_ref, down_ref, before_ref, act_ref, rows_ref, out_ref, w_up_ref, w_down_ref, sum_ref
):
    grad = grad_ref[...]
    before = before_ref[...]
    factor = math.sqrt(2.0 / math.pi)
    square = before * before
    bend = jnp.tanh(factor * (before + 0.044715 * (square * before)))
    slope = 0.5 * (1.0 + bend) + (0.5 * factor) * before * (1.0 - bend * bend) * (
        1.0 + (3.0 * 0.044715) * square
    )
    grad_up = dot_nt(grad, down_ref[...]) * slope
    sum_ref[0] = jnp.sum(grad_up, axis=0, keepdims=True)
    grad_up = low(grad_up)
    w_up_ref[...] = low(dot_tn(grad_up, rows_ref[...]))
    w_down_ref[...] = low(dot_tn(act_ref[...], grad))
    term = dot_nn(grad_up, up_ref[...])

    @pl.when(pl.program_id(0) == 0)
    def _():
        out_ref[...] = term

    @pl.when(pl.program_id(0) > 0)
    def _():
        out_ref[...] += term


def feed_backward(grad, up, up_start, down, down_start, before, act, rows):
    count, width = rows.shape
    whole, up_spec, down_spec, line, column = feed_specs(count, width, up_start, down_start)
    block = pl.BlockSpec((FEED_BLOCK, width), lambda j: (j, 0))
    return pl.pallas_call(
        feed_backward_kernel,
        out_shape=(
            jax.ShapeDtypeStruct((count, width), jnp.float32),
            jax.ShapeDtypeStruct((FF, width), jnp.bfloat16),
            jax.ShapeDtypeStruct((FF, width), jnp.bfloat16),
            jax.ShapeDtypeStruct((FF // FEED_BLOCK, 1, FEED_BLOCK), jnp.float32),
        ),
        grid=(FF // FEED_BLOCK,),
        in_specs=[whole, up_spec, down_spec, column, column, whole],
        out_specs=(whole, block, block, line),
        compiler_params=pltpu.CompilerParams(vmem_limit_bytes=VMEM_BYTES),
    )(grad, up, down, before, act, rows)


def caption_grad_kernel(rows_ref, grad_ref, out_ref):
    out_ref[...] = low(dot_tn(rows_ref[...], grad_ref[...]))


def caption_grad(rows, grad):
    count, depth = rows.shape
    block = 512
    return pl.pallas_call(
        caption_grad_kernel,
        out_shape=jax.ShapeDtypeStruct((depth, grad.shape[1]), jnp.bfloat16),
        grid=(depth // block,),
        in_specs=[
            pl.BlockSpec((count, block), lambda j: (0, j)),
            pl.BlockSpec(grad.shape, lambda j: (0, 0)),
        ],
        out_specs=pl.BlockSpec((block, grad.shape[1]), lambda j: (j, 0)),
        compiler_params=pltpu.CompilerParams(vmem_limit_bytes=VMEM_BYTES),
    )(rows, grad)


def adamw(param, grad, first, second, rate, decay):
    first_new = beta_one * first + (1.0 - beta_one) * grad
    second_new = beta_two * second + (1.0 - beta_two) * grad * grad
    step_dir = (
        first_new
        / (1.0 - beta_one**STEP)
        / (jnp.sqrt(second_new / (1.0 - beta_two**STEP)) + adam_eps)
    )
    return (param - rate * (step_dir + decay * param), first_new, second_new)


def per_device(
    latents,
    noise,
    captions,
    image_sizes,
    caption_lengths,
    timesteps,
    weights,
    vectors,
    weights_m,
    weights_v,
    vectors_m,
    vectors_v,
):
    width = weights.shape[1]
    seq_count = lax.axis_size("seq")
    dp_count = lax.axis_size("dp")
    seq_index = lax.axis_index("seq")
    row_index = lax.axis_index("dp")
    devices = dp_count * seq_count
    layout = matrix_rows(width)
    shard_rows = weights.shape[0]
    paired = dp_count == 4 and seq_count == 8
    weights_low = weights.astype(jnp.bfloat16)
    if paired:
        shard = weights_low.reshape(shard_rows // UNIT, UNIT, width)
        rows_all, rows_late = gather_rows((0, 2176), (23, 19), 8, devices, 7, shard)
        flat = (-1, width)
        self_head = 384
        (
            time_one,
            time_two,
            time_block,
            text_one,
            text_two,
            joint_qkv,
            self_out_head,
        ) = split_rows(rows_all.reshape(flat), layout[:6] + (self_head,))
    else:
        gathered = lax.all_gather(weights_low, both_axes, axis=0, tiled=True)
        (
            time_one,
            time_two,
            time_block,
            text_one,
            text_two,
            joint_qkv,
            self_out,
            cross_query,
            cross_kv,
            cross_out,
            mlp_up,
            mlp_down,
        ) = split_rows(gathered, layout)
    (
        table,
        final_table,
        patch_in,
        patch_out,
        b_patch,
        b_time_one,
        b_time_two,
        b_block,
        b_text_one,
        b_text_two,
        b_query,
        b_value,
        b_self_out,
        b_cross_query,
        b_cross_value,
        b_cross_out,
        b_up,
        b_down,
    ) = split_rows(vectors.astype(jnp.bfloat16).astype(jnp.float32), vector_rows(width))
    head_dim = width // HEADS
    heads = HEADS // seq_count
    part = heads * head_dim
    images = image_sizes.shape[2]
    slots = latents.shape[2]
    assert slots == BLOCK and images == seq_count
    rows = MICRO * slots
    wide = (MICRO, slots, width)
    image_count = jnp.sum((image_sizes > 0).astype(jnp.float32))
    loss_scale = 1.0 / image_count

    ends_all = jnp.cumsum(image_sizes, axis=2)
    firsts = jnp.arange(seq_count, dtype=jnp.int32) * BLOCK
    segment_all = jnp.sum(
        (ends_all[:, :, None, :] <= firsts[None, None, :, None]).astype(jnp.int32), axis=3
    )
    onehot_all = (
        segment_all[:, :, :, None] == jnp.arange(images, dtype=jnp.int32)[None, None, None, :]
    )
    size_all = jnp.sum(jnp.where(onehot_all, image_sizes[:, :, None, :], 0), axis=3)
    start_all = jnp.sum(jnp.where(onehot_all, (ends_all - image_sizes)[:, :, None, :], 0), axis=3)
    step_all = jnp.sum(jnp.where(onehot_all, timesteps[:, :, None, :], 0), axis=3)
    length_all = jnp.sum(jnp.where(onehot_all, caption_lengths[:, :, None, :], 0), axis=3)
    row_start = start_all[:, row_index]
    row_size = size_all[:, row_index]
    kv_start = row_start // BLOCK
    kv_big = (row_size == LARGE).astype(jnp.int32)
    own_segment = segment_all[:, row_index, seq_index]
    own_size = row_size[:, seq_index]
    own_start = row_start[:, seq_index]
    own_step = step_all[:, row_index, seq_index]
    own_length = length_all[:, row_index, seq_index]

    quarter = width // 4
    omega = 1.0 / 10000.0 ** (jnp.arange(quarter, dtype=jnp.float32) / quarter)
    angle = jnp.arange(2 * SIDE, dtype=jnp.float32)[:, None] * omega[None, :]
    angle_table = jnp.concatenate([jnp.sin(angle), jnp.cos(angle)], axis=1)
    within = (
        seq_index * BLOCK - own_start[:, None] + jnp.arange(slots, dtype=jnp.int32)[None, :]
    ).reshape(rows)
    side = jnp.where(own_size == LARGE, 2 * SIDE, SIDE).astype(jnp.int32)
    side = jnp.broadcast_to(side[:, None], (MICRO, slots)).reshape(rows)
    places = jnp.arange(2 * SIDE, dtype=jnp.int32)[None, :]
    pick_row = ((within // side)[:, None] == places).astype(jnp.float32)
    pick_col = ((within % side)[:, None] == places).astype(jnp.float32)
    position = jnp.concatenate(
        [
            jnp.dot(pick_row, angle_table, precision=exact),
            jnp.dot(pick_col, angle_table, precision=exact),
        ],
        axis=1,
    )

    level = noise_level(own_step)[:, None, None]
    level_prev = noise_level(own_step - 1)[:, None, None]
    beta_log, tilde_log = variance_logs(level, level_prev)
    target = noise[:, 0].astype(jnp.float32)
    noisy = jnp.sqrt(level) * latents[:, 0].astype(jnp.float32) + jnp.sqrt(1.0 - level) * target
    noisy = noisy.reshape(rows, PATCH)

    time_low = low(time_features(own_step))
    time_first = dot_nn(time_low, time_one) + b_time_one
    time_act, time_act_back = jax.vjp(jax.nn.silu, time_first)
    time_act_low = low(time_act)
    time_embed = dot_nn(time_act_low, time_two) + b_time_two
    embed_act, embed_act_back = jax.vjp(jax.nn.silu, time_embed)
    embed_low = low(embed_act)
    block_mod = dot_nt(embed_low, time_block) + b_block.reshape(1, -1) + table.reshape(1, -1)
    shift_one, scale_one, gate_one, shift_two, scale_two, gate_two = [
        piece[:, None, :] for piece in jnp.split(block_mod, 6, axis=1)
    ]
    shift_final = (final_table[0][None, :] + time_embed)[:, None, :]
    scale_final = (final_table[1][None, :] + time_embed)[:, None, :]

    hidden_zero = (jnp.dot(noisy, patch_in, precision=exact) + b_patch + position).reshape(wide)
    normed_one, mod_one_back = jax.vjp(modulate, hidden_zero, shift_one, scale_one)
    normed_one_low = low(normed_one).reshape(rows, width)
    joint_bias = jnp.concatenate([b_query, jnp.zeros_like(b_query), b_value], axis=0)
    joint_bias = jnp.transpose(joint_bias.reshape(3, seq_count, part), (1, 0, 2))
    qkv = joint_forward(normed_one_low, joint_qkv, joint_bias.reshape(seq_count, 1, 3 * part))
    caption_low = captions[:, 0].reshape(MICRO * CAP, TEXT_W)
    caption_first = dot_nn(caption_low, text_one) + b_text_one
    caption_act, caption_act_back = jax.vjp(gelu_tanh, caption_first)
    caption_act_low = low(caption_act)
    text = dot_nn(caption_act_low, text_two) + b_text_two
    lengths_slot = lax.dynamic_slice_in_dim(caption_lengths[:, row_index], seq_index, 1, 1)
    token_live = (jnp.arange(CAP, dtype=jnp.int32)[None, :] < lengths_slot).astype(jnp.float32)
    lengths_slot_float = lengths_slot.astype(jnp.float32)
    caption_pool = (
        jnp.sum(text.reshape(MICRO, CAP, width) * token_live[:, :, None], axis=1) / lengths_slot_float
    )
    text_own = low(text)
    if paired:
        qkv, text_own, rows_late = lax.optimization_barrier((qkv, text_own, rows_late))
    qkv = lax.all_to_all(qkv, "seq", split_axis=0, concat_axis=0, tiled=True)
    text_all = lax.all_gather(text_own.reshape(MICRO, CAP, width), "seq", axis=0)
    if paired:
        rows_late, words_all = spread_rows(rows_late, caption_pool.reshape(-1, 128), devices, 8)
        qkv, rows_late = lax.optimization_barrier((qkv, rows_late))
        rows_late = rows_late.reshape(flat)
        self_out_tail, cross_query, cross_kv, cross_out = split_rows(
            rows_late, (layout[6] - self_head,) + layout[7:10]
        )
        up_start = (layout[6] - self_head + sum(layout[7:10])) // FEED_BLOCK
        feed_weights = (rows_late, up_start, rows_late, up_start + FF // FEED_BLOCK)
    else:
        feed_weights = (mlp_up, 0, mlp_down, 0)
    if paired:
        self_out = jnp.concatenate([self_out_head, self_out_tail], axis=0)
    qkv = qkv.reshape(seq_count, MICRO, slots, 3 * part)
    mixed = self_forward(kv_start, kv_big, qkv, heads, head_dim)
    mixed = lax.all_to_all(
        mixed.reshape(seq_count, rows, part), "seq", split_axis=0, concat_axis=0, tiled=True
    )
    mixed_low = jnp.transpose(mixed, (1, 0, 2)).reshape(rows, width)
    attended = (dot_nn(mixed_low, self_out) + b_self_out).reshape(wide)
    hidden_one = hidden_zero + gate_one * attended

    text_low = jnp.concatenate(
        [
            lax.dynamic_slice(text_all, (own_segment[m], m, 0, 0), (1, 1, CAP, width))[0, 0]
            for m in range(MICRO)
        ],
        axis=0,
    )
    text_kv = dot_nt(text_low, cross_kv)
    pad_rows = ((0, 0), (0, CAP_PAD - CAP), (0, 0))
    key_text = jnp.pad(low(text_kv[:, :width]).reshape(MICRO, CAP, width), pad_rows)
    value_text = jnp.pad(
        low(text_kv[:, width:] + b_cross_value).reshape(MICRO, CAP, width), pad_rows
    )
    hidden_one_low = low(hidden_one).reshape(rows, width)
    query_cross = low(dot_nn(hidden_one_low, cross_query) + b_cross_query).reshape(wide)
    cross_low = cross_call(
        functools.partial(cross_forward_kernel, head_dim),
        own_length,
        (query_cross, key_text, value_text),
        jax.ShapeDtypeStruct(wide, jnp.bfloat16),
    ).reshape(rows, width)
    hidden_two = hidden_one + (dot_nn(cross_low, cross_out) + b_cross_out).reshape(wide)
    normed_two, mod_two_back = jax.vjp(modulate, hidden_two, shift_two, scale_two)
    normed_two_low = low(normed_two).reshape(rows, width)
    upward, upward_low, feed = feed_forward(normed_two_low, *feed_weights, b_up, b_down)
    feed = feed.reshape(wide)
    hidden_three = hidden_two + gate_two * feed
    final_normed, final_back = jax.vjp(modulate, hidden_three, shift_final, scale_final)
    final_flat = final_normed.reshape(rows, width)
    predicted = jnp.dot(final_flat, patch_out.T, precision=exact).reshape(MICRO, slots, 2 * PATCH)
    error = predicted[:, :, :PATCH] - target
    frac = (predicted[:, :, PATCH:] + 1.0) * 0.5
    model_log = frac * beta_log + (1.0 - frac) * tilde_log
    ratio = jnp.exp(tilde_log - model_log)
    spread = 0.5 * (model_log - tilde_log - 1.0 + ratio) / log_two
    error_weight = (1.0 / (float(PATCH) * own_size.astype(jnp.float32)))[:, None, None]
    squared_loss = jnp.sum((error * error + spread) * error_weight)

    pooled = jnp.sum(final_normed, axis=1)
    if paired:
        pooled_all = share(pooled.reshape(-1, 128), devices, 1)
    else:
        pooled_all = lax.all_gather(pooled, both_axes, axis=0)
        words_all = lax.all_gather(caption_pool, both_axes, axis=0)
    each = (devices, MICRO, width)
    pooled_all = jnp.concatenate([pooled_all.reshape(each), words_all.reshape(each)], axis=1)
    pooled_all = jnp.transpose(pooled_all, (1, 0, 2))
    size_float = jnp.maximum(image_sizes.astype(jnp.float32), 1.0)
    pick = onehot_all.astype(jnp.float32) / size_float[:, :, None, :]
    same_row = jnp.eye(dp_count, dtype=jnp.float32)
    pick = jnp.einsum("mrsi,rq->mriqs", pick, same_row, precision=exact).reshape(
        MICRO, dp_count * images, devices
    )
    valid = (image_sizes > 0).astype(jnp.float32).reshape(MICRO, dp_count * images)
    grad_pool, grad_caption, contrast_value = contrast(pooled_all, pick, valid, loss_scale)
    contrast_value = contrast_value[0, 0]
    own_pool = row_index * images + own_segment
    grad_pool_own = jnp.concatenate(
        [lax.dynamic_slice(grad_pool, (m, own_pool[m], 0), (1, 1, width))[0] for m in range(MICRO)]
    ) / own_size.astype(jnp.float32)[:, None]
    grad_caption = lax.dynamic_slice_in_dim(
        grad_caption, row_index * images + seq_index, 1, 1
    )[:, 0]

    grad_spread = 0.5 * (1.0 - ratio) / log_two * 0.5 * (beta_log - tilde_log)
    grad_predicted = (
        loss_scale * error_weight * jnp.concatenate([2.0 * error, grad_spread], axis=2)
    ).reshape(rows, 2 * PATCH)
    grad_final = grad_pool_own[:, None, :] + jnp.dot(
        grad_predicted, patch_out, precision=exact
    ).reshape(wide)
    grad_patch_out = lax.dot_general(
        grad_predicted, final_flat, (((0,), (0,)), ((), ())), precision=exact
    )
    grad_three, grad_shift_final, grad_scale_final = final_back(grad_final)
    grad_shift_final = grad_shift_final[:, 0]
    grad_scale_final = grad_scale_final[:, 0]
    grad_final_table = jnp.stack([grad_shift_final.sum(axis=0), grad_scale_final.sum(axis=0)])
    grad_embed = grad_shift_final + grad_scale_final

    grad_feed = (grad_three * gate_two).reshape(rows, width)
    grad_feed_low = low(grad_feed)
    grad_normed_two, weight_up, weight_down, grad_b_up = feed_backward(
        grad_feed_low, *feed_weights, upward, upward_low, normed_two_low
    )
    grad_two_mod, grad_shift_two, grad_scale_two = mod_two_back(grad_normed_two.reshape(wide))
    grad_gate_two = jnp.sum(grad_three * feed, axis=1, keepdims=True)
    grad_two = grad_three + grad_two_mod
    grad_two_flat = grad_two.reshape(rows, width)
    grad_two_low = low(grad_two_flat)
    weight_cross_out = dot_tn(cross_low, grad_two_low)
    grad_cross_low = low(dot_nt(grad_two_low, cross_out)).reshape(wide)
    padded = jax.ShapeDtypeStruct((MICRO, CAP_PAD, width), jnp.float32)
    grad_query_cross, grad_key_text, grad_value_text = cross_call(
        functools.partial(cross_backward_kernel, head_dim),
        own_length,
        (query_cross, key_text, value_text, grad_cross_low),
        (jax.ShapeDtypeStruct(wide, jnp.float32), padded, padded),
    )
    grad_query_cross = grad_query_cross.reshape(rows, width)
    grad_query_low = low(grad_query_cross)
    weight_cross_query = dot_tn(hidden_one_low, grad_query_low)
    grad_one = grad_two + dot_nt(grad_query_low, cross_query).reshape(wide)

    grad_kv = jnp.concatenate([grad_key_text[:, :CAP], grad_value_text[:, :CAP]], axis=2).reshape(
        MICRO * CAP, 2 * width
    )
    grad_kv_low = low(grad_kv)
    weight_cross_kv = dot_tn(grad_kv_low, text_low)
    grad_text_part = low(dot_nn(grad_kv_low, cross_kv)).reshape(MICRO, CAP, width)
    grad_text_all = lax.all_gather(grad_text_part, "seq", axis=0).astype(jnp.float32)
    mine = (segment_all[:, row_index] == seq_index).astype(jnp.float32)
    grad_text = jnp.sum(grad_text_all * jnp.transpose(mine)[:, :, None, None], axis=0) + (
        (grad_caption / lengths_slot_float)[:, None, :] * token_live[:, :, None]
    )
    grad_text = grad_text.reshape(MICRO * CAP, width)
    grad_text_low = low(grad_text)
    weight_text_two = dot_tn(caption_act_low, grad_text_low)
    grad_caption_first = caption_act_back(dot_nt(grad_text_low, text_two))[0]
    grad_caption_low = low(grad_caption_first)
    head_rows = TILE_START * UNIT - sum(layout[:3]) + TILE * UNIT // 2 if paired else 0
    weight_text_one = caption_grad(caption_low, grad_caption_low)

    grad_attended = (grad_one * gate_one).reshape(rows, width)
    grad_gate_one = jnp.sum(grad_one * attended, axis=1, keepdims=True)
    grad_attended_low = low(grad_attended)
    weight_self_out = dot_tn(mixed_low, grad_attended_low)
    grad_mixed = low(dot_nt(grad_attended_low, self_out)).reshape(rows, seq_count, part)
    grad_mixed = jnp.transpose(grad_mixed, (1, 0, 2))
    if paired:
        weight_up, weight_down, grad_mixed = lax.optimization_barrier(
            (low(weight_up), low(weight_down), grad_mixed)
        )
    grad_mixed = lax.all_to_all(grad_mixed, "seq", split_axis=0, concat_axis=0, tiled=True)
    if paired:
        summed_feed = reduce_rows(
            ((19, 31),), shard_rows // UNIT, devices, 2, ((weight_up, 0, 12), (weight_down, 0, 12))
        )
        grad_mixed, summed_feed = lax.optimization_barrier((grad_mixed, summed_feed))
    grad_mixed = grad_mixed.reshape(seq_count, MICRO, slots, part)
    grad_qkv, head_sums = self_backward(kv_start, kv_big, qkv, grad_mixed, heads, head_dim)
    head_sums = jnp.sum(head_sums[:, 0], axis=0)
    column = seq_index * part
    grad_bias_query = lax.dynamic_update_slice(
        jnp.zeros((width,), jnp.float32), head_sums[:part], (column,)
    )
    grad_bias_value = lax.dynamic_update_slice(
        jnp.zeros((width,), jnp.float32), head_sums[part:], (column,)
    )
    grad_qkv = grad_qkv.reshape(seq_count, rows, 3 * part)
    if paired:
        time_rows = layout[0] + layout[1]
        block_rows = layout[2]
        weight_self_out = low(weight_self_out)
        first_half = jnp.pad(weight_text_one[:head_rows], ((TILE * UNIT // 2 - head_rows, 0), (0, 0)))
        (
            first_half,
            weight_text_one,
            weight_text_two,
            weight_self_out,
            weight_cross_query,
            weight_cross_kv,
            weight_cross_out,
            grad_qkv,
        ) = lax.optimization_barrier(
            (
                first_half,
                low(weight_text_one),
                low(weight_text_two),
                weight_self_out,
                low(weight_cross_query),
                low(weight_cross_kv),
                low(weight_cross_out),
                grad_qkv,
            )
        )
    grad_qkv = lax.all_to_all(
        grad_qkv, "seq", split_axis=0, concat_axis=0, tiled=True
    )
    if paired:
        summed_middle = reduce_rows(
            ((0, 7), (12, 19)),
            shard_rows // UNIT,
            devices,
            3,
            (
                (first_half, 0, 1),
                (weight_text_one, head_rows // UNIT, 10),
                (weight_text_two, 0, 3),
                (weight_self_out, TILE // 2, 2),
                (weight_cross_query, 0, 3),
                (weight_cross_kv, 0, 6),
                (weight_cross_out, 0, 3),
            ),
        )
        grad_qkv, summed_middle = lax.optimization_barrier((grad_qkv, summed_middle))
    grad_normed_one, weight_joint = joint_backward(grad_qkv, joint_qkv, normed_one_low)
    grad_zero_mod, grad_shift_one, grad_scale_one = mod_one_back(grad_normed_one.reshape(wide))
    grad_zero = (grad_one + grad_zero_mod).reshape(rows, width)
    grad_patch_in = lax.dot_general(noisy, grad_zero, (((0,), (0,)), ((), ())), precision=exact)

    grad_mod = jnp.concatenate(
        [grad_shift_one, grad_scale_one, grad_gate_one, grad_shift_two, grad_scale_two, grad_gate_two],
        axis=1,
    )
    grad_table = jnp.sum(grad_mod, axis=0)
    grad_mod_low = low(grad_mod.reshape(MICRO, 6 * width))
    weight_block = dot_tn(grad_mod_low, embed_low)
    grad_embed = grad_embed + embed_act_back(dot_nn(grad_mod_low, time_block))[0]
    grad_embed_low = low(grad_embed)
    weight_time_two = dot_tn(time_act_low, grad_embed_low)
    grad_time_first = time_act_back(dot_nt(grad_embed_low, time_two))[0]
    weight_time_one = dot_tn(time_low, low(grad_time_first))

    grad_vector = jnp.concatenate(
        [
            grad_table,
            grad_final_table,
            grad_patch_in,
            grad_patch_out,
            jnp.sum(grad_zero, axis=0)[None, :],
            jnp.sum(grad_time_first, axis=0)[None, :],
            jnp.sum(grad_embed, axis=0)[None, :],
            grad_table,
            jnp.sum(grad_caption_first, axis=0)[None, :],
            jnp.sum(grad_text, axis=0)[None, :],
            grad_bias_query[None, :],
            grad_bias_value[None, :],
            jnp.sum(grad_attended, axis=0)[None, :],
            jnp.sum(grad_query_cross, axis=0)[None, :],
            jnp.sum(grad_kv[:, width:], axis=0)[None, :],
            jnp.sum(grad_two_flat, axis=0)[None, :],
            grad_b_up.reshape(-1, width),
            jnp.sum(grad_feed, axis=0)[None, :],
            jnp.full((2, width), squared_loss),
        ],
        axis=0,
    )
    if paired:
        tile_size = UNIT * 128
        tile_count = -(-grad_vector.size // (tile_size * devices))
        parts = jnp.pad(
            grad_vector.reshape(-1), (0, tile_count * tile_size * devices - grad_vector.size)
        ).reshape(devices, tile_count, UNIT, 128)
        holders = -(-(time_rows + block_rows) // shard_rows)
        own_grads = jnp.concatenate(
            [grad_mod_low, grad_embed_low, low(grad_time_first), embed_low, time_act_low, time_low],
            axis=1,
        )
        summed_joint, grads_all, vector_got = reduce_rows(
            ((7, 12),),
            shard_rows // UNIT,
            devices,
            4,
            ((low(weight_joint), 0, 9), (weight_self_out, 0, 1)),
            (own_grads.reshape(-1, 128), parts),
            holders,
        )
        vector_part = jnp.sum(vector_got, axis=0)
        grads_all = jnp.where(device_index() < holders, grads_all, 0)
        grads_all = grads_all.reshape(devices * MICRO, -1)
        ends = [6 * width, 7 * width, 8 * width, 9 * width, 10 * width]
        grad_block_all, grad_two_all, grad_one_all, embed_all, act_all, features_all = jnp.split(
            grads_all, ends, axis=1
        )
        first_row = device_index() * shard_rows

        def own_columns(array, start):
            stop = start + array.shape[1]
            spread = jnp.pad(array, ((0, 0), (start, shard_rows + (-stop) % shard_rows)))
            place = jnp.minimum(first_row, spread.shape[1] - shard_rows)
            return lax.dynamic_slice(spread, (0, place), (array.shape[0], shard_rows))

        summed_time = (
            dot_tn(own_columns(features_all, 0), grad_one_all)
            + dot_tn(own_columns(act_all, layout[0]), grad_two_all)
            + dot_tn(own_columns(grad_block_all, time_rows), embed_all)
        )
        row = first_row + jnp.arange(shard_rows, dtype=jnp.int32)
        tile = ((row - TILE_START * UNIT) // (TILE * UNIT))[:, None]
        flat = (shard_rows, width)
        reduced = jnp.where(
            tile >= 19,
            summed_feed.reshape(flat),
            jnp.where(
                (tile >= 7) & (tile < 12), summed_joint.reshape(flat), summed_middle.reshape(flat)
            ),
        ).astype(jnp.float32)
        summed = jnp.where(row[:, None] < time_rows + block_rows, summed_time, reduced)
    else:
        grad_weights = jnp.concatenate(
            [
                low(piece)
                for piece in (
                    weight_time_one,
                    weight_time_two,
                    weight_block,
                    weight_text_one,
                    weight_text_two,
                    weight_joint,
                    weight_self_out,
                    weight_cross_query,
                    weight_cross_kv,
                    weight_cross_out,
                    weight_up,
                    weight_down,
                )
            ],
            axis=0,
        )
        summed = lax.psum_scatter(
            grad_weights, both_axes, scatter_dimension=0, tiled=True
        ).astype(jnp.float32)
    squares = jnp.sum(summed * summed)
    if paired:
        last = jnp.concatenate([vector_part, jnp.full((1, UNIT, 128), squares)], axis=0)
        last = share(last, devices, 6)
        squares_all = jnp.sum(last[:, -1, 0, 0])
        grad_vectors = last[:, :-1].reshape(-1)[: grad_vector.size].reshape(grad_vector.shape)
    else:
        grad_vectors, squares_all = lax.psum((grad_vector, squares), both_axes)
    loss_sum = grad_vectors[vectors.shape[0], 0] + contrast_value
    grad_vectors = grad_vectors[: vectors.shape[0]]
    down_bias_grad = grad_vectors[grad_vectors.shape[0] - 1]
    grad_norm = jnp.sqrt(squares_all + jnp.sum(grad_vectors * grad_vectors))
    factor = jnp.minimum(1.0, clip_norm / (grad_norm + 1e-06))
    new_w, first_w, second_w = adamw(
        weights, summed * factor, weights_m, weights_v, rate_matrix, weight_decay
    )
    new_v, first_v, second_v = adamw(
        vectors, grad_vectors * factor, vectors_m, vectors_v, rate_vector, 0.0
    )
    return (
        new_w,
        first_w,
        second_w,
        new_v,
        first_v,
        second_v,
        loss_sum,
        image_count,
        grad_norm,
        down_bias_grad,
    )


def solution(mesh):
    shard = P(both_axes, None)
    data = P(None, "dp", "seq", None)
    return jax.shard_map(
        per_device,
        mesh=mesh,
        in_specs=(data, data, data, P(), P(), P(), shard, P(), shard, shard, P(), P()),
        out_specs=(shard, shard, shard, P(), P(), P(), P(), P(), P(), P()),
        check_vma=False,
    )
```

```python
import functools
import math

import jax
import jax.numpy as jnp
from jax import lax
from jax.experimental import pallas as pl
from jax.experimental.pallas import tpu as pltpu
from jax.sharding import PartitionSpec as P

HEADS = 16
FF = 4608
TEXT_W = 4096
FREQ = 256
CAP = 120
CAP_PAD = 128
SIDE = 16
PATCH = 16
MICRO = 2
STEP = 10
BLOCK = 256
LARGE = 1024
VMEM_BYTES = 56 * 1024 * 1024

exact = lax.Precision.HIGHEST
clip_norm = 0.002
contrastive_sharpness_divisor = 0.1
beta_one = 0.9
beta_two = 0.999
adam_eps = 1e-08
weight_decay = 0.01
rate_matrix = 0.05
rate_vector = 0.3
norm_eps = 1e-06
neg_large = -1e30
log_two = math.log(2.0)
both_axes = ("dp", "seq")


def matrix_rows(width):
    return (FREQ, width, 6 * width, TEXT_W, width, 3 * width, width, width, 2 * width, width, FF, FF)


def vector_rows(width):
    return (6, 2, PATCH, 2 * PATCH, 1, 1, 1, 6, 1, 1, 1, 1, 1, 1, 1, 1, FF // width, 1)


def split_rows(whole, rows):
    pieces = []
    offset = 0
    for number in rows:
        pieces.append(whole[offset : offset + number])
        offset = offset + number
    return pieces


def device_index():
    return lax.axis_index("dp") * lax.axis_size("seq") + lax.axis_index("seq")


def modulate(hidden, shift, scale):
    centre = hidden - jnp.mean(hidden, axis=-1, keepdims=True)
    normed = centre * lax.rsqrt(jnp.mean(centre * centre, axis=-1, keepdims=True) + norm_eps)
    return normed * (1.0 + scale) + shift


def gelu_tanh(values):
    return jax.nn.gelu(values, approximate=True)


def time_features(steps_now):
    half_size = FREQ // 2
    frequency = jnp.exp(-math.log(10000.0) * jnp.arange(half_size, dtype=jnp.float32) / half_size)
    angles = steps_now.astype(jnp.float32)[:, None] * frequency[None, :]
    return jnp.concatenate([jnp.cos(angles), jnp.sin(angles)], axis=1)


def noise_level(steps_now):
    phase = (steps_now.astype(jnp.float32) / 1000.0 + 0.008) / 1.008 * (math.pi / 2.0)
    return jnp.cos(phase) ** 2


def variance_logs(level, level_prev):
    beta_now = jnp.minimum(1.0 - level / level_prev, 0.999)
    tilde_log = jnp.log(beta_now * (1.0 - level_prev) / (1.0 - level))
    return (jnp.log(beta_now), tilde_log)


def dot_nn(left, right):
    return lax.dot_general(left, right, (((1,), (0,)), ((), ())), preferred_element_type=jnp.float32)


def dot_nt(left, right):
    return lax.dot_general(left, right, (((1,), (1,)), ((), ())), preferred_element_type=jnp.float32)


def dot_tn(left, right):
    return lax.dot_general(left, right, (((0,), (0,)), ((), ())), preferred_element_type=jnp.float32)


def low(values):
    return values.astype(jnp.bfloat16)


def self_forward_kernel(heads, dim, start_ref, big_ref, qkv_ref, out_ref, key_s, value_s):
    micro = pl.program_id(0)
    blocks = qkv_ref.shape[0]
    scale = dim ** (-0.5)
    for b in range(blocks):
        for h in range(heads):
            rows = pl.ds(b * BLOCK, BLOCK)
            key_s[h, rows, :] = qkv_ref[b, 0, :, (heads + h) * dim : (heads + h + 1) * dim]
            value_s[h, rows, :] = qkv_ref[b, 0, :, (2 * heads + h) * dim : (2 * heads + h + 1) * dim]

    def one_block(b, carry):
        start = pl.multiple_of(start_ref[micro, b] * BLOCK, BLOCK)
        queries = qkv_ref[b, 0]

        def go(span):
            outs = []
            for h in range(heads):
                key = key_s[h, pl.ds(start, span), :]
                value = value_s[h, pl.ds(start, span), :]
                scores = dot_nt(queries[:, h * dim : (h + 1) * dim], key) * scale
                top = jnp.max(scores, axis=-1, keepdims=True)
                weight = jnp.exp(scores - top)
                total = jnp.sum(weight, axis=-1, keepdims=True)
                probs = low(weight * (1.0 / total))
                outs.append(low(dot_nn(probs, value)))
            out_ref[b, 0] = jnp.concatenate(outs, axis=-1)

        big = big_ref[micro, b]

        @pl.when(big == 1)
        def _():
            go(LARGE)

        @pl.when(big == 0)
        def _():
            go(BLOCK)

        return carry

    lax.fori_loop(0, blocks, one_block, 0)


def self_forward(start, big, qkv, heads, dim):
    blocks, micros = qkv.shape[0], qkv.shape[1]
    span = blocks * BLOCK
    return pl.pallas_call(
        functools.partial(self_forward_kernel, heads, dim),
        out_shape=jax.ShapeDtypeStruct((blocks, micros, BLOCK, heads * dim), jnp.bfloat16),
        grid_spec=pltpu.PrefetchScalarGridSpec(
            num_scalar_prefetch=2,
            grid=(micros,),
            in_specs=[pl.BlockSpec((blocks, 1, BLOCK, 3 * heads * dim), lambda m, s, g: (0, m, 0, 0))],
            out_specs=pl.BlockSpec((blocks, 1, BLOCK, heads * dim), lambda m, s, g: (0, m, 0, 0)),
            scratch_shapes=[
                pltpu.VMEM((heads, span, dim), jnp.bfloat16),
                pltpu.VMEM((heads, span, dim), jnp.bfloat16),
            ],
        ),
        compiler_params=pltpu.CompilerParams(vmem_limit_bytes=VMEM_BYTES),
    )(start, big, qkv)


def self_backward_kernel(
    heads, dim, start_ref, big_ref, qkv_ref, grad_ref, out_ref, sum_ref, key_s, value_s, dq_s, dk_s, dv_s
):
    micro = pl.program_id(0)
    blocks = qkv_ref.shape[0]
    scale = dim ** (-0.5)
    for b in range(blocks):
        for h in range(heads):
            rows = pl.ds(b * BLOCK, BLOCK)
            key_s[h, rows, :] = qkv_ref[b, 0, :, (heads + h) * dim : (heads + h + 1) * dim]
            value_s[h, rows, :] = qkv_ref[b, 0, :, (2 * heads + h) * dim : (2 * heads + h + 1) * dim]
    dk_s[...] = jnp.zeros_like(dk_s)
    dv_s[...] = jnp.zeros_like(dv_s)

    def one_block(b, carry):
        start = pl.multiple_of(start_ref[micro, b] * BLOCK, BLOCK)
        place = pl.multiple_of(b * BLOCK, BLOCK)
        queries = qkv_ref[b, 0]
        grads = grad_ref[b, 0]

        def go(span):
            keep = pl.ds(start, span)
            for h in range(heads):
                query = queries[:, h * dim : (h + 1) * dim]
                grad = grads[:, h * dim : (h + 1) * dim]
                key = key_s[h, keep, :]
                value = value_s[h, keep, :]
                scores = dot_nt(key, query) * scale
                top = jnp.max(scores, axis=0, keepdims=True)
                weight = jnp.exp(scores - top)
                probs = weight * (1.0 / jnp.sum(weight, axis=0, keepdims=True))
                dv_s[h, keep, :] += dot_nn(low(probs), grad)
                grad_probs = dot_nt(value, grad)
                inner = jnp.sum(probs * grad_probs, axis=0, keepdims=True)
                grad_scores = low(probs * (grad_probs - inner) * scale)
                dk_s[h, keep, :] += dot_nn(grad_scores, query)
                dq_s[h, pl.ds(place, BLOCK), :] = dot_tn(grad_scores, key)

        big = big_ref[micro, b]

        @pl.when(big == 1)
        def _():
            go(LARGE)

        @pl.when(big == 0)
        def _():
            go(BLOCK)

        return carry

    lax.fori_loop(0, blocks, one_block, 0)
    for b in range(blocks):
        rows = pl.ds(b * BLOCK, BLOCK)
        out_ref[b, 0] = jnp.concatenate(
            [low(part[h, rows, :]) for part in (dq_s, dk_s, dv_s) for h in range(heads)], axis=-1
        )
    sum_ref[0] = jnp.concatenate(
        [jnp.sum(part[h], axis=0, keepdims=True) for part in (dq_s, dv_s) for h in range(heads)], axis=-1
    )


def self_backward(start, big, qkv, grad, heads, dim):
    blocks, micros = qkv.shape[0], qkv.shape[1]
    span = blocks * BLOCK
    wide = pltpu.VMEM((heads, span, dim), jnp.float32)
    narrow = pltpu.VMEM((heads, span, dim), jnp.bfloat16)
    return pl.pallas_call(
        functools.partial(self_backward_kernel, heads, dim),
        out_shape=(
            jax.ShapeDtypeStruct((blocks, micros, BLOCK, 3 * heads * dim), jnp.bfloat16),
            jax.ShapeDtypeStruct((micros, 1, 2 * heads * dim), jnp.float32),
        ),
        grid_spec=pltpu.PrefetchScalarGridSpec(
            num_scalar_prefetch=2,
            grid=(micros,),
            in_specs=[
                pl.BlockSpec((blocks, 1, BLOCK, 3 * heads * dim), lambda m, s, g: (0, m, 0, 0)),
                pl.BlockSpec((blocks, 1, BLOCK, heads * dim), lambda m, s, g: (0, m, 0, 0)),
            ],
            out_specs=(
                pl.BlockSpec((blocks, 1, BLOCK, 3 * heads * dim), lambda m, s, g: (0, m, 0, 0)),
                pl.BlockSpec((1, 1, 2 * heads * dim), lambda m, s, g: (m, 0, 0)),
            ),
            scratch_shapes=[narrow, narrow, wide, wide, wide],
        ),
        compiler_params=pltpu.CompilerParams(vmem_limit_bytes=VMEM_BYTES),
    )(start, big, qkv, grad)


def cross_forward_kernel(dim, length_ref, query_ref, key_ref, value_ref, out_ref):
    length = length_ref[pl.program_id(0)]
    scale = dim ** (-0.5)
    live = lax.broadcasted_iota(jnp.int32, (BLOCK, CAP_PAD), 1) < length
    outs = []
    for h in range(HEADS):
        part = slice(h * dim, (h + 1) * dim)
        scores = jnp.where(live, dot_nt(query_ref[0, :, part], key_ref[0, :, part]) * scale, neg_large)
        weight = jnp.exp(scores - jnp.max(scores, axis=-1, keepdims=True))
        probs = low(weight * (1.0 / jnp.sum(weight, axis=-1, keepdims=True)))
        outs.append(low(dot_nn(probs, value_ref[0, :, part])))
    out_ref[0] = jnp.concatenate(outs, axis=-1)


def cross_backward_kernel(
    dim, length_ref, query_ref, key_ref, value_ref, grad_ref, dq_ref, dk_ref, dv_ref
):
    length = length_ref[pl.program_id(0)]
    scale = dim ** (-0.5)
    live = lax.broadcasted_iota(jnp.int32, (CAP_PAD, BLOCK), 0) < length
    dq, dk, dv = [], [], []
    for h in range(HEADS):
        part = slice(h * dim, (h + 1) * dim)
        query, key, value, grad = (
            query_ref[0, :, part],
            key_ref[0, :, part],
            value_ref[0, :, part],
            grad_ref[0, :, part],
        )
        scores = jnp.where(live, dot_nt(key, query) * scale, neg_large)
        weight = jnp.exp(scores - jnp.max(scores, axis=0, keepdims=True))
        probs = weight * (1.0 / jnp.sum(weight, axis=0, keepdims=True))
        dv.append(dot_nn(low(probs), grad))
        grad_probs = dot_nt(value, grad)
        inner = jnp.sum(probs * grad_probs, axis=0, keepdims=True)
        grad_scores = low(probs * (grad_probs - inner) * scale)
        dk.append(dot_nn(grad_scores, query))
        dq.append(dot_tn(grad_scores, key))
    dq_ref[0] = jnp.concatenate(dq, axis=-1)
    dk_ref[0] = jnp.concatenate(dk, axis=-1)
    dv_ref[0] = jnp.concatenate(dv, axis=-1)


def cross_call(kernel, length, arrays, outs):
    def spec(array):
        return pl.BlockSpec((1,) + array.shape[1:], lambda m, s: (m, 0, 0))

    return pl.pallas_call(
        kernel,
        out_shape=outs,
        grid_spec=pltpu.PrefetchScalarGridSpec(
            num_scalar_prefetch=1,
            grid=(MICRO,),
            in_specs=[spec(array) for array in arrays],
            out_specs=jax.tree.map(spec, outs),
        ),
        compiler_params=pltpu.CompilerParams(vmem_limit_bytes=VMEM_BYTES),
    )(length, *arrays)


UNIT = 8
SPLIT = 640
PIECE = 3
TILE = 96
TILE_START = 1024
LAG = 3
RING = LAG + 1
HOP_LAG = 2
HOPS = 3 * HOP_LAG + 1
MESH = pl.DeviceIdType.MESH


def my_place():
    row, seq = lax.axis_index("dp"), lax.axis_index("seq")
    return lax.div(row, 2), lax.rem(row, 2), lax.div(seq, 2), lax.rem(seq, 2)


def peer(y, core, z, x):
    return (y * 2 + core, z * 2 + x)


def greet_all(devices, seq_count):
    me = lax.axis_index("dp") * seq_count + lax.axis_index("seq")
    barrier = pltpu.get_barrier_semaphore()

    def one(step, carry):
        other = lax.rem(me + step, devices)
        pl.semaphore_signal(
            barrier,
            inc=1,
            device_id=(lax.div(other, seq_count), lax.rem(other, seq_count)),
            device_id_type=MESH,
        )
        return carry

    lax.fori_loop(1, devices, one, 0)
    pl.semaphore_wait(barrier, devices - 1)


def global_tile(ranges, index):
    tile = index + ranges[0][0]
    at = ranges[0][1] - ranges[0][0]
    for start, stop in ranges[1:]:
        tile = jnp.where(index >= at, index - at + start, tile)
        at += stop - start
    return tile


def reduce_kernel(
    ranges,
    shard_units,
    devices,
    sources,
    receivers,
    *refs,
):
    rows_refs, refs = refs[: len(sources)], list(refs[len(sources) :])
    if receivers:
        block_ref, parts_ref = refs.pop(0), refs.pop(0)
        all_ref, got_ref = refs.pop(1), refs.pop(1)
        refs, push, push_parts = refs[:-6], refs[-6:-3], refs[-3:]
    (
    out_ref,
    own_s,
    core_s,
    first_s,
    second_s,
    first_y_s,
    second_x_s,
    first_two_s,
    second_two_s,
    first_x_s,
    second_y_s,
    third_s,
    along_s,
    leaf_s,
    load_sem,
    core_send,
    core_recv,
    one_send,
    one_recv,
    two_send,
    two_recv,
    z_send,
    z_recv,
    leaf_send,
    leaf_recv,
    ) = refs
    tiles = core_s.shape[0]
    seq_count = devices // 4
    y, core, z, x = my_place()
    me = (y * 2 + core) * seq_count + z * 2 + x
    stride = 5 if tiles % 5 else 3
    half, quarter, eighth = TILE // 2, TILE // 4, TILE // 8
    across_core = peer(y, 1 - core, z, x)
    across_y = peer(1 - y, core, z, x)
    across_x = peer(y, core, z, 1 - x)

    def remote(source, target, send, recv, device):
        return pltpu.make_async_remote_copy(
            src_ref=source,
            dst_ref=target,
            send_sem=send,
            recv_sem=recv,
            device_id=device,
            device_id_type=MESH,
        )

    def core_copy(t, rows_ref=None, start=0):
        source = own_s.at[0] if rows_ref is None else rows_ref.at[pl.ds(start, half)]
        return remote(source, core_s.at[t], core_send.at[t], core_recv.at[t], across_core)

    def load(t, rows_ref=None, start=0):
        slot = lax.rem(t, 2)
        source = rows_refs[-1] if rows_ref is None else rows_ref
        return pltpu.make_async_copy(
            source.at[pl.ds(start, half)], own_s.at[slot], load_sem.at[slot]
        )

    def start_from(copy, t, side):
        index = lax.rem(t * stride, tiles) * 2 + side
        at = 0
        for rows_ref, (start, count) in zip(rows_refs, sources):

            @pl.when((index >= at) & (index < at + count))
            def _(rows_ref=rows_ref, start=start, at=at):
                copy(t, rows_ref, start + (index - at) * half).start()

            at += count

    def first_one(t):
        return remote(
            first_s.at[lax.rem(t, RING), pl.ds((1 - y) * quarter, quarter)],
            first_y_s.at[t],
            one_send.at[lax.rem(t, RING), 0],
            one_recv.at[t, 0],
            across_y,
        )

    def second_one(t, side):
        return remote(
            second_s.at[lax.rem(t, RING), pl.ds(side * quarter + (1 - x) * eighth, eighth)],
            second_x_s.at[t, pl.ds(side * eighth, eighth)],
            one_send.at[lax.rem(t, RING), 1 + side],
            one_recv.at[t, 1 + side],
            across_x,
        )

    def first_two(t):
        return remote(
            first_two_s.at[lax.rem(t, RING), pl.ds((1 - x) * eighth, eighth)],
            first_x_s.at[t],
            two_send.at[lax.rem(t, RING), 0],
            two_recv.at[t, 0],
            across_x,
        )

    def second_two(t):
        return remote(
            second_two_s.at[lax.rem(t, RING), pl.ds((1 - y) * eighth, eighth)],
            second_y_s.at[t],
            two_send.at[lax.rem(t, RING), 1],
            two_recv.at[t, 1],
            across_y,
        )

    def each_three(t, visit):
        tile = global_tile(ranges, lax.rem(t * stride, tiles))

        def one(index, carry):
            row = index * PIECE
            unit = TILE_START + tile * TILE + ((core * 2 + y) * 2 + x) * eighth + row
            owner = lax.div(unit, shard_units)
            at = unit - owner * shard_units

            @pl.when(at + PIECE <= shard_units)
            def _():
                visit(row, index, PIECE, owner, at)

            @pl.when(at + PIECE > shard_units)
            def _():
                for part in range(PIECE):
                    over = at + part >= shard_units
                    visit(
                        row + part,
                        4 + part,
                        1,
                        jnp.where(over, owner + 1, owner),
                        jnp.where(over, at + part - shard_units, at + part),
                    )

            return carry

        lax.fori_loop(0, eighth // PIECE, one, 0)

    def z_copy(t, row, slot, count, way):
        other = (jnp.maximum(z - 1, 0), jnp.minimum(z + 1, 3))[way]
        return remote(
            third_s.at[lax.rem(t, HOPS), pl.ds(row, count)],
            along_s.at[t, way, pl.ds(row, count)],
            z_send.at[lax.rem(t, HOPS), slot],
            z_recv.at[t, way, slot],
            peer(y, core, other, x),
        )

    def arrived(t, row, slot, count, way):
        part = along_s.at[t, way, pl.ds(row, count)]
        pltpu.make_async_copy(part, part, z_recv.at[t, way, slot]).wait()

    def total_of(t, row, count, *ways):
        total = third_s[lax.rem(t, HOPS), pl.ds(row, count)].astype(jnp.float32)
        for way in ways:
            total = total + along_s[t, way, pl.ds(row, count)].astype(jnp.float32)
        return total.astype(jnp.bfloat16)

    def owner_plane(owner):
        return lax.rem(lax.div(owner, 2), 4)

    def hop(t, number):
        def visit(row, slot, count, owner, at):
            to = owner_plane(owner)
            for way, here, more in (
                (0, (z > to) & (3 - z == number), z < 3),
                (1, (z < to) & (z == number), z > 0),
            ):

                @pl.when(here)
                def _(way=way, more=more):
                    @pl.when(more)
                    def _():
                        arrived(t, row, slot, count, way)
                        total = total_of(t, row, count, way)
                        third_s[lax.rem(t, HOPS), pl.ds(row, count)] = total

                    z_copy(t, row, slot, count, way).start()

        each_three(t, visit)

    def hand_over(t):
        def visit(row, slot, count, owner, at):
            to = owner_plane(owner)

            @pl.when(to == z)
            def _():
                for here, ways in (
                    (z == 0, (0,)),
                    ((z > 0) & (z < 3), (0, 1)),
                    (z == 3, (1,)),
                ):

                    @pl.when(here)
                    def _(ways=ways):
                        for way in ways:
                            arrived(t, row, slot, count, way)
                        leaf_s[t, pl.ds(row, count)] = total_of(t, row, count, *ways)

                leaf_copy(t, row, slot, count, owner, at, 0)

            @pl.when(to != z)
            def _():
                z_copy(t, row, slot, count, 0).wait_send()

        each_three(t, visit)

    def leaf_copy(t, row, slot, count, owner, at, stage):
        source = leaf_s.at[t, pl.ds(row, count)]
        target = out_ref.at[pl.ds(at, count)]
        sending = remote(
            source,
            target,
            leaf_send.at[t, slot],
            leaf_recv.at[at],
            (lax.div(owner, seq_count), lax.rem(owner, seq_count)),
        )

        @pl.when(owner != me)
        def _():
            if stage == 0:
                sending.start()
            else:
                sending.wait_send()

        if stage == 0:

            @pl.when(owner == me)
            def _():
                pltpu.make_async_copy(source, target, leaf_recv.at[at]).start()

    def leaf_done(t):
        def visit(row, slot, count, owner, at):
            @pl.when(owner_plane(owner) == z)
            def _():
                leaf_copy(t, row, slot, count, owner, at, 1)

        each_three(t, visit)

    for t in range(min(2, tiles)):
        start_from(load, t, core)
    greet_all(devices, seq_count)

    def start_core(t, carry):
        start_from(core_copy, t, 1 - core)
        return carry

    lax.fori_loop(0, tiles, start_core, 0)
    if receivers:
        start_push(parts_ref, got_ref, devices, devices, me, *push_parts, scatter=True)
        start_push(block_ref, all_ref, devices, receivers, me, *push)

    def one_step(step, carry):
        @pl.when(step < tiles)
        def _():
            t = step
            slot = lax.rem(t, RING)
            load(t).wait()
            core_copy(t).wait_recv()

            def one(index, inner):
                at = pl.ds(index * 4, 4)
                total = own_s[lax.rem(t, 2), at].astype(jnp.float32) + core_s[t, at].astype(jnp.float32)
                total = total.astype(jnp.bfloat16)
                first_s[slot, at] = total[:, :, :SPLIT]
                second_s[slot, at] = total[:, :, SPLIT:]
                return inner

            lax.fori_loop(0, half // 4, one, 0)
            first_one(t).start()
            second_one(t, 0).start()
            second_one(t, 1).start()

            @pl.when(t + 2 < tiles)
            def _():
                start_from(load, t + 2, core)

        @pl.when((step >= LAG) & (step < tiles + LAG))
        def _():
            t = step - LAG
            slot = lax.rem(t, RING)
            first_one(t).wait()

            def one(index, inner):
                at = pl.ds(index * 4, 4)
                mine = first_s[slot, pl.ds(y * quarter + index * 4, 4)].astype(jnp.float32)
                total = mine + first_y_s[t, at].astype(jnp.float32)
                first_two_s[slot, at] = total.astype(jnp.bfloat16)
                return inner

            lax.fori_loop(0, quarter // 4, one, 0)
            first_two(t).start()
            for side in range(2):
                second_one(t, side).wait()

                def two(index, inner):
                    mine = second_s[slot, pl.ds(side * quarter + x * eighth + index * 4, 4)]
                    at = pl.ds(side * eighth + index * 4, 4)
                    total = mine.astype(jnp.float32) + second_x_s[t, at].astype(jnp.float32)
                    second_two_s[slot, at] = total.astype(jnp.bfloat16)
                    return inner

                lax.fori_loop(0, eighth // 4, two, 0)
            second_two(t).start()

        @pl.when((step >= 2 * LAG) & (step < tiles + 2 * LAG))
        def _():
            t = step - 2 * LAG
            slot = lax.rem(t, RING)
            first_two(t).wait()
            second_two(t).wait()

            def one(index, inner):
                at = pl.ds(index * 4, 4)
                mine = first_two_s[slot, pl.ds(x * eighth + index * 4, 4)].astype(jnp.float32)
                total = mine + first_x_s[t, at].astype(jnp.float32)
                third_s[lax.rem(t, HOPS), at, :, :SPLIT] = total.astype(jnp.bfloat16)
                mine = second_two_s[slot, pl.ds(y * eighth + index * 4, 4)].astype(jnp.float32)
                total = mine + second_y_s[t, at].astype(jnp.float32)
                third_s[lax.rem(t, HOPS), at, :, SPLIT:] = total.astype(jnp.bfloat16)
                return inner

            lax.fori_loop(0, eighth // 4, one, 0)

        for number in range(4):
            old = step - 2 * LAG - number * HOP_LAG

            @pl.when((old >= 0) & (old < tiles))
            def _(old=old, number=number):
                if number < 3:
                    hop(old, number)
                else:
                    hand_over(old)

        return carry

    lax.fori_loop(0, tiles + 2 * LAG + 3 * HOP_LAG, one_step, 0)

    def finish(t, carry):
        core_copy(t).wait_send()
        leaf_done(t)
        return carry

    lax.fori_loop(0, tiles, finish, 0)
    if receivers:
        finish_push(parts_ref, got_ref, devices, devices, me, *push_parts, scatter=True)
        finish_push(block_ref, all_ref, devices, receivers, me, *push)
    far = TILE_START - TILE * (TILE_START // TILE)
    begin = me * shard_units
    first_at = lax.rem(PIECE - lax.rem(begin + PIECE - far % PIECE, PIECE), PIECE)

    def arrive(index, count):
        unit = begin + index
        inside = False
        for start, stop in ranges:
            low_end, high_end = TILE_START + start * TILE, TILE_START + stop * TILE
            inside = inside | ((unit >= low_end) & (unit < high_end))

        @pl.when(inside)
        def _():
            part = out_ref.at[pl.ds(index, count)]
            pltpu.make_async_copy(part, part, leaf_recv.at[index]).wait()

    def arrive_three(step, carry):
        index = first_at + step * PIECE

        @pl.when(index + PIECE <= shard_units)
        def _():
            arrive(index, PIECE)

        return carry

    steps = shard_units // PIECE
    lax.fori_loop(0, steps, arrive_three, 0)
    covered = first_at + lax.div(shard_units - first_at, PIECE) * PIECE
    for step in range(PIECE - 1):

        @pl.when(step < first_at)
        def _():
            arrive(step, 1)

        @pl.when(covered + step < shard_units)
        def _():
            arrive(covered + step, 1)


def push_copy(block_ref, all_ref, devices, me, step, send_sem, recv_sem, scatter):
    seq_count = devices // 4
    other = lax.rem(me + step, devices)
    return other, pltpu.make_async_remote_copy(
        src_ref=block_ref.at[other] if scatter else block_ref,
        dst_ref=all_ref.at[me],
        send_sem=send_sem.at[step],
        recv_sem=recv_sem.at[me],
        device_id=(lax.div(other, seq_count), lax.rem(other, seq_count)),
        device_id_type=MESH,
    )


def start_push(block_ref, all_ref, devices, receivers, me, send_sem, recv_sem, keep_sem, scatter=False):
    own_ref = block_ref.at[me] if scatter else block_ref

    @pl.when(me < receivers)
    def _():
        pltpu.make_async_copy(own_ref, all_ref.at[me], keep_sem).start()

    def send(step, carry):
        other, sending = push_copy(
            block_ref, all_ref, devices, me, step, send_sem, recv_sem, scatter
        )

        @pl.when(other < receivers)
        def _():
            sending.start()

        return carry

    lax.fori_loop(1, devices, send, 0)


def finish_push(
    block_ref, all_ref, devices, receivers, me, send_sem, recv_sem, keep_sem, scatter=False
):
    own_ref = block_ref.at[me] if scatter else block_ref

    @pl.when(me < receivers)
    def _():
        pltpu.make_async_copy(own_ref, all_ref.at[me], keep_sem).wait()

    def finish(step, carry):
        other, sending = push_copy(
            block_ref, all_ref, devices, me, step, send_sem, recv_sem, scatter
        )

        @pl.when(other < receivers)
        def _():
            sending.wait_send()

        source = lax.rem(me + devices - step, devices)

        @pl.when(me < receivers)
        def _():
            pltpu.make_async_copy(own_ref, all_ref.at[source], recv_sem.at[source]).wait()

        return carry

    lax.fori_loop(1, devices, finish, 0)


def push_sems(devices):
    dma = pltpu.SemaphoreType.DMA
    return [dma((devices,)), dma((devices,)), dma]


def reduce_rows(ranges, shard_units, devices, collective_id, pieces, blocks=(), receivers=0):
    tiles = sum(stop - start for start, stop in ranges)
    width = pieces[0][0].shape[1]
    sources = tuple(piece[1:] for piece in pieces)
    assert sum(count for _, count in sources) == 2 * tiles
    half, quarter, eighth = TILE // 2, TILE // 4, TILE // 8
    rest = width - SPLIT

    def vmem(*shape):
        return pltpu.VMEM(shape, jnp.bfloat16)

    dma = pltpu.SemaphoreType.DMA
    outs = [jax.ShapeDtypeStruct((shard_units, UNIT, width), jnp.bfloat16)]
    if blocks:
        outs.append(jax.ShapeDtypeStruct((devices,) + blocks[0].shape, blocks[0].dtype))
        outs.append(jax.ShapeDtypeStruct(blocks[1].shape, blocks[1].dtype))
    out = pl.pallas_call(
        functools.partial(reduce_kernel, ranges, shard_units, devices, sources, receivers),
        out_shape=outs,
        in_specs=[pl.BlockSpec(memory_space=pl.ANY)] * (len(pieces) + len(blocks)),
        out_specs=[pl.BlockSpec(memory_space=pl.ANY)] * len(outs),
        scratch_shapes=[
            vmem(2, half, UNIT, width),
            vmem(tiles, half, UNIT, width),
            vmem(RING, half, UNIT, SPLIT),
            vmem(RING, half, UNIT, rest),
            vmem(tiles, quarter, UNIT, SPLIT),
            vmem(tiles, quarter, UNIT, rest),
            vmem(RING, quarter, UNIT, SPLIT),
            vmem(RING, quarter, UNIT, rest),
            vmem(tiles, eighth, UNIT, SPLIT),
            vmem(tiles, eighth, UNIT, rest),
            vmem(HOPS, eighth, UNIT, width),
            vmem(tiles, 2, eighth, UNIT, width),
            vmem(tiles, eighth, UNIT, width),
            dma((2,)),
            dma((tiles,)),
            dma((tiles,)),
            dma((RING, 3)),
            dma((tiles, 3)),
            dma((RING, 2)),
            dma((tiles, 2)),
            dma((HOPS, 7)),
            dma((tiles, 2, 7)),
            dma((tiles, 7)),
            dma((shard_units,)),
        ]
        + (push_sems(devices) + push_sems(devices) if blocks else []),
        compiler_params=pltpu.CompilerParams(
            collective_id=collective_id, has_side_effects=True, vmem_limit_bytes=VMEM_BYTES
        ),
    )(*[piece[0].reshape(-1, UNIT, width) for piece in pieces], *blocks)
    return out if blocks else out[0]


STRIDE = 3
Z_LAG = 2
Z_RING = 3 * Z_LAG + 1


def gather_kernel(
    openings,
    ahead,
    devices,
    shard_ref,
    out_ref,
    later_ref,
    deal_send,
    deal_recv,
    z_send,
    z_recv,
    one_send,
    one_recv,
    two_send,
    two_recv,
    core_send,
    core_recv,
):
    shard_units = shard_ref.shape[0]
    seq_count = devices // 4
    width = shard_ref.shape[2]
    tiles = out_ref.shape[0] // TILE
    later_tiles = later_ref.shape[0] // TILE
    streams = ((openings[0], tiles, out_ref, 0), (openings[1], later_tiles, later_ref, tiles))
    y, core, z, x = my_place()
    me = (y * 2 + core) * seq_count + z * 2 + x
    half, quarter, eighth = TILE // 2, TILE // 4, TILE // 8
    leaves = TILE // PIECE
    upward = peer(y, core, jnp.minimum(z + 1, 3), x)
    downward = peer(y, core, jnp.maximum(z - 1, 0), x)

    def bounds(stream):
        begin = me * shard_units - stream[0]
        finish = begin + shard_units
        return begin, finish, lax.div(begin + PIECE - 1, PIECE), lax.div(finish, PIECE)

    def deal_some(stream, stage, three, part, count):
        begin = bounds(stream)[0]
        ref = stream[2]
        tile = lax.div(three, leaves)
        leaf = three - tile * leaves
        eight = lax.div(leaf, 4)
        slot = leaf - eight * 4 if count == PIECE else 4 + part
        holder_core = lax.div(eight, 4)
        holder_y = lax.rem(lax.div(eight, 2), 2)
        holder_x = lax.rem(eight, 2)
        holder = (holder_y * 2 + holder_core) * seq_count + z * 2 + holder_x
        index = three * PIECE + part - begin
        source = shard_ref.at[pl.ds(index, count)]
        target = ref.at[pl.ds(three * PIECE + part, count)]
        recv = deal_recv.at[stream[3] + tile, slot]
        sending = pltpu.make_async_remote_copy(
            src_ref=source,
            dst_ref=target,
            send_sem=deal_send.at[0 if stream[3] == 0 else 1, index],
            recv_sem=recv,
            device_id=peer(holder_y, holder_core, z, holder_x),
            device_id_type=MESH,
        )

        @pl.when(holder != me)
        def _():
            if stage == 0:
                sending.start()
            else:
                sending.wait_send()

        if stage == 0:

            @pl.when(holder == me)
            def _():
                pltpu.make_async_copy(source, target, recv).start()

    def deal_between(stream, stage, low_three, count, base):
        begin, finish, first_three, last_three = bounds(stream)
        base = first_three if base is None else base

        @pl.when((low_three <= last_three) & (low_three + count >= first_three))
        def _():
            def one(step, carry):
                three = base + step

                @pl.when(
                    (three >= first_three)
                    & (three < last_three)
                    & (three >= low_three)
                    & (three < low_three + count)
                )
                def _():
                    deal_some(stream, stage, three, 0, PIECE)

                return carry

            lax.fori_loop(0, min(count, shard_units // PIECE + 1), one, 0)
            for step in range(PIECE - 1):
                three = first_three - 1
                here = (three >= low_three) & (three < low_three + count)

                @pl.when(here & (begin + step < first_three * PIECE))
                def _(three=three):
                    deal_some(stream, stage, three, begin + step - three * PIECE, 1)

                three = last_three
                here = (three >= low_three) & (three < low_three + count)

                @pl.when(here & (three * PIECE + step < finish))
                def _(three=three):
                    deal_some(stream, stage, three, step, 1)

    def deal_tile(stream, step):
        low_three = tile_at(step, stream[1]) * leaves
        deal_between(stream, 0, low_three, leaves, low_three)

    def each_three(stream, t, visit):
        def one(index, carry):
            row = t * TILE + ((core * 2 + y) * 2 + x) * eighth + index * PIECE
            unit = stream[0] + row
            owner = lax.div(unit, shard_units)
            at = unit - owner * shard_units

            @pl.when(at + PIECE <= shard_units)
            def _():
                visit(row, index, PIECE, lax.rem(lax.div(owner, 2), 4))

            @pl.when(at + PIECE > shard_units)
            def _():
                for part in range(PIECE):
                    holder = jnp.where(at + part >= shard_units, owner + 1, owner)
                    visit(row + part, 4 + part, 1, lax.rem(lax.div(holder, 2), 4))

            return carry

        lax.fori_loop(0, eighth // PIECE, one, 0)

    def wait_units(ref, count, sem):
        part = ref.at[pl.ds(0, count)]
        pltpu.make_async_copy(part, part, sem).wait()

    def z_copy(stream, step, row, slot, count, way):
        part = stream[2].at[pl.ds(row, count)]
        which = 0 if stream[3] == 0 else 1
        return pltpu.make_async_remote_copy(
            src_ref=part,
            dst_ref=part,
            send_sem=z_send.at[which, lax.rem(step, Z_RING), slot, way],
            recv_sem=z_recv.at[stream[3] + tile_at(step, stream[1]), slot],
            device_id=(upward, downward)[way],
            device_id_type=MESH,
        )

    def along_z(stream, step, distance):
        t = tile_at(step, stream[1])

        def visit(row, slot, count, owner_z):
            @pl.when(jnp.abs(owner_z - z) == distance)
            def _():
                sem = deal_recv if distance == 0 else z_recv
                wait_units(out_ref, count, sem.at[stream[3] + t, slot])

                @pl.when((owner_z <= z) & (z < 3))
                def _():
                    z_copy(stream, step, row, slot, count, 0).start()

                @pl.when((owner_z >= z) & (z > 0))
                def _():
                    z_copy(stream, step, row, slot, count, 1).start()

        each_three(stream, t, visit)

    def along_z_done(stream, step):
        t = tile_at(step, stream[1])

        def visit(row, slot, count, owner_z):
            @pl.when((owner_z <= z) & (z < 3))
            def _():
                z_copy(stream, step, row, slot, count, 0).wait_send()

            @pl.when((owner_z >= z) & (z > 0))
            def _():
                z_copy(stream, step, row, slot, count, 1).wait_send()

        each_three(stream, t, visit)

    def z_stage(stream, step):
        for distance in range(4):
            old = step - distance * Z_LAG

            @pl.when((old >= 0) & (old < stream[1]))
            def _(old=old, distance=distance):
                along_z(stream, old, distance)
                if distance == 3:
                    along_z_done(stream, old)

    spreading = spread_steps(
        out_ref, one_send, one_recv, two_send, two_recv, core_send, core_recv
    )
    main, late = streams
    greet_all(devices, seq_count)
    for step in range(min(ahead, tiles)):
        deal_tile(main, step)
    for step in range(min(ahead, later_tiles)):
        deal_tile(late, step)

    def one_step(step, carry):
        @pl.when(step + ahead < tiles)
        def _():
            deal_tile(main, step + ahead)

        @pl.when(step + ahead < later_tiles)
        def _():
            deal_tile(late, step + ahead)

        z_stage(main, step)
        spreading(step - 3 * Z_LAG)
        z_stage(late, step)
        return carry

    lax.fori_loop(0, tiles + 3 * LAG + 3 * Z_LAG, one_step, 0)
    for stream in streams:
        deal_between(stream, 1, 0, stream[1] * leaves, None)


def tile_at(step, tiles):
    return lax.rem(step * STRIDE, tiles)


def spread_steps(out_ref, one_send, one_recv, two_send, two_recv, core_send, core_recv):
    tiles = out_ref.shape[0] // TILE
    width = out_ref.shape[2]
    y, core, z, x = my_place()
    half, quarter, eighth = TILE // 2, TILE // 4, TILE // 8
    left, right = pl.ds(0, SPLIT), pl.ds(SPLIT, width - SPLIT)
    whole = pl.ds(0, width)
    across_core = peer(y, 1 - core, z, x)
    across_y = peer(1 - y, core, z, x)
    across_x = peer(y, core, z, 1 - x)

    def remote(start, count, columns, send, recv, device):
        part = out_ref.at[pl.ds(start, count), :, columns]
        return pltpu.make_async_remote_copy(
            src_ref=part,
            dst_ref=part,
            send_sem=send,
            recv_sem=recv,
            device_id=device,
            device_id_type=MESH,
        )

    def block(t, y_at, x_at):
        return t * TILE + ((core * 2 + y_at) * 2 + x_at) * eighth

    def one_first(step):
        t = tile_at(step, tiles)
        sems = (one_send.at[lax.rem(step, RING), 0], one_recv.at[t, 0])
        return remote(block(t, y, x), eighth, left, *sems, across_x)

    def one_second(step):
        t = tile_at(step, tiles)
        sems = (one_send.at[lax.rem(step, RING), 1], one_recv.at[t, 1])
        return remote(block(t, y, x), eighth, right, *sems, across_y)

    def two_first(step):
        t = tile_at(step, tiles)
        sems = (two_send.at[lax.rem(step, RING), 0], two_recv.at[t, 0])
        return remote(block(t, y, 0), quarter, left, *sems, across_y)

    def two_second(step, side):
        t = tile_at(step, tiles)
        sems = (two_send.at[lax.rem(step, RING), 1 + side], two_recv.at[t, 1 + side])
        return remote(block(t, side, x), eighth, right, *sems, across_x)

    def core_copy(step):
        t = tile_at(step, tiles)
        sems = (core_send.at[lax.rem(step, RING)], core_recv.at[t])
        return remote(t * TILE + core * half, half, whole, *sems, across_core)

    def go(step):
        @pl.when((step >= 0) & (step < tiles))
        def _():
            one_first(step).start()
            one_second(step).start()

        @pl.when((step >= LAG) & (step < tiles + LAG))
        def _():
            old = step - LAG
            one_first(old).wait()
            two_first(old).start()
            one_second(old).wait()
            for side in range(2):
                two_second(old, side).start()

        @pl.when((step >= 2 * LAG) & (step < tiles + 2 * LAG))
        def _():
            old = step - 2 * LAG
            two_first(old).wait()
            for side in range(2):
                two_second(old, side).wait()
            core_copy(old).start()

        @pl.when(step >= 3 * LAG)
        def _():
            core_copy(step - 3 * LAG).wait()

    return go


def spread_sems(tiles):
    dma = pltpu.SemaphoreType.DMA
    return [
        dma((RING, 2)),
        dma((tiles, 2)),
        dma((RING, 3)),
        dma((tiles, 3)),
        dma((RING,)),
        dma((tiles,)),
    ]


def spread_kernel(devices, rows_ref, block_ref, out_ref, all_ref, *sems):
    seq_count = devices // 4
    me = lax.axis_index("dp") * seq_count + lax.axis_index("seq")
    sems, push = sems[:-3], sems[-3:]
    greet_all(devices, seq_count)
    start_push(block_ref, all_ref, devices, devices, me, *push)
    spreading = spread_steps(out_ref, *sems)

    def one_step(step, carry):
        spreading(step)
        return carry

    lax.fori_loop(0, out_ref.shape[0] // TILE + 3 * LAG, one_step, 0)
    finish_push(block_ref, all_ref, devices, devices, me, *push)


def spread_rows(rows, block, devices, collective_id):
    return pl.pallas_call(
        functools.partial(spread_kernel, devices),
        out_shape=(
            jax.ShapeDtypeStruct(rows.shape, rows.dtype),
            jax.ShapeDtypeStruct((devices,) + block.shape, block.dtype),
        ),
        in_specs=[pl.BlockSpec(memory_space=pl.ANY)] * 2,
        out_specs=(pl.BlockSpec(memory_space=pl.ANY), pl.BlockSpec(memory_space=pl.ANY)),
        scratch_shapes=spread_sems(rows.shape[0] // TILE) + push_sems(devices),
        input_output_aliases={0: 0},
        compiler_params=pltpu.CompilerParams(
            collective_id=collective_id, has_side_effects=True, vmem_limit_bytes=VMEM_BYTES
        ),
    )(rows, block)


def gather_rows(openings, counts, ahead, devices, collective_id, shard):
    units, _, width = shard.shape
    assert all(count % STRIDE for count in counts) and counts[1] <= counts[0]
    dma = pltpu.SemaphoreType.DMA
    anywhere = pl.BlockSpec(memory_space=pl.ANY)
    return pl.pallas_call(
        functools.partial(gather_kernel, openings, ahead, devices),
        out_shape=[
            jax.ShapeDtypeStruct((count * TILE, UNIT, width), jnp.bfloat16) for count in counts
        ],
        in_specs=[anywhere],
        out_specs=[anywhere, anywhere],
        scratch_shapes=[
            dma((2, units)),
            dma((sum(counts), 7)),
            dma((2, Z_RING, 7, 2)),
            dma((sum(counts), 7)),
        ]
        + spread_sems(counts[0]),
        compiler_params=pltpu.CompilerParams(
            collective_id=collective_id, has_side_effects=True, vmem_limit_bytes=VMEM_BYTES
        ),
    )(shard)


def share_kernel(devices, block_ref, out_ref, *sems):
    seq_count = devices // 4
    me = lax.axis_index("dp") * seq_count + lax.axis_index("seq")
    greet_all(devices, seq_count)
    start_push(block_ref, out_ref, devices, devices, me, *sems)
    finish_push(block_ref, out_ref, devices, devices, me, *sems)


def share(block, devices, collective_id):
    return pl.pallas_call(
        functools.partial(share_kernel, devices),
        out_shape=jax.ShapeDtypeStruct((devices,) + block.shape, block.dtype),
        in_specs=[pl.BlockSpec(memory_space=pltpu.VMEM)],
        out_specs=pl.BlockSpec(memory_space=pltpu.VMEM),
        scratch_shapes=push_sems(devices),
        compiler_params=pltpu.CompilerParams(
            collective_id=collective_id, has_side_effects=True, vmem_limit_bytes=16 * 1024 * 1024
        ),
    )(block)


def contrast_kernel(pooled_ref, pick_ref, row_ref, col_ref, scale_ref, pool_ref, text_ref, loss_ref):
    count = pick_ref.shape[1]
    scale = scale_ref[0, 0] / contrastive_sharpness_divisor
    diagonal = lax.broadcasted_iota(jnp.int32, (count, count), 0) == lax.broadcasted_iota(
        jnp.int32, (count, count), 1
    )
    loss = jnp.zeros((1, 1), jnp.float32)
    for m in range(MICRO):
        row = row_ref[m]
        col = col_ref[m] > 0.0
        image = jnp.dot(
            pick_ref[m], pooled_ref[m], precision=exact, preferred_element_type=jnp.float32
        )
        words = pooled_ref[MICRO + m]
        image_norm = lax.rsqrt(jnp.sum(image * image, axis=-1, keepdims=True) + norm_eps)
        words_norm = lax.rsqrt(jnp.sum(words * words, axis=-1, keepdims=True) + norm_eps)
        image = image * image_norm
        words = words * words_norm
        cosines = lax.dot_general(
            image,
            words,
            (((1,), (1,)), ((), ())),
            precision=exact,
            preferred_element_type=jnp.float32,
        )
        cosines = jnp.where(col, cosines / contrastive_sharpness_divisor, neg_large)
        top = jnp.max(cosines, axis=-1, keepdims=True)
        weight = jnp.exp(cosines - top)
        total = jnp.sum(weight, axis=-1, keepdims=True)
        matched = jnp.sum(jnp.where(diagonal, cosines, 0.0), axis=-1, keepdims=True)
        lost = jnp.where(row > 0.0, top + jnp.log(total) - matched, 0.0)
        loss = loss + jnp.sum(lost, axis=0, keepdims=True)
        grad = weight / total - jnp.where(diagonal, 1.0, 0.0)
        grad = jnp.where((row > 0.0) & col, grad * scale, 0.0)
        grad_image = jnp.dot(grad, words, precision=exact, preferred_element_type=jnp.float32)
        grad_words = lax.dot_general(
            grad,
            image,
            (((0,), (0,)), ((), ())),
            precision=exact,
            preferred_element_type=jnp.float32,
        )
        inner = jnp.sum(image * grad_image, axis=-1, keepdims=True)
        pool_ref[m] = image_norm * (grad_image - image * inner)
        inner = jnp.sum(words * grad_words, axis=-1, keepdims=True)
        text_ref[m] = words_norm * (grad_words - words * inner)
    loss_ref[...] = jnp.broadcast_to(loss, loss_ref.shape)


def contrast(pooled, pick, valid, scale):
    count, width = pooled.shape[1], pooled.shape[2]
    grads = jax.ShapeDtypeStruct((MICRO, count, width), jnp.float32)
    return pl.pallas_call(
        contrast_kernel,
        out_shape=(grads, grads, jax.ShapeDtypeStruct((1, 128), jnp.float32)),
        compiler_params=pltpu.CompilerParams(vmem_limit_bytes=VMEM_BYTES),
    )(pooled, pick, valid[:, :, None], valid[:, None, :], scale.reshape(1, 1))


def joint_forward_kernel(rows_ref, matrix_ref, bias_ref, out_ref):
    part, width = matrix_ref.shape[2], matrix_ref.shape[3]
    matrix = matrix_ref[...].reshape(3 * part, width)
    out_ref[0] = low(dot_nt(rows_ref[...], matrix) + bias_ref[0])


def joint_forward(rows, matrix, bias):
    count, width = rows.shape
    groups, _, columns = bias.shape
    return pl.pallas_call(
        joint_forward_kernel,
        out_shape=jax.ShapeDtypeStruct((groups, count, columns), jnp.bfloat16),
        grid=(groups,),
        in_specs=[
            pl.BlockSpec((count, width), lambda j: (0, 0)),
            pl.BlockSpec((3, 1, columns // 3, width), lambda j: (0, j, 0, 0)),
            pl.BlockSpec((1, 1, columns), lambda j: (j, 0, 0)),
        ],
        out_specs=pl.BlockSpec((1, count, columns), lambda j: (j, 0, 0)),
        compiler_params=pltpu.CompilerParams(vmem_limit_bytes=VMEM_BYTES),
    )(rows, matrix.reshape(3, groups, columns // 3, width), bias)


def joint_backward_kernel(grad_ref, matrix_ref, rows_ref, out_ref, weight_ref):
    part, width = matrix_ref.shape[2], matrix_ref.shape[3]
    grad = grad_ref[0]
    term = dot_nn(grad, matrix_ref[...].reshape(3 * part, width))
    weight_ref[...] = low(dot_tn(grad, rows_ref[...])).reshape(3, 1, part, width)

    @pl.when(pl.program_id(0) == 0)
    def _():
        out_ref[...] = term

    @pl.when(pl.program_id(0) > 0)
    def _():
        out_ref[...] += term


def joint_backward(grad, matrix, rows):
    groups, count, columns = grad.shape
    width = rows.shape[1]
    part = columns // 3
    out, weight = pl.pallas_call(
        joint_backward_kernel,
        out_shape=(
            jax.ShapeDtypeStruct((count, width), jnp.float32),
            jax.ShapeDtypeStruct((3, groups, part, width), jnp.bfloat16),
        ),
        grid=(groups,),
        in_specs=[
            pl.BlockSpec((1, count, columns), lambda j: (j, 0, 0)),
            pl.BlockSpec((3, 1, part, width), lambda j: (0, j, 0, 0)),
            pl.BlockSpec((count, width), lambda j: (0, 0)),
        ],
        out_specs=(
            pl.BlockSpec((count, width), lambda j: (0, 0)),
            pl.BlockSpec((3, 1, part, width), lambda j: (0, j, 0, 0)),
        ),
        compiler_params=pltpu.CompilerParams(vmem_limit_bytes=VMEM_BYTES),
    )(grad, matrix.reshape(3, groups, part, width), rows)
    return out, weight.reshape(3 * groups * part, width)


FEED_BLOCK = 768


def feed_forward_kernel(rows_ref, up_ref, down_ref, b_up_ref, b_down_ref, before_ref, act_ref, out_ref):
    before = dot_nt(rows_ref[...], up_ref[...]) + b_up_ref[0]
    before_ref[...] = before
    act = low(gelu_tanh(before))
    act_ref[...] = act
    term = dot_nn(act, down_ref[...])

    @pl.when(pl.program_id(0) == 0)
    def _():
        out_ref[...] = term + b_down_ref[...]

    @pl.when(pl.program_id(0) > 0)
    def _():
        out_ref[...] += term


def feed_specs(count, width, up_start, down_start):
    return (
        pl.BlockSpec((count, width), lambda j: (0, 0)),
        pl.BlockSpec((FEED_BLOCK, width), lambda j: (up_start + j, 0)),
        pl.BlockSpec((FEED_BLOCK, width), lambda j: (down_start + j, 0)),
        pl.BlockSpec((1, 1, FEED_BLOCK), lambda j: (j, 0, 0)),
        pl.BlockSpec((count, FEED_BLOCK), lambda j: (0, j)),
    )


def feed_forward(rows, up, up_start, down, down_start, b_up, b_down):
    count, width = rows.shape
    whole, up_spec, down_spec, line, column = feed_specs(count, width, up_start, down_start)
    return pl.pallas_call(
        feed_forward_kernel,
        out_shape=(
            jax.ShapeDtypeStruct((count, FF), jnp.float32),
            jax.ShapeDtypeStruct((count, FF), jnp.bfloat16),
            jax.ShapeDtypeStruct((count, width), jnp.float32),
        ),
        grid=(FF // FEED_BLOCK,),
        in_specs=[whole, up_spec, down_spec, line, pl.BlockSpec((1, width), lambda j: (0, 0))],
        out_specs=(column, column, whole),
        compiler_params=pltpu.CompilerParams(vmem_limit_bytes=VMEM_BYTES),
    )(rows, up, down, b_up.reshape(-1, 1, FEED_BLOCK), b_down)


def feed_backward_kernel(
    grad_ref, up_ref, down_ref, before_ref, act_ref, rows_ref, out_ref, w_up_ref, w_down_ref, sum_ref
):
    grad = grad_ref[...]
    before = before_ref[...]
    factor = math.sqrt(2.0 / math.pi)
    square = before * before
    bend = jnp.tanh(factor * (before + 0.044715 * (square * before)))
    slope = 0.5 * (1.0 + bend) + (0.5 * factor) * before * (1.0 - bend * bend) * (
        1.0 + (3.0 * 0.044715) * square
    )
    grad_up = dot_nt(grad, down_ref[...]) * slope
    sum_ref[0] = jnp.sum(grad_up, axis=0, keepdims=True)
    grad_up = low(grad_up)
    w_up_ref[...] = low(dot_tn(grad_up, rows_ref[...]))
    w_down_ref[...] = low(dot_tn(act_ref[...], grad))
    term = dot_nn(grad_up, up_ref[...])

    @pl.when(pl.program_id(0) == 0)
    def _():
        out_ref[...] = term

    @pl.when(pl.program_id(0) > 0)
    def _():
        out_ref[...] += term


def feed_backward(grad, up, up_start, down, down_start, before, act, rows):
    count, width = rows.shape
    whole, up_spec, down_spec, line, column = feed_specs(count, width, up_start, down_start)
    block = pl.BlockSpec((FEED_BLOCK, width), lambda j: (j, 0))
    return pl.pallas_call(
        feed_backward_kernel,
        out_shape=(
            jax.ShapeDtypeStruct((count, width), jnp.float32),
            jax.ShapeDtypeStruct((FF, width), jnp.bfloat16),
            jax.ShapeDtypeStruct((FF, width), jnp.bfloat16),
            jax.ShapeDtypeStruct((FF // FEED_BLOCK, 1, FEED_BLOCK), jnp.float32),
        ),
        grid=(FF // FEED_BLOCK,),
        in_specs=[whole, up_spec, down_spec, column, column, whole],
        out_specs=(whole, block, block, line),
        compiler_params=pltpu.CompilerParams(vmem_limit_bytes=VMEM_BYTES),
    )(grad, up, down, before, act, rows)


def caption_grad_kernel(rows_ref, grad_ref, out_ref):
    out_ref[...] = low(dot_tn(rows_ref[...], grad_ref[...]))


def caption_grad(rows, grad):
    count, depth = rows.shape
    block = 512
    return pl.pallas_call(
        caption_grad_kernel,
        out_shape=jax.ShapeDtypeStruct((depth, grad.shape[1]), jnp.bfloat16),
        grid=(depth // block,),
        in_specs=[
            pl.BlockSpec((count, block), lambda j: (0, j)),
            pl.BlockSpec(grad.shape, lambda j: (0, 0)),
        ],
        out_specs=pl.BlockSpec((block, grad.shape[1]), lambda j: (j, 0)),
        compiler_params=pltpu.CompilerParams(vmem_limit_bytes=VMEM_BYTES),
    )(rows, grad)


def adamw(param, grad, first, second, rate, decay):
    first_new = beta_one * first + (1.0 - beta_one) * grad
    second_new = beta_two * second + (1.0 - beta_two) * grad * grad
    step_dir = (
        first_new
        / (1.0 - beta_one**STEP)
        / (jnp.sqrt(second_new / (1.0 - beta_two**STEP)) + adam_eps)
    )
    return (param - rate * (step_dir + decay * param), first_new, second_new)


def per_device(
    latents,
    noise,
    captions,
    image_sizes,
    caption_lengths,
    timesteps,
    weights,
    vectors,
    weights_m,
    weights_v,
    vectors_m,
    vectors_v,
):
    width = weights.shape[1]
    seq_count = lax.axis_size("seq")
    dp_count = lax.axis_size("dp")
    seq_index = lax.axis_index("seq")
    row_index = lax.axis_index("dp")
    devices = dp_count * seq_count
    layout = matrix_rows(width)
    shard_rows = weights.shape[0]
    paired = dp_count == 4 and seq_count == 8
    weights_low = weights.astype(jnp.bfloat16)
    if paired:
        shard = weights_low.reshape(shard_rows // UNIT, UNIT, width)
        rows_all, rows_late = gather_rows((0, 2176), (23, 19), 8, devices, 7, shard)
        flat = (-1, width)
        self_head = 384
        (
            time_one,
            time_two,
            time_block,
            text_one,
            text_two,
            joint_qkv,
            self_out_head,
        ) = split_rows(rows_all.reshape(flat), layout[:6] + (self_head,))
    else:
        gathered = lax.all_gather(weights_low, both_axes, axis=0, tiled=True)
        (
            time_one,
            time_two,
            time_block,
            text_one,
            text_two,
            joint_qkv,
            self_out,
            cross_query,
            cross_kv,
            cross_out,
            mlp_up,
            mlp_down,
        ) = split_rows(gathered, layout)
    (
        table,
        final_table,
        patch_in,
        patch_out,
        b_patch,
        b_time_one,
        b_time_two,
        b_block,
        b_text_one,
        b_text_two,
        b_query,
        b_value,
        b_self_out,
        b_cross_query,
        b_cross_value,
        b_cross_out,
        b_up,
        b_down,
    ) = split_rows(vectors.astype(jnp.bfloat16).astype(jnp.float32), vector_rows(width))
    head_dim = width // HEADS
    heads = HEADS // seq_count
    part = heads * head_dim
    images = image_sizes.shape[2]
    slots = latents.shape[2]
    assert slots == BLOCK and images == seq_count
    rows = MICRO * slots
    wide = (MICRO, slots, width)
    image_count = jnp.sum((image_sizes > 0).astype(jnp.float32))
    loss_scale = 1.0 / image_count

    ends_all = jnp.cumsum(image_sizes, axis=2)
    firsts = jnp.arange(seq_count, dtype=jnp.int32) * BLOCK
    segment_all = jnp.sum(
        (ends_all[:, :, None, :] <= firsts[None, None, :, None]).astype(jnp.int32), axis=3
    )
    onehot_all = (
        segment_all[:, :, :, None] == jnp.arange(images, dtype=jnp.int32)[None, None, None, :]
    )
    size_all = jnp.sum(jnp.where(onehot_all, image_sizes[:, :, None, :], 0), axis=3)
    start_all = jnp.sum(jnp.where(onehot_all, (ends_all - image_sizes)[:, :, None, :], 0), axis=3)
    step_all = jnp.sum(jnp.where(onehot_all, timesteps[:, :, None, :], 0), axis=3)
    length_all = jnp.sum(jnp.where(onehot_all, caption_lengths[:, :, None, :], 0), axis=3)
    row_start = start_all[:, row_index]
    row_size = size_all[:, row_index]
    kv_start = row_start // BLOCK
    kv_big = (row_size == LARGE).astype(jnp.int32)
    own_segment = segment_all[:, row_index, seq_index]
    own_size = row_size[:, seq_index]
    own_start = row_start[:, seq_index]
    own_step = step_all[:, row_index, seq_index]
    own_length = length_all[:, row_index, seq_index]

    quarter = width // 4
    omega = 1.0 / 10000.0 ** (jnp.arange(quarter, dtype=jnp.float32) / quarter)
    angle = jnp.arange(2 * SIDE, dtype=jnp.float32)[:, None] * omega[None, :]
    angle_table = jnp.concatenate([jnp.sin(angle), jnp.cos(angle)], axis=1)
    within = (
        seq_index * BLOCK - own_start[:, None] + jnp.arange(slots, dtype=jnp.int32)[None, :]
    ).reshape(rows)
    side = jnp.where(own_size == LARGE, 2 * SIDE, SIDE).astype(jnp.int32)
    side = jnp.broadcast_to(side[:, None], (MICRO, slots)).reshape(rows)
    places = jnp.arange(2 * SIDE, dtype=jnp.int32)[None, :]
    pick_row = ((within // side)[:, None] == places).astype(jnp.float32)
    pick_col = ((within % side)[:, None] == places).astype(jnp.float32)
    position = jnp.concatenate(
        [
            jnp.dot(pick_row, angle_table, precision=exact),
            jnp.dot(pick_col, angle_table, precision=exact),
        ],
        axis=1,
    )

    level = noise_level(own_step)[:, None, None]
    level_prev = noise_level(own_step - 1)[:, None, None]
    beta_log, tilde_log = variance_logs(level, level_prev)
    target = noise[:, 0].astype(jnp.float32)
    noisy = jnp.sqrt(level) * latents[:, 0].astype(jnp.float32) + jnp.sqrt(1.0 - level) * target
    noisy = noisy.reshape(rows, PATCH)

    time_low = low(time_features(own_step))
    time_first = dot_nn(time_low, time_one) + b_time_one
    time_act, time_act_back = jax.vjp(jax.nn.silu, time_first)
    time_act_low = low(time_act)
    time_embed = dot_nn(time_act_low, time_two) + b_time_two
    embed_act, embed_act_back = jax.vjp(jax.nn.silu, time_embed)
    embed_low = low(embed_act)
    block_mod = dot_nt(embed_low, time_block) + b_block.reshape(1, -1) + table.reshape(1, -1)
    shift_one, scale_one, gate_one, shift_two, scale_two, gate_two = [
        piece[:, None, :] for piece in jnp.split(block_mod, 6, axis=1)
    ]
    shift_final = (final_table[0][None, :] + time_embed)[:, None, :]
    scale_final = (final_table[1][None, :] + time_embed)[:, None, :]

    hidden_zero = (jnp.dot(noisy, patch_in, precision=exact) + b_patch + position).reshape(wide)
    normed_one, mod_one_back = jax.vjp(modulate, hidden_zero, shift_one, scale_one)
    normed_one_low = low(normed_one).reshape(rows, width)
    joint_bias = jnp.concatenate([b_query, jnp.zeros_like(b_query), b_value], axis=0)
    joint_bias = jnp.transpose(joint_bias.reshape(3, seq_count, part), (1, 0, 2))
    qkv = joint_forward(normed_one_low, joint_qkv, joint_bias.reshape(seq_count, 1, 3 * part))
    caption_low = captions[:, 0].reshape(MICRO * CAP, TEXT_W)
    caption_first = dot_nn(caption_low, text_one) + b_text_one
    caption_act, caption_act_back = jax.vjp(gelu_tanh, caption_first)
    caption_act_low = low(caption_act)
    text = dot_nn(caption_act_low, text_two) + b_text_two
    lengths_slot = lax.dynamic_slice_in_dim(caption_lengths[:, row_index], seq_index, 1, 1)
    token_live = (jnp.arange(CAP, dtype=jnp.int32)[None, :] < lengths_slot).astype(jnp.float32)
    lengths_slot_float = lengths_slot.astype(jnp.float32)
    caption_pool = (
        jnp.sum(text.reshape(MICRO, CAP, width) * token_live[:, :, None], axis=1) / lengths_slot_float
    )
    text_own = low(text)
    if paired:
        qkv, text_own, rows_late = lax.optimization_barrier((qkv, text_own, rows_late))
    qkv = lax.all_to_all(qkv, "seq", split_axis=0, concat_axis=0, tiled=True)
    text_all = lax.all_gather(text_own.reshape(MICRO, CAP, width), "seq", axis=0)
    if paired:
        rows_late, words_all = spread_rows(rows_late, caption_pool.reshape(-1, 128), devices, 8)
        qkv, rows_late = lax.optimization_barrier((qkv, rows_late))
        rows_late = rows_late.reshape(flat)
        self_out_tail, cross_query, cross_kv, cross_out = split_rows(
            rows_late, (layout[6] - self_head,) + layout[7:10]
        )
        up_start = (layout[6] - self_head + sum(layout[7:10])) // FEED_BLOCK
        feed_weights = (rows_late, up_start, rows_late, up_start + FF // FEED_BLOCK)
    else:
        feed_weights = (mlp_up, 0, mlp_down, 0)
    if paired:
        self_out = jnp.concatenate([self_out_head, self_out_tail], axis=0)
    qkv = qkv.reshape(seq_count, MICRO, slots, 3 * part)
    mixed = self_forward(kv_start, kv_big, qkv, heads, head_dim)
    mixed = lax.all_to_all(
        mixed.reshape(seq_count, rows, part), "seq", split_axis=0, concat_axis=0, tiled=True
    )
    mixed_low = jnp.transpose(mixed, (1, 0, 2)).reshape(rows, width)
    attended = (dot_nn(mixed_low, self_out) + b_self_out).reshape(wide)
    hidden_one = hidden_zero + gate_one * attended

    text_low = jnp.concatenate(
        [
            lax.dynamic_slice(text_all, (own_segment[m], m, 0, 0), (1, 1, CAP, width))[0, 0]
            for m in range(MICRO)
        ],
        axis=0,
    )
    text_kv = dot_nt(text_low, cross_kv)
    pad_rows = ((0, 0), (0, CAP_PAD - CAP), (0, 0))
    key_text = jnp.pad(low(text_kv[:, :width]).reshape(MICRO, CAP, width), pad_rows)
    value_text = jnp.pad(
        low(text_kv[:, width:] + b_cross_value).reshape(MICRO, CAP, width), pad_rows
    )
    hidden_one_low = low(hidden_one).reshape(rows, width)
    query_cross = low(dot_nn(hidden_one_low, cross_query) + b_cross_query).reshape(wide)
    cross_low = cross_call(
        functools.partial(cross_forward_kernel, head_dim),
        own_length,
        (query_cross, key_text, value_text),
        jax.ShapeDtypeStruct(wide, jnp.bfloat16),
    ).reshape(rows, width)
    hidden_two = hidden_one + (dot_nn(cross_low, cross_out) + b_cross_out).reshape(wide)
    normed_two, mod_two_back = jax.vjp(modulate, hidden_two, shift_two, scale_two)
    normed_two_low = low(normed_two).reshape(rows, width)
    upward, upward_low, feed = feed_forward(normed_two_low, *feed_weights, b_up, b_down)
    feed = feed.reshape(wide)
    hidden_three = hidden_two + gate_two * feed
    final_normed, final_back = jax.vjp(modulate, hidden_three, shift_final, scale_final)
    final_flat = final_normed.reshape(rows, width)
    predicted = jnp.dot(final_flat, patch_out.T, precision=exact).reshape(MICRO, slots, 2 * PATCH)
    error = predicted[:, :, :PATCH] - target
    frac = (predicted[:, :, PATCH:] + 1.0) * 0.5
    model_log = frac * beta_log + (1.0 - frac) * tilde_log
    ratio = jnp.exp(tilde_log - model_log)
    spread = 0.5 * (model_log - tilde_log - 1.0 + ratio) / log_two
    error_weight = (1.0 / (float(PATCH) * own_size.astype(jnp.float32)))[:, None, None]
    squared_loss = jnp.sum((error * error + spread) * error_weight)

    pooled = jnp.sum(final_normed, axis=1)
    if paired:
        pooled_all = share(pooled.reshape(-1, 128), devices, 1)
    else:
        pooled_all = lax.all_gather(pooled, both_axes, axis=0)
        words_all = lax.all_gather(caption_pool, both_axes, axis=0)
    each = (devices, MICRO, width)
    pooled_all = jnp.concatenate([pooled_all.reshape(each), words_all.reshape(each)], axis=1)
    pooled_all = jnp.transpose(pooled_all, (1, 0, 2))
    size_float = jnp.maximum(image_sizes.astype(jnp.float32), 1.0)
    pick = onehot_all.astype(jnp.float32) / size_float[:, :, None, :]
    same_row = jnp.eye(dp_count, dtype=jnp.float32)
    pick = jnp.einsum("mrsi,rq->mriqs", pick, same_row, precision=exact).reshape(
        MICRO, dp_count * images, devices
    )
    valid = (image_sizes > 0).astype(jnp.float32).reshape(MICRO, dp_count * images)
    grad_pool, grad_caption, contrast_value = contrast(pooled_all, pick, valid, loss_scale)
    contrast_value = contrast_value[0, 0]
    own_pool = row_index * images + own_segment
    grad_pool_own = jnp.concatenate(
        [lax.dynamic_slice(grad_pool, (m, own_pool[m], 0), (1, 1, width))[0] for m in range(MICRO)]
    ) / own_size.astype(jnp.float32)[:, None]
    grad_caption = lax.dynamic_slice_in_dim(
        grad_caption, row_index * images + seq_index, 1, 1
    )[:, 0]

    grad_spread = 0.5 * (1.0 - ratio) / log_two * 0.5 * (beta_log - tilde_log)
    grad_predicted = (
        loss_scale * error_weight * jnp.concatenate([2.0 * error, grad_spread], axis=2)
    ).reshape(rows, 2 * PATCH)
    grad_final = grad_pool_own[:, None, :] + jnp.dot(
        grad_predicted, patch_out, precision=exact
    ).reshape(wide)
    grad_patch_out = lax.dot_general(
        grad_predicted, final_flat, (((0,), (0,)), ((), ())), precision=exact
    )
    grad_three, grad_shift_final, grad_scale_final = final_back(grad_final)
    grad_shift_final = grad_shift_final[:, 0]
    grad_scale_final = grad_scale_final[:, 0]
    grad_final_table = jnp.stack([grad_shift_final.sum(axis=0), grad_scale_final.sum(axis=0)])
    grad_embed = grad_shift_final + grad_scale_final

    grad_feed = (grad_three * gate_two).reshape(rows, width)
    grad_feed_low = low(grad_feed)
    grad_normed_two, weight_up, weight_down, grad_b_up = feed_backward(
        grad_feed_low, *feed_weights, upward, upward_low, normed_two_low
    )
    grad_two_mod, grad_shift_two, grad_scale_two = mod_two_back(grad_normed_two.reshape(wide))
    grad_gate_two = jnp.sum(grad_three * feed, axis=1, keepdims=True)
    grad_two = grad_three + grad_two_mod
    grad_two_flat = grad_two.reshape(rows, width)
    grad_two_low = low(grad_two_flat)
    weight_cross_out = dot_tn(cross_low, grad_two_low)
    grad_cross_low = low(dot_nt(grad_two_low, cross_out)).reshape(wide)
    padded = jax.ShapeDtypeStruct((MICRO, CAP_PAD, width), jnp.float32)
    grad_query_cross, grad_key_text, grad_value_text = cross_call(
        functools.partial(cross_backward_kernel, head_dim),
        own_length,
        (query_cross, key_text, value_text, grad_cross_low),
        (jax.ShapeDtypeStruct(wide, jnp.float32), padded, padded),
    )
    grad_query_cross = grad_query_cross.reshape(rows, width)
    grad_query_low = low(grad_query_cross)
    weight_cross_query = dot_tn(hidden_one_low, grad_query_low)
    grad_one = grad_two + dot_nt(grad_query_low, cross_query).reshape(wide)

    grad_kv = jnp.concatenate([grad_key_text[:, :CAP], grad_value_text[:, :CAP]], axis=2).reshape(
        MICRO * CAP, 2 * width
    )
    grad_kv_low = low(grad_kv)
    weight_cross_kv = dot_tn(grad_kv_low, text_low)
    grad_text_part = low(dot_nn(grad_kv_low, cross_kv)).reshape(MICRO, CAP, width)
    grad_text_all = lax.all_gather(grad_text_part, "seq", axis=0).astype(jnp.float32)
    mine = (segment_all[:, row_index] == seq_index).astype(jnp.float32)
    grad_text = jnp.sum(grad_text_all * jnp.transpose(mine)[:, :, None, None], axis=0) + (
        (grad_caption / lengths_slot_float)[:, None, :] * token_live[:, :, None]
    )
    grad_text = grad_text.reshape(MICRO * CAP, width)
    grad_text_low = low(grad_text)
    weight_text_two = dot_tn(caption_act_low, grad_text_low)
    grad_caption_first = caption_act_back(dot_nt(grad_text_low, text_two))[0]
    grad_caption_low = low(grad_caption_first)
    head_rows = TILE_START * UNIT - sum(layout[:3]) + TILE * UNIT // 2 if paired else 0
    weight_text_one = caption_grad(caption_low, grad_caption_low)

    grad_attended = (grad_one * gate_one).reshape(rows, width)
    grad_gate_one = jnp.sum(grad_one * attended, axis=1, keepdims=True)
    grad_attended_low = low(grad_attended)
    weight_self_out = dot_tn(mixed_low, grad_attended_low)
    grad_mixed = low(dot_nt(grad_attended_low, self_out)).reshape(rows, seq_count, part)
    grad_mixed = jnp.transpose(grad_mixed, (1, 0, 2))
    if paired:
        weight_up, weight_down, grad_mixed = lax.optimization_barrier(
            (low(weight_up), low(weight_down), grad_mixed)
        )
    grad_mixed = lax.all_to_all(grad_mixed, "seq", split_axis=0, concat_axis=0, tiled=True)
    if paired:
        summed_feed = reduce_rows(
            ((19, 31),), shard_rows // UNIT, devices, 2, ((weight_up, 0, 12), (weight_down, 0, 12))
        )
        grad_mixed, summed_feed = lax.optimization_barrier((grad_mixed, summed_feed))
    grad_mixed = grad_mixed.reshape(seq_count, MICRO, slots, part)
    grad_qkv, head_sums = self_backward(kv_start, kv_big, qkv, grad_mixed, heads, head_dim)
    head_sums = jnp.sum(head_sums[:, 0], axis=0)
    column = seq_index * part
    grad_bias_query = lax.dynamic_update_slice(
        jnp.zeros((width,), jnp.float32), head_sums[:part], (column,)
    )
    grad_bias_value = lax.dynamic_update_slice(
        jnp.zeros((width,), jnp.float32), head_sums[part:], (column,)
    )
    grad_qkv = grad_qkv.reshape(seq_count, rows, 3 * part)
    if paired:
        time_rows = layout[0] + layout[1]
        block_rows = layout[2]
        weight_self_out = low(weight_self_out)
        first_half = jnp.pad(weight_text_one[:head_rows], ((TILE * UNIT // 2 - head_rows, 0), (0, 0)))
        (
            first_half,
            weight_text_one,
            weight_text_two,
            weight_self_out,
            weight_cross_query,
            weight_cross_kv,
            weight_cross_out,
            grad_qkv,
        ) = lax.optimization_barrier(
            (
                first_half,
                low(weight_text_one),
                low(weight_text_two),
                weight_self_out,
                low(weight_cross_query),
                low(weight_cross_kv),
                low(weight_cross_out),
                grad_qkv,
            )
        )
    grad_qkv = lax.all_to_all(
        grad_qkv, "seq", split_axis=0, concat_axis=0, tiled=True
    )
    if paired:
        summed_middle = reduce_rows(
            ((0, 7), (12, 19)),
            shard_rows // UNIT,
            devices,
            3,
            (
                (first_half, 0, 1),
                (weight_text_one, head_rows // UNIT, 10),
                (weight_text_two, 0, 3),
                (weight_self_out, TILE // 2, 2),
                (weight_cross_query, 0, 3),
                (weight_cross_kv, 0, 6),
                (weight_cross_out, 0, 3),
            ),
        )
        grad_qkv, summed_middle = lax.optimization_barrier((grad_qkv, summed_middle))
    grad_normed_one, weight_joint = joint_backward(grad_qkv, joint_qkv, normed_one_low)
    grad_zero_mod, grad_shift_one, grad_scale_one = mod_one_back(grad_normed_one.reshape(wide))
    grad_zero = (grad_one + grad_zero_mod).reshape(rows, width)
    grad_patch_in = lax.dot_general(noisy, grad_zero, (((0,), (0,)), ((), ())), precision=exact)

    grad_mod = jnp.concatenate(
        [grad_shift_one, grad_scale_one, grad_gate_one, grad_shift_two, grad_scale_two, grad_gate_two],
        axis=1,
    )
    grad_table = jnp.sum(grad_mod, axis=0)
    grad_mod_low = low(grad_mod.reshape(MICRO, 6 * width))
    weight_block = dot_tn(grad_mod_low, embed_low)
    grad_embed = grad_embed + embed_act_back(dot_nn(grad_mod_low, time_block))[0]
    grad_embed_low = low(grad_embed)
    weight_time_two = dot_tn(time_act_low, grad_embed_low)
    grad_time_first = time_act_back(dot_nt(grad_embed_low, time_two))[0]
    weight_time_one = dot_tn(time_low, low(grad_time_first))

    grad_vector = jnp.concatenate(
        [
            grad_table,
            grad_final_table,
            grad_patch_in,
            grad_patch_out,
            jnp.sum(grad_zero, axis=0)[None, :],
            jnp.sum(grad_time_first, axis=0)[None, :],
            jnp.sum(grad_embed, axis=0)[None, :],
            grad_table,
            jnp.sum(grad_caption_first, axis=0)[None, :],
            jnp.sum(grad_text, axis=0)[None, :],
            grad_bias_query[None, :],
            grad_bias_value[None, :],
            jnp.sum(grad_attended, axis=0)[None, :],
            jnp.sum(grad_query_cross, axis=0)[None, :],
            jnp.sum(grad_kv[:, width:], axis=0)[None, :],
            jnp.sum(grad_two_flat, axis=0)[None, :],
            grad_b_up.reshape(-1, width),
            jnp.sum(grad_feed, axis=0)[None, :],
            jnp.full((2, width), squared_loss),
        ],
        axis=0,
    )
    if paired:
        tile_size = UNIT * 128
        tile_count = -(-grad_vector.size // (tile_size * devices))
        parts = jnp.pad(
            grad_vector.reshape(-1), (0, tile_count * tile_size * devices - grad_vector.size)
        ).reshape(devices, tile_count, UNIT, 128)
        holders = -(-(time_rows + block_rows) // shard_rows)
        own_grads = jnp.concatenate(
            [grad_mod_low, grad_embed_low, low(grad_time_first), embed_low, time_act_low, time_low],
            axis=1,
        )
        summed_joint, grads_all, vector_got = reduce_rows(
            ((7, 12),),
            shard_rows // UNIT,
            devices,
            4,
            ((low(weight_joint), 0, 9), (weight_self_out, 0, 1)),
            (own_grads.reshape(-1, 128), parts),
            holders,
        )
        vector_part = jnp.sum(vector_got, axis=0)
        grads_all = jnp.where(device_index() < holders, grads_all, 0)
        grads_all = grads_all.reshape(devices * MICRO, -1)
        ends = [6 * width, 7 * width, 8 * width, 9 * width, 10 * width]
        grad_block_all, grad_two_all, grad_one_all, embed_all, act_all, features_all = jnp.split(
            grads_all, ends, axis=1
        )
        first_row = device_index() * shard_rows

        def own_columns(array, start):
            stop = start + array.shape[1]
            spread = jnp.pad(array, ((0, 0), (start, shard_rows + (-stop) % shard_rows)))
            place = jnp.minimum(first_row, spread.shape[1] - shard_rows)
            return lax.dynamic_slice(spread, (0, place), (array.shape[0], shard_rows))

        summed_time = (
            dot_tn(own_columns(features_all, 0), grad_one_all)
            + dot_tn(own_columns(act_all, layout[0]), grad_two_all)
            + dot_tn(own_columns(grad_block_all, time_rows), embed_all)
        )
        row = first_row + jnp.arange(shard_rows, dtype=jnp.int32)
        tile = ((row - TILE_START * UNIT) // (TILE * UNIT))[:, None]
        flat = (shard_rows, width)
        reduced = jnp.where(
            tile >= 19,
            summed_feed.reshape(flat),
            jnp.where(
                (tile >= 7) & (tile < 12), summed_joint.reshape(flat), summed_middle.reshape(flat)
            ),
        ).astype(jnp.float32)
        summed = jnp.where(row[:, None] < time_rows + block_rows, summed_time, reduced)
    else:
        grad_weights = jnp.concatenate(
            [
                low(piece)
                for piece in (
                    weight_time_one,
                    weight_time_two,
                    weight_block,
                    weight_text_one,
                    weight_text_two,
                    weight_joint,
                    weight_self_out,
                    weight_cross_query,
                    weight_cross_kv,
                    weight_cross_out,
                    weight_up,
                    weight_down,
                )
            ],
            axis=0,
        )
        summed = lax.psum_scatter(
            grad_weights, both_axes, scatter_dimension=0, tiled=True
        ).astype(jnp.float32)
    squares = jnp.sum(summed * summed)
    if paired:
        last = jnp.concatenate([vector_part, jnp.full((1, UNIT, 128), squares)], axis=0)
        last = share(last, devices, 6)
        squares_all = jnp.sum(last[:, -1, 0, 0])
        grad_vectors = last[:, :-1].reshape(-1)[: grad_vector.size].reshape(grad_vector.shape)
    else:
        grad_vectors, squares_all = lax.psum((grad_vector, squares), both_axes)
    loss_sum = grad_vectors[vectors.shape[0], 0] + contrast_value
    grad_vectors = grad_vectors[: vectors.shape[0]]
    down_bias_grad = grad_vectors[grad_vectors.shape[0] - 1]
    grad_norm = jnp.sqrt(squares_all + jnp.sum(grad_vectors * grad_vectors))
    factor = jnp.minimum(1.0, clip_norm / (grad_norm + 1e-06))
    new_w, first_w, second_w = adamw(
        weights, summed * factor, weights_m, weights_v, rate_matrix, weight_decay
    )
    new_v, first_v, second_v = adamw(
        vectors, grad_vectors * factor, vectors_m, vectors_v, rate_vector, 0.0
    )
    return (
        new_w,
        first_w,
        second_w,
        new_v,
        first_v,
        second_v,
        loss_sum,
        image_count,
        grad_norm,
        down_bias_grad,
    )


def solution(mesh):
    shard = P(both_axes, None)
    data = P(None, "dp", "seq", None)
    return jax.shard_map(
        per_device,
        mesh=mesh,
        in_specs=(data, data, data, P(), P(), P(), shard, P(), shard, shard, P(), P()),
        out_specs=(shard, shard, shard, P(), P(), P(), P(), P(), P(), P()),
        check_vma=False,
    )
```
